32 devices in a mesh: dp: 8 (over z, x), mlp: 4 (over y, core).
Axes of the slice: x: 2, y: 2, z: 4, core: 2. Of those that a mesh axis runs over, the one named last changes fastest.
Arguments:
- clean_patches: float32 [8192, 16], P(('dp', 'mlp')), may hold values from -6 to 6
- noise_patches: float32 [8192, 16], P(('dp', 'mlp')), may hold values from -6 to 6
- patch_grid: int32 [32, 2], P(('dp', 'mlp')), may hold values from 1 to 16, as said below
- labels: int32 [32], P(('dp', 'mlp')), may hold values from 0 to 1000
- timesteps: int32 [32], P(('dp', 'mlp')), may hold values from 20 to 999
- matrices: float32 [1152, 15008], P('dp'), may hold values from -0.94280904 to 0.94280904
- embeddings: float32 [1273, 1152], P(None, 'dp'), may hold values from -4 to 4
- swiglu_weights: float32 [3, 1152, 3072], P(None, 'dp', 'mlp'), may hold values from -0.1875 to 0.1875
- biases: float32 [17312], replicated, may hold values from -1 to 3
- matrices_first: float32 [1152, 15008], P('dp'), may hold values from -0.00012207031 to 0.00012207031
- embeddings_first: float32 [1273, 1152], P(None, 'dp'), may hold values from -0.00012207031 to 0.00012207031
- swiglu_first: float32 [3, 1152, 3072], P(None, 'dp', 'mlp'), may hold values from -0.00012207031 to 0.00012207031
- biases_first: float32 [17312], replicated, may hold values from -0.00030517578 to 0.00030517578
- matrices_second: float32 [1152, 15008], P('dp'), may hold values from 3.4025345e-11 to 1.3610138e-10
- embeddings_second: float32 [1273, 1152], P(None, 'dp'), may hold values from 3.4025345e-11 to 1.3610138e-10
- swiglu_second: float32 [3, 1152, 3072], P(None, 'dp', 'mlp'), may hold values from 3.4025345e-11 to 1.3610138e-10
- biases_second: float32 [17312], replicated, may hold values from 2.7220276e-10 to 1.088811e-09
- matrices_average: float32 [1152, 15008], P('dp'), may hold values from -0.1875 to 0.1875
- embeddings_average: float32 [1273, 1152], P(None, 'dp'), may hold values from -3 to 3
- swiglu_average: float32 [3, 1152, 3072], P(None, 'dp', 'mlp'), may hold values from -0.1875 to 0.1875
- biases_average: float32 [17312], replicated, may hold values from -1.75 to 1.75
Outputs:
- loss_sum: float32 [], replicated
- grad_norm: float32 [], replicated
- matrices_new: float32 [1152, 15008], P('dp')
- embeddings_new: float32 [1273, 1152], P(None, 'dp')
- swiglu_new: float32 [3, 1152, 3072], P(None, 'dp', 'mlp')
- biases_new: float32 [17312], replicated
- matrices_first_new: float32 [1152, 15008], P('dp')
- embeddings_first_new: float32 [1273, 1152], P(None, 'dp')
- swiglu_first_new: float32 [3, 1152, 3072], P(None, 'dp', 'mlp')
- biases_first_new: float32 [17312], replicated
- matrices_second_new: float32 [1152, 15008], P('dp')
- embeddings_second_new: float32 [1273, 1152], P(None, 'dp')
- swiglu_second_new: float32 [3, 1152, 3072], P(None, 'dp', 'mlp')
- biases_second_new: float32 [17312], replicated
- matrices_average_new: float32 [1152, 15008], P('dp')
- embeddings_average_new: float32 [1273, 1152], P(None, 'dp')
- swiglu_average_new: float32 [3, 1152, 3072], P(None, 'dp', 'mlp')
- biases_average_new: float32 [17312], replicated
- biases_grad: float32 [17312], replicated
The draws below stay inside these ranges and needn't reach their ends.
Inputs may be any that keep to these rules, and one draw needn't show every extreme that they name: `patch_grid`: patch rows and columns of each image; the last image of the batch is 16 x 16. `labels`: label 1000 is the null class.
All inputs are finite; a program needn't handle non-finite values.
Results may differ from the reference program's by a relative error of at most 0.012.
Values may be sent and summed in bfloat16 or wider, within the bound.
A program may use at most 320 MiB of HBM per device.

```python
import math
import jax
import jax.numpy as jnp
from jax import lax

HEADS = 16
HDIM = 72
D = 1152
FF = 3072
CH = 16
CLASSES = 1000
FREQ = 256
SIDE = 16
SEQ = 256
IMG_DEV = 1
STEP = 10
IMAGES = 32
TOKENS = 8192
NPARAM = 29389856


def draw_patch_grid(key, part):
    key = jax.random.fold_in(key, 1)
    image_index = jnp.arange(IMAGES, dtype=jnp.int32)
    owner = image_index // IMG_DEV
    spots = IMAGES // IMG_DEV
    upper = SIDE // 2 + (SIDE - SIDE // 2) * owner // max(1, spots - 1)
    lower = jnp.maximum(1, upper - upper // 3)
    key_rows, key_cols = jax.random.split(key)
    grid_rows = jax.random.randint(key_rows, (IMAGES,), lower, upper + 1)
    grid_cols = jax.random.randint(key_cols, (IMAGES,), lower, upper + 1)
    final_image = image_index == IMAGES - 1
    grid_rows = jnp.where(final_image, SIDE, grid_rows)
    grid_cols = jnp.where(final_image, SIDE, grid_cols)
    return jnp.stack([grid_rows, grid_cols], axis=1).astype(jnp.int32)


def base_draw(key, shape):
    return jax.random.truncated_normal(key, -4.0, 4.0, shape, jnp.float32)


def draw_matrices(key, part):
    key = jax.random.fold_in(key, 2)
    width = 13 * D + 2 * CH
    column = jnp.arange(width)
    scale_by = jnp.where(column < D, 1.0, 0.3)
    scale_by = jnp.where(column >= 9 * D, 0.6, scale_by)
    scale_by = jnp.where(column >= 12 * D, 0.5 * SEQ ** 0.5, scale_by)
    scale_by = jnp.where(column >= 13 * D, 1.0, scale_by)
    return base_draw(key, (D, width)) * scale_by[None, :] / D ** 0.5


def draw_embeddings(key, part):
    key = jax.random.fold_in(key, 3)
    height = CH + FREQ + CLASSES + 1
    row_index = jnp.arange(height)
    scale_by = jnp.where(row_index < CH, CH ** (-0.5), jnp.where(row_index < CH + FREQ, 1.4 * FREQ ** (-0.5), 1.0))
    return base_draw(key, (height, D)) * scale_by[:, None]


def draw_biases(key, part):
    key = jax.random.fold_in(key, 4)
    length = 15 * D + 2 * CH
    spot = jnp.arange(length)
    within = (spot % D).astype(jnp.float32) / D
    rising = (spot >= 4 * D) & (spot < 5 * D) | (spot >= 7 * D) & (spot < 8 * D) | (spot >= 10 * D) & (spot < 11 * D)
    gating = (spot >= 5 * D) & (spot < 6 * D) | (spot >= 8 * D) & (spot < 9 * D)
    base = 0.2 * base_draw(key, (length,))
    return jnp.where(rising, base + 2.0 * within, jnp.where(gating, base + 1.0, base))


def place_ends(drawn, own_key, smallest, top_value):
    extent = drawn.shape
    spot = [jax.random.randint(jax.random.fold_in(own_key, axis), (), 0, extent[axis]) for axis in range(len(extent))]
    drawn = drawn.at[tuple(spot)].set(smallest)
    longest = extent.index(max(extent))
    spot[longest] = (spot[longest] + 1) % extent[longest]
    return drawn.at[tuple(spot)].set(top_value)


def level_of(stream_key, dims, cuts, smallest, high):
    loudness, own = 1.0, jax.random.fold_in(stream_key, 6)
    for position, blocks in cuts:
        heights = jnp.exp(jax.random.uniform(jax.random.fold_in(own, position), (blocks,), jnp.float32, smallest / len(cuts), high / len(cuts)))
        loudness = loudness * jnp.repeat(heights, dims[position] // blocks).reshape([-1 if axis == position else 1 for axis in range(len(dims))])
    return loudness


def bell_draw(key, extent, spread, bound, shards=(), kind=jnp.bfloat16):
    level = level_of(key, extent, shards, -0.22, 0.18) if shards else 1.0
    result = jax.random.normal(key, extent, jnp.float32) * spread * level
    return jnp.minimum(jnp.maximum(result, -bound), bound).astype(kind)


def setup_inputs(seed: int = 0) -> dict:
    streams_of = jax.random.split(jax.random.key(seed), 22)
    return {
        "clean_patches": bell_draw(streams_of[0], (TOKENS, CH), 1.0, 6.0, ((0, 32),), jnp.float32),
        "noise_patches": bell_draw(streams_of[1], (TOKENS, CH), 1.0, 6.0, ((0, 32),), jnp.float32),
        "patch_grid": draw_patch_grid(jax.random.fold_in(streams_of[21], 71), 0),
        "labels": place_ends(jax.random.randint(streams_of[3], (IMAGES,), 0, CLASSES + 1), jax.random.fold_in(streams_of[3], 1), 0, CLASSES).astype(jnp.int32),
        "timesteps": place_ends(jax.random.randint(streams_of[4], (IMAGES,), 20, 1000), jax.random.fold_in(streams_of[4], 1), 20, 999).astype(jnp.int32),
        "matrices": draw_matrices(jax.random.fold_in(streams_of[21], 71), 0),
        "embeddings": draw_embeddings(jax.random.fold_in(streams_of[21], 71), 0),
        "swiglu_weights": bell_draw(streams_of[7], (3, D, FF), D ** -0.5, 0.1875, ((1, 8), (2, 4)), jnp.float32),
        "biases": draw_biases(jax.random.fold_in(streams_of[21], 71), 0),
        "matrices_first": bell_draw(streams_of[9], (D, 13 * D + 2 * CH), (0.111 / NPARAM ** 0.5), 0.00012207031, ((0, 8),), jnp.float32),
        "embeddings_first": bell_draw(streams_of[10], (CH + FREQ + CLASSES + 1, D), (0.111 / NPARAM ** 0.5), 0.00012207031, ((1, 8),), jnp.float32),
        "swiglu_first": bell_draw(streams_of[11], (3, D, FF), (0.111 / NPARAM ** 0.5), 0.00012207031, ((1, 8), (2, 4)), jnp.float32),
        "biases_first": bell_draw(streams_of[12], (15 * D + 2 * CH,), (0.3 / NPARAM ** 0.5), 0.00030517578, (), jnp.float32),
        "matrices_second": jnp.clip(jnp.exp(math.log(1.3610138016595386e-10) - 1.3862944 * jax.random.uniform(streams_of[13], (D, 13 * D + 2 * CH), jnp.float32) ** level_of(streams_of[13], (D, 13 * D + 2 * CH), ((0, 8),), -0.2, 0.2)), 3.4025345041488464e-11, 1.3610138016595386e-10),
        "embeddings_second": jnp.clip(jnp.exp(math.log(1.3610138016595386e-10) - 1.3862944 * jax.random.uniform(streams_of[14], (CH + FREQ + CLASSES + 1, D), jnp.float32) ** level_of(streams_of[14], (CH + FREQ + CLASSES + 1, D), ((1, 8),), -0.2, 0.2)), 3.4025345041488464e-11, 1.3610138016595386e-10),
        "swiglu_second": jnp.clip(jnp.exp(math.log(1.3610138016595386e-10) - 1.3862944 * jax.random.uniform(streams_of[15], (3, D, FF), jnp.float32) ** level_of(streams_of[15], (3, D, FF), ((1, 8), (2, 4)), -0.2, 0.2)), 3.4025345041488464e-11, 1.3610138016595386e-10),
        "biases_second": jnp.clip(jnp.exp(jax.random.uniform(streams_of[16], (15 * D + 2 * CH,), jnp.float32, math.log(2.722027603319077e-10), math.log(1.0888110413276308e-09))), 2.722027603319077e-10, 1.0888110413276308e-09),
        "matrices_average": bell_draw(streams_of[17], (D, 13 * D + 2 * CH), D ** -0.5, 0.1875, ((0, 8),), jnp.float32),
        "embeddings_average": bell_draw(streams_of[18], (CH + FREQ + CLASSES + 1, D), 0.5, 3.0, ((1, 8),), jnp.float32),
        "swiglu_average": bell_draw(streams_of[19], (3, D, FF), D ** -0.5, 0.1875, ((1, 8), (2, 4)), jnp.float32),
        "biases_average": bell_draw(streams_of[20], (15 * D + 2 * CH,), 0.3, 1.75, (), jnp.float32),
    }


@jax.custom_vjp
def low(v):
    return lax.optimization_barrier(v.astype(jnp.bfloat16)).astype(jnp.float32)

@jax.custom_vjp
def low_back(v):
    return v

def low_keep(v):
    return (low(v), None)

def low_pass(kept, grad):
    return (grad,)

def back_keep(v):
    return (v, None)

def back_low(kept, grad):
    return (low(grad),)
low.defvjp(low_keep, low_pass)
low_back.defvjp(back_keep, back_low)
CLIP_LIMIT = 1.0
LEARN_RATE = 0.03
TABLE_RATE = 0.4
FIRST_DECAY = 0.9
SECOND_DECAY = 0.999
ADAM_EPSILON = 1e-08
WEIGHT_DECAY = 0.01
AVERAGE_DECAY = 0.9999

def product(left, right):
    return jnp.dot(left, right, precision=lax.Precision.HIGHEST, preferred_element_type=jnp.float32)

def plan(steps_in):
    step_index = jnp.arange(1000, dtype=jnp.int32)
    beta_table = 0.0001 + (0.02 - 0.0001) * step_index.astype(jnp.float32) / 999.0
    logbar = jnp.cumsum(jnp.log1p(-beta_table))

    def lookup(values, wanted):
        return lax.optimization_barrier(jnp.sum(jnp.where(wanted[:, None] == step_index[None, :], values[None, :], 0.0), axis=1))
    return (lookup(beta_table, steps_in), jnp.exp(lookup(logbar, steps_in)), jnp.exp(lookup(logbar, steps_in - 1)))

def sinusoid(steps_in):
    halfway = FREQ // 2
    frequency = jnp.exp(-math.log(10000.0) * jnp.arange(halfway, dtype=jnp.float32) / halfway)
    angles = steps_in.astype(jnp.float32)[:, None] * frequency[None, :]
    return jnp.concatenate([jnp.cos(angles), jnp.sin(angles)], axis=1)

def places(patch_grid, length):
    slot_index = jnp.arange(length, dtype=jnp.int32)[None, :]
    grid_rows = patch_grid[:, 0:1]
    grid_cols = patch_grid[:, 1:2]
    valid_slot = slot_index < grid_rows * grid_cols
    row_place = (slot_index // grid_cols).astype(jnp.float32)
    col_place = (slot_index % grid_cols).astype(jnp.float32)
    quarter = HDIM // 4
    frequency = jnp.exp(-math.log(10000.0) * jnp.arange(quarter, dtype=jnp.float32) / quarter)
    row_angle = row_place[..., None] * frequency
    col_angle = col_place[..., None] * frequency
    return ((jnp.cos(row_angle), jnp.sin(row_angle), jnp.cos(col_angle), jnp.sin(col_angle)), valid_slot)

def rotate(values, tables):
    cos_row, sin_row, cos_col, sin_col = tables
    quarter = HDIM // 4

    def turn(halfpart, cosine, sine_part):
        first = halfpart[..., :quarter]
        second = halfpart[..., quarter:]
        cosine = cosine[:, :, None, :]
        sine_part = sine_part[:, :, None, :]
        return jnp.concatenate([first * cosine - second * sine_part, first * sine_part + second * cosine], axis=-1)
    return jnp.concatenate([turn(values[..., :2 * quarter], cos_row, sin_row), turn(values[..., 2 * quarter:], cos_col, sin_col)], axis=-1)

def modulate(hidden, shift_by, scale_by):
    row_mean = lax.optimization_barrier(jnp.mean(hidden, axis=-1, keepdims=True))
    centered = hidden - row_mean
    variance = lax.optimization_barrier(jnp.mean(centered * centered, axis=-1, keepdims=True))
    return centered * lax.rsqrt(variance + 1e-06) * (1.0 + scale_by[:, None, :]) + shift_by[:, None, :]

def noisy_input(clean_patches, noise_patches, steps_in):
    beta_now, bar_now, bar_prev = plan(steps_in)
    bar_now = bar_now[:, None, None]
    return jnp.sqrt(bar_now) * clean_patches + jnp.sqrt(1.0 - bar_now) * noise_patches

def loss_terms(output, clean_patches, noise_patches, steps_in, valid_slot):
    beta_now, bar_now, bar_prev = plan(steps_in)
    beta_now = beta_now[:, None, None]
    bar_now = bar_now[:, None, None]
    bar_prev = bar_prev[:, None, None]
    noisy = jnp.sqrt(bar_now) * clean_patches + jnp.sqrt(1.0 - bar_now) * noise_patches
    eps_pred = output[..., :CH]
    var_raw = output[..., CH:]
    squared = lax.optimization_barrier(jnp.sum((eps_pred - noise_patches) ** 2, axis=-1))
    post_log = jnp.log(beta_now * (1.0 - bar_prev) / (1.0 - bar_now))
    fraction = (var_raw + 1.0) * 0.5
    model_log = fraction * jnp.log(beta_now) + (1.0 - fraction) * post_log
    coefficient = beta_now * jnp.sqrt(bar_prev) / (1.0 - bar_now)
    start_est = (noisy - jnp.sqrt(1.0 - bar_now) * eps_pred) / jnp.sqrt(bar_now)
    mean_gap = coefficient * (clean_patches - start_est)
    divergence = 0.5 * (-1.0 + model_log - post_log + jnp.exp(post_log - model_log) + mean_gap * mean_gap * jnp.exp(-model_log)) / math.log(2.0)
    return jnp.sum(jnp.where(valid_slot, squared + lax.optimization_barrier(jnp.sum(divergence, axis=-1)), 0.0))

def adam_step(weight, first, second, gradient, average, factor, rate):
    average_decay = min(AVERAGE_DECAY, (1.0 + STEP) / (10.0 + STEP))
    clipped = gradient * factor
    first = FIRST_DECAY * first + (1.0 - FIRST_DECAY) * clipped
    second = SECOND_DECAY * second + (1.0 - SECOND_DECAY) * clipped * clipped
    ratio = first / (1.0 - FIRST_DECAY ** STEP) / (jnp.sqrt(second / (1.0 - SECOND_DECAY ** STEP)) + ADAM_EPSILON)
    weight = weight - rate * (ratio + WEIGHT_DECAY * weight)
    return (weight, first, second, average_decay * average + (1.0 - average_decay) * weight)

def block_loss(params, block_data):
    matrices, embeddings, swiglu_weights, biases = params
    clean_patches, noise_patches, patch_grid, labels, steps_in = block_data
    matrices = low(matrices)
    embeddings = low(embeddings)
    swiglu_weights = low(swiglu_weights)
    images = labels.shape[0]
    time_second = matrices[:, :D]
    mod_weight = matrices[:, D:9 * D]
    qkv_weight = matrices[:, 9 * D:12 * D]
    out_weight = matrices[:, 12 * D:13 * D]
    final_weight = matrices[:, 13 * D:]
    patch_weight = embeddings[:CH]
    time_first = embeddings[CH:CH + FREQ]
    class_table = embeddings[CH + FREQ:]
    patch_bias = biases[:D]
    first_bias = biases[D:2 * D]
    second_bias = biases[2 * D:3 * D]
    mod_bias = biases[3 * D:11 * D]
    qkv_bias = biases[11 * D:14 * D]
    out_bias = biases[14 * D:15 * D]
    final_bias = biases[15 * D:]
    sinus_emb = low(sinusoid(steps_in))
    time_pre = product(sinus_emb, time_first) + first_bias
    time_emb = low_back(product(low(jax.nn.silu(time_pre)), time_second) + second_bias)
    onehot = (labels[:, None] == jnp.arange(CLASSES + 1, dtype=jnp.int32)[None, :]).astype(jnp.float32)
    condition = time_emb + product(onehot, class_table)
    modulation = low_back(product(low(jax.nn.silu(condition)), mod_weight) + mod_bias)
    shift_one, scale_one, gate_one, shift_two, scale_two, gate_two, shift_end, scale_end = jnp.split(modulation, 8, axis=1)
    tables, valid_slot = places(patch_grid, SEQ)
    clean_patches = clean_patches.reshape(images, SEQ, CH)
    noise_patches = noise_patches.reshape(images, SEQ, CH)
    hidden = low_back(product(low(noisy_input(clean_patches, noise_patches, steps_in)), patch_weight) + patch_bias)
    normed_one = low(modulate(hidden, shift_one, scale_one))
    qkv = low_back(product(normed_one, qkv_weight) + qkv_bias).reshape(images, SEQ, 3, HEADS, HDIM)
    queries = low(rotate(qkv[:, :, 0], tables))
    keys_in = low(rotate(qkv[:, :, 1], tables))
    values = low(qkv[:, :, 2])
    scores = low_back(jnp.einsum('bqhd,bkhd->bhqk', queries, keys_in, precision=lax.Precision.HIGHEST) / math.sqrt(HDIM))
    masked = jnp.where(valid_slot[:, None, None, :], scores, -1e+30)
    row_max = lax.optimization_barrier(jnp.max(masked, axis=-1, keepdims=True))
    exponent = jnp.exp(masked - row_max)
    attn_probs = exponent / lax.optimization_barrier(jnp.sum(exponent, axis=-1, keepdims=True))
    attended = low_back(low(jnp.einsum('bhqk,bkhd->bqhd', low(attn_probs), values, precision=lax.Precision.HIGHEST))).reshape(images, SEQ, D)
    branch = low_back(product(attended, out_weight) + out_bias)
    hidden_mid = hidden + gate_one[:, None, :] * branch
    normed_two = low(modulate(hidden_mid, shift_two, scale_two))
    gate_val = low_back(product(normed_two, swiglu_weights[0]))
    up_val = low_back(product(normed_two, swiglu_weights[1]))
    inner_act = low(jax.nn.silu(gate_val) * up_val)
    mixed = low_back(jnp.einsum('bsf,df->bsd', inner_act, swiglu_weights[2], precision=lax.Precision.HIGHEST))
    hidden_end = hidden_mid + gate_two[:, None, :] * mixed
    normed_end = low(modulate(hidden_end, shift_end, scale_end))
    output = low_back(product(normed_end, final_weight) + final_bias)
    return loss_terms(output, clean_patches, noise_patches, steps_in, valid_slot)

def reference(clean_patches, noise_patches, patch_grid, labels, timesteps, matrices, embeddings, swiglu_weights, biases, matrices_first, embeddings_first, swiglu_first, biases_first, matrices_second, embeddings_second, swiglu_second, biases_second, matrices_average, embeddings_average, swiglu_average, biases_average):
    block_size = math.gcd(IMAGES, max(1, 4096 // SEQ))
    block_count = IMAGES // block_size
    stacked = (clean_patches.reshape(block_count, block_size, SEQ, CH), noise_patches.reshape(block_count, block_size, SEQ, CH), patch_grid.reshape(block_count, block_size, 2), labels.reshape(block_count, block_size), timesteps.reshape(block_count, block_size))

    def total_loss(params):

        def scan_step(running, block_data):
            return (running + jax.checkpoint(block_loss)(params, block_data), None)
        summed, unused = lax.scan(scan_step, jnp.zeros((), jnp.float32), stacked)
        return summed
    params = (matrices, embeddings, swiglu_weights, biases)
    loss_sum, pull_back = jax.vjp(total_loss, params)
    gradients = pull_back(jnp.asarray(1.0 / IMAGES, jnp.float32))[0]
    grad_norm = jnp.sqrt(sum((jnp.sum(entry * entry) for entry in gradients)))
    factor = jnp.minimum(1.0, CLIP_LIMIT / grad_norm)
    mats_out = adam_step(matrices, matrices_first, matrices_second, gradients[0], matrices_average, factor, LEARN_RATE)
    embed_out = adam_step(embeddings, embeddings_first, embeddings_second, gradients[1], embeddings_average, factor, TABLE_RATE)
    swiglu_out = adam_step(swiglu_weights, swiglu_first, swiglu_second, gradients[2], swiglu_average, factor, LEARN_RATE)
    bias_out = adam_step(biases, biases_first, biases_second, gradients[3], biases_average, factor, TABLE_RATE)
    return (loss_sum, grad_norm, mats_out[0], embed_out[0], swiglu_out[0], bias_out[0], mats_out[1], embed_out[1], swiglu_out[1], bias_out[1], mats_out[2], embed_out[2], swiglu_out[2], bias_out[2], mats_out[3], embed_out[3], swiglu_out[3], bias_out[3], gradients[3] * factor)
```

```python
import functools
import math

import jax
import jax.numpy as jnp
from jax import lax
from jax.experimental import pallas as pl
from jax.experimental.pallas import tpu as pltpu
from jax.sharding import PartitionSpec as P

HEADS = 16
HDIM = 72
D = 1152
CH = 16
CLASSES = 1000
FREQ = 256
STEP = 10


CLIP_LIMIT = 1.0
LEARN_RATE = 0.03
TABLE_RATE = 0.4
FIRST_DECAY = 0.9
SECOND_DECAY = 0.999
ADAM_EPSILON = 1e-08
WEIGHT_DECAY = 0.01
AVERAGE_DECAY = 0.9999


def plan(steps_in):
    step_index = jnp.arange(1000, dtype=jnp.int32)
    beta_table = 0.0001 + (0.02 - 0.0001) * step_index.astype(jnp.float32) / 999.0
    logbar = jnp.cumsum(jnp.log1p(-beta_table))

    def lookup(values, wanted):
        return jnp.sum(
            jnp.where(wanted[:, None] == step_index[None, :], values[None, :], 0.0), axis=1
        )

    return (
        lookup(beta_table, steps_in),
        jnp.exp(lookup(logbar, steps_in)),
        jnp.exp(lookup(logbar, steps_in - 1)),
    )


def sinusoid(steps_in):
    halfway = FREQ // 2
    frequency = jnp.exp(-math.log(10000.0) * jnp.arange(halfway, dtype=jnp.float32) / halfway)
    angles = steps_in.astype(jnp.float32)[:, None] * frequency[None, :]
    return jnp.concatenate([jnp.cos(angles), jnp.sin(angles)], axis=1)


def modulate(hidden, shift_by, scale_by):
    row_mean = jnp.mean(hidden, axis=-1, keepdims=True)
    centered = hidden - row_mean
    variance = jnp.mean(centered * centered, axis=-1, keepdims=True)
    return (
        centered * lax.rsqrt(variance + 1e-06) * (1.0 + scale_by[:, None, :]) + shift_by[:, None, :]
    )


def noisy_input(clean_patches, noise_patches, steps_in):
    beta_now, bar_now, bar_prev = plan(steps_in)
    bar_now = bar_now[:, None, None]
    return jnp.sqrt(bar_now) * clean_patches + jnp.sqrt(1.0 - bar_now) * noise_patches


def loss_terms(output, clean_patches, noise_patches, steps_in, valid_slot):
    beta_now, bar_now, bar_prev = plan(steps_in)
    beta_now = beta_now[:, None, None]
    bar_now = bar_now[:, None, None]
    bar_prev = bar_prev[:, None, None]
    noisy = jnp.sqrt(bar_now) * clean_patches + jnp.sqrt(1.0 - bar_now) * noise_patches
    eps_pred = output[..., :CH]
    var_raw = output[..., CH:]
    squared = jnp.sum((eps_pred - noise_patches) ** 2, axis=-1)
    post_log = jnp.log(beta_now * (1.0 - bar_prev) / (1.0 - bar_now))
    fraction = (var_raw + 1.0) * 0.5
    model_log = fraction * jnp.log(beta_now) + (1.0 - fraction) * post_log
    coefficient = beta_now * jnp.sqrt(bar_prev) / (1.0 - bar_now)
    start_est = (noisy - jnp.sqrt(1.0 - bar_now) * eps_pred) / jnp.sqrt(bar_now)
    mean_gap = coefficient * (clean_patches - start_est)
    divergence = (
        0.5
        * (
            -1.0
            + model_log
            - post_log
            + jnp.exp(post_log - model_log)
            + mean_gap * mean_gap * jnp.exp(-model_log)
        )
        / math.log(2.0)
    )
    return jnp.sum(jnp.where(valid_slot, squared + jnp.sum(divergence, axis=-1), 0.0))


def adam_step(weight, first, second, gradient, average, factor, rate):
    average_decay = min(AVERAGE_DECAY, (1.0 + STEP) / (10.0 + STEP))
    clipped = gradient * factor
    first = FIRST_DECAY * first + (1.0 - FIRST_DECAY) * clipped
    second = SECOND_DECAY * second + (1.0 - SECOND_DECAY) * clipped * clipped
    ratio = (
        first
        / (1.0 - FIRST_DECAY**STEP)
        / (jnp.sqrt(second / (1.0 - SECOND_DECAY**STEP)) + ADAM_EPSILON)
    )
    weight = weight - rate * (ratio + WEIGHT_DECAY * weight)
    return (weight, first, second, average_decay * average + (1.0 - average_decay) * weight)


def backward_product(gradient, weight):
    return lax.dot_general(
        gradient,
        weight,
        (((gradient.ndim - 1,), (1,)), ((), ())),
        preferred_element_type=jnp.float32,
    )


def weight_grad(inputs, gradient):
    flat_in = inputs.reshape(-1, inputs.shape[-1])
    flat_grad = gradient.reshape(-1, gradient.shape[-1])
    return lax.dot_general(
        flat_in, flat_grad, (((0,), (0,)), ((), ())), preferred_element_type=jnp.float32
    )


def column_sum(gradient):
    return jnp.sum(gradient.astype(jnp.float32).reshape(-1, gradient.shape[-1]), axis=0)


def cut_columns(values, start, amount):
    return lax.dynamic_slice_in_dim(values, start, amount, 1)


MESH_IDS = pl.DeviceIdType.MESH
KERNEL_VMEM = 48 * 2**20


def exchange_kernel(axes, sizes, modes, *refs):
    count = len(modes)
    ins, outs = refs[:count], refs[count : 2 * count]
    send_sem, recv_sem = refs[2 * count :]
    if axes == "dp":
        total = sizes[0]
        me = lax.axis_index("dp")
    else:
        total = sizes[0] * sizes[1]
        me = lax.axis_index("dp") * sizes[1] + lax.axis_index("mlp")

    def device(spot):
        if axes == "dp":
            return (spot, lax.axis_index("mlp"))
        return (lax.div(spot, sizes[1]), lax.rem(spot, sizes[1]))

    barrier = pltpu.get_barrier_semaphore()

    def greet(step, carry):
        pl.semaphore_signal(
            barrier, inc=1, device_id=device(lax.rem(me + step, total)), device_id_type=MESH_IDS
        )
        return carry

    lax.fori_loop(1, total, greet, 0)
    pl.semaphore_wait(barrier, total - 1)

    def make(item, step):
        peer = lax.rem(me + step, total)
        source = ins[item].at[peer] if modes[item] == "each" else ins[item]
        return pltpu.make_async_remote_copy(
            src_ref=source,
            dst_ref=outs[item].at[me],
            send_sem=send_sem.at[item, step - 1],
            recv_sem=recv_sem.at[item, step - 1],
            device_id=device(peer),
            device_id_type=MESH_IDS,
        )

    def begin(step, carry):
        for item in range(count):
            make(item, step).start()
        return carry

    lax.fori_loop(1, total, begin, 0)
    for item in range(count):
        if modes[item] == "each":
            outs[item][me] = ins[item][me]
        else:
            outs[item][me] = ins[item][...]

    def finish(step, carry):
        for item in range(count):
            make(item, step).wait()
        return carry

    lax.fori_loop(1, total, finish, 0)


def exchange(items, axes, sizes, collective):
    total = sizes[0] if axes == "dp" else sizes[0] * sizes[1]
    modes = tuple(mode for _, mode in items)
    arrays = [array for array, _ in items]
    shapes = [
        jax.ShapeDtypeStruct(
            array.shape if mode == "each" else (total, *array.shape), array.dtype
        )
        for array, mode in items
    ]
    space = pl.BlockSpec(memory_space=pltpu.VMEM)
    return pl.pallas_call(
        functools.partial(exchange_kernel, axes, sizes, modes),
        out_shape=shapes,
        in_specs=[space] * len(items),
        out_specs=[space] * len(items),
        scratch_shapes=[
            pltpu.SemaphoreType.DMA((len(items), total - 1)),
            pltpu.SemaphoreType.DMA((len(items), total - 1)),
        ],
        compiler_params=pltpu.CompilerParams(
            collective_id=collective, has_side_effects=True, vmem_limit_bytes=KERNEL_VMEM
        ),
    )(*arrays)


def place_kernel(targets, *refs):
    pieces, out, sem = refs[:-2], refs[-2], refs[-1]
    copies = []
    for spot, (piece, target) in enumerate(zip(pieces, targets)):
        copy = pltpu.make_async_copy(piece, target(out), sem.at[spot])
        copy.start()
        copies.append(copy)
    for copy in copies:
        copy.wait()


def place(pieces, targets, shape, dtype):
    return pl.pallas_call(
        functools.partial(place_kernel, targets),
        out_shape=jax.ShapeDtypeStruct(shape, dtype),
        in_specs=[pl.BlockSpec(memory_space=pl.ANY)] * len(pieces),
        out_specs=pl.BlockSpec(memory_space=pl.ANY),
        scratch_shapes=[pltpu.SemaphoreType.DMA((len(pieces),))],
        compiler_params=pltpu.CompilerParams(vmem_limit_bytes=KERNEL_VMEM),
    )(*pieces)


NX = 2


def ring_pairs(depth, shift):
    return [
        (z * NX + x, ((z + shift) % depth) * NX + x) for z in range(depth) for x in range(NX)
    ]


def swap_pairs(count):
    return [(spot, spot ^ 1) for spot in range(count)]


def ring_pieces(half, depth, shift):
    arrived = [half]
    for _ in range(depth - 1):
        arrived.append(lax.ppermute(arrived[-1], "dp", ring_pairs(depth, shift)))
    return arrived


def gather_dp(first, second, selects, shape, depth):
    swaps = swap_pairs(depth * NX)
    pieces, targets = [], []

    def source(step, shift, other):
        def spot():
            d = lax.axis_index("dp")
            z, x = lax.div(d, NX), lax.rem(d, NX)
            z = lax.rem(z - step * shift + depth * NX, depth)
            x = 1 - x if other else x
            return z * NX + x

        return spot

    for half, shift, select in ((first, 1, selects[0]), (second, -1, selects[1])):
        for step, piece in enumerate(ring_pieces(half, depth, shift)):
            other = lax.ppermute(piece, "dp", swaps)
            for swapped, value in ((False, piece), (True, other)):
                pieces.append(value)
                spot = source(step, shift, swapped)
                targets.append(functools.partial(lambda sel, at, out: sel(out, at()), select, spot))
    return place(pieces, targets, shape, first.dtype)


def reduce_ring(blocks, depth, shift):
    z = lax.div(lax.axis_index("dp"), NX)

    def block(offset):
        return lax.dynamic_index_in_dim(
            blocks, lax.rem(z + offset + 2 * depth, depth), 0, keepdims=False
        )

    running = block(-shift)
    for step in range(1, depth):
        arrived = lax.ppermute(running.astype(jnp.bfloat16), "dp", ring_pairs(depth, shift))
        running = arrived.astype(jnp.float32) + block(-shift * (step + 1))
    return running


def reduce_dp(value, count, cut):
    if count != 8:
        return lax.psum_scatter(
            value.astype(jnp.bfloat16), "dp", scatter_dimension=0, tiled=True
        )[0].astype(jnp.float32)
    depth = count // NX
    x = lax.rem(lax.axis_index("dp"), NX)
    paired = value.reshape(depth, NX, *value.shape[1:])
    give = lax.dynamic_index_in_dim(paired, 1 - x, 1, keepdims=False).astype(jnp.bfloat16)
    got = lax.ppermute(give, "dp", swap_pairs(count)).astype(jnp.float32)
    blocks = lax.dynamic_index_in_dim(paired, x, 1, keepdims=False) + got
    return jnp.concatenate(
        [
            reduce_ring(blocks[:, :, :cut], depth, 1),
            reduce_ring(blocks[:, :, cut:], depth, -1),
        ],
        axis=1,
    )


def flip(value, bit, count):
    return lax.ppermute(value, "mlp", [(spot, spot ^ bit) for spot in range(count)])


def gather_rows(own, count):
    far = flip(own, 2, count)
    near = flip(own, 1, count)
    return own, near, far, flip(far, 1, count)


def scatter_rows(far_parts, near_parts, count):
    single = jnp.float32
    got = flip(far_parts[1], 1, count)
    far = flip((far_parts[0].astype(single) + got.astype(single)).astype(jnp.bfloat16), 2, count)
    near = flip(near_parts[1], 1, count)
    return near_parts[0].astype(single) + near.astype(single) + far.astype(single)


def out_pairs(depth, ranks, step, shift):
    pairs = []
    for rank in range(ranks):
        for x in range(NX):
            start = (rank + (step - 1) * shift) % depth
            stop = (rank + step * shift) % depth
            pairs.append(((start * NX + x) * ranks + rank, (stop * NX + x) * ranks + rank))
    return pairs


def gather_out(shard, sizes):
    n_data, n_model = sizes
    if n_data != 8 or n_model != 4:
        whole = lax.all_gather(shard, "dp", axis=0, tiled=True)
        height = D // n_model
        return lax.dynamic_slice_in_dim(whole, lax.axis_index("mlp") * height, height, 0)
    depth = n_data // NX
    d = lax.axis_index("dp")
    z, x = lax.div(d, NX), lax.rem(d, NX)
    mine = z == lax.axis_index("mlp")
    halves = []
    for part, shift in ((shard[:80], 1), (shard[80:], -1)):
        total = jnp.where(mine, part, jnp.zeros_like(part))
        moving = part
        for step in range(1, depth):
            moving = lax.ppermute(moving, ("dp", "mlp"), out_pairs(depth, n_model, step, shift))
            total = total + moving
        halves.append(total)
    own = jnp.concatenate(halves, axis=0)
    other = lax.ppermute(own, "dp", swap_pairs(n_data))
    low = jnp.where(x == 0, own, other)
    high = jnp.where(x == 0, other, own)
    return jnp.concatenate([low, high], axis=0)


def reduce_out(value, sizes):
    n_data, n_model = sizes
    single, bfloat = jnp.float32, jnp.bfloat16
    if n_data != 8 or n_model != 4:
        whole = jnp.zeros((D, D), single)
        whole = lax.dynamic_update_slice_in_dim(
            whole, value, lax.axis_index("mlp") * value.shape[0], 0
        )
        part = lax.psum_scatter(whole.astype(bfloat), "dp", scatter_dimension=0, tiled=True)
        return lax.psum(part.astype(single), "mlp")
    depth = n_data // NX
    d = lax.axis_index("dp")
    z, x = lax.div(d, NX), lax.rem(d, NX)
    mine = z == lax.axis_index("mlp")
    paired = value.reshape(NX, D // n_data, D)
    give = lax.dynamic_index_in_dim(paired, 1 - x, 0, keepdims=False).astype(bfloat)
    got = lax.ppermute(give, "dp", swap_pairs(n_data)).astype(single)
    blocks = lax.dynamic_index_in_dim(paired, x, 0, keepdims=False) + got
    halves = []
    for part, shift in ((blocks[:80], 1), (blocks[80:], -1)):
        running = part
        for step in range(1, depth):
            pairs = [
                (source, target)
                for source, target in out_pairs(depth, n_model, step + 1, shift)
            ]
            arrived = lax.ppermute(running.astype(bfloat), ("dp", "mlp"), pairs)
            running = arrived.astype(single) + part
        halves.append(running)
    summed = jnp.concatenate(halves, axis=0)
    shared = jnp.where(mine, summed, 0.0).astype(bfloat)
    shared = shared + flip(shared, 1, n_model)
    shared = shared + flip(shared, 2, n_model)
    return shared.astype(single)


def swapped(values):
    quarter = HDIM // 4
    return jnp.concatenate(
        [
            values[:, quarter : 2 * quarter],
            values[:, :quarter],
            values[:, 3 * quarter :],
            values[:, 2 * quarter : 3 * quarter],
        ],
        axis=1,
    )


def attention_kernel(heads, qkv_ref, cos_ref, sin_ref, mask_ref, low_ref, out_ref, total_ref):
    width = heads * HDIM
    cosine, sine, mask = cos_ref[0], sin_ref[0], mask_ref[0]
    totals = []
    for head in range(heads):
        start = head * HDIM

        def part(which):
            return qkv_ref[0, :, which * width + start : which * width + start + HDIM]

        raw_q, raw_k = part(0), part(1)
        query = (raw_q * cosine + swapped(raw_q) * sine).astype(jnp.bfloat16)
        key = (raw_k * cosine + swapped(raw_k) * sine).astype(jnp.bfloat16)
        value = part(2).astype(jnp.bfloat16)
        for which, kept in enumerate((query, key, value)):
            low_ref[0, :, which * width + start : which * width + start + HDIM] = kept
        scores = lax.dot_general(
            query, key, (((1,), (1,)), ((), ())), preferred_element_type=jnp.float32
        ) * (1.0 / math.sqrt(HDIM))
        scores = jnp.where(mask > 0.0, scores, -1e30)
        row_max = jnp.max(scores, axis=-1, keepdims=True)
        exponent = jnp.exp(scores - row_max)
        row_sum = jnp.sum(exponent, axis=-1, keepdims=True)
        probs = exponent / row_sum
        out_ref[0, :, start : start + HDIM] = jnp.dot(
            probs.astype(jnp.bfloat16), value, preferred_element_type=jnp.float32
        ).astype(jnp.bfloat16)
        totals.append(row_max + jnp.log(row_sum))
    total_ref[0] = jnp.concatenate(totals, axis=1)


def attention(qkv, cosine, sine, mask, heads):
    images, length, width = qkv.shape
    per_image = lambda *dims: pl.BlockSpec((1, *dims), lambda i: (i, 0, 0))
    return pl.pallas_call(
        functools.partial(attention_kernel, heads),
        grid=(images,),
        out_shape=[
            jax.ShapeDtypeStruct((images, length, width), jnp.bfloat16),
            jax.ShapeDtypeStruct((images, length, heads * HDIM), jnp.bfloat16),
            jax.ShapeDtypeStruct((images, length, heads), jnp.float32),
        ],
        in_specs=[
            per_image(length, width),
            per_image(length, HDIM),
            per_image(length, HDIM),
            per_image(1, length),
        ],
        out_specs=[
            per_image(length, width),
            per_image(length, heads * HDIM),
            per_image(length, heads),
        ],
        compiler_params=pltpu.CompilerParams(vmem_limit_bytes=KERNEL_VMEM),
    )(qkv, cosine, sine, mask)


def attention_back_kernel(
    heads, low_ref, total_ref, grad_ref, cos_ref, sin_ref, mask_ref, out_ref
):
    width = heads * HDIM
    scale_by = 1.0 / math.sqrt(HDIM)
    cosine, sine, mask = cos_ref[0], sin_ref[0], mask_ref[0]

    def contract(left, right, dims):
        return lax.dot_general(left, right, (dims, ((), ())), preferred_element_type=jnp.float32)

    for head in range(heads):
        start = head * HDIM

        def spot(which):
            return slice(which * width + start, which * width + start + HDIM)

        query, key, value = (low_ref[0, :, spot(which)] for which in range(3))
        grad = grad_ref[0, :, start : start + HDIM]
        scores = contract(query, key, ((1,), (1,))) * scale_by
        scores = jnp.where(mask > 0.0, scores, -1e30)
        probs = jnp.exp(scores - total_ref[0, :, head : head + 1])
        d_probs = contract(grad, value, ((1,), (1,)))
        row = jnp.sum(probs * d_probs, axis=-1, keepdims=True)
        d_scores = (probs * (d_probs - row)).astype(jnp.bfloat16)
        d_query = contract(d_scores, key, ((1,), (0,))) * scale_by
        d_key = contract(d_scores, query, ((0,), (0,))) * scale_by
        d_value = contract(probs.astype(jnp.bfloat16), grad, ((0,), (0,)))
        for which, turned in ((0, d_query), (1, d_key)):
            back = turned * cosine + swapped(turned * sine)
            out_ref[0, :, spot(which)] = back.astype(jnp.bfloat16)
        out_ref[0, :, spot(2)] = d_value.astype(jnp.bfloat16)


def attention_back(low, totals, grad, cosine, sine, mask, heads):
    images, length, width = low.shape
    per_image = lambda *dims: pl.BlockSpec((1, *dims), lambda i: (i, 0, 0))
    return pl.pallas_call(
        functools.partial(attention_back_kernel, heads),
        grid=(images,),
        out_shape=jax.ShapeDtypeStruct((images, length, width), jnp.bfloat16),
        in_specs=[
            per_image(length, width),
            per_image(length, heads),
            per_image(length, heads * HDIM),
            per_image(length, HDIM),
            per_image(length, HDIM),
            per_image(1, length),
        ],
        out_specs=per_image(length, width),
        compiler_params=pltpu.CompilerParams(vmem_limit_bytes=KERNEL_VMEM),
    )(low, totals, grad, cosine, sine, mask)


def turn_tables(patch_grid, length):
    slot_index = jnp.arange(length, dtype=jnp.int32)[None, :]
    grid_cols = patch_grid[:, 1:2]
    valid_slot = slot_index < patch_grid[:, 0:1] * grid_cols
    row_place = (slot_index // grid_cols).astype(jnp.float32)
    col_place = (slot_index % grid_cols).astype(jnp.float32)
    quarter = HDIM // 4
    frequency = jnp.exp(-math.log(10000.0) * jnp.arange(quarter, dtype=jnp.float32) / quarter)
    row_angle = row_place[..., None] * frequency
    col_angle = col_place[..., None] * frequency
    cos_row, sin_row = jnp.cos(row_angle), jnp.sin(row_angle)
    cos_col, sin_col = jnp.cos(col_angle), jnp.sin(col_angle)
    return (
        jnp.concatenate([cos_row, cos_row, cos_col, cos_col], axis=-1),
        jnp.concatenate([-sin_row, sin_row, -sin_col, sin_col], axis=-1),
        valid_slot.astype(jnp.float32)[:, None, :],
    )


def valid_slots(patch_grid, length):
    return jnp.arange(length, dtype=jnp.int32)[None, :] < patch_grid[:, 0:1] * patch_grid[:, 1:2]


def on_device(
    clean_patches,
    noise_patches,
    patch_grid,
    labels,
    timesteps,
    matrices,
    embeddings,
    swiglu_weights,
    biases,
    matrices_first,
    embeddings_first,
    swiglu_first,
    biases_first,
    matrices_second,
    embeddings_second,
    swiglu_second,
    biases_second,
    matrices_average,
    embeddings_average,
    swiglu_average,
    biases_average,
):
    bfloat = jnp.bfloat16
    single = jnp.float32
    images = labels.shape[0]
    length = clean_patches.shape[0] // images
    n_model = lax.axis_size("mlp")
    n_data = lax.axis_size("dp")
    sizes = (n_data, n_model)
    total_images = images * n_data * n_model
    rows = D // n_data
    owned_start = lax.axis_index("dp") * rows
    data_index = lax.axis_index("dp")
    model_index = lax.axis_index("mlp")
    heads = HEADS // n_model
    head_cols = heads * HDIM
    hidden_units = swiglu_weights.shape[2]

    qkv_shard = jnp.concatenate(
        [
            cut_columns(matrices, 9 * D + part * D + model_index * head_cols, head_cols)
            for part in range(3)
        ],
        axis=1,
    ).astype(bfloat)
    out_shard = matrices[:, 12 * D : 13 * D].astype(bfloat)
    swiglu_shard = swiglu_weights.astype(bfloat)
    if n_data == 8:
        depth = n_data // NX
        qkv_weight = gather_dp(
            qkv_shard[:80],
            qkv_shard[80:],
            (lambda out, at: out.at[at, 0:80], lambda out, at: out.at[at, 80:144]),
            (n_data, rows, 3 * head_cols),
            depth,
        ).reshape(D, 3 * head_cols)
        half = hidden_units // 2
        swiglu_use = gather_dp(
            swiglu_shard[:, :, :half],
            swiglu_shard[:, :, half:],
            (
                lambda out, at: out.at[:, at, :, 0:half],
                lambda out, at: out.at[:, at, :, half : 2 * half],
            ),
            (3, n_data, rows, hidden_units),
            depth,
        ).reshape(3, D, hidden_units)
    else:
        qkv_weight = lax.all_gather(qkv_shard, "dp", axis=0, tiled=True)
        swiglu_use = lax.all_gather(swiglu_shard, "dp", axis=1, tiled=True)
    out_weight = gather_out(out_shard, sizes)

    time_second = matrices[:, :D].astype(bfloat)
    mod_weight = matrices[:, D : 9 * D].astype(bfloat)
    time_first = embeddings[CH : CH + FREQ].astype(bfloat)
    class_table = embeddings[CH + FREQ :].astype(bfloat)
    patch_bias = biases[:D]
    first_bias = biases[D : 2 * D]
    second_bias = biases[2 * D : 3 * D]
    mod_bias = biases[3 * D : 11 * D]
    qkv_bias = biases[11 * D : 14 * D]
    out_bias = biases[14 * D : 15 * D]
    final_bias = biases[15 * D :]

    facts = jnp.concatenate([timesteps[:, None], labels[:, None], patch_grid], axis=1)
    facts = jnp.pad(facts, ((0, 8 - images), (0, 124)))
    (facts_all,) = exchange([(facts, "all")], "both", sizes, 0)
    facts_all = facts_all[:, 0, :4]
    steps_all, labels_all, grid_all = facts_all[:, 0], facts_all[:, 1], facts_all[:, 2:4]
    sinus_all = sinusoid(steps_all).astype(bfloat)
    first_bias_own = lax.dynamic_slice_in_dim(first_bias, owned_start, rows)
    second_bias_own = lax.dynamic_slice_in_dim(second_bias, owned_start, rows)
    time_pre = jnp.dot(sinus_all, time_first, preferred_element_type=single) + first_bias_own
    time_act = jax.nn.silu(time_pre).astype(bfloat)
    time_part = jnp.dot(time_act, time_second, preferred_element_type=single)
    small_shard = jnp.concatenate(
        [embeddings[:CH], matrices[:, 13 * D :].T], axis=0
    ).astype(bfloat)
    time_parts, small_all = exchange(
        [
            (time_part.reshape(total_images, n_data, rows).transpose(1, 0, 2), "each"),
            (small_shard, "all"),
        ],
        "dp",
        sizes,
        1,
    )
    small_all = small_all.transpose(1, 0, 2).reshape(3 * CH, D)
    patch_weight = small_all[:CH]
    final_weight = small_all[CH:].T
    time_emb = jnp.sum(time_parts, axis=0) + second_bias_own
    onehot = (labels_all[:, None] == jnp.arange(CLASSES + 1, dtype=jnp.int32)[None, :]).astype(
        bfloat
    )
    condition = time_emb + jnp.dot(onehot, class_table, preferred_element_type=single)
    cond_act = jax.nn.silu(condition).astype(bfloat)
    cond_rank = lax.dynamic_index_in_dim(
        cond_act.reshape(n_data, n_model, rows), model_index, 1, keepdims=False
    )
    mod_part = jnp.dot(cond_rank, mod_weight, preferred_element_type=single)
    (mod_parts,) = exchange(
        [(mod_part.reshape(n_data, 8, D), "each")],
        "dp",
        sizes,
        2,
    )
    modulation = jnp.sum(mod_parts, axis=0).reshape(1, 8 * D) + mod_bias
    shift_one, scale_one, gate_one, shift_two, scale_two, gate_two, shift_end, scale_end = (
        jnp.split(modulation, 8, axis=1)
    )

    group_grid = lax.dynamic_slice_in_dim(grid_all, data_index * n_model, n_model, 0)
    group_grid = jnp.stack(
        [
            lax.dynamic_index_in_dim(group_grid, model_index ^ rank, 0, keepdims=False)
            for rank in range(n_model)
        ]
    )
    cosine, sine, mask = turn_tables(group_grid, length)
    valid_slot = valid_slots(patch_grid, length)
    clean_three = clean_patches.reshape(images, length, CH)
    noise_three = noise_patches.reshape(images, length, CH)
    noisy_low = noisy_input(clean_three, noise_three, timesteps).astype(bfloat)
    hidden = jnp.dot(noisy_low, patch_weight, preferred_element_type=single) + patch_bias
    normed_one = modulate(hidden, shift_one, scale_one).astype(bfloat)
    one_rows = jnp.concatenate(gather_rows(normed_one.reshape(length, D), n_model), axis=0)
    qkv_bias_own = jnp.concatenate(
        [
            lax.dynamic_slice_in_dim(qkv_bias, part * D + model_index * head_cols, head_cols)
            for part in range(3)
        ]
    )
    qkv = jnp.dot(one_rows, qkv_weight, preferred_element_type=single) + qkv_bias_own
    low, attended, log_total = attention(
        qkv.reshape(n_model, length, 3 * head_cols), cosine, sine, mask, heads
    )
    attended_rows = attended.reshape(n_model * length, head_cols)
    branch_part = jnp.dot(attended_rows, out_weight, preferred_element_type=single).astype(bfloat)
    branch_part = branch_part.reshape(n_model, length, D)
    branch = (
        scatter_rows(
            (branch_part[2], branch_part[3]), (branch_part[0], branch_part[1]), n_model
        )[None]
        + out_bias
    )
    hidden_mid = hidden + gate_one[:, None, :] * branch
    normed_two = modulate(hidden_mid, shift_two, scale_two).astype(bfloat)

    two_rows = gather_rows(normed_two.reshape(length, D), n_model)
    two_halves = (
        jnp.concatenate(two_rows[:2], axis=0),
        jnp.concatenate(two_rows[2:], axis=0),
    )
    gates, ups, acts, parts = [], [], [], []
    for part in two_halves:
        gate_val = jnp.dot(part, swiglu_use[0], preferred_element_type=single)
        up_val = jnp.dot(part, swiglu_use[1], preferred_element_type=single)
        act = (jax.nn.silu(gate_val) * up_val).astype(bfloat)
        gates.append(gate_val)
        ups.append(up_val)
        acts.append(act)
        parts.append(backward_product(act, swiglu_use[2]).astype(bfloat).reshape(2, length, D))
    mixed = scatter_rows(parts[1], parts[0], n_model)[None]
    hidden_end = hidden_mid + gate_two[:, None, :] * mixed
    normed_end = modulate(hidden_end, shift_end, scale_end).astype(bfloat)
    output = jnp.dot(normed_end, final_weight, preferred_element_type=single) + final_bias
    local_loss, loss_pull = jax.vjp(
        lambda values_out: loss_terms(values_out, clean_three, noise_three, timesteps, valid_slot),
        output,
    )
    d_output = loss_pull(jnp.asarray(1.0 / total_images, single))[0].astype(bfloat)
    d_normed_end = backward_product(d_output, final_weight)
    unused, pull_end = jax.vjp(modulate, hidden_end, shift_end, scale_end)
    d_hidden_end, d_shift_end, d_scale_end = pull_end(d_normed_end)
    d_mixed = (gate_two[:, None, :] * d_hidden_end).astype(bfloat)
    d_gate_two = jnp.sum(mixed * d_hidden_end, axis=1)
    dmixed_rows = gather_rows(d_mixed.reshape(length, D), n_model)
    dmixed_halves = (
        jnp.concatenate(dmixed_rows[:2], axis=0),
        jnp.concatenate(dmixed_rows[2:], axis=0),
    )
    d_gates, d_ups, d_parts = [], [], []
    for part, gate_val, up_val in zip(dmixed_halves, gates, ups):
        d_inner = jnp.dot(part, swiglu_use[2], preferred_element_type=single)
        unused, pull_glu = jax.vjp(
            lambda gate_in, up_in: jax.nn.silu(gate_in) * up_in, gate_val, up_val
        )
        d_gate, d_up = pull_glu(d_inner)
        d_gate, d_up = d_gate.astype(bfloat), d_up.astype(bfloat)
        d_gates.append(d_gate)
        d_ups.append(d_up)
        d_parts.append(
            (backward_product(d_gate, swiglu_use[0]) + backward_product(d_up, swiglu_use[1]))
            .astype(bfloat)
            .reshape(2, length, D)
        )
    d_normed_two = scatter_rows(d_parts[1], d_parts[0], n_model)[None]
    rows_ready = jnp.concatenate(two_halves, axis=0)
    dmixed_ready = jnp.concatenate(dmixed_halves, axis=0)
    half = hidden_units // 2

    def owned(gradient, cut):
        return reduce_dp(gradient.reshape(n_data, rows, -1), n_data, cut)

    grad_swiglu = jnp.stack(
        [
            owned(weight_grad(rows_ready, jnp.concatenate(d_gates, axis=0)), half),
            owned(weight_grad(rows_ready, jnp.concatenate(d_ups, axis=0)), half),
            owned(weight_grad(dmixed_ready, jnp.concatenate(acts, axis=0)), half),
        ]
    )
    unused, pull_two = jax.vjp(modulate, hidden_mid, shift_two, scale_two)
    d_mid_part, d_shift_two, d_scale_two = pull_two(d_normed_two)
    d_hidden_mid = d_hidden_end + d_mid_part
    d_branch = (gate_one[:, None, :] * d_hidden_mid).astype(bfloat)
    d_gate_one = jnp.sum(branch * d_hidden_mid, axis=1)

    dbranch_rows = jnp.concatenate(gather_rows(d_branch.reshape(length, D), n_model), axis=0)
    d_attended = backward_product(dbranch_rows, out_weight).astype(bfloat)
    d_qkv = attention_back(
        low,
        log_total,
        d_attended.reshape(n_model, length, head_cols),
        cosine,
        sine,
        mask,
        heads,
    ).reshape(n_model * length, 3 * head_cols)
    grad_out = reduce_out(weight_grad(attended_rows, dbranch_rows), sizes)
    grad_qkv_own = owned(weight_grad(one_rows, d_qkv), 384)
    d_one_part = backward_product(d_qkv, qkv_weight).astype(bfloat).reshape(n_model, length, D)
    d_normed_one = scatter_rows(
        (d_one_part[2], d_one_part[3]), (d_one_part[0], d_one_part[1]), n_model
    )[None]
    unused, pull_one = jax.vjp(modulate, hidden, shift_one, scale_one)
    d_hidden_part, d_shift_one, d_scale_one = pull_one(d_normed_one)
    d_hidden = (d_hidden_mid + d_hidden_part).astype(bfloat)

    qkv_blocks = gather_rows(grad_qkv_own.astype(bfloat), n_model)
    qkv_stack = jnp.stack(qkv_blocks)
    qkv_stack = jnp.stack(
        [
            lax.dynamic_index_in_dim(qkv_stack, model_index ^ rank, 0, keepdims=False)
            for rank in range(n_model)
        ]
    ).astype(single)
    grad_qkv = (
        qkv_stack.reshape(n_model, rows, 3, head_cols).transpose(1, 2, 0, 3).reshape(rows, 3 * D)
    )

    d_modulation = jnp.concatenate(
        [
            d_shift_one,
            d_scale_one,
            d_gate_one,
            d_shift_two,
            d_scale_two,
            d_gate_two,
            d_shift_end,
            d_scale_end,
        ],
        axis=1,
    ).astype(bfloat)
    (dmod_all,) = exchange(
        [(d_modulation.reshape(16, D // 2), "all")], "both", sizes, 3
    )
    dmod_all = dmod_all.reshape(total_images, 8 * D)
    d_cond_act = backward_product(dmod_all, mod_weight)
    unused, pull_cond = jax.vjp(jax.nn.silu, condition)
    d_condition = pull_cond(d_cond_act)[0]
    d_time_emb = d_condition.astype(bfloat)
    (dtime_parts,) = exchange([(d_time_emb, "all")], "dp", sizes, 4)
    dtime_all = dtime_parts.transpose(1, 0, 2).reshape(total_images, D)
    d_time_act = backward_product(dtime_all, time_second)
    unused, pull_time = jax.vjp(jax.nn.silu, time_pre)
    d_time_pre = pull_time(d_time_act)[0]
    grad_time_second = weight_grad(time_act, dtime_all)
    grad_mod = weight_grad(cond_act, dmod_all)
    grad_time_first = jnp.dot(
        sinus_all.astype(single).T,
        d_time_pre,
        precision=lax.Precision.HIGHEST,
        preferred_element_type=single,
    )
    grad_table = jnp.dot(
        onehot.astype(single).T,
        d_condition,
        precision=lax.Precision.HIGHEST,
        preferred_element_type=single,
    )
    grad_final_patch = weight_grad(noisy_low, d_hidden)
    grad_final = weight_grad(normed_end, d_output)

    qkv_sums = column_sum(d_qkv).reshape(3, head_cols)
    qkv_bias_part = lax.dynamic_update_slice(
        jnp.zeros((3, D), single), qkv_sums, (0, model_index * head_cols)
    )
    local_sums = jnp.concatenate(
        [
            column_sum(d_hidden),
            qkv_bias_part.reshape(-1),
            column_sum(d_branch),
            column_sum(d_output),
            local_loss.reshape(1),
            jnp.zeros((95,), single),
            grad_final_patch.reshape(-1),
            grad_final.T.reshape(-1),
        ]
    )
    everyone = n_data * n_model
    chunk_rows = -(-local_sums.shape[0] // (everyone * 1024)) * 8
    local_sums = jnp.pad(local_sums, (0, everyone * chunk_rows * 128 - local_sums.shape[0]))
    (sum_parts,) = exchange(
        [(local_sums.reshape(everyone, chunk_rows, 128), "each")], "both", sizes, 5
    )
    chunk = jnp.sum(sum_parts, axis=0)
    local_squares = (
        jnp.sum(grad_time_second * grad_time_second)
        + jnp.sum(grad_mod * grad_mod)
        + jnp.sum(grad_out * grad_out)
        + jnp.sum(grad_time_first * grad_time_first)
        + jnp.sum(grad_table * grad_table)
    ) / n_model + jnp.sum(grad_swiglu * grad_swiglu) + jnp.sum(grad_qkv_own * grad_qkv_own)
    extra = jnp.concatenate([jnp.sum(d_time_pre, axis=0), local_squares.reshape(1)])
    extra = jnp.pad(extra, (0, 1024 - extra.shape[0])).reshape(8, 128)
    (late,) = exchange([(jnp.concatenate([chunk, extra], axis=0), "all")], "both", sizes, 6)
    sums = late[:, :chunk_rows].reshape(-1)
    extras = late[:, chunk_rows:].reshape(everyone, 1024)
    first_bias_grad = extras.reshape(n_data, n_model, 1024)[:, 0, :rows].reshape(D)
    squares = jnp.sum(extras[:, rows])
    ends = [D, 4 * D, 5 * D, 5 * D + 2 * CH, 5 * D + 2 * CH + 1]
    base = 5 * D + 128
    loss_sum = sums[5 * D + 2 * CH]
    grad_patch = sums[base : base + CH * D].reshape(CH, D)
    grad_final = sums[base + CH * D : base + 3 * CH * D].reshape(2 * CH, D)
    grad_patch = cut_columns(grad_patch, owned_start, rows)
    grad_final_own = cut_columns(grad_final, owned_start, rows).T
    grad_bias = jnp.concatenate(
        [
            sums[:D],
            first_bias_grad,
            column_sum(dtime_all),
            column_sum(dmod_all),
            sums[D : 4 * D],
            sums[4 * D : 5 * D],
            sums[5 * D : 5 * D + 2 * CH],
        ]
    )
    shared = sums[base : base + 3 * CH * D]
    squares = squares + jnp.sum(grad_bias * grad_bias) + jnp.sum(shared * shared)
    grad_norm = jnp.sqrt(squares)
    factor = jnp.minimum(1.0, CLIP_LIMIT / grad_norm)
    grad_mats = jnp.concatenate(
        [grad_time_second, grad_mod, grad_qkv, grad_out, grad_final_own], axis=1
    )
    grad_embed = jnp.concatenate([grad_patch, grad_time_first, grad_table], axis=0)
    mats_out = adam_step(
        matrices, matrices_first, matrices_second, grad_mats, matrices_average, factor, LEARN_RATE
    )
    embed_out = adam_step(
        embeddings,
        embeddings_first,
        embeddings_second,
        grad_embed,
        embeddings_average,
        factor,
        TABLE_RATE,
    )
    swiglu_out = adam_step(
        swiglu_weights, swiglu_first, swiglu_second, grad_swiglu, swiglu_average, factor, LEARN_RATE
    )
    bias_out = adam_step(
        biases, biases_first, biases_second, grad_bias, biases_average, factor, TABLE_RATE
    )
    return (
        loss_sum,
        grad_norm,
        mats_out[0],
        embed_out[0],
        swiglu_out[0],
        bias_out[0],
        mats_out[1],
        embed_out[1],
        swiglu_out[1],
        bias_out[1],
        mats_out[2],
        embed_out[2],
        swiglu_out[2],
        bias_out[2],
        mats_out[3],
        embed_out[3],
        swiglu_out[3],
        bias_out[3],
        grad_bias * factor,
    )


def solution(mesh):
    placed = (
        P(("dp", "mlp"), None),
        P(("dp", "mlp"), None),
        P(("dp", "mlp"), None),
        P(("dp", "mlp")),
        P(("dp", "mlp")),
        P("dp", None),
        P(None, "dp"),
        P(None, "dp", "mlp"),
        P(),
        P("dp", None),
        P(None, "dp"),
        P(None, "dp", "mlp"),
        P(),
        P("dp", None),
        P(None, "dp"),
        P(None, "dp", "mlp"),
        P(),
        P("dp", None),
        P(None, "dp"),
        P(None, "dp", "mlp"),
        P(),
    )
    return jax.shard_map(
        on_device,
        mesh=mesh,
        in_specs=placed,
        out_specs=(
            P(),
            P(),
            P("dp", None),
            P(None, "dp"),
            P(None, "dp", "mlp"),
            P(),
            P("dp", None),
            P(None, "dp"),
            P(None, "dp", "mlp"),
            P(),
            P("dp", None),
            P(None, "dp"),
            P(None, "dp", "mlp"),
            P(),
            P("dp", None),
            P(None, "dp"),
            P(None, "dp", "mlp"),
            P(),
            P(),
        ),
        check_vma=False,
    )
```

```python
import functools
import math

import jax
import jax.numpy as jnp
from jax import lax
from jax.experimental import pallas as pl
from jax.experimental.pallas import tpu as pltpu
from jax.sharding import PartitionSpec as P

HEADS = 16
HDIM = 72
D = 1152
CH = 16
CLASSES = 1000
FREQ = 256
STEP = 10


CLIP_LIMIT = 1.0
LEARN_RATE = 0.03
TABLE_RATE = 0.4
FIRST_DECAY = 0.9
SECOND_DECAY = 0.999
ADAM_EPSILON = 1e-08
WEIGHT_DECAY = 0.01
AVERAGE_DECAY = 0.9999


def plan(steps_in):
    step_index = jnp.arange(1000, dtype=jnp.int32)
    beta_table = 0.0001 + (0.02 - 0.0001) * step_index.astype(jnp.float32) / 999.0
    logbar = jnp.cumsum(jnp.log1p(-beta_table))

    def lookup(values, wanted):
        return jnp.sum(
            jnp.where(wanted[:, None] == step_index[None, :], values[None, :], 0.0), axis=1
        )

    return (
        lookup(beta_table, steps_in),
        jnp.exp(lookup(logbar, steps_in)),
        jnp.exp(lookup(logbar, steps_in - 1)),
    )


def sinusoid(steps_in):
    halfway = FREQ // 2
    frequency = jnp.exp(-math.log(10000.0) * jnp.arange(halfway, dtype=jnp.float32) / halfway)
    angles = steps_in.astype(jnp.float32)[:, None] * frequency[None, :]
    return jnp.concatenate([jnp.cos(angles), jnp.sin(angles)], axis=1)


def modulate(hidden, shift_by, scale_by):
    row_mean = jnp.mean(hidden, axis=-1, keepdims=True)
    centered = hidden - row_mean
    variance = jnp.mean(centered * centered, axis=-1, keepdims=True)
    return (
        centered * lax.rsqrt(variance + 1e-06) * (1.0 + scale_by[:, None, :]) + shift_by[:, None, :]
    )


def noisy_input(clean_patches, noise_patches, steps_in):
    beta_now, bar_now, bar_prev = plan(steps_in)
    bar_now = bar_now[:, None, None]
    return jnp.sqrt(bar_now) * clean_patches + jnp.sqrt(1.0 - bar_now) * noise_patches


def loss_terms(output, clean_patches, noise_patches, steps_in, valid_slot):
    beta_now, bar_now, bar_prev = plan(steps_in)
    beta_now = beta_now[:, None, None]
    bar_now = bar_now[:, None, None]
    bar_prev = bar_prev[:, None, None]
    noisy = jnp.sqrt(bar_now) * clean_patches + jnp.sqrt(1.0 - bar_now) * noise_patches
    eps_pred = output[..., :CH]
    var_raw = output[..., CH:]
    squared = jnp.sum((eps_pred - noise_patches) ** 2, axis=-1)
    post_log = jnp.log(beta_now * (1.0 - bar_prev) / (1.0 - bar_now))
    fraction = (var_raw + 1.0) * 0.5
    model_log = fraction * jnp.log(beta_now) + (1.0 - fraction) * post_log
    coefficient = beta_now * jnp.sqrt(bar_prev) / (1.0 - bar_now)
    start_est = (noisy - jnp.sqrt(1.0 - bar_now) * eps_pred) / jnp.sqrt(bar_now)
    mean_gap = coefficient * (clean_patches - start_est)
    divergence = (
        0.5
        * (
            -1.0
            + model_log
            - post_log
            + jnp.exp(post_log - model_log)
            + mean_gap * mean_gap * jnp.exp(-model_log)
        )
        / math.log(2.0)
    )
    return jnp.sum(jnp.where(valid_slot, squared + jnp.sum(divergence, axis=-1), 0.0))


def adam_step(weight, first, second, gradient, average, factor, rate):
    average_decay = min(AVERAGE_DECAY, (1.0 + STEP) / (10.0 + STEP))
    clipped = gradient * factor
    first = FIRST_DECAY * first + (1.0 - FIRST_DECAY) * clipped
    second = SECOND_DECAY * second + (1.0 - SECOND_DECAY) * clipped * clipped
    ratio = (
        first
        / (1.0 - FIRST_DECAY**STEP)
        / (jnp.sqrt(second / (1.0 - SECOND_DECAY**STEP)) + ADAM_EPSILON)
    )
    weight = weight - rate * (ratio + WEIGHT_DECAY * weight)
    return (weight, first, second, average_decay * average + (1.0 - average_decay) * weight)


def backward_product(gradient, weight):
    return lax.dot_general(
        gradient,
        weight,
        (((gradient.ndim - 1,), (1,)), ((), ())),
        preferred_element_type=jnp.float32,
    )


def weight_grad(inputs, gradient):
    flat_in = inputs.reshape(-1, inputs.shape[-1])
    flat_grad = gradient.reshape(-1, gradient.shape[-1])
    return lax.dot_general(
        flat_in, flat_grad, (((0,), (0,)), ((), ())), preferred_element_type=jnp.float32
    )


def column_sum(gradient):
    return jnp.sum(gradient.astype(jnp.float32).reshape(-1, gradient.shape[-1]), axis=0)


def cut_columns(values, start, amount):
    return lax.dynamic_slice_in_dim(values, start, amount, 1)


MESH_IDS = pl.DeviceIdType.MESH
KERNEL_VMEM = 48 * 2**20


def exchange_kernel(axes, sizes, modes, *refs):
    count = len(modes)
    ins, outs = refs[:count], refs[count : 2 * count]
    send_sem, recv_sem = refs[2 * count :]
    if axes == "dp":
        total = sizes[0]
        me = lax.axis_index("dp")
    else:
        total = sizes[0] * sizes[1]
        me = lax.axis_index("dp") * sizes[1] + lax.axis_index("mlp")

    def device(spot):
        if axes == "dp":
            return (spot, lax.axis_index("mlp"))
        return (lax.div(spot, sizes[1]), lax.rem(spot, sizes[1]))

    barrier = pltpu.get_barrier_semaphore()

    def greet(step, carry):
        pl.semaphore_signal(
            barrier, inc=1, device_id=device(lax.rem(me + step, total)), device_id_type=MESH_IDS
        )
        return carry

    lax.fori_loop(1, total, greet, 0)
    pl.semaphore_wait(barrier, total - 1)

    def make(item, step):
        peer = lax.rem(me + step, total)
        source = ins[item].at[peer] if modes[item] == "each" else ins[item]
        return pltpu.make_async_remote_copy(
            src_ref=source,
            dst_ref=outs[item].at[me],
            send_sem=send_sem.at[item, step - 1],
            recv_sem=recv_sem.at[item, step - 1],
            device_id=device(peer),
            device_id_type=MESH_IDS,
        )

    def begin(step, carry):
        for item in range(count):
            make(item, step).start()
        return carry

    lax.fori_loop(1, total, begin, 0)
    for item in range(count):
        if modes[item] == "each":
            outs[item][me] = ins[item][me]
        else:
            outs[item][me] = ins[item][...]

    def finish(step, carry):
        for item in range(count):
            make(item, step).wait()
        return carry

    lax.fori_loop(1, total, finish, 0)


def exchange(items, axes, sizes, collective):
    total = sizes[0] if axes == "dp" else sizes[0] * sizes[1]
    modes = tuple(mode for _, mode in items)
    arrays = [array for array, _ in items]
    shapes = [
        jax.ShapeDtypeStruct(
            array.shape if mode == "each" else (total, *array.shape), array.dtype
        )
        for array, mode in items
    ]
    space = pl.BlockSpec(memory_space=pltpu.VMEM)
    return pl.pallas_call(
        functools.partial(exchange_kernel, axes, sizes, modes),
        out_shape=shapes,
        in_specs=[space] * len(items),
        out_specs=[space] * len(items),
        scratch_shapes=[
            pltpu.SemaphoreType.DMA((len(items), total - 1)),
            pltpu.SemaphoreType.DMA((len(items), total - 1)),
        ],
        compiler_params=pltpu.CompilerParams(
            collective_id=collective, has_side_effects=True, vmem_limit_bytes=KERNEL_VMEM
        ),
    )(*arrays)


def place_kernel(targets, *refs):
    pieces, out, sem = refs[:-2], refs[-2], refs[-1]
    copies = []
    for spot, (piece, target) in enumerate(zip(pieces, targets)):
        copy = pltpu.make_async_copy(piece, target(out), sem.at[spot])
        copy.start()
        copies.append(copy)
    for copy in copies:
        copy.wait()


def place(pieces, targets, shape, dtype):
    return pl.pallas_call(
        functools.partial(place_kernel, targets),
        out_shape=jax.ShapeDtypeStruct(shape, dtype),
        in_specs=[pl.BlockSpec(memory_space=pl.ANY)] * len(pieces),
        out_specs=pl.BlockSpec(memory_space=pl.ANY),
        scratch_shapes=[pltpu.SemaphoreType.DMA((len(pieces),))],
        compiler_params=pltpu.CompilerParams(vmem_limit_bytes=KERNEL_VMEM),
    )(*pieces)


NX = 2


def ring_pairs(depth, shift):
    return [
        (z * NX + x, ((z + shift) % depth) * NX + x) for z in range(depth) for x in range(NX)
    ]


def swap_pairs(count):
    return [(spot, spot ^ 1) for spot in range(count)]


def ring_pieces(half, depth, shift):
    arrived = [half]
    for _ in range(depth - 1):
        arrived.append(lax.ppermute(arrived[-1], "dp", ring_pairs(depth, shift)))
    return arrived


def gather_dp(first, second, selects, shape, depth):
    swaps = swap_pairs(depth * NX)
    pieces, targets = [], []

    def source(step, shift, other):
        def spot():
            d = lax.axis_index("dp")
            z, x = lax.div(d, NX), lax.rem(d, NX)
            z = lax.rem(z - step * shift + depth * NX, depth)
            x = 1 - x if other else x
            return z * NX + x

        return spot

    for half, shift, select in ((first, 1, selects[0]), (second, -1, selects[1])):
        for step, piece in enumerate(ring_pieces(half, depth, shift)):
            other = lax.ppermute(piece, "dp", swaps)
            for swapped, value in ((False, piece), (True, other)):
                pieces.append(value)
                spot = source(step, shift, swapped)
                targets.append(functools.partial(lambda sel, at, out: sel(out, at()), select, spot))
    return place(pieces, targets, shape, first.dtype)


def reduce_ring(blocks, depth, shift):
    z = lax.div(lax.axis_index("dp"), NX)

    def block(offset):
        return lax.dynamic_index_in_dim(
            blocks, lax.rem(z + offset + 2 * depth, depth), 0, keepdims=False
        )

    running = block(-shift)
    for step in range(1, depth):
        arrived = lax.ppermute(running.astype(jnp.bfloat16), "dp", ring_pairs(depth, shift))
        running = arrived.astype(jnp.float32) + block(-shift * (step + 1))
    return running


def reduce_dp(value, count, cut):
    if count != 8:
        return lax.psum_scatter(
            value.astype(jnp.bfloat16), "dp", scatter_dimension=0, tiled=True
        )[0].astype(jnp.float32)
    depth = count // NX
    x = lax.rem(lax.axis_index("dp"), NX)
    paired = value.reshape(depth, NX, *value.shape[1:])
    give = lax.dynamic_index_in_dim(paired, 1 - x, 1, keepdims=False).astype(jnp.bfloat16)
    got = lax.ppermute(give, "dp", swap_pairs(count)).astype(jnp.float32)
    blocks = lax.dynamic_index_in_dim(paired, x, 1, keepdims=False) + got
    return jnp.concatenate(
        [
            reduce_ring(blocks[:, :, :cut], depth, 1),
            reduce_ring(blocks[:, :, cut:], depth, -1),
        ],
        axis=1,
    )


def flip(value, bit, count):
    return lax.ppermute(value, "mlp", [(spot, spot ^ bit) for spot in range(count)])


def gather_rows(own, count):
    far = flip(own, 2, count)
    near = flip(own, 1, count)
    return own, near, far, flip(far, 1, count)


def scatter_rows(far_parts, near_parts, count):
    single = jnp.float32
    got = flip(far_parts[1], 1, count)
    far = flip((far_parts[0].astype(single) + got.astype(single)).astype(jnp.bfloat16), 2, count)
    near = flip(near_parts[1], 1, count)
    return near_parts[0].astype(single) + near.astype(single) + far.astype(single)


def out_pairs(depth, ranks, step, shift):
    pairs = []
    for rank in range(ranks):
        for x in range(NX):
            start = (rank + (step - 1) * shift) % depth
            stop = (rank + step * shift) % depth
            pairs.append(((start * NX + x) * ranks + rank, (stop * NX + x) * ranks + rank))
    return pairs


def gather_out(shard, sizes):
    n_data, n_model = sizes
    if n_data != 8 or n_model != 4:
        whole = lax.all_gather(shard, "dp", axis=0, tiled=True)
        height = D // n_model
        return lax.dynamic_slice_in_dim(whole, lax.axis_index("mlp") * height, height, 0)
    depth = n_data // NX
    d = lax.axis_index("dp")
    z, x = lax.div(d, NX), lax.rem(d, NX)
    mine = z == lax.axis_index("mlp")
    halves = []
    for part, shift in ((shard[:80], 1), (shard[80:], -1)):
        total = jnp.where(mine, part, jnp.zeros_like(part))
        moving = part
        for step in range(1, depth):
            moving = lax.ppermute(moving, ("dp", "mlp"), out_pairs(depth, n_model, step, shift))
            total = total + moving
        halves.append(total)
    own = jnp.concatenate(halves, axis=0)
    other = lax.ppermute(own, "dp", swap_pairs(n_data))
    low = jnp.where(x == 0, own, other)
    high = jnp.where(x == 0, other, own)
    return jnp.concatenate([low, high], axis=0)


def reduce_out(value, sizes):
    n_data, n_model = sizes
    single, bfloat = jnp.float32, jnp.bfloat16
    if n_data != 8 or n_model != 4:
        whole = jnp.zeros((D, D), single)
        whole = lax.dynamic_update_slice_in_dim(
            whole, value, lax.axis_index("mlp") * value.shape[0], 0
        )
        part = lax.psum_scatter(whole.astype(bfloat), "dp", scatter_dimension=0, tiled=True)
        return lax.psum(part.astype(single), "mlp")
    depth = n_data // NX
    d = lax.axis_index("dp")
    z, x = lax.div(d, NX), lax.rem(d, NX)
    mine = z == lax.axis_index("mlp")
    paired = value.reshape(NX, D // n_data, D)
    give = lax.dynamic_index_in_dim(paired, 1 - x, 0, keepdims=False).astype(bfloat)
    got = lax.ppermute(give, "dp", swap_pairs(n_data)).astype(single)
    blocks = lax.dynamic_index_in_dim(paired, x, 0, keepdims=False) + got
    halves = []
    for part, shift in ((blocks[:80], 1), (blocks[80:], -1)):
        running = part
        for step in range(1, depth):
            pairs = [
                (source, target)
                for source, target in out_pairs(depth, n_model, step + 1, shift)
            ]
            arrived = lax.ppermute(running.astype(bfloat), ("dp", "mlp"), pairs)
            running = arrived.astype(single) + part
        halves.append(running)
    summed = jnp.concatenate(halves, axis=0)
    shared = jnp.where(mine, summed, 0.0).astype(bfloat)
    shared = shared + flip(shared, 1, n_model)
    shared = shared + flip(shared, 2, n_model)
    return shared.astype(single)


def swapped(values):
    quarter = HDIM // 4
    return jnp.concatenate(
        [
            values[:, quarter : 2 * quarter],
            values[:, :quarter],
            values[:, 3 * quarter :],
            values[:, 2 * quarter : 3 * quarter],
        ],
        axis=1,
    )


def attention_kernel(heads, qkv_ref, cos_ref, sin_ref, mask_ref, low_ref, out_ref, total_ref):
    width = heads * HDIM
    cosine, sine, mask = cos_ref[0], sin_ref[0], mask_ref[0]
    totals = []
    for head in range(heads):
        start = head * HDIM

        def part(which):
            return qkv_ref[0, :, which * width + start : which * width + start + HDIM]

        raw_q, raw_k = part(0), part(1)
        query = (raw_q * cosine + swapped(raw_q) * sine).astype(jnp.bfloat16)
        key = (raw_k * cosine + swapped(raw_k) * sine).astype(jnp.bfloat16)
        value = part(2).astype(jnp.bfloat16)
        for which, kept in enumerate((query, key, value)):
            low_ref[0, :, which * width + start : which * width + start + HDIM] = kept
        scores = lax.dot_general(
            query, key, (((1,), (1,)), ((), ())), preferred_element_type=jnp.float32
        ) * (1.0 / math.sqrt(HDIM))
        scores = jnp.where(mask > 0.0, scores, -1e30)
        row_max = jnp.max(scores, axis=-1, keepdims=True)
        exponent = jnp.exp(scores - row_max)
        row_sum = jnp.sum(exponent, axis=-1, keepdims=True)
        probs = exponent / row_sum
        out_ref[0, :, start : start + HDIM] = jnp.dot(
            probs.astype(jnp.bfloat16), value, preferred_element_type=jnp.float32
        ).astype(jnp.bfloat16)
        totals.append(row_max + jnp.log(row_sum))
    total_ref[0] = jnp.concatenate(totals, axis=1)


def attention(qkv, cosine, sine, mask, heads):
    images, length, width = qkv.shape
    per_image = lambda *dims: pl.BlockSpec((1, *dims), lambda i: (i, 0, 0))
    return pl.pallas_call(
        functools.partial(attention_kernel, heads),
        grid=(images,),
        out_shape=[
            jax.ShapeDtypeStruct((images, length, width), jnp.bfloat16),
            jax.ShapeDtypeStruct((images, length, heads * HDIM), jnp.bfloat16),
            jax.ShapeDtypeStruct((images, length, heads), jnp.float32),
        ],
        in_specs=[
            per_image(length, width),
            per_image(length, HDIM),
            per_image(length, HDIM),
            per_image(1, length),
        ],
        out_specs=[
            per_image(length, width),
            per_image(length, heads * HDIM),
            per_image(length, heads),
        ],
        compiler_params=pltpu.CompilerParams(vmem_limit_bytes=KERNEL_VMEM),
    )(qkv, cosine, sine, mask)


def attention_back_kernel(
    heads, low_ref, total_ref, grad_ref, cos_ref, sin_ref, mask_ref, out_ref
):
    width = heads * HDIM
    scale_by = 1.0 / math.sqrt(HDIM)
    cosine, sine, mask = cos_ref[0], sin_ref[0], mask_ref[0]

    def contract(left, right, dims):
        return lax.dot_general(left, right, (dims, ((), ())), preferred_element_type=jnp.float32)

    for head in range(heads):
        start = head * HDIM

        def spot(which):
            return slice(which * width + start, which * width + start + HDIM)

        query, key, value = (low_ref[0, :, spot(which)] for which in range(3))
        grad = grad_ref[0, :, start : start + HDIM]
        scores = contract(query, key, ((1,), (1,))) * scale_by
        scores = jnp.where(mask > 0.0, scores, -1e30)
        probs = jnp.exp(scores - total_ref[0, :, head : head + 1])
        d_probs = contract(grad, value, ((1,), (1,)))
        row = jnp.sum(probs * d_probs, axis=-1, keepdims=True)
        d_scores = (probs * (d_probs - row)).astype(jnp.bfloat16)
        d_query = contract(d_scores, key, ((1,), (0,))) * scale_by
        d_key = contract(d_scores, query, ((0,), (0,))) * scale_by
        d_value = contract(probs.astype(jnp.bfloat16), grad, ((0,), (0,)))
        for which, turned in ((0, d_query), (1, d_key)):
            back = turned * cosine + swapped(turned * sine)
            out_ref[0, :, spot(which)] = back.astype(jnp.bfloat16)
        out_ref[0, :, spot(2)] = d_value.astype(jnp.bfloat16)


def attention_back(low, totals, grad, cosine, sine, mask, heads):
    images, length, width = low.shape
    per_image = lambda *dims: pl.BlockSpec((1, *dims), lambda i: (i, 0, 0))
    return pl.pallas_call(
        functools.partial(attention_back_kernel, heads),
        grid=(images,),
        out_shape=jax.ShapeDtypeStruct((images, length, width), jnp.bfloat16),
        in_specs=[
            per_image(length, width),
            per_image(length, heads),
            per_image(length, heads * HDIM),
            per_image(length, HDIM),
            per_image(length, HDIM),
            per_image(1, length),
        ],
        out_specs=per_image(length, width),
        compiler_params=pltpu.CompilerParams(vmem_limit_bytes=KERNEL_VMEM),
    )(low, totals, grad, cosine, sine, mask)


def turn_tables(patch_grid, length):
    slot_index = jnp.arange(length, dtype=jnp.int32)[None, :]
    grid_cols = patch_grid[:, 1:2]
    valid_slot = slot_index < patch_grid[:, 0:1] * grid_cols
    row_place = (slot_index // grid_cols).astype(jnp.float32)
    col_place = (slot_index % grid_cols).astype(jnp.float32)
    quarter = HDIM // 4
    frequency = jnp.exp(-math.log(10000.0) * jnp.arange(quarter, dtype=jnp.float32) / quarter)
    row_angle = row_place[..., None] * frequency
    col_angle = col_place[..., None] * frequency
    cos_row, sin_row = jnp.cos(row_angle), jnp.sin(row_angle)
    cos_col, sin_col = jnp.cos(col_angle), jnp.sin(col_angle)
    return (
        jnp.concatenate([cos_row, cos_row, cos_col, cos_col], axis=-1),
        jnp.concatenate([-sin_row, sin_row, -sin_col, sin_col], axis=-1),
        valid_slot.astype(jnp.float32)[:, None, :],
    )


def valid_slots(patch_grid, length):
    return jnp.arange(length, dtype=jnp.int32)[None, :] < patch_grid[:, 0:1] * patch_grid[:, 1:2]


def device_parts():
    d, m = lax.axis_index("dp"), lax.axis_index("mlp")
    return d, m, lax.div(d, NX), lax.rem(d, NX)


class Sender:
    def __init__(self, send_sem, recv_sem):
        self.send_sem, self.recv_sem = send_sem, recv_sem

    def __call__(self, spot, source, target, device):
        spot = spot if isinstance(spot, tuple) else (spot,)
        return pltpu.make_async_remote_copy(
            src_ref=source,
            dst_ref=target,
            send_sem=self.send_sem.at[spot],
            recv_sem=self.recv_sem.at[spot],
            device_id=device,
            device_id_type=MESH_IDS,
        )


def modulate_rows(values, shift_by, scale_by):
    row_mean = jnp.mean(values, axis=-1, keepdims=True)
    centered = values - row_mean
    variance = jnp.mean(centered * centered, axis=-1, keepdims=True)
    return centered * lax.rsqrt(variance + 1e-06) * (1.0 + scale_by) + shift_by


FORWARD_IN = (
    "facts", "trig", "small", "time_first", "first_bias", "second_bias", "time_blocks",
    "class_table", "mod_weight", "mod_bias", "noisy", "patch_bias", "qkv_shard", "out_shard",
    "ff_shard", "qkv_bias", "out_bias",
)
FORWARD_OUT = (
    "facts_all", "trig_all", "small_all", "time_pre", "condition", "modulation", "hidden",
    "one_rows", "qkv_weight", "out_weight", "ff", "low", "attended", "totals", "branch",
    "hidden_mid", "two_rows",
)
FORWARD_SCRATCH = (
    "time_send", "time_recv", "mod_send", "mod_recv", "mod_low", "qkv", "parts_send",
    "parts_recv", "facts_s", "facts_r", "small_s", "small_r", "time_s", "time_r",
    "mods_s", "mods_r", "trig_s", "trig_r", "one_s", "one_r", "two_s", "two_r", "part_s",
    "part_r", "qz_s", "qz_r", "qx_s", "qx_r", "oz_s", "oz_r", "ox_s", "ox_r", "fz_s", "fz_r",
    "fx_s", "fx_r", "local_sem",
)


def forward_kernel(sizes, *refs):
    names = FORWARD_IN + FORWARD_OUT + FORWARD_SCRATCH
    r = dict(zip(names, refs, strict=True))
    bfloat, single = jnp.bfloat16, jnp.float32
    n_data, n_model = sizes
    everyone = n_data * n_model
    d, m, z, x = device_parts()
    me = d * n_model + m
    depth = n_data // NX
    rows = D // n_data
    heads = HEADS // n_model
    head_cols = heads * HDIM
    length = r["noisy"].shape[0]
    units = r["ff_shard"].shape[2]
    half = units // 2

    def at_dp(spot):
        return (spot, m)

    def at_mlp(bit):
        flipped = m + 1 - 2 * lax.rem(m, 2) if bit == 1 else lax.rem(m + 2, 4)
        return (d, flipped)

    up = lax.rem(z + 1, depth) * NX + x
    down = lax.rem(z + depth - 1, depth) * NX + x
    side = z * NX + 1 - x

    barrier = pltpu.get_barrier_semaphore()

    def greet(step, carry):
        peer = lax.rem(me + step, everyone)
        pl.semaphore_signal(
            barrier,
            inc=1,
            device_id=(lax.div(peer, n_model), lax.rem(peer, n_model)),
            device_id_type=MESH_IDS,
        )
        return carry

    lax.fori_loop(1, everyone, greet, 0)

    load_mod = pltpu.make_async_copy(r["mod_weight"], r["mod_low"], r["local_sem"].at[0])
    load_mod.start()
    own_ff = pltpu.make_async_copy(
        r["ff_shard"],
        r["ff"].at[:, pl.ds(pl.multiple_of(d * rows, 16), rows)],
        r["local_sem"].at[1],
    )
    own_ff.start()
    pl.semaphore_wait(barrier, everyone - 1)

    send_facts = Sender(r["facts_s"], r["facts_r"])

    def facts_copy(step):
        peer = lax.rem(me + step, everyone)
        return send_facts(
            step - 1,
            r["facts"],
            r["facts_all"].at[me],
            (lax.div(peer, n_model), lax.rem(peer, n_model)),
        )

    def loop(first, last, body):
        def step_body(step, carry):
            body(step)
            return carry

        lax.fori_loop(first, last, step_body, 0)

    loop(1, everyone, lambda step: facts_copy(step).start())
    r["facts_all"][me] = r["facts"][...]

    def qkv_rows(spot, part):
        if part == 0:
            return r["qkv_weight"].at[pl.ds(pl.multiple_of(spot * rows, 16), 80)]
        return r["qkv_weight"].at[pl.ds(pl.multiple_of(spot * rows + 80, 16), rows - 80)]

    def ff_block(spot, part, which):
        return r["ff"].at[
            which,
            pl.ds(pl.multiple_of(spot * rows, 16), rows),
            pl.ds(half * part, half),
        ]

    def origin(step, part):
        return lax.rem(z + (depth - step if part == 0 else step), depth) * NX + x

    qz, qx = Sender(r["qz_s"], r["qz_r"]), Sender(r["qx_s"], r["qx_r"])
    fz, fx = Sender(r["fz_s"], r["fz_r"]), Sender(r["fx_s"], r["fx_r"])

    def qkv_along(step, part):
        block = qkv_rows(origin(step - 1, part), part)
        return qz((part, step - 1), block, block, at_dp(up if part == 0 else down))

    def qkv_aside(step, part):
        block = qkv_rows(origin(step, part), part)
        return qx((part, step), block, block, at_dp(side))

    def ff_along(step, part, which):
        block = ff_block(origin(step - 1, part), part, which)
        return fz((part, step - 1, which), block, block, at_dp(up if part == 0 else down))

    def ff_aside(step, part, which):
        block = ff_block(origin(step, part), part, which)
        return fx((part, step, which), block, block, at_dp(side))

    own_rows = pl.ds(pl.multiple_of(d * rows, 16), rows)
    r["qkv_weight"][own_rows] = r["qkv_shard"][...]
    for part in range(2):
        qkv_along(1, part).start()
        qkv_aside(0, part).start()

    send_small = Sender(r["small_s"], r["small_r"])

    def small_copy(step):
        return send_small(
            step - 1,
            r["small"],
            r["small_all"].at[own_rows],
            at_dp(lax.rem(d + step, n_data)),
        )

    loop(1, n_data, lambda step: small_copy(step).start())
    r["small_all"][own_rows] = r["small"][...]
    r["trig_all"][0] = r["trig"][...]

    def spread(send, buffer):
        return (
            send(0, buffer.at[0], buffer.at[1], at_mlp(1)),
            send(1, buffer.at[0], buffer.at[2], at_mlp(2)),
            send(2, buffer.at[2], buffer.at[3], at_mlp(1)),
        )

    trig_near, trig_far, trig_on = spread(Sender(r["trig_s"], r["trig_r"]), r["trig_all"])
    trig_near.start()
    trig_far.start()

    oz, ox = Sender(r["oz_s"], r["oz_r"]), Sender(r["ox_s"], r["ox_r"])
    out_place = r["out_weight"].at[pl.ds(pl.multiple_of(x * rows, 16), rows)]
    owner = z == m

    def out_along(step):
        return oz(step - 1, out_place, out_place, at_dp(lax.rem(z + step, depth) * NX + x))

    out_aside = ox(0, out_place, out_place, at_dp(side))

    @pl.when(owner)
    def _():
        r["out_weight"][pl.ds(pl.multiple_of(x * rows, 16), rows)] = r["out_shard"][...]
        for step in range(1, depth):
            out_along(step).start()
        out_aside.start()

    loop(1, everyone, lambda step: facts_copy(step).wait())
    facts_all = r["facts_all"][...]
    sinus = jnp.concatenate([facts_all[:, 0], facts_all[:, 1]], axis=1).astype(bfloat)
    labels = facts_all[:, 2, 0:1]
    time_pre = (
        jnp.dot(sinus, r["time_first"][...], preferred_element_type=single) + r["first_bias"][...]
    )
    r["time_pre"][...] = time_pre
    time_act = (time_pre * jax.nn.sigmoid(time_pre)).astype(bfloat)
    send_time = Sender(r["time_s"], r["time_r"])

    def time_copy(step):
        peer = lax.rem(d + step, n_data)
        return send_time(
            step - 1, r["time_send"].at[peer], r["time_recv"].at[d], at_dp(peer)
        )

    for spot in range(n_data):
        r["time_send"][spot] = jnp.dot(
            time_act, r["time_blocks"][spot], preferred_element_type=single
        )
    loop(1, n_data, lambda step: time_copy(step).start())
    r["time_recv"][d] = r["time_send"][d]
    for part in range(2):
        for which in range(3):
            own = r["ff_shard"].at[which, :, pl.ds(half * part, half)]
            fz(
                (part, 0, which),
                own,
                ff_block(d, part, which),
                at_dp(up if part == 0 else down),
            ).start()
            fx((part, 0, which), own, ff_block(d, part, which), at_dp(side)).start()
    onehot = (
        labels == lax.broadcasted_iota(jnp.int32, (everyone, CLASSES + 1), 1).astype(single)
    ).astype(bfloat)
    picked = jnp.dot(onehot, r["class_table"][...], preferred_element_type=single)
    load_mod.wait()

    def qkv_service(step):
        for part in range(2):
            qkv_along(step, part).wait_recv()
            if step < depth - 1:
                qkv_along(step + 1, part).start()
            qkv_aside(step, part).start()

    loop(1, n_data, lambda step: time_copy(step).wait())
    condition = jnp.sum(r["time_recv"][...], axis=0) + r["second_bias"][...] + picked
    r["condition"][...] = condition
    cond_act = (condition * jax.nn.sigmoid(condition)).astype(bfloat)
    pick = (
        lax.broadcasted_iota(jnp.int32, (n_data, everyone), 1)
        == lax.broadcasted_iota(jnp.int32, (n_data, everyone), 0) * n_model + m
    ).astype(bfloat)
    cond_rank = jnp.dot(pick, cond_act, preferred_element_type=single).astype(bfloat)
    for kind in range(8):
        block = jnp.dot(
            cond_rank, r["mod_low"][:, kind * D : (kind + 1) * D], preferred_element_type=single
        )
        for spot in range(n_data):
            r["mod_send"][spot, kind : kind + 1] = block[spot : spot + 1]
    send_mods = Sender(r["mods_s"], r["mods_r"])

    def mods_copy(step):
        peer = lax.rem(d + step, n_data)
        return send_mods(step - 1, r["mod_send"].at[peer], r["mod_recv"].at[d], at_dp(peer))

    loop(1, n_data, lambda step: mods_copy(step).start())
    r["mod_recv"][d] = r["mod_send"][d]
    qkv_service(1)
    loop(1, n_data, lambda step: small_copy(step).wait())
    trig_far.wait_recv()
    trig_on.start()
    hidden = (
        lax.dot_general(
            r["noisy"][...],
            r["small_all"][:, 0:CH],
            (((1,), (1,)), ((), ())),
            preferred_element_type=single,
        )
        + r["patch_bias"][...]
    )
    r["hidden"][...] = hidden
    loop(1, n_data, lambda step: mods_copy(step).wait())
    modulation = jnp.sum(r["mod_recv"][...], axis=0) + r["mod_bias"][...]
    r["modulation"][...] = modulation

    def kind_of(kind):
        return r["modulation"][kind : kind + 1]

    r["one_rows"][0] = modulate_rows(r["hidden"][...], kind_of(0), kind_of(1)).astype(bfloat)
    one_near, one_far, one_on = spread(Sender(r["one_s"], r["one_r"]), r["one_rows"])
    one_far.start()
    one_near.start()
    qkv_service(2)
    qkv_service(3)

    @pl.when(jnp.logical_not(owner))
    def _():
        oz(
            lax.rem(z + depth - m, depth) - 1, out_place, out_place, at_dp(up)
        ).wait_recv()
        out_aside.start()

    own_ff.wait()

    def ff_service(step, which):
        for part in range(2):
            ff_along(step, part, which).wait_recv()
            if step < depth - 1:
                ff_along(step + 1, part, which).start()
            ff_aside(step, part, which).start()

    ff_service(1, 0)
    one_far.wait_recv()
    one_on.start()
    for part in range(2):
        for step in range(depth):
            qkv_aside(step, part).wait_recv()
    one_near.wait_recv()
    one_on.wait_recv()
    trig_near.wait_recv()
    trig_on.wait_recv()
    ff_service(1, 1)
    ff_service(1, 2)

    def image_body(step, carry):
        image = n_model - 1 - step
        r["qkv"][...] = (
            jnp.dot(r["one_rows"][image], r["qkv_weight"][...], preferred_element_type=single)
            + r["qkv_bias"][...]
        )
        rank = (
            2 * lax.rem(lax.div(m, 2) + lax.div(image, 2), 2)
            + lax.rem(lax.rem(m, 2) + lax.rem(image, 2), 2)
        )
        count = r["facts_all"][d * n_model + rank, 2:3, 1:2]
        mask = lax.broadcasted_iota(jnp.int32, (1, length), 1).astype(single) < count
        cosine, sine = r["trig_all"][image, 0], r["trig_all"][image, 1]
        totals = []
        for head in range(heads):
            start = head * HDIM

            def part(which):
                return r["qkv"][:, which * head_cols + start : which * head_cols + start + HDIM]

            raw_q, raw_k = part(0), part(1)
            query = (raw_q * cosine + swapped(raw_q) * sine).astype(bfloat)
            key = (raw_k * cosine + swapped(raw_k) * sine).astype(bfloat)
            value = part(2).astype(bfloat)
            for which, kept in enumerate((query, key, value)):
                low = which * head_cols + start
                r["low"][image, :, low : low + HDIM] = kept
            scores = lax.dot_general(
                query, key, (((1,), (1,)), ((), ())), preferred_element_type=single
            ) * (1.0 / math.sqrt(HDIM))
            scores = jnp.where(mask, scores, -1e30)
            row_max = jnp.max(scores, axis=-1, keepdims=True)
            exponent = jnp.exp(scores - row_max)
            row_sum = jnp.sum(exponent, axis=-1, keepdims=True)
            probs = exponent / row_sum
            r["attended"][image, :, start : start + HDIM] = jnp.dot(
                probs.astype(bfloat), value, preferred_element_type=single
            ).astype(bfloat)
            totals.append(row_max + jnp.log(row_sum))
        r["totals"][image] = jnp.concatenate(totals, axis=1)
        return carry

    lax.fori_loop(0, 2, image_body, 0)
    for which in range(3):
        ff_service(2, which)
    lax.fori_loop(2, n_model, image_body, 0)

    @pl.when(owner)
    def _():
        for step in range(1, depth):
            out_along(step).wait_send()

    out_aside.wait()

    def partial(image):
        return jnp.dot(
            r["attended"][image], r["out_weight"][...], preferred_element_type=single
        )

    send_part = Sender(r["part_s"], r["part_r"])
    to_core = send_part(0, r["parts_send"].at[0], r["parts_recv"].at[0], at_mlp(1))
    to_far = send_part(1, r["parts_send"].at[1], r["parts_recv"].at[1], at_mlp(2))
    to_near = send_part(2, r["parts_send"].at[2], r["parts_recv"].at[2], at_mlp(1))
    r["parts_send"][0] = partial(3).astype(bfloat)
    to_core.start()
    second = partial(2)
    to_core.wait_recv()
    r["parts_send"][1] = (second + r["parts_recv"][0].astype(single)).astype(bfloat)
    to_far.start()
    r["parts_send"][2] = partial(1).astype(bfloat)
    to_near.start()
    own_part = partial(0) + r["out_bias"][...]
    for which in range(3):
        ff_service(3, which)
    to_near.wait_recv()
    to_far.wait_recv()
    branch = own_part + r["parts_recv"][2].astype(single) + r["parts_recv"][1].astype(single)
    r["branch"][...] = branch
    hidden_mid = r["hidden"][...] + kind_of(2) * branch
    r["hidden_mid"][...] = hidden_mid
    r["two_rows"][0] = modulate_rows(hidden_mid, kind_of(3), kind_of(4)).astype(bfloat)
    two_near, two_far, two_on = spread(Sender(r["two_s"], r["two_r"]), r["two_rows"])
    two_far.start()
    two_near.start()
    two_far.wait_recv()
    two_on.start()

    for part in range(2):
        for step in range(depth):
            for which in range(3):
                ff_aside(step, part, which).wait()
            qkv_aside(step, part).wait_send()
            if step:
                for which in range(3):
                    ff_along(step, part, which).wait_send()
                qkv_along(step, part).wait_send()
    for copy in (two_near, two_on):
        copy.wait()
    two_far.wait_send()
    for copy in (trig_near, trig_far, trig_on, one_near, one_far, one_on, to_core, to_far, to_near):
        copy.wait_send()


def forward_all(values, sizes, collective):
    n_data, n_model = sizes
    bfloat, single = jnp.bfloat16, jnp.float32
    everyone = n_data * n_model
    rows = D // n_data
    heads = HEADS // n_model
    head_cols = heads * HDIM
    length = values["noisy"].shape[0]
    units = values["ff_shard"].shape[2]
    depth = n_data // NX
    shapes = dict(
        facts_all=((everyone, 8, 128), single),
        trig_all=((n_model, 2, length, HDIM), single),
        small_all=((D, 128), bfloat),
        time_pre=((everyone, rows), single),
        condition=((everyone, rows), single),
        modulation=((8, D), single),
        hidden=((length, D), single),
        one_rows=((n_model, length, D), bfloat),
        qkv_weight=((D, 3 * head_cols), bfloat),
        out_weight=((head_cols, D), bfloat),
        ff=((3, D, units), bfloat),
        low=((n_model, length, 3 * head_cols), bfloat),
        attended=((n_model, length, head_cols), bfloat),
        totals=((n_model, length, heads), single),
        branch=((length, D), single),
        hidden_mid=((length, D), single),
        two_rows=((n_model, length, D), bfloat),
    )
    dma = pltpu.SemaphoreType.DMA
    scratch = dict(
        time_send=pltpu.VMEM((n_data, everyone, rows), single),
        time_recv=pltpu.VMEM((n_data, everyone, rows), single),
        mod_send=pltpu.VMEM((n_data, 8, D), single),
        mod_recv=pltpu.VMEM((n_data, 8, D), single),
        mod_low=pltpu.VMEM((rows, 8 * D), bfloat),
        qkv=pltpu.VMEM((length, 3 * head_cols), single),
        parts_send=pltpu.VMEM((3, length, D), bfloat),
        parts_recv=pltpu.VMEM((3, length, D), bfloat),
        local_sem=dma((2,)),
    )
    counts = dict(
        facts=(everyone - 1,),
        small=(n_data - 1,),
        time=(n_data - 1,),
        mods=(n_data - 1,),
        trig=(3,),
        one=(3,),
        two=(3,),
        part=(3,),
        qz=(2, depth - 1),
        qx=(2, depth),
        oz=(depth - 1,),
        ox=(1,),
        fz=(2, depth - 1, 3),
        fx=(2, depth, 3),
    )
    for name, count in counts.items():
        scratch[name + "_s"] = dma(count)
        scratch[name + "_r"] = dma(count)
    far = {"mod_weight", "ff_shard", "ff"}

    def space(name):
        return pl.BlockSpec(memory_space=pl.ANY if name in far else pltpu.VMEM)

    outs = pl.pallas_call(
        functools.partial(forward_kernel, sizes),
        out_shape=[jax.ShapeDtypeStruct(*shapes[name]) for name in FORWARD_OUT],
        in_specs=[space(name) for name in FORWARD_IN],
        out_specs=[space(name) for name in FORWARD_OUT],
        scratch_shapes=[scratch[name] for name in FORWARD_SCRATCH],
        compiler_params=pltpu.CompilerParams(
            collective_id=collective, has_side_effects=True, vmem_limit_bytes=56 * 2**20
        ),
    )(*[values[name] for name in FORWARD_IN])
    return dict(zip(FORWARD_OUT, outs))


BACK_IN = (
    "ff", "two_rows", "hidden_mid", "hidden", "branch", "modulation", "small_all", "final_bias",
    "clean", "noise", "consts", "valid", "noisy", "low", "totals", "trig_all", "facts_all",
    "attended", "one_rows", "qkv_weight", "out_weight",
)
BACK_OUT = (
    "grad_ff", "grad_qkv", "grad_out", "d_modulation", "hidden_sum", "branch_sum", "qkv_sum",
    "output_sum", "loss", "grad_patch", "grad_final",
)
BACK_SCRATCH = (
    "mixed", "d_end", "dm_rows", "db_rows", "hold_far", "hold_near", "parts_send", "parts_recv",
    "normed_end", "g_ff", "x_ff", "z_ff", "g_qkv", "x_qkv", "z_qkv", "g_out", "x_out",
    "z_out", "out_mine", "dm_s", "dm_r", "db_s", "db_r", "pa_s", "pa_r",
    "pb_s", "pb_r", "pc_s", "pc_r", "fx_s", "fx_r", "fz_s", "fz_r", "qx_s", "qx_r", "qz_s",
    "qz_r", "ox_s", "ox_r", "oz_s", "oz_r", "qa_s", "qa_r", "oa_s", "oa_r", "local_sem",
)
ROW_CHUNK = 16


def modulate_back(values, grad, scale_by):
    row_mean = jnp.mean(values, axis=-1, keepdims=True)
    centered = values - row_mean
    variance = jnp.mean(centered * centered, axis=-1, keepdims=True)
    inverse = lax.rsqrt(variance + 1e-06)
    normal = centered * inverse
    inner = grad * (1.0 + scale_by)
    back = inverse * (
        inner
        - jnp.mean(inner, axis=-1, keepdims=True)
        - normal * jnp.mean(inner * normal, axis=-1, keepdims=True)
    )
    return back, normal


def fold(values):
    total = values[:8]
    for start in range(8, values.shape[0], 8):
        total = total + values[start : start + 8]
    return total


def back_kernel(sizes, total_images, *refs):
    names = BACK_IN + BACK_OUT + BACK_SCRATCH
    r = dict(zip(names, refs, strict=True))
    bfloat, single = jnp.bfloat16, jnp.float32
    n_data, n_model = sizes
    d, m, z, x = device_parts()
    depth = n_data // NX
    rows = D // n_data
    heads = HEADS // n_model
    head_cols = heads * HDIM
    length = r["clean"].shape[0]
    units = r["ff"].shape[2]
    half = units // 2

    def at_dp(spot):
        return (spot, m)

    near_rank = m + 1 - 2 * lax.rem(m, 2)
    far_rank = lax.rem(m + 2, 4)

    def at_mlp(bit):
        return (d, near_rank if bit == 1 else far_rank)

    up = lax.rem(z + 1, depth) * NX + x
    down = lax.rem(z + depth - 1, depth) * NX + x
    side = z * NX + 1 - x
    barrier = pltpu.get_barrier_semaphore()
    peers = [at_dp(lax.rem(z + step, depth) * NX + x) for step in range(1, depth)]
    peers += [at_dp(side), at_mlp(1), at_mlp(2), (d, lax.rem(near_rank + 2, 4))]
    for peer in peers:
        pl.semaphore_signal(barrier, inc=1, device_id=peer, device_id_type=MESH_IDS)
    pl.semaphore_wait(barrier, len(peers))

    def chunks(body, carry, amount=ROW_CHUNK, count=length):
        def step_body(step, held):
            return body(pl.ds(pl.multiple_of(step * amount, amount), amount), held)

        return lax.fori_loop(0, count // amount, step_body, carry)

    def kind_of(kind):
        return r["modulation"][kind : kind + 1]

    def dot(left, right, dims):
        return lax.dot_general(left, right, (dims, ((), ())), preferred_element_type=single)

    zeros = jnp.zeros((8, D), single)

    def spread(send, buffer):
        return (
            send(0, buffer.at[0], buffer.at[1], at_mlp(1)),
            send(1, buffer.at[0], buffer.at[2], at_mlp(2)),
            send(2, buffer.at[2], buffer.at[3], at_mlp(1)),
        )

    def part_copies(tag):
        send = Sender(r[tag + "_s"], r[tag + "_r"])
        return tuple(
            send(spot, r["parts_send"].at[spot], r["parts_recv"].at[spot], at_mlp(bit))
            for spot, bit in ((0, 1), (1, 2), (2, 1))
        )

    def add_far(copies):
        to_core, to_far, to_near = copies
        to_core.wait_recv()

        def body(at, held):
            r["parts_send"][1, at] = (
                r["hold_far"][at] + r["parts_recv"][0, at].astype(single)
            ).astype(bfloat)
            return held

        chunks(body, 0)
        to_far.start()

    fx, fz = Sender(r["fx_s"], r["fx_r"]), Sender(r["fz_s"], r["fz_r"])
    qx, qz = Sender(r["qx_s"], r["qx_r"]), Sender(r["qz_s"], r["qz_r"])

    def block_rows(z_spot, x_spot):
        return pl.ds(pl.multiple_of((z_spot * NX + x_spot) * rows, 16), rows)

    def ff_aside(which, step):
        z_spot = lax.rem(z + step, depth)
        return fx(
            (which, step),
            r["g_ff"].at[which, block_rows(z_spot, 1 - x)],
            r["x_ff"].at[which, z_spot],
            at_dp(side),
        )

    def target_of(step, part):
        return lax.rem(z + (depth - 1 - step if part == 0 else 1 + step), depth)

    def ff_along(which, step, part):
        lanes = pl.ds(half * part, half)
        return fz(
            (which, step, part),
            r["g_ff"].at[which, block_rows(target_of(step, part), x), lanes],
            r["z_ff"].at[which, step, part],
            at_dp(up if part == 0 else down),
        )

    def ff_start(which):
        for step in range(depth):
            ff_aside(which, step).start()

    def ff_beside(which):
        for step in range(depth):
            ff_aside(which, step).wait_recv()

        def body(step, held):
            at = block_rows(step, x)
            r["g_ff"][which, at] = (
                r["g_ff"][which, at].astype(single) + r["x_ff"][which, step].astype(single)
            ).astype(bfloat)
            return held

        lax.fori_loop(0, depth, body, 0)
        for part in range(2):
            ff_along(which, 0, part).start()

    def ff_service(which, step):
        for part in range(2):
            ff_along(which, step, part).wait_recv()
            lanes = pl.ds(half * part, half)
            at = block_rows(target_of(step + 1, part), x)
            running = r["z_ff"][which, step, part].astype(single) + r["g_ff"][
                which, at, lanes
            ].astype(single)
            if step < depth - 2:
                r["g_ff"][which, at, lanes] = running.astype(bfloat)
                ff_along(which, step + 1, part).start()
            else:
                r["grad_ff"][which, :, lanes] = running

    tops = (pl.ds(0, 80), pl.ds(80, rows - 80))

    def part_rows(z_spot, part):
        start = (z_spot * NX + x) * rows + 80 * part
        return pl.ds(pl.multiple_of(start, 16), 80 if part == 0 else rows - 80)

    def qkv_aside(step):
        z_spot = lax.rem(z + step, depth)
        return qx(
            step,
            r["g_qkv"].at[block_rows(z_spot, 1 - x)],
            r["x_qkv"].at[z_spot],
            at_dp(side),
        )

    def qkv_along(step, part):
        return qz(
            (step, part),
            r["g_qkv"].at[part_rows(target_of(step, part), part)],
            r["z_qkv"].at[step, tops[part]],
            at_dp(up if part == 0 else down),
        )

    def qkv_beside():
        for step in range(depth):
            qkv_aside(step).wait_recv()

        def body(step, held):
            at = block_rows(step, x)
            r["g_qkv"][at] = (
                r["g_qkv"][at].astype(single) + r["x_qkv"][step].astype(single)
            ).astype(bfloat)
            return held

        lax.fori_loop(0, depth, body, 0)
        for part in range(2):
            qkv_along(0, part).start()

    def qkv_service(step):
        for part in range(2):
            qkv_along(step, part).wait_recv()
            at = part_rows(target_of(step + 1, part), part)
            running = (
                r["z_qkv"][step, tops[part]].astype(single) + r["g_qkv"][at].astype(single)
            ).astype(bfloat)
            if step < depth - 2:
                r["g_qkv"][at] = running
                qkv_along(step + 1, part).start()
            else:
                r["grad_qkv"][0, tops[part]] = running

    dm_near, dm_far, dm_on = spread(Sender(r["dm_s"], r["dm_r"]), r["dm_rows"])
    first_parts, second_parts, third_parts = (part_copies(tag) for tag in ("pa", "pb", "pc"))

    def swiglu(ff, two_rows, gates, ups, acts, d_gates, d_ups):
        load_ff = pltpu.make_async_copy(r["ff"], ff, r["local_sem"].at[0])
        load_two = pltpu.make_async_copy(r["two_rows"], two_rows, r["local_sem"].at[1])
        load_ff.start()
        load_two.start()
        load_two.wait()
        load_ff.wait()
        wide = 2 * length

        def rows_of(ref, which):
            return ref[2 * which : 2 * which + 2].reshape(wide, D)

        def inner(which):
            part = rows_of(two_rows, which)
            spot = pl.ds(which * wide, wide)
            gates[spot] = dot(part, ff[0], ((1,), (0,)))
            ups[spot] = dot(part, ff[1], ((1,), (0,)))

            def body(at, held):
                at = pl.ds(pl.multiple_of(at.start + which * wide, 32), 32)
                gate = gates[at]
                acts[at] = (gate * jax.nn.sigmoid(gate) * ups[at]).astype(bfloat)
                return held

            chunks(body, 0, 32, wide)

        def outer(image):
            return dot(acts[image * length : (image + 1) * length], ff[2], ((1,), (1,)))

        inner(1)
        r["parts_send"][0] = outer(3).astype(bfloat)
        first_parts[0].start()
        r["hold_far"][...] = outer(2)
        inner(0)
        add_far(first_parts)
        r["parts_send"][2] = outer(1).astype(bfloat)
        first_parts[2].start()
        r["hold_near"][...] = outer(0)
        first_parts[2].wait_recv()
        first_parts[1].wait_recv()

        def ending(at, held):
            mixed = (
                r["hold_near"][at]
                + r["parts_recv"][2, at].astype(single)
                + r["parts_recv"][1, at].astype(single)
            )
            r["mixed"][at] = mixed
            end = r["hidden_mid"][at] + kind_of(5) * mixed
            r["normed_end"][at] = modulate_rows(end, kind_of(6), kind_of(7)).astype(bfloat)
            return held

        chunks(ending, 0)

        eps_weight, var_weight = r["small_all"][:, 32:48], r["small_all"][:, 48:64]
        normed_end = r["normed_end"][...]
        eps = dot(normed_end, eps_weight, ((1,), (0,))) + r["final_bias"][0:1]
        var = dot(normed_end, var_weight, ((1,), (0,))) + r["final_bias"][1:2]
        clean, noise, valid = r["clean"][...], r["noise"][...], r["valid"][...]
        root_bar, root_rest, log_beta, post_log, coefficient = (
            r["consts"][0:1, spot : spot + 1] for spot in range(5)
        )
        noisy = root_bar * clean + root_rest * noise
        fraction = (var + 1.0) * 0.5
        model_log = fraction * log_beta + (1.0 - fraction) * post_log
        start_est = (noisy - root_rest * eps) / root_bar
        gap = coefficient * (clean - start_est)
        ratio = jnp.exp(post_log - model_log)
        gap_part = gap * gap * jnp.exp(-model_log)
        scale_by = 0.5 / math.log(2.0)
        terms = (eps - noise) * (eps - noise) + scale_by * (
            -1.0 + model_log - post_log + ratio + gap_part
        )
        terms = jnp.where(valid > 0.0, terms, 0.0)
        r["loss"][...] = jnp.sum(jnp.sum(terms, axis=1, keepdims=True), axis=0, keepdims=True)
        d_eps = 2.0 * (eps - noise) + 2.0 * scale_by * gap * jnp.exp(-model_log) * (
            coefficient * root_rest / root_bar
        )
        d_var = scale_by * (1.0 - ratio - gap_part) * (0.5 * (log_beta - post_log))
        share = 1.0 / total_images
        d_eps = jnp.where(valid > 0.0, d_eps * share, 0.0).astype(bfloat)
        d_var = jnp.where(valid > 0.0, d_var * share, 0.0).astype(bfloat)
        r["output_sum"][0:1] = jnp.sum(d_eps.astype(single), axis=0, keepdims=True)
        r["output_sum"][1:2] = jnp.sum(d_var.astype(single), axis=0, keepdims=True)
        r["grad_final"][0] = dot(d_eps, normed_end, ((0,), (0,)))
        r["grad_final"][1] = dot(d_var, normed_end, ((0,), (0,)))
        r["hold_far"][...] = dot(d_eps, eps_weight, ((1,), (1,))) + dot(
            d_var, var_weight, ((1,), (1,))
        )

        def end_back(at, held):
            shift_sum, scale_sum, gate_sum = held
            mixed, grad = r["mixed"][at], r["hold_far"][at]
            end = r["hidden_mid"][at] + kind_of(5) * mixed
            back, normal = modulate_back(end, grad, kind_of(7))
            r["d_end"][at] = back
            r["dm_rows"][0, at] = (kind_of(5) * back).astype(bfloat)
            return (
                shift_sum + fold(grad),
                scale_sum + fold(grad * normal),
                gate_sum + fold(mixed * back),
            )

        shift_sum, scale_sum, gate_sum = chunks(end_back, (zeros, zeros, zeros))
        dm_far.start()
        dm_near.start()
        for kind, value in ((6, shift_sum), (7, scale_sum), (5, gate_sum)):
            r["d_modulation"][kind : kind + 1] = jnp.sum(value, axis=0, keepdims=True)

        def inner_back(which):
            spot = pl.ds(which * wide, wide)
            gradient = dot(rows_of(r["dm_rows"], which), ff[2], ((1,), (0,)))
            gate, up_val = gates[spot], ups[spot]
            sigma = jax.nn.sigmoid(gate)
            d_ups[spot] = (gradient * gate * sigma).astype(bfloat)
            d_gates[spot] = (gradient * up_val * (sigma * (1.0 + gate * (1.0 - sigma)))).astype(
                bfloat
            )

        def outer_back(image):
            spot = pl.ds(image * length, length)
            return dot(d_gates[spot], ff[0], ((1,), (1,))) + dot(d_ups[spot], ff[1], ((1,), (1,)))

        dm_near.wait_recv()
        inner_back(0)
        dm_far.wait_recv()
        dm_on.start()
        dm_on.wait_recv()
        inner_back(1)
        for copy in first_parts:
            copy.wait_send()
        r["parts_send"][0] = outer_back(3).astype(bfloat)
        second_parts[0].start()
        r["hold_far"][...] = outer_back(2)
        r["g_ff"][2] = dot(
            r["dm_rows"][...].reshape(2 * wide, D), acts[...], ((0,), (0,))
        ).astype(bfloat)
        ff_start(2)
        add_far(second_parts)
        r["parts_send"][2] = outer_back(1).astype(bfloat)
        second_parts[2].start()
        r["hold_near"][...] = outer_back(0)
        flat = two_rows[...].reshape(2 * wide, D)
        r["g_ff"][0] = dot(flat, d_gates[...], ((0,), (0,))).astype(bfloat)
        ff_start(0)
        r["g_ff"][1] = dot(flat, d_ups[...], ((0,), (0,))).astype(bfloat)
        ff_start(1)

    pl.run_scoped(
        swiglu,
        pltpu.VMEM((3, D, units), bfloat),
        pltpu.VMEM((n_model, length, D), bfloat),
        pltpu.VMEM((n_model * length, units), single),
        pltpu.VMEM((n_model * length, units), single),
        pltpu.VMEM((n_model * length, units), bfloat),
        pltpu.VMEM((n_model * length, units), bfloat),
        pltpu.VMEM((n_model * length, units), bfloat),
    )

    db_near, db_far, db_on = spread(Sender(r["db_s"], r["db_r"]), r["db_rows"])
    ox, oz = Sender(r["ox_s"], r["ox_r"]), Sender(r["oz_s"], r["oz_r"])
    out_aside = ox(0, r["g_out"].at[1 - x], r["x_out"], at_dp(side))
    owner = z == m
    behind = lax.rem(z + depth - m, depth)
    out_along = oz(
        lax.rem(behind + depth - 1, depth),
        r["g_out"].at[x],
        r["z_out"].at[lax.rem(behind + depth - 1, depth)],
        at_dp(m * NX + x),
    )

    def attend(low, attended, trig, one_rows, qkv_weight, out_weight, d_attended, d_qkv):
        loads = []
        for spot, (name, place) in enumerate(
            (
                ("out_weight", out_weight),
                ("low", low),
                ("trig_all", trig),
                ("attended", attended),
                ("one_rows", one_rows),
                ("qkv_weight", qkv_weight),
            )
        ):
            load = pltpu.make_async_copy(r[name], place, r["local_sem"].at[2 + spot])
            load.start()
            loads.append(load)
        second_parts[2].wait_recv()
        second_parts[1].wait_recv()

        def mid_back(at, held):
            shift_sum, scale_sum, gate_sum, branch_sum = held
            grad = (
                r["hold_near"][at]
                + r["parts_recv"][2, at].astype(single)
                + r["parts_recv"][1, at].astype(single)
            )
            back, normal = modulate_back(r["hidden_mid"][at], grad, kind_of(4))
            total = r["d_end"][at] + back
            r["d_end"][at] = total
            d_branch = (kind_of(2) * total).astype(bfloat)
            r["db_rows"][0, at] = d_branch
            return (
                shift_sum + fold(grad),
                scale_sum + fold(grad * normal),
                gate_sum + fold(r["branch"][at] * total),
                branch_sum + fold(d_branch.astype(single)),
            )

        sums = chunks(mid_back, (zeros, zeros, zeros, zeros))
        db_far.start()
        db_near.start()
        for kind, value in zip((3, 4, 2), sums):
            r["d_modulation"][kind : kind + 1] = jnp.sum(value, axis=0, keepdims=True)
        r["branch_sum"][...] = jnp.sum(sums[3], axis=0, keepdims=True)
        for load in loads:
            load.wait()

        def image_body(image, carry):
            d_attended[...] = dot(
                r["db_rows"][image], out_weight[...], ((1,), (1,))
            ).astype(bfloat)
            rank = (
                2 * lax.rem(lax.div(m, 2) + lax.div(image, 2), 2)
                + lax.rem(lax.rem(m, 2) + lax.rem(image, 2), 2)
            )
            count = r["facts_all"][d * n_model + rank, 2:3, 1:2]
            mask = lax.broadcasted_iota(jnp.int32, (1, length), 1).astype(single) < count
            cosine, sine = trig[image, 0], trig[image, 1]
            scale_by = 1.0 / math.sqrt(HDIM)
            for head in range(heads):
                start = head * HDIM

                def spot(which):
                    begin = which * head_cols + start
                    return slice(begin, begin + HDIM)

                query, key, value = (low[image, :, spot(which)] for which in range(3))
                grad = d_attended[:, start : start + HDIM]
                scores = dot(query, key, ((1,), (1,))) * scale_by
                scores = jnp.where(mask, scores, -1e30)
                probs = jnp.exp(scores - r["totals"][image, :, head : head + 1])
                d_probs = dot(grad, value, ((1,), (1,)))
                row = jnp.sum(probs * d_probs, axis=-1, keepdims=True)
                d_scores = (probs * (d_probs - row)).astype(bfloat)
                d_query = dot(d_scores, key, ((1,), (0,))) * scale_by
                d_key = dot(d_scores, query, ((0,), (0,))) * scale_by
                d_value = dot(probs.astype(bfloat), grad, ((0,), (0,)))
                for which, turned in ((0, d_query), (1, d_key)):
                    back = turned * cosine + swapped(turned * sine)
                    d_qkv[image, :, spot(which)] = back.astype(bfloat)
                d_qkv[image, :, spot(2)] = d_value.astype(bfloat)
            return carry

        db_near.wait_recv()
        lax.fori_loop(0, 2, image_body, 0)
        db_far.wait_recv()
        db_on.start()
        ff_beside(2)
        db_on.wait_recv()
        lax.fori_loop(2, n_model, image_body, 0)

        def one_part(image):
            return dot(d_qkv[image], qkv_weight[...], ((1,), (1,)))

        for copy in second_parts:
            copy.wait_send()
        r["parts_send"][0] = one_part(3).astype(bfloat)
        third_parts[0].start()
        r["hold_far"][...] = one_part(2)
        ff_beside(0)
        ff_service(2, 0)
        add_far(third_parts)
        r["parts_send"][2] = one_part(1).astype(bfloat)
        third_parts[2].start()
        r["hold_near"][...] = one_part(0)
        flat_grad = d_qkv[...].reshape(n_model * length, 3 * head_cols)
        r["g_qkv"][...] = dot(
            one_rows[...].reshape(n_model * length, D), flat_grad, ((0,), (0,))
        ).astype(bfloat)
        for step in range(depth):
            qkv_aside(step).start()
        r["g_out"][...] = (
            dot(
                attended[...].reshape(n_model * length, head_cols),
                r["db_rows"][...].reshape(n_model * length, D),
                ((0,), (0,)),
            )
            .astype(bfloat)
            .reshape(NX, rows, D)
        )
        out_aside.start()
        ones = jnp.ones((8, n_model * length), bfloat)
        r["qkv_sum"][...] = dot(ones, flat_grad, ((1,), (0,)))[0:1]

    pl.run_scoped(
        attend,
        pltpu.VMEM((n_model, length, 3 * head_cols), bfloat),
        pltpu.VMEM((n_model, length, head_cols), bfloat),
        pltpu.VMEM((n_model, 2, length, HDIM), single),
        pltpu.VMEM((n_model, length, D), bfloat),
        pltpu.VMEM((D, 3 * head_cols), bfloat),
        pltpu.VMEM((head_cols, D), bfloat),
        pltpu.VMEM((length, head_cols), bfloat),
        pltpu.VMEM((n_model, length, 3 * head_cols), bfloat),
    )
    ff_beside(1)
    ff_service(0, 0)
    ff_service(2, 1)
    third_parts[2].wait_recv()
    third_parts[1].wait_recv()

    def first_back(at, held):
        shift_sum, scale_sum, hidden_sum = held
        grad = (
            r["hold_near"][at]
            + r["parts_recv"][2, at].astype(single)
            + r["parts_recv"][1, at].astype(single)
        )
        back, normal = modulate_back(r["hidden"][at], grad, kind_of(1))
        d_hidden = (r["d_end"][at] + back).astype(bfloat)
        r["normed_end"][at] = d_hidden
        return (
            shift_sum + fold(grad),
            scale_sum + fold(grad * normal),
            hidden_sum + fold(d_hidden.astype(single)),
        )

    sums = chunks(first_back, (zeros, zeros, zeros))
    for kind in range(2):
        r["d_modulation"][kind : kind + 1] = jnp.sum(sums[kind], axis=0, keepdims=True)
    r["hidden_sum"][...] = jnp.sum(sums[2], axis=0, keepdims=True)
    r["grad_patch"][...] = dot(r["noisy"][...], r["normed_end"][...], ((0,), (0,)))

    ff_service(1, 0)
    ff_service(0, 1)
    ff_service(2, 2)
    ff_service(1, 1)
    ff_service(0, 2)
    ff_service(1, 2)
    qkv_beside()
    out_aside.wait()
    r["g_out"][x] = (r["g_out"][x].astype(single) + r["x_out"][...].astype(single)).astype(bfloat)

    @pl.when(jnp.logical_not(owner))
    def _():
        out_along.start()

    for step in range(depth - 1):
        qkv_service(step)
    qkv_near, qkv_far, qkv_on = spread(Sender(r["qa_s"], r["qa_r"]), r["grad_qkv"])
    qkv_far.start()
    qkv_near.start()
    give = Sender(r["oa_s"], r["oa_r"])
    partners = [(d, near_rank), (d, far_rank), (d, lax.rem(near_rank + 2, 4))]
    gives = [
        give(spot, r["out_mine"], r["out_mine"], partner) for spot, partner in enumerate(partners)
    ]

    @pl.when(owner)
    def _():
        total = r["g_out"][x].astype(single)
        for step in range(depth - 1):
            oz(step, r["g_out"].at[x], r["z_out"].at[step], at_dp(up)).wait_recv()
            total = total + r["z_out"][step].astype(single)
        r["out_mine"][...] = total.astype(bfloat)
        for copy in gives:
            copy.start()

    for spot, partner in enumerate(partners):

        @pl.when(z == partner[1])
        def _():
            gives[spot].wait_recv()

    qkv_far.wait_recv()
    qkv_on.start()
    r["grad_out"][...] = r["out_mine"][...]

    @pl.when(owner)
    def _():
        for copy in gives:
            copy.wait_send()

    @pl.when(jnp.logical_not(owner))
    def _():
        out_along.wait_send()

    qkv_near.wait()
    qkv_on.wait()
    qkv_far.wait_send()
    for copy in (dm_near, dm_far, dm_on, db_near, db_far, db_on, *third_parts):
        copy.wait_send()
    for step in range(depth):
        qkv_aside(step).wait_send()
        for which in range(3):
            ff_aside(which, step).wait_send()
    for step in range(depth - 1):
        for part in range(2):
            qkv_along(step, part).wait_send()
            for which in range(3):
                ff_along(which, step, part).wait_send()


def backward_all(values, sizes, total_images, collective):
    n_data, n_model = sizes
    bfloat, single = jnp.bfloat16, jnp.float32
    rows = D // n_data
    heads = HEADS // n_model
    head_cols = heads * HDIM
    length = values["clean"].shape[0]
    units = values["ff"].shape[2]
    half = units // 2
    depth = n_data // NX
    shapes = dict(
        grad_ff=((3, rows, units), single),
        grad_qkv=((n_model, rows, 3 * head_cols), bfloat),
        grad_out=((rows, D), bfloat),
        d_modulation=((8, D), single),
        hidden_sum=((1, D), single),
        branch_sum=((1, D), single),
        qkv_sum=((1, 3 * head_cols), single),
        output_sum=((2, CH), single),
        loss=((1, 1), single),
        grad_patch=((CH, D), single),
        grad_final=((2, CH, D), single),
    )
    vmem, dma = pltpu.VMEM, pltpu.SemaphoreType.DMA
    scratch = dict(
        mixed=vmem((length, D), single),
        d_end=vmem((length, D), single),
        dm_rows=vmem((n_model, length, D), bfloat),
        db_rows=vmem((n_model, length, D), bfloat),
        hold_far=vmem((length, D), single),
        hold_near=vmem((length, D), single),
        parts_send=vmem((3, length, D), bfloat),
        parts_recv=vmem((3, length, D), bfloat),
        normed_end=vmem((length, D), bfloat),
        g_ff=vmem((3, D, units), bfloat),
        x_ff=vmem((3, depth, rows, units), bfloat),
        z_ff=vmem((3, depth - 1, 2, rows, half), bfloat),
        g_qkv=vmem((D, 3 * head_cols), bfloat),
        x_qkv=vmem((depth, rows, 3 * head_cols), bfloat),
        z_qkv=vmem((depth - 1, rows, 3 * head_cols), bfloat),
        g_out=vmem((NX, rows, D), bfloat),
        x_out=vmem((rows, D), bfloat),
        z_out=vmem((depth - 1, rows, D), bfloat),
        out_mine=vmem((rows, D), bfloat),
        local_sem=dma((8,)),
    )
    counts = dict(
        dm=(3,),
        db=(3,),
        pa=(3,),
        pb=(3,),
        pc=(3,),
        fx=(3, depth),
        fz=(3, depth - 1, 2),
        qx=(depth,),
        qz=(depth - 1, 2),
        ox=(1,),
        oz=(depth - 1,),
        qa=(3,),
        oa=(3,),
    )
    for name, count in counts.items():
        scratch[name + "_s"] = dma(count)
        scratch[name + "_r"] = dma(count)
    far = {
        "ff", "two_rows", "low", "trig_all", "attended", "one_rows", "qkv_weight", "out_weight"
    }

    def space(name):
        return pl.BlockSpec(memory_space=pl.ANY if name in far else pltpu.VMEM)

    outs = pl.pallas_call(
        functools.partial(back_kernel, sizes, total_images),
        out_shape=[jax.ShapeDtypeStruct(*shapes[name]) for name in BACK_OUT],
        in_specs=[space(name) for name in BACK_IN],
        out_specs=[space(name) for name in BACK_OUT],
        scratch_shapes=[scratch[name] for name in BACK_SCRATCH],
        compiler_params=pltpu.CompilerParams(
            collective_id=collective, has_side_effects=True, vmem_limit_bytes=60 * 2**20
        ),
    )(*[values[name] for name in BACK_IN])
    return dict(zip(BACK_OUT, outs))


def forward_plain(clean_three, noise_three, patch_grid, labels, timesteps, matrices, embeddings, swiglu_weights, biases):
    bfloat = jnp.bfloat16
    single = jnp.float32
    images = labels.shape[0]
    length = clean_three.shape[1]
    n_model = lax.axis_size("mlp")
    n_data = lax.axis_size("dp")
    sizes = (n_data, n_model)
    total_images = images * n_data * n_model
    rows = D // n_data
    owned_start = lax.axis_index("dp") * rows
    data_index = lax.axis_index("dp")
    model_index = lax.axis_index("mlp")
    heads = HEADS // n_model
    head_cols = heads * HDIM
    qkv_shard = jnp.concatenate(
        [
            cut_columns(matrices, 9 * D + part * D + model_index * head_cols, head_cols)
            for part in range(3)
        ],
        axis=1,
    ).astype(bfloat)
    out_shard = matrices[:, 12 * D : 13 * D].astype(bfloat)
    swiglu_shard = swiglu_weights.astype(bfloat)
    qkv_weight = lax.all_gather(qkv_shard, "dp", axis=0, tiled=True)
    swiglu_use = lax.all_gather(swiglu_shard, "dp", axis=1, tiled=True)
    out_weight = gather_out(out_shard, sizes)

    time_second = matrices[:, :D].astype(bfloat)
    mod_weight = matrices[:, D : 9 * D].astype(bfloat)
    time_first = embeddings[CH : CH + FREQ].astype(bfloat)
    class_table = embeddings[CH + FREQ :].astype(bfloat)
    patch_bias = biases[:D]
    first_bias = biases[D : 2 * D]
    second_bias = biases[2 * D : 3 * D]
    mod_bias = biases[3 * D : 11 * D]
    qkv_bias = biases[11 * D : 14 * D]
    out_bias = biases[14 * D : 15 * D]
    final_bias = biases[15 * D :]

    facts = jnp.concatenate([timesteps[:, None], labels[:, None], patch_grid], axis=1)
    facts = jnp.pad(facts, ((0, 8 - images), (0, 124)))
    (facts_all,) = exchange([(facts, "all")], "both", sizes, 0)
    facts_all = facts_all[:, 0, :4]
    steps_all, labels_all, grid_all = facts_all[:, 0], facts_all[:, 1], facts_all[:, 2:4]
    sinus_all = sinusoid(steps_all).astype(bfloat)
    first_bias_own = lax.dynamic_slice_in_dim(first_bias, owned_start, rows)
    second_bias_own = lax.dynamic_slice_in_dim(second_bias, owned_start, rows)
    time_pre = jnp.dot(sinus_all, time_first, preferred_element_type=single) + first_bias_own
    time_act = jax.nn.silu(time_pre).astype(bfloat)
    time_part = jnp.dot(time_act, time_second, preferred_element_type=single)
    small_shard = jnp.concatenate(
        [embeddings[:CH], matrices[:, 13 * D :].T], axis=0
    ).astype(bfloat)
    time_parts, small_all = exchange(
        [
            (time_part.reshape(total_images, n_data, rows).transpose(1, 0, 2), "each"),
            (small_shard, "all"),
        ],
        "dp",
        sizes,
        1,
    )
    small_all = small_all.transpose(1, 0, 2).reshape(3 * CH, D)
    patch_weight = small_all[:CH]
    final_weight = small_all[CH:].T
    time_emb = jnp.sum(time_parts, axis=0) + second_bias_own
    onehot = (labels_all[:, None] == jnp.arange(CLASSES + 1, dtype=jnp.int32)[None, :]).astype(
        bfloat
    )
    condition = time_emb + jnp.dot(onehot, class_table, preferred_element_type=single)
    cond_act = jax.nn.silu(condition).astype(bfloat)
    cond_rank = lax.dynamic_index_in_dim(
        cond_act.reshape(n_data, n_model, rows), model_index, 1, keepdims=False
    )
    mod_part = jnp.dot(cond_rank, mod_weight, preferred_element_type=single)
    (mod_parts,) = exchange(
        [(mod_part.reshape(n_data, 8, D), "each")],
        "dp",
        sizes,
        2,
    )
    modulation = jnp.sum(mod_parts, axis=0).reshape(1, 8 * D) + mod_bias
    shift_one, scale_one, gate_one, shift_two, scale_two, gate_two, shift_end, scale_end = (
        jnp.split(modulation, 8, axis=1)
    )

    group_grid = lax.dynamic_slice_in_dim(grid_all, data_index * n_model, n_model, 0)
    group_grid = jnp.stack(
        [
            lax.dynamic_index_in_dim(group_grid, model_index ^ rank, 0, keepdims=False)
            for rank in range(n_model)
        ]
    )
    cosine, sine, mask = turn_tables(group_grid, length)
    noisy_low = noisy_input(clean_three, noise_three, timesteps).astype(bfloat)
    hidden = jnp.dot(noisy_low, patch_weight, preferred_element_type=single) + patch_bias
    normed_one = modulate(hidden, shift_one, scale_one).astype(bfloat)
    one_rows = jnp.concatenate(gather_rows(normed_one.reshape(length, D), n_model), axis=0)
    qkv_bias_own = jnp.concatenate(
        [
            lax.dynamic_slice_in_dim(qkv_bias, part * D + model_index * head_cols, head_cols)
            for part in range(3)
        ]
    )
    qkv = jnp.dot(one_rows, qkv_weight, preferred_element_type=single) + qkv_bias_own
    low, attended, log_total = attention(
        qkv.reshape(n_model, length, 3 * head_cols), cosine, sine, mask, heads
    )
    attended_rows = attended.reshape(n_model * length, head_cols)
    branch_part = jnp.dot(attended_rows, out_weight, preferred_element_type=single).astype(bfloat)
    branch_part = branch_part.reshape(n_model, length, D)
    branch = (
        scatter_rows(
            (branch_part[2], branch_part[3]), (branch_part[0], branch_part[1]), n_model
        )[None]
        + out_bias
    )
    hidden_mid = hidden + gate_one[:, None, :] * branch
    normed_two = modulate(hidden_mid, shift_two, scale_two).astype(bfloat)
    two_rows = gather_rows(normed_two.reshape(length, D), n_model)
    return dict(
        steps=sinus_all,
        onehot=onehot,
        time_pre=time_pre,
        condition=condition,
        modulation=modulation,
        hidden=hidden,
        one_rows=one_rows,
        qkv_weight=qkv_weight,
        out_weight=out_weight,
        swiglu=swiglu_use,
        low=low,
        attended=attended,
        totals=log_total,
        branch=branch,
        hidden_mid=hidden_mid,
        two_rows=two_rows,
        final_weight=final_weight,
        tables=(cosine, sine, mask),
    )


def forward_fused(clean_three, noise_three, patch_grid, labels, timesteps, matrices, embeddings, swiglu_weights, biases):
    bfloat = jnp.bfloat16
    single = jnp.float32
    length = clean_three.shape[1]
    n_model = lax.axis_size("mlp")
    n_data = lax.axis_size("dp")
    everyone = n_data * n_model
    rows = D // n_data
    owned_start = lax.axis_index("dp") * rows
    model_index = lax.axis_index("mlp")
    head_cols = HEADS // n_model * HDIM

    def own_bias(start, amount, offset):
        return lax.dynamic_slice_in_dim(biases, start + offset, amount)[None]

    sinus = sinusoid(timesteps).astype(bfloat).astype(single).reshape(2, 128)
    facts = jnp.concatenate(
        [labels, patch_grid[:, 0] * patch_grid[:, 1]]
    ).astype(single)
    facts = jnp.concatenate(
        [sinus, jnp.pad(facts[None], ((0, 0), (0, 126))), jnp.zeros((5, 128), single)], axis=0
    )
    cosine, sine, _ = turn_tables(patch_grid, length)
    small = jnp.concatenate(
        [
            embeddings[:CH].T,
            jnp.zeros((rows, CH), single),
            matrices[:, 13 * D :],
            jnp.zeros((rows, 64), single),
        ],
        axis=1,
    ).astype(bfloat)
    values = dict(
        facts=facts,
        trig=jnp.concatenate([cosine, sine], axis=0),
        small=small,
        time_first=embeddings[CH : CH + FREQ].astype(bfloat),
        first_bias=own_bias(D, rows, owned_start),
        second_bias=own_bias(2 * D, rows, owned_start),
        time_blocks=matrices[:, :D].astype(bfloat).reshape(rows, n_data, rows).transpose(1, 0, 2),
        class_table=embeddings[CH + FREQ :].astype(bfloat),
        mod_weight=matrices[:, D : 9 * D].astype(bfloat),
        mod_bias=biases[3 * D : 11 * D].reshape(8, D),
        noisy=noisy_input(clean_three, noise_three, timesteps).astype(bfloat)[0],
        patch_bias=biases[None, :D],
        qkv_shard=jnp.concatenate(
            [
                cut_columns(matrices, (9 + part) * D + model_index * head_cols, head_cols)
                for part in range(3)
            ],
            axis=1,
        ).astype(bfloat),
        out_shard=matrices[:, 12 * D : 13 * D].astype(bfloat),
        ff_shard=swiglu_weights.astype(bfloat),
        qkv_bias=jnp.concatenate(
            [
                own_bias((11 + part) * D, head_cols, model_index * head_cols)
                for part in range(3)
            ],
            axis=1,
        ),
        out_bias=biases[None, 14 * D : 15 * D],
    )
    out = forward_all(values, (n_data, n_model), 0)
    raw = {name: out[name] for name in BACK_IN if name in out}
    facts_all = out["facts_all"]
    group = lax.dynamic_slice_in_dim(
        facts_all[:, 2, 1], lax.axis_index("dp") * n_model, n_model
    )
    spots = model_index ^ jnp.arange(n_model)
    counts = jnp.sum(
        jnp.where(spots[:, None] == jnp.arange(n_model)[None, :], group[None, :], 0.0), axis=1
    )
    mask = jnp.arange(length, dtype=jnp.int32)[None, None, :] < counts[:, None, None]
    return dict(
        raw=dict(raw, noisy=values["noisy"]),
        steps=facts_all[:, :2].reshape(everyone, FREQ).astype(bfloat),
        onehot=(
            facts_all[:, 2, 0:1] == jnp.arange(CLASSES + 1, dtype=jnp.int32)[None].astype(single)
        ).astype(bfloat),
        time_pre=out["time_pre"],
        condition=out["condition"],
        modulation=out["modulation"].reshape(1, 8 * D),
        hidden=out["hidden"][None],
        one_rows=out["one_rows"].reshape(n_model * length, D),
        qkv_weight=out["qkv_weight"],
        out_weight=out["out_weight"],
        swiglu=out["ff"],
        low=out["low"],
        attended=out["attended"],
        totals=out["totals"],
        branch=out["branch"][None],
        hidden_mid=out["hidden_mid"][None],
        two_rows=tuple(out["two_rows"]),
        final_weight=out["small_all"][:, 2 * CH : 4 * CH],
        tables=(out["trig_all"][:, 0], out["trig_all"][:, 1], mask.astype(single)),
    )


def backward_plain(
    kept, clean_three, noise_three, patch_grid, timesteps, swiglu_weights, biases, total_images
):
    bfloat = jnp.bfloat16
    single = jnp.float32
    images, length = clean_three.shape[:2]
    n_model = lax.axis_size("mlp")
    n_data = lax.axis_size("dp")
    sizes = (n_data, n_model)
    rows = D // n_data
    model_index = lax.axis_index("mlp")
    heads = HEADS // n_model
    head_cols = heads * HDIM
    hidden_units = swiglu_weights.shape[2]
    valid_slot = valid_slots(patch_grid, length)
    final_bias = biases[15 * D :]
    noisy_low = noisy_input(clean_three, noise_three, timesteps).astype(bfloat)
    modulation, hidden, hidden_mid, branch = (
        kept[name] for name in ("modulation", "hidden", "hidden_mid", "branch")
    )
    shift_one, scale_one, gate_one, shift_two, scale_two, gate_two, shift_end, scale_end = (
        jnp.split(modulation, 8, axis=1)
    )
    qkv_weight, out_weight, swiglu_use = kept["qkv_weight"], kept["out_weight"], kept["swiglu"]
    final_weight, one_rows, two_rows = kept["final_weight"], kept["one_rows"], kept["two_rows"]
    low, log_total = kept["low"], kept["totals"]
    attended_rows = kept["attended"].reshape(n_model * length, head_cols)
    cosine, sine, mask = kept["tables"]
    two_halves = (
        jnp.concatenate(two_rows[:2], axis=0),
        jnp.concatenate(two_rows[2:], axis=0),
    )
    gates, ups, acts, parts = [], [], [], []
    for part in two_halves:
        gate_val = jnp.dot(part, swiglu_use[0], preferred_element_type=single)
        up_val = jnp.dot(part, swiglu_use[1], preferred_element_type=single)
        act = (jax.nn.silu(gate_val) * up_val).astype(bfloat)
        gates.append(gate_val)
        ups.append(up_val)
        acts.append(act)
        parts.append(backward_product(act, swiglu_use[2]).astype(bfloat).reshape(2, length, D))
    mixed = scatter_rows(parts[1], parts[0], n_model)[None]
    hidden_end = hidden_mid + gate_two[:, None, :] * mixed
    normed_end = modulate(hidden_end, shift_end, scale_end).astype(bfloat)
    output = jnp.dot(normed_end, final_weight, preferred_element_type=single) + final_bias
    local_loss, loss_pull = jax.vjp(
        lambda values_out: loss_terms(values_out, clean_three, noise_three, timesteps, valid_slot),
        output,
    )
    d_output = loss_pull(jnp.asarray(1.0 / total_images, single))[0].astype(bfloat)
    d_normed_end = backward_product(d_output, final_weight)
    unused, pull_end = jax.vjp(modulate, hidden_end, shift_end, scale_end)
    d_hidden_end, d_shift_end, d_scale_end = pull_end(d_normed_end)
    d_mixed = (gate_two[:, None, :] * d_hidden_end).astype(bfloat)
    d_gate_two = jnp.sum(mixed * d_hidden_end, axis=1)
    dmixed_rows = gather_rows(d_mixed.reshape(length, D), n_model)
    dmixed_halves = (
        jnp.concatenate(dmixed_rows[:2], axis=0),
        jnp.concatenate(dmixed_rows[2:], axis=0),
    )
    d_gates, d_ups, d_parts = [], [], []
    for part, gate_val, up_val in zip(dmixed_halves, gates, ups):
        d_inner = jnp.dot(part, swiglu_use[2], preferred_element_type=single)
        unused, pull_glu = jax.vjp(
            lambda gate_in, up_in: jax.nn.silu(gate_in) * up_in, gate_val, up_val
        )
        d_gate, d_up = pull_glu(d_inner)
        d_gate, d_up = d_gate.astype(bfloat), d_up.astype(bfloat)
        d_gates.append(d_gate)
        d_ups.append(d_up)
        d_parts.append(
            (backward_product(d_gate, swiglu_use[0]) + backward_product(d_up, swiglu_use[1]))
            .astype(bfloat)
            .reshape(2, length, D)
        )
    d_normed_two = scatter_rows(d_parts[1], d_parts[0], n_model)[None]
    rows_ready = jnp.concatenate(two_halves, axis=0)
    dmixed_ready = jnp.concatenate(dmixed_halves, axis=0)
    half = hidden_units // 2

    def owned(gradient, cut):
        return reduce_dp(gradient.reshape(n_data, rows, -1), n_data, cut)

    grad_swiglu = jnp.stack(
        [
            owned(weight_grad(rows_ready, jnp.concatenate(d_gates, axis=0)), half),
            owned(weight_grad(rows_ready, jnp.concatenate(d_ups, axis=0)), half),
            owned(weight_grad(dmixed_ready, jnp.concatenate(acts, axis=0)), half),
        ]
    )
    unused, pull_two = jax.vjp(modulate, hidden_mid, shift_two, scale_two)
    d_mid_part, d_shift_two, d_scale_two = pull_two(d_normed_two)
    d_hidden_mid = d_hidden_end + d_mid_part
    d_branch = (gate_one[:, None, :] * d_hidden_mid).astype(bfloat)
    d_gate_one = jnp.sum(branch * d_hidden_mid, axis=1)

    dbranch_rows = jnp.concatenate(gather_rows(d_branch.reshape(length, D), n_model), axis=0)
    d_attended = backward_product(dbranch_rows, out_weight).astype(bfloat)
    d_qkv = attention_back(
        low,
        log_total,
        d_attended.reshape(n_model, length, head_cols),
        cosine,
        sine,
        mask,
        heads,
    ).reshape(n_model * length, 3 * head_cols)
    grad_out = reduce_out(weight_grad(attended_rows, dbranch_rows), sizes)
    grad_qkv_own = owned(weight_grad(one_rows, d_qkv), 384)
    d_one_part = backward_product(d_qkv, qkv_weight).astype(bfloat).reshape(n_model, length, D)
    d_normed_one = scatter_rows(
        (d_one_part[2], d_one_part[3]), (d_one_part[0], d_one_part[1]), n_model
    )[None]
    unused, pull_one = jax.vjp(modulate, hidden, shift_one, scale_one)
    d_hidden_part, d_shift_one, d_scale_one = pull_one(d_normed_one)
    d_hidden = (d_hidden_mid + d_hidden_part).astype(bfloat)

    return dict(
        d_modulation=jnp.concatenate(
            [
                d_shift_one,
                d_scale_one,
                d_gate_one,
                d_shift_two,
                d_scale_two,
                d_gate_two,
                d_shift_end,
                d_scale_end,
            ],
            axis=1,
        ),
        hidden_sum=column_sum(d_hidden),
        branch_sum=column_sum(d_branch),
        qkv_sum=column_sum(d_qkv),
        output_sum=column_sum(d_output),
        loss=local_loss.reshape(1),
        grad_patch=weight_grad(noisy_low, d_hidden),
        grad_final=weight_grad(normed_end, d_output).T,
        grad_swiglu=grad_swiglu,
        grad_out=grad_out,
        grad_qkv=jnp.stack(gather_rows(grad_qkv_own.astype(bfloat), n_model)).astype(single),
    )


def backward_fused(
    kept, clean_three, noise_three, patch_grid, timesteps, swiglu_weights, biases, total_images
):
    single = jnp.float32
    length = clean_three.shape[1]
    sizes = (lax.axis_size("dp"), lax.axis_size("mlp"))
    beta_now, bar_now, bar_prev = plan(timesteps)
    consts = jnp.stack(
        [
            jnp.sqrt(bar_now),
            jnp.sqrt(1.0 - bar_now),
            jnp.log(beta_now),
            jnp.log(beta_now * (1.0 - bar_prev) / (1.0 - bar_now)),
            beta_now * jnp.sqrt(bar_prev) / (1.0 - bar_now),
        ],
        axis=1,
    )
    values = dict(
        kept["raw"],
        final_bias=biases[15 * D :].reshape(2, CH),
        clean=clean_three[0],
        noise=noise_three[0],
        consts=jnp.pad(consts, ((0, 7), (0, 123))),
        valid=valid_slots(patch_grid, length).astype(single).reshape(length, 1),
    )
    out = backward_all(values, sizes, total_images, 1)
    return dict(
        d_modulation=out["d_modulation"].reshape(1, 8 * D),
        hidden_sum=out["hidden_sum"].reshape(-1),
        branch_sum=out["branch_sum"].reshape(-1),
        qkv_sum=out["qkv_sum"].reshape(-1),
        output_sum=out["output_sum"].reshape(-1),
        loss=out["loss"].reshape(1),
        grad_patch=out["grad_patch"],
        grad_final=out["grad_final"].reshape(2 * CH, D),
        grad_swiglu=out["grad_ff"],
        grad_out=out["grad_out"].astype(single),
        grad_qkv=out["grad_qkv"].astype(single),
    )


def on_device(
    clean_patches,
    noise_patches,
    patch_grid,
    labels,
    timesteps,
    matrices,
    embeddings,
    swiglu_weights,
    biases,
    matrices_first,
    embeddings_first,
    swiglu_first,
    biases_first,
    matrices_second,
    embeddings_second,
    swiglu_second,
    biases_second,
    matrices_average,
    embeddings_average,
    swiglu_average,
    biases_average,
):
    bfloat = jnp.bfloat16
    single = jnp.float32
    images = labels.shape[0]
    length = clean_patches.shape[0] // images
    n_model = lax.axis_size("mlp")
    n_data = lax.axis_size("dp")
    sizes = (n_data, n_model)
    total_images = images * n_data * n_model
    rows = D // n_data
    owned_start = lax.axis_index("dp") * rows
    data_index = lax.axis_index("dp")
    model_index = lax.axis_index("mlp")
    heads = HEADS // n_model
    head_cols = heads * HDIM
    hidden_units = swiglu_weights.shape[2]

    clean_three = clean_patches.reshape(images, length, CH)
    noise_three = noise_patches.reshape(images, length, CH)
    fused = (n_data, n_model, images) == (8, 4, 1)
    forward = forward_fused if fused else forward_plain
    backward = backward_fused if fused else backward_plain
    kept = forward(
        clean_three,
        noise_three,
        patch_grid,
        labels,
        timesteps,
        matrices,
        embeddings,
        swiglu_weights,
        biases,
    )
    time_pre, condition, onehot, sinus_all = (
        kept[name] for name in ("time_pre", "condition", "onehot", "steps")
    )
    time_act = jax.nn.silu(time_pre).astype(bfloat)
    cond_act = jax.nn.silu(condition).astype(bfloat)
    time_second = matrices[:, :D].astype(bfloat)
    mod_weight = matrices[:, D : 9 * D].astype(bfloat)

    grads = backward(
        kept,
        clean_three,
        noise_three,
        patch_grid,
        timesteps,
        swiglu_weights,
        biases,
        total_images,
    )
    grad_swiglu, grad_out = grads["grad_swiglu"], grads["grad_out"]
    grad_qkv_own = grads["grad_qkv"][0]
    qkv_stack = jnp.stack(
        [
            lax.dynamic_index_in_dim(grads["grad_qkv"], model_index ^ rank, 0, keepdims=False)
            for rank in range(n_model)
        ]
    )
    grad_qkv = (
        qkv_stack.reshape(n_model, rows, 3, head_cols).transpose(1, 2, 0, 3).reshape(rows, 3 * D)
    )

    d_modulation = grads["d_modulation"].astype(bfloat)
    (dmod_all,) = exchange(
        [(d_modulation.reshape(16, D // 2), "all")], "both", sizes, 3
    )
    dmod_all = dmod_all.reshape(total_images, 8 * D)
    d_cond_act = backward_product(dmod_all, mod_weight)
    unused, pull_cond = jax.vjp(jax.nn.silu, condition)
    d_condition = pull_cond(d_cond_act)[0]
    d_time_emb = d_condition.astype(bfloat)
    (dtime_parts,) = exchange([(d_time_emb, "all")], "dp", sizes, 4)
    dtime_all = dtime_parts.transpose(1, 0, 2).reshape(total_images, D)
    d_time_act = backward_product(dtime_all, time_second)
    unused, pull_time = jax.vjp(jax.nn.silu, time_pre)
    d_time_pre = pull_time(d_time_act)[0]
    grad_time_second = weight_grad(time_act, dtime_all)
    grad_mod = weight_grad(cond_act, dmod_all)
    grad_time_first = jnp.dot(
        sinus_all.astype(single).T,
        d_time_pre,
        precision=lax.Precision.HIGHEST,
        preferred_element_type=single,
    )
    grad_table = jnp.dot(
        onehot.astype(single).T,
        d_condition,
        precision=lax.Precision.HIGHEST,
        preferred_element_type=single,
    )

    qkv_sums = grads["qkv_sum"].reshape(3, head_cols)
    qkv_bias_part = lax.dynamic_update_slice(
        jnp.zeros((3, D), single), qkv_sums, (0, model_index * head_cols)
    )
    local_sums = jnp.concatenate(
        [
            grads["hidden_sum"],
            qkv_bias_part.reshape(-1),
            grads["branch_sum"],
            grads["output_sum"],
            grads["loss"],
            jnp.zeros((95,), single),
            grads["grad_patch"].reshape(-1),
            grads["grad_final"].reshape(-1),
        ]
    )
    everyone = n_data * n_model
    chunk_rows = -(-local_sums.shape[0] // (everyone * 1024)) * 8
    local_sums = jnp.pad(local_sums, (0, everyone * chunk_rows * 128 - local_sums.shape[0]))
    (sum_parts,) = exchange(
        [(local_sums.reshape(everyone, chunk_rows, 128), "each")], "both", sizes, 5
    )
    chunk = jnp.sum(sum_parts, axis=0)
    local_squares = (
        jnp.sum(grad_time_second * grad_time_second)
        + jnp.sum(grad_mod * grad_mod)
        + jnp.sum(grad_out * grad_out)
        + jnp.sum(grad_time_first * grad_time_first)
        + jnp.sum(grad_table * grad_table)
    ) / n_model + jnp.sum(grad_swiglu * grad_swiglu) + jnp.sum(grad_qkv_own * grad_qkv_own)
    extra = jnp.concatenate([jnp.sum(d_time_pre, axis=0), local_squares.reshape(1)])
    extra = jnp.pad(extra, (0, 1024 - extra.shape[0])).reshape(8, 128)
    (late,) = exchange([(jnp.concatenate([chunk, extra], axis=0), "all")], "both", sizes, 6)
    sums = late[:, :chunk_rows].reshape(-1)
    extras = late[:, chunk_rows:].reshape(everyone, 1024)
    first_bias_grad = extras.reshape(n_data, n_model, 1024)[:, 0, :rows].reshape(D)
    squares = jnp.sum(extras[:, rows])
    ends = [D, 4 * D, 5 * D, 5 * D + 2 * CH, 5 * D + 2 * CH + 1]
    base = 5 * D + 128
    loss_sum = sums[5 * D + 2 * CH]
    grad_patch = sums[base : base + CH * D].reshape(CH, D)
    grad_final = sums[base + CH * D : base + 3 * CH * D].reshape(2 * CH, D)
    grad_patch = cut_columns(grad_patch, owned_start, rows)
    grad_final_own = cut_columns(grad_final, owned_start, rows).T
    grad_bias = jnp.concatenate(
        [
            sums[:D],
            first_bias_grad,
            column_sum(dtime_all),
            column_sum(dmod_all),
            sums[D : 4 * D],
            sums[4 * D : 5 * D],
            sums[5 * D : 5 * D + 2 * CH],
        ]
    )
    shared = sums[base : base + 3 * CH * D]
    squares = squares + jnp.sum(grad_bias * grad_bias) + jnp.sum(shared * shared)
    grad_norm = jnp.sqrt(squares)
    factor = jnp.minimum(1.0, CLIP_LIMIT / grad_norm)
    grad_mats = jnp.concatenate(
        [grad_time_second, grad_mod, grad_qkv, grad_out, grad_final_own], axis=1
    )
    grad_embed = jnp.concatenate([grad_patch, grad_time_first, grad_table], axis=0)
    mats_out = adam_step(
        matrices, matrices_first, matrices_second, grad_mats, matrices_average, factor, LEARN_RATE
    )
    embed_out = adam_step(
        embeddings,
        embeddings_first,
        embeddings_second,
        grad_embed,
        embeddings_average,
        factor,
        TABLE_RATE,
    )
    swiglu_out = adam_step(
        swiglu_weights, swiglu_first, swiglu_second, grad_swiglu, swiglu_average, factor, LEARN_RATE
    )
    bias_out = adam_step(
        biases, biases_first, biases_second, grad_bias, biases_average, factor, TABLE_RATE
    )
    return (
        loss_sum,
        grad_norm,
        mats_out[0],
        embed_out[0],
        swiglu_out[0],
        bias_out[0],
        mats_out[1],
        embed_out[1],
        swiglu_out[1],
        bias_out[1],
        mats_out[2],
        embed_out[2],
        swiglu_out[2],
        bias_out[2],
        mats_out[3],
        embed_out[3],
        swiglu_out[3],
        bias_out[3],
        grad_bias * factor,
    )


def solution(mesh):
    placed = (
        P(("dp", "mlp"), None),
        P(("dp", "mlp"), None),
        P(("dp", "mlp"), None),
        P(("dp", "mlp")),
        P(("dp", "mlp")),
        P("dp", None),
        P(None, "dp"),
        P(None, "dp", "mlp"),
        P(),
        P("dp", None),
        P(None, "dp"),
        P(None, "dp", "mlp"),
        P(),
        P("dp", None),
        P(None, "dp"),
        P(None, "dp", "mlp"),
        P(),
        P("dp", None),
        P(None, "dp"),
        P(None, "dp", "mlp"),
        P(),
    )
    return jax.shard_map(
        on_device,
        mesh=mesh,
        in_specs=placed,
        out_specs=(
            P(),
            P(),
            P("dp", None),
            P(None, "dp"),
            P(None, "dp", "mlp"),
            P(),
            P("dp", None),
            P(None, "dp"),
            P(None, "dp", "mlp"),
            P(),
            P("dp", None),
            P(None, "dp"),
            P(None, "dp", "mlp"),
            P(),
            P("dp", None),
            P(None, "dp"),
            P(None, "dp", "mlp"),
            P(),
            P(),
        ),
        check_vma=False,
    )
```

```python
import functools
import math
from types import SimpleNamespace
from typing import Any, NamedTuple

import jax
import jax.numpy as jnp
from jax import lax
from jax.experimental import pallas as pl
from jax.experimental.pallas import tpu as pltpu
from jax.sharding import PartitionSpec as P

HEADS = 16
HDIM = 72
D = 1152
CH = 16
CLASSES = 1000
FREQ = 256
STEP = 10


CLIP_LIMIT = 1.0
LEARN_RATE = 0.03
TABLE_RATE = 0.4
FIRST_DECAY = 0.9
SECOND_DECAY = 0.999
ADAM_EPSILON = 1e-08
WEIGHT_DECAY = 0.01
AVERAGE_DECAY = 0.9999


def plan(steps_in):
    step_index = jnp.arange(1000, dtype=jnp.int32)
    beta_table = 0.0001 + (0.02 - 0.0001) * step_index.astype(jnp.float32) / 999.0
    logbar = jnp.cumsum(jnp.log1p(-beta_table))

    def lookup(values, wanted):
        return jnp.sum(
            jnp.where(wanted[:, None] == step_index[None, :], values[None, :], 0.0), axis=1
        )

    return (
        lookup(beta_table, steps_in),
        jnp.exp(lookup(logbar, steps_in)),
        jnp.exp(lookup(logbar, steps_in - 1)),
    )


def sinusoid(steps_in):
    halfway = FREQ // 2
    frequency = jnp.exp(-math.log(10000.0) * jnp.arange(halfway, dtype=jnp.float32) / halfway)
    angles = steps_in.astype(jnp.float32)[:, None] * frequency[None, :]
    return jnp.concatenate([jnp.cos(angles), jnp.sin(angles)], axis=1)


def modulate(hidden, shift_by, scale_by):
    row_mean = jnp.mean(hidden, axis=-1, keepdims=True)
    centered = hidden - row_mean
    variance = jnp.mean(centered * centered, axis=-1, keepdims=True)
    return (
        centered * lax.rsqrt(variance + 1e-06) * (1.0 + scale_by[:, None, :]) + shift_by[:, None, :]
    )


def noisy_input(clean_patches, noise_patches, steps_in):
    beta_now, bar_now, bar_prev = plan(steps_in)
    bar_now = bar_now[:, None, None]
    return jnp.sqrt(bar_now) * clean_patches + jnp.sqrt(1.0 - bar_now) * noise_patches


def loss_terms(output, clean_patches, noise_patches, steps_in, valid_slot):
    beta_now, bar_now, bar_prev = plan(steps_in)
    beta_now = beta_now[:, None, None]
    bar_now = bar_now[:, None, None]
    bar_prev = bar_prev[:, None, None]
    noisy = jnp.sqrt(bar_now) * clean_patches + jnp.sqrt(1.0 - bar_now) * noise_patches
    eps_pred = output[..., :CH]
    var_raw = output[..., CH:]
    squared = jnp.sum((eps_pred - noise_patches) ** 2, axis=-1)
    post_log = jnp.log(beta_now * (1.0 - bar_prev) / (1.0 - bar_now))
    fraction = (var_raw + 1.0) * 0.5
    model_log = fraction * jnp.log(beta_now) + (1.0 - fraction) * post_log
    coefficient = beta_now * jnp.sqrt(bar_prev) / (1.0 - bar_now)
    start_est = (noisy - jnp.sqrt(1.0 - bar_now) * eps_pred) / jnp.sqrt(bar_now)
    mean_gap = coefficient * (clean_patches - start_est)
    divergence = (
        0.5
        * (
            -1.0
            + model_log
            - post_log
            + jnp.exp(post_log - model_log)
            + mean_gap * mean_gap * jnp.exp(-model_log)
        )
        / math.log(2.0)
    )
    return jnp.sum(jnp.where(valid_slot, squared + jnp.sum(divergence, axis=-1), 0.0))


def adam_step(weight, first, second, gradient, average, factor, rate):
    average_decay = min(AVERAGE_DECAY, (1.0 + STEP) / (10.0 + STEP))
    clipped = gradient * factor
    first = FIRST_DECAY * first + (1.0 - FIRST_DECAY) * clipped
    second = SECOND_DECAY * second + (1.0 - SECOND_DECAY) * clipped * clipped
    ratio = (
        first
        / (1.0 - FIRST_DECAY**STEP)
        / (jnp.sqrt(second / (1.0 - SECOND_DECAY**STEP)) + ADAM_EPSILON)
    )
    weight = weight - rate * (ratio + WEIGHT_DECAY * weight)
    return (weight, first, second, average_decay * average + (1.0 - average_decay) * weight)


def backward_product(gradient, weight):
    return lax.dot_general(
        gradient,
        weight,
        (((gradient.ndim - 1,), (1,)), ((), ())),
        preferred_element_type=jnp.float32,
    )


def weight_grad(inputs, gradient):
    flat_in = inputs.reshape(-1, inputs.shape[-1])
    flat_grad = gradient.reshape(-1, gradient.shape[-1])
    return lax.dot_general(
        flat_in, flat_grad, (((0,), (0,)), ((), ())), preferred_element_type=jnp.float32
    )


def column_sum(gradient):
    return jnp.sum(gradient.astype(jnp.float32).reshape(-1, gradient.shape[-1]), axis=0)


def cut_columns(values, start, amount):
    return lax.dynamic_slice_in_dim(values, start, amount, 1)


MESH_IDS = pl.DeviceIdType.MESH
KERNEL_VMEM = 48 * 2**20


def exchange_kernel(axes, sizes, modes, *refs):
    count = len(modes)
    ins, outs = refs[:count], refs[count : 2 * count]
    send_sem, recv_sem = refs[2 * count :]
    if axes == "dp":
        total = sizes[0]
        me = lax.axis_index("dp")
    else:
        total = sizes[0] * sizes[1]
        me = lax.axis_index("dp") * sizes[1] + lax.axis_index("mlp")

    def device(spot):
        if axes == "dp":
            return (spot, lax.axis_index("mlp"))
        return (lax.div(spot, sizes[1]), lax.rem(spot, sizes[1]))

    barrier = pltpu.get_barrier_semaphore()

    def greet(step, carry):
        pl.semaphore_signal(
            barrier, inc=1, device_id=device(lax.rem(me + step, total)), device_id_type=MESH_IDS
        )
        return carry

    lax.fori_loop(1, total, greet, 0)
    pl.semaphore_wait(barrier, total - 1)

    def make(item, step):
        peer = lax.rem(me + step, total)
        source = ins[item].at[peer] if modes[item] == "each" else ins[item]
        return pltpu.make_async_remote_copy(
            src_ref=source,
            dst_ref=outs[item].at[me],
            send_sem=send_sem.at[item, step - 1],
            recv_sem=recv_sem.at[item, step - 1],
            device_id=device(peer),
            device_id_type=MESH_IDS,
        )

    def begin(step, carry):
        for item in range(count):
            make(item, step).start()
        return carry

    lax.fori_loop(1, total, begin, 0)
    for item in range(count):
        if modes[item] == "each":
            outs[item][me] = ins[item][me]
        else:
            outs[item][me] = ins[item][...]

    def finish(step, carry):
        for item in range(count):
            make(item, step).wait()
        return carry

    lax.fori_loop(1, total, finish, 0)


def exchange(items, axes, sizes, collective):
    total = sizes[0] if axes == "dp" else sizes[0] * sizes[1]
    modes = tuple(mode for _, mode in items)
    arrays = [array for array, _ in items]
    shapes = [
        jax.ShapeDtypeStruct(
            array.shape if mode == "each" else (total, *array.shape), array.dtype
        )
        for array, mode in items
    ]
    space = pl.BlockSpec(memory_space=pltpu.VMEM)
    return pl.pallas_call(
        functools.partial(exchange_kernel, axes, sizes, modes),
        out_shape=shapes,
        in_specs=[space] * len(items),
        out_specs=[space] * len(items),
        scratch_shapes=[
            pltpu.SemaphoreType.DMA((len(items), total - 1)),
            pltpu.SemaphoreType.DMA((len(items), total - 1)),
        ],
        compiler_params=pltpu.CompilerParams(
            collective_id=collective, has_side_effects=True, vmem_limit_bytes=KERNEL_VMEM
        ),
    )(*arrays)


NX = 2


def reduce_dp(value):
    return lax.psum_scatter(value.astype(jnp.bfloat16), "dp", scatter_dimension=0, tiled=True)[
        0
    ].astype(jnp.float32)


def flip(value, bit, count):
    return lax.ppermute(value, "mlp", [(spot, spot ^ bit) for spot in range(count)])


def gather_rows(own, count):
    far = flip(own, 2, count)
    near = flip(own, 1, count)
    return own, near, far, flip(far, 1, count)


def scatter_rows(far_parts, near_parts, count):
    single = jnp.float32
    got = flip(far_parts[1], 1, count)
    far = flip((far_parts[0].astype(single) + got.astype(single)).astype(jnp.bfloat16), 2, count)
    near = flip(near_parts[1], 1, count)
    return near_parts[0].astype(single) + near.astype(single) + far.astype(single)


def gather_out(shard):
    whole = lax.all_gather(shard, "dp", axis=0, tiled=True)
    height = D // lax.axis_size("mlp")
    return lax.dynamic_slice_in_dim(whole, lax.axis_index("mlp") * height, height, 0)


def reduce_out(value):
    whole = lax.dynamic_update_slice_in_dim(
        jnp.zeros((D, D), jnp.float32), value, lax.axis_index("mlp") * value.shape[0], 0
    )
    part = lax.psum_scatter(whole.astype(jnp.bfloat16), "dp", scatter_dimension=0, tiled=True)
    return lax.psum(part.astype(jnp.float32), "mlp")


def swapped(values):
    quarter = HDIM // 4
    return jnp.concatenate(
        [
            values[:, quarter : 2 * quarter],
            values[:, :quarter],
            values[:, 3 * quarter :],
            values[:, 2 * quarter : 3 * quarter],
        ],
        axis=1,
    )


def attention_kernel(heads, qkv_ref, cos_ref, sin_ref, mask_ref, low_ref, out_ref, total_ref):
    width = heads * HDIM
    cosine, sine, mask = cos_ref[0], sin_ref[0], mask_ref[0]
    totals = []
    for head in range(heads):
        start = head * HDIM

        def part(which):
            return qkv_ref[0, :, which * width + start : which * width + start + HDIM]

        raw_q, raw_k = part(0), part(1)
        query = (raw_q * cosine + swapped(raw_q) * sine).astype(jnp.bfloat16)
        key = (raw_k * cosine + swapped(raw_k) * sine).astype(jnp.bfloat16)
        value = part(2).astype(jnp.bfloat16)
        for which, kept in enumerate((query, key, value)):
            low_ref[0, :, which * width + start : which * width + start + HDIM] = kept
        scores = lax.dot_general(
            query, key, (((1,), (1,)), ((), ())), preferred_element_type=jnp.float32
        ) * (1.0 / math.sqrt(HDIM))
        scores = jnp.where(mask > 0.0, scores, -1e30)
        row_max = jnp.max(scores, axis=-1, keepdims=True)
        exponent = jnp.exp(scores - row_max)
        row_sum = jnp.sum(exponent, axis=-1, keepdims=True)
        probs = exponent / row_sum
        out_ref[0, :, start : start + HDIM] = jnp.dot(
            probs.astype(jnp.bfloat16), value, preferred_element_type=jnp.float32
        ).astype(jnp.bfloat16)
        totals.append(row_max + jnp.log(row_sum))
    total_ref[0] = jnp.concatenate(totals, axis=1)


def attention(qkv, cosine, sine, mask, heads):
    images, length, width = qkv.shape
    per_image = lambda *dims: pl.BlockSpec((1, *dims), lambda i: (i, 0, 0))
    return pl.pallas_call(
        functools.partial(attention_kernel, heads),
        grid=(images,),
        out_shape=[
            jax.ShapeDtypeStruct((images, length, width), jnp.bfloat16),
            jax.ShapeDtypeStruct((images, length, heads * HDIM), jnp.bfloat16),
            jax.ShapeDtypeStruct((images, length, heads), jnp.float32),
        ],
        in_specs=[
            per_image(length, width),
            per_image(length, HDIM),
            per_image(length, HDIM),
            per_image(1, length),
        ],
        out_specs=[
            per_image(length, width),
            per_image(length, heads * HDIM),
            per_image(length, heads),
        ],
        compiler_params=pltpu.CompilerParams(vmem_limit_bytes=KERNEL_VMEM),
    )(qkv, cosine, sine, mask)


def attention_back_kernel(
    heads, low_ref, total_ref, grad_ref, cos_ref, sin_ref, mask_ref, out_ref
):
    width = heads * HDIM
    scale_by = 1.0 / math.sqrt(HDIM)
    cosine, sine, mask = cos_ref[0], sin_ref[0], mask_ref[0]

    def contract(left, right, dims):
        return lax.dot_general(left, right, (dims, ((), ())), preferred_element_type=jnp.float32)

    for head in range(heads):
        start = head * HDIM

        def spot(which):
            return slice(which * width + start, which * width + start + HDIM)

        query, key, value = (low_ref[0, :, spot(which)] for which in range(3))
        grad = grad_ref[0, :, start : start + HDIM]
        scores = contract(query, key, ((1,), (1,))) * scale_by
        scores = jnp.where(mask > 0.0, scores, -1e30)
        probs = jnp.exp(scores - total_ref[0, :, head : head + 1])
        d_probs = contract(grad, value, ((1,), (1,)))
        row = jnp.sum(probs * d_probs, axis=-1, keepdims=True)
        d_scores = (probs * (d_probs - row)).astype(jnp.bfloat16)
        d_query = contract(d_scores, key, ((1,), (0,))) * scale_by
        d_key = contract(d_scores, query, ((0,), (0,))) * scale_by
        d_value = contract(probs.astype(jnp.bfloat16), grad, ((0,), (0,)))
        for which, turned in ((0, d_query), (1, d_key)):
            back = turned * cosine + swapped(turned * sine)
            out_ref[0, :, spot(which)] = back.astype(jnp.bfloat16)
        out_ref[0, :, spot(2)] = d_value.astype(jnp.bfloat16)


def attention_back(low, totals, grad, cosine, sine, mask, heads):
    images, length, width = low.shape
    per_image = lambda *dims: pl.BlockSpec((1, *dims), lambda i: (i, 0, 0))
    return pl.pallas_call(
        functools.partial(attention_back_kernel, heads),
        grid=(images,),
        out_shape=jax.ShapeDtypeStruct((images, length, width), jnp.bfloat16),
        in_specs=[
            per_image(length, width),
            per_image(length, heads),
            per_image(length, heads * HDIM),
            per_image(length, HDIM),
            per_image(length, HDIM),
            per_image(1, length),
        ],
        out_specs=per_image(length, width),
        compiler_params=pltpu.CompilerParams(vmem_limit_bytes=KERNEL_VMEM),
    )(low, totals, grad, cosine, sine, mask)


def turn_tables(patch_grid, length):
    slot_index = jnp.arange(length, dtype=jnp.int32)[None, :]
    grid_cols = patch_grid[:, 1:2]
    valid_slot = slot_index < patch_grid[:, 0:1] * grid_cols
    row_place = (slot_index // grid_cols).astype(jnp.float32)
    col_place = (slot_index % grid_cols).astype(jnp.float32)
    quarter = HDIM // 4
    frequency = jnp.exp(-math.log(10000.0) * jnp.arange(quarter, dtype=jnp.float32) / quarter)
    row_angle = row_place[..., None] * frequency
    col_angle = col_place[..., None] * frequency
    cos_row, sin_row = jnp.cos(row_angle), jnp.sin(row_angle)
    cos_col, sin_col = jnp.cos(col_angle), jnp.sin(col_angle)
    return (
        jnp.concatenate([cos_row, cos_row, cos_col, cos_col], axis=-1),
        jnp.concatenate([-sin_row, sin_row, -sin_col, sin_col], axis=-1),
        valid_slot.astype(jnp.float32)[:, None, :],
    )


def valid_slots(patch_grid, length):
    return jnp.arange(length, dtype=jnp.int32)[None, :] < patch_grid[:, 0:1] * patch_grid[:, 1:2]


def device_parts():
    d, m = lax.axis_index("dp"), lax.axis_index("mlp")
    return d, m, lax.div(d, NX), lax.rem(d, NX)


class Sender:
    def __init__(self, send_sem, recv_sem):
        self.send_sem, self.recv_sem = send_sem, recv_sem

    def __call__(self, spot, source, target, device):
        spot = spot if isinstance(spot, tuple) else (spot,)
        return pltpu.make_async_remote_copy(
            src_ref=source,
            dst_ref=target,
            send_sem=self.send_sem.at[spot],
            recv_sem=self.recv_sem.at[spot],
            device_id=device,
            device_id_type=MESH_IDS,
        )


def modulate_rows(values, shift_by, scale_by):
    row_mean = jnp.mean(values, axis=-1, keepdims=True)
    centered = values - row_mean
    variance = jnp.mean(centered * centered, axis=-1, keepdims=True)
    return centered * lax.rsqrt(variance + 1e-06) * (1.0 + scale_by) + shift_by


def named(inputs, outputs, scratch, refs):
    ends = len(inputs._fields), len(inputs._fields) + len(outputs._fields)
    parts = inputs(*refs[: ends[0]]), outputs(*refs[ends[0] : ends[1]]), scratch(*refs[ends[1] :])
    return SimpleNamespace(**{k: v for part in parts for k, v in part._asdict().items()})


class ForwardIn(NamedTuple):
    facts: Any
    trig: Any
    small: Any
    time_first: Any
    first_bias: Any
    second_bias: Any
    time_blocks: Any
    class_table: Any
    mod_weight: Any
    mod_bias: Any
    noisy: Any
    patch_bias: Any
    qkv_shard: Any
    out_shard: Any
    ff_shard: Any
    qkv_bias: Any
    out_bias: Any


class ForwardOut(NamedTuple):
    facts_all: Any
    trig_all: Any
    small_all: Any
    time_pre: Any
    condition: Any
    modulation: Any
    hidden: Any
    one_rows: Any
    qkv_weight: Any
    out_weight: Any
    ff: Any
    low: Any
    attended: Any
    totals: Any
    branch: Any
    hidden_mid: Any
    two_rows: Any


class ForwardScratch(NamedTuple):
    time_send: Any
    time_recv: Any
    mod_send: Any
    mod_recv: Any
    mod_low: Any
    qkv: Any
    parts_send: Any
    parts_recv: Any
    facts_s: Any
    facts_r: Any
    small_s: Any
    small_r: Any
    time_s: Any
    time_r: Any
    mods_s: Any
    mods_r: Any
    trig_s: Any
    trig_r: Any
    one_s: Any
    one_r: Any
    two_s: Any
    two_r: Any
    part_s: Any
    part_r: Any
    qz_s: Any
    qz_r: Any
    qx_s: Any
    qx_r: Any
    oz_s: Any
    oz_r: Any
    ox_s: Any
    ox_r: Any
    fz_s: Any
    fz_r: Any
    fx_s: Any
    fx_r: Any
    local_sem: Any


def forward_kernel(sizes, *refs):
    r = named(ForwardIn, ForwardOut, ForwardScratch, refs)
    bfloat, single = jnp.bfloat16, jnp.float32
    n_data, n_model = sizes
    everyone = n_data * n_model
    d, m, z, x = device_parts()
    me = d * n_model + m
    depth = n_data // NX
    rows = D // n_data
    heads = HEADS // n_model
    head_cols = heads * HDIM
    length = r.noisy.shape[0]
    units = r.ff_shard.shape[2]
    half = units // 2

    def at_dp(spot):
        return (spot, m)

    def at_mlp(bit):
        flipped = m + 1 - 2 * lax.rem(m, 2) if bit == 1 else lax.rem(m + 2, 4)
        return (d, flipped)

    up = lax.rem(z + 1, depth) * NX + x
    down = lax.rem(z + depth - 1, depth) * NX + x
    side = z * NX + 1 - x

    barrier = pltpu.get_barrier_semaphore()

    def greet(step, carry):
        peer = lax.rem(me + step, everyone)
        pl.semaphore_signal(
            barrier,
            inc=1,
            device_id=(lax.div(peer, n_model), lax.rem(peer, n_model)),
            device_id_type=MESH_IDS,
        )
        return carry

    lax.fori_loop(1, everyone, greet, 0)

    load_mod = pltpu.make_async_copy(r.mod_weight, r.mod_low, r.local_sem.at[0])
    load_mod.start()
    own_ff = pltpu.make_async_copy(
        r.ff_shard,
        r.ff.at[:, pl.ds(pl.multiple_of(d * rows, 16), rows)],
        r.local_sem.at[1],
    )
    own_ff.start()
    pl.semaphore_wait(barrier, everyone - 1)

    send_facts = Sender(r.facts_s, r.facts_r)

    def facts_copy(step):
        peer = lax.rem(me + step, everyone)
        return send_facts(
            step - 1,
            r.facts,
            r.facts_all.at[me],
            (lax.div(peer, n_model), lax.rem(peer, n_model)),
        )

    def loop(first, last, body):
        def step_body(step, carry):
            body(step)
            return carry

        lax.fori_loop(first, last, step_body, 0)

    loop(1, everyone, lambda step: facts_copy(step).start())
    r.facts_all[me] = r.facts[...]

    def qkv_rows(spot, part):
        if part == 0:
            return r.qkv_weight.at[pl.ds(pl.multiple_of(spot * rows, 16), 80)]
        return r.qkv_weight.at[pl.ds(pl.multiple_of(spot * rows + 80, 16), rows - 80)]

    def ff_block(spot, part, which):
        return r.ff.at[
            which,
            pl.ds(pl.multiple_of(spot * rows, 16), rows),
            pl.ds(half * part, half),
        ]

    def origin(step, part):
        return lax.rem(z + (depth - step if part == 0 else step), depth) * NX + x

    qz, qx = Sender(r.qz_s, r.qz_r), Sender(r.qx_s, r.qx_r)
    fz, fx = Sender(r.fz_s, r.fz_r), Sender(r.fx_s, r.fx_r)

    def qkv_along(step, part):
        block = qkv_rows(origin(step - 1, part), part)
        return qz((part, step - 1), block, block, at_dp(up if part == 0 else down))

    def qkv_aside(step, part):
        block = qkv_rows(origin(step, part), part)
        return qx((part, step), block, block, at_dp(side))

    def ff_along(step, part, which):
        block = ff_block(origin(step - 1, part), part, which)
        return fz((part, step - 1, which), block, block, at_dp(up if part == 0 else down))

    def ff_aside(step, part, which):
        block = ff_block(origin(step, part), part, which)
        return fx((part, step, which), block, block, at_dp(side))

    own_rows = pl.ds(pl.multiple_of(d * rows, 16), rows)
    r.qkv_weight[own_rows] = r.qkv_shard[...]
    for part in range(2):
        qkv_along(1, part).start()
        qkv_aside(0, part).start()

    send_small = Sender(r.small_s, r.small_r)

    def small_copy(step):
        return send_small(
            step - 1,
            r.small,
            r.small_all.at[own_rows],
            at_dp(lax.rem(d + step, n_data)),
        )

    loop(1, n_data, lambda step: small_copy(step).start())
    r.small_all[own_rows] = r.small[...]
    r.trig_all[0] = r.trig[...]

    def spread(send, buffer):
        return (
            send(0, buffer.at[0], buffer.at[1], at_mlp(1)),
            send(1, buffer.at[0], buffer.at[2], at_mlp(2)),
            send(2, buffer.at[2], buffer.at[3], at_mlp(1)),
        )

    trig_near, trig_far, trig_on = spread(Sender(r.trig_s, r.trig_r), r.trig_all)
    trig_near.start()
    trig_far.start()

    oz, ox = Sender(r.oz_s, r.oz_r), Sender(r.ox_s, r.ox_r)
    out_place = r.out_weight.at[pl.ds(pl.multiple_of(x * rows, 16), rows)]
    owner = z == m

    def out_along(step):
        return oz(step - 1, out_place, out_place, at_dp(lax.rem(z + step, depth) * NX + x))

    out_aside = ox(0, out_place, out_place, at_dp(side))

    @pl.when(owner)
    def _():
        r.out_weight[pl.ds(pl.multiple_of(x * rows, 16), rows)] = r.out_shard[...]
        for step in range(1, depth):
            out_along(step).start()
        out_aside.start()

    loop(1, everyone, lambda step: facts_copy(step).wait())
    facts_all = r.facts_all[...]
    sinus = jnp.concatenate([facts_all[:, 0], facts_all[:, 1]], axis=1).astype(bfloat)
    labels = facts_all[:, 2, 0:1]
    time_pre = (
        jnp.dot(sinus, r.time_first[...], preferred_element_type=single) + r.first_bias[...]
    )
    r.time_pre[...] = time_pre
    time_act = (time_pre * jax.nn.sigmoid(time_pre)).astype(bfloat)
    send_time = Sender(r.time_s, r.time_r)

    def time_copy(step):
        peer = lax.rem(d + step, n_data)
        return send_time(
            step - 1, r.time_send.at[peer], r.time_recv.at[d], at_dp(peer)
        )

    for spot in range(n_data):
        r.time_send[spot] = jnp.dot(
            time_act, r.time_blocks[spot], preferred_element_type=single
        )
    loop(1, n_data, lambda step: time_copy(step).start())
    r.time_recv[d] = r.time_send[d]
    for part in range(2):
        for which in range(3):
            own = r.ff_shard.at[which, :, pl.ds(half * part, half)]
            fz(
                (part, 0, which),
                own,
                ff_block(d, part, which),
                at_dp(up if part == 0 else down),
            ).start()
            fx((part, 0, which), own, ff_block(d, part, which), at_dp(side)).start()
    onehot = (
        labels == lax.broadcasted_iota(jnp.int32, (everyone, CLASSES + 1), 1).astype(single)
    ).astype(bfloat)
    picked = jnp.dot(onehot, r.class_table[...], preferred_element_type=single)
    load_mod.wait()

    def qkv_service(step):
        for part in range(2):
            qkv_along(step, part).wait_recv()
            if step < depth - 1:
                qkv_along(step + 1, part).start()
            qkv_aside(step, part).start()

    loop(1, n_data, lambda step: time_copy(step).wait())
    condition = jnp.sum(r.time_recv[...], axis=0) + r.second_bias[...] + picked
    r.condition[...] = condition
    cond_act = (condition * jax.nn.sigmoid(condition)).astype(bfloat)
    pick = (
        lax.broadcasted_iota(jnp.int32, (n_data, everyone), 1)
        == lax.broadcasted_iota(jnp.int32, (n_data, everyone), 0) * n_model + m
    ).astype(bfloat)
    cond_rank = jnp.dot(pick, cond_act, preferred_element_type=single).astype(bfloat)
    for kind in range(8):
        block = jnp.dot(
            cond_rank, r.mod_low[:, kind * D : (kind + 1) * D], preferred_element_type=single
        )
        for spot in range(n_data):
            r.mod_send[spot, kind : kind + 1] = block[spot : spot + 1]
    send_mods = Sender(r.mods_s, r.mods_r)

    def mods_copy(step):
        peer = lax.rem(d + step, n_data)
        return send_mods(step - 1, r.mod_send.at[peer], r.mod_recv.at[d], at_dp(peer))

    loop(1, n_data, lambda step: mods_copy(step).start())
    r.mod_recv[d] = r.mod_send[d]
    qkv_service(1)
    loop(1, n_data, lambda step: small_copy(step).wait())
    trig_far.wait_recv()
    trig_on.start()
    hidden = (
        lax.dot_general(
            r.noisy[...],
            r.small_all[:, 0:CH],
            (((1,), (1,)), ((), ())),
            preferred_element_type=single,
        )
        + r.patch_bias[...]
    )
    r.hidden[...] = hidden
    loop(1, n_data, lambda step: mods_copy(step).wait())
    modulation = jnp.sum(r.mod_recv[...], axis=0) + r.mod_bias[...]
    r.modulation[...] = modulation

    def kind_of(kind):
        return r.modulation[kind : kind + 1]

    r.one_rows[0] = modulate_rows(r.hidden[...], kind_of(0), kind_of(1)).astype(bfloat)
    one_near, one_far, one_on = spread(Sender(r.one_s, r.one_r), r.one_rows)
    one_far.start()
    one_near.start()
    qkv_service(2)
    qkv_service(3)

    @pl.when(jnp.logical_not(owner))
    def _():
        oz(
            lax.rem(z + depth - m, depth) - 1, out_place, out_place, at_dp(up)
        ).wait_recv()
        out_aside.start()

    own_ff.wait()

    def ff_service(step, which):
        for part in range(2):
            ff_along(step, part, which).wait_recv()
            if step < depth - 1:
                ff_along(step + 1, part, which).start()
            ff_aside(step, part, which).start()

    ff_service(1, 0)
    one_far.wait_recv()
    one_on.start()
    for part in range(2):
        for step in range(depth):
            qkv_aside(step, part).wait_recv()
    one_near.wait_recv()
    one_on.wait_recv()
    trig_near.wait_recv()
    trig_on.wait_recv()
    ff_service(1, 1)
    ff_service(1, 2)

    def image_body(step, carry):
        image = n_model - 1 - step
        r.qkv[...] = (
            jnp.dot(r.one_rows[image], r.qkv_weight[...], preferred_element_type=single)
            + r.qkv_bias[...]
        )
        rank = (
            2 * lax.rem(lax.div(m, 2) + lax.div(image, 2), 2)
            + lax.rem(lax.rem(m, 2) + lax.rem(image, 2), 2)
        )
        count = r.facts_all[d * n_model + rank, 2:3, 1:2]
        mask = lax.broadcasted_iota(jnp.int32, (1, length), 1).astype(single) < count
        cosine, sine = r.trig_all[image, 0], r.trig_all[image, 1]
        totals = []
        for head in range(heads):
            start = head * HDIM

            def part(which):
                return r.qkv[:, which * head_cols + start : which * head_cols + start + HDIM]

            raw_q, raw_k = part(0), part(1)
            query = (raw_q * cosine + swapped(raw_q) * sine).astype(bfloat)
            key = (raw_k * cosine + swapped(raw_k) * sine).astype(bfloat)
            value = part(2).astype(bfloat)
            for which, kept in enumerate((query, key, value)):
                low = which * head_cols + start
                r.low[image, :, low : low + HDIM] = kept
            scores = lax.dot_general(
                query, key, (((1,), (1,)), ((), ())), preferred_element_type=single
            ) * (1.0 / math.sqrt(HDIM))
            scores = jnp.where(mask, scores, -1e30)
            row_max = jnp.max(scores, axis=-1, keepdims=True)
            exponent = jnp.exp(scores - row_max)
            row_sum = jnp.sum(exponent, axis=-1, keepdims=True)
            probs = exponent / row_sum
            r.attended[image, :, start : start + HDIM] = jnp.dot(
                probs.astype(bfloat), value, preferred_element_type=single
            ).astype(bfloat)
            totals.append(row_max + jnp.log(row_sum))
        r.totals[image] = jnp.concatenate(totals, axis=1)
        return carry

    lax.fori_loop(0, 2, image_body, 0)
    for which in range(3):
        ff_service(2, which)
    lax.fori_loop(2, n_model, image_body, 0)

    @pl.when(owner)
    def _():
        for step in range(1, depth):
            out_along(step).wait_send()

    out_aside.wait()

    def partial(image):
        return jnp.dot(
            r.attended[image], r.out_weight[...], preferred_element_type=single
        )

    send_part = Sender(r.part_s, r.part_r)
    to_core = send_part(0, r.parts_send.at[0], r.parts_recv.at[0], at_mlp(1))
    to_far = send_part(1, r.parts_send.at[1], r.parts_recv.at[1], at_mlp(2))
    to_near = send_part(2, r.parts_send.at[2], r.parts_recv.at[2], at_mlp(1))
    r.parts_send[0] = partial(3).astype(bfloat)
    to_core.start()
    second = partial(2)
    to_core.wait_recv()
    r.parts_send[1] = (second + r.parts_recv[0].astype(single)).astype(bfloat)
    to_far.start()
    r.parts_send[2] = partial(1).astype(bfloat)
    to_near.start()
    own_part = partial(0) + r.out_bias[...]
    for which in range(3):
        ff_service(3, which)
    to_near.wait_recv()
    to_far.wait_recv()
    branch = own_part + r.parts_recv[2].astype(single) + r.parts_recv[1].astype(single)
    r.branch[...] = branch
    hidden_mid = r.hidden[...] + kind_of(2) * branch
    r.hidden_mid[...] = hidden_mid
    r.two_rows[0] = modulate_rows(hidden_mid, kind_of(3), kind_of(4)).astype(bfloat)
    two_near, two_far, two_on = spread(Sender(r.two_s, r.two_r), r.two_rows)
    two_far.start()
    two_near.start()
    two_far.wait_recv()
    two_on.start()

    for part in range(2):
        for step in range(depth):
            for which in range(3):
                ff_aside(step, part, which).wait()
            qkv_aside(step, part).wait_send()
            if step:
                for which in range(3):
                    ff_along(step, part, which).wait_send()
                qkv_along(step, part).wait_send()
    for copy in (two_near, two_on):
        copy.wait()
    two_far.wait_send()
    for copy in (trig_near, trig_far, trig_on, one_near, one_far, one_on, to_core, to_far, to_near):
        copy.wait_send()


def forward_all(values, sizes, collective):
    n_data, n_model = sizes
    bfloat, single = jnp.bfloat16, jnp.float32
    everyone = n_data * n_model
    rows = D // n_data
    heads = HEADS // n_model
    head_cols = heads * HDIM
    length = values.noisy.shape[0]
    units = values.ff_shard.shape[2]
    depth = n_data // NX
    shapes = dict(
        facts_all=((everyone, 8, 128), single),
        trig_all=((n_model, 2, length, HDIM), single),
        small_all=((D, 128), bfloat),
        time_pre=((everyone, rows), single),
        condition=((everyone, rows), single),
        modulation=((8, D), single),
        hidden=((length, D), single),
        one_rows=((n_model, length, D), bfloat),
        qkv_weight=((D, 3 * head_cols), bfloat),
        out_weight=((head_cols, D), bfloat),
        ff=((3, D, units), bfloat),
        low=((n_model, length, 3 * head_cols), bfloat),
        attended=((n_model, length, head_cols), bfloat),
        totals=((n_model, length, heads), single),
        branch=((length, D), single),
        hidden_mid=((length, D), single),
        two_rows=((n_model, length, D), bfloat),
    )
    dma = pltpu.SemaphoreType.DMA
    scratch = dict(
        time_send=pltpu.VMEM((n_data, everyone, rows), single),
        time_recv=pltpu.VMEM((n_data, everyone, rows), single),
        mod_send=pltpu.VMEM((n_data, 8, D), single),
        mod_recv=pltpu.VMEM((n_data, 8, D), single),
        mod_low=pltpu.VMEM((rows, 8 * D), bfloat),
        qkv=pltpu.VMEM((length, 3 * head_cols), single),
        parts_send=pltpu.VMEM((3, length, D), bfloat),
        parts_recv=pltpu.VMEM((3, length, D), bfloat),
        local_sem=dma((2,)),
    )
    counts = dict(
        facts=(everyone - 1,),
        small=(n_data - 1,),
        time=(n_data - 1,),
        mods=(n_data - 1,),
        trig=(3,),
        one=(3,),
        two=(3,),
        part=(3,),
        qz=(2, depth - 1),
        qx=(2, depth),
        oz=(depth - 1,),
        ox=(1,),
        fz=(2, depth - 1, 3),
        fx=(2, depth, 3),
    )
    for name, count in counts.items():
        scratch[name + "_s"] = dma(count)
        scratch[name + "_r"] = dma(count)
    far = {"mod_weight", "ff_shard", "ff"}

    def space(name):
        return pl.BlockSpec(memory_space=pl.ANY if name in far else pltpu.VMEM)

    outs = pl.pallas_call(
        functools.partial(forward_kernel, sizes),
        out_shape=[jax.ShapeDtypeStruct(*shapes[name]) for name in ForwardOut._fields],
        in_specs=[space(name) for name in ForwardIn._fields],
        out_specs=[space(name) for name in ForwardOut._fields],
        scratch_shapes=[scratch[name] for name in ForwardScratch._fields],
        compiler_params=pltpu.CompilerParams(
            collective_id=collective, has_side_effects=True, vmem_limit_bytes=56 * 2**20
        ),
    )(*values)
    return ForwardOut(*outs)


class BackIn(NamedTuple):
    ff: Any
    two_rows: Any
    hidden_mid: Any
    hidden: Any
    branch: Any
    modulation: Any
    small_all: Any
    final_bias: Any
    clean: Any
    noise: Any
    consts: Any
    valid: Any
    noisy: Any
    low: Any
    totals: Any
    trig_all: Any
    facts_all: Any
    attended: Any
    one_rows: Any
    qkv_weight: Any
    out_weight: Any
    mod_weight: Any
    time_second: Any
    time_pre: Any
    condition: Any


class BackOut(NamedTuple):
    late: Any
    dmod: Any
    dtime: Any
    d_condition: Any
    d_time_pre: Any
    grad_ff: Any
    grad_qkv: Any
    grad_out: Any


class BackScratch(NamedTuple):
    d_modulation: Any
    local: Any
    sums: Any
    sums_recv: Any
    pay: Any
    dmod_row: Any
    dmod_all: Any
    dmod_wide: Any
    dtime_mine: Any
    dtime_recv: Any
    dtime_wide: Any
    loss: Any
    sm_s: Any
    sm_r: Any
    dl_s: Any
    dl_r: Any
    dt_s: Any
    dt_r: Any
    lt_s: Any
    lt_r: Any
    d_end: Any
    dm_rows: Any
    db_rows: Any
    hold_far: Any
    hold_near: Any
    parts_send: Any
    parts_recv: Any
    normed_end: Any
    g_ff: Any
    x_ff: Any
    z_ff: Any
    g_qkv: Any
    x_qkv: Any
    z_qkv: Any
    g_out: Any
    x_out: Any
    z_out: Any
    out_mine: Any
    dm_s: Any
    dm_r: Any
    db_s: Any
    db_r: Any
    pa_s: Any
    pa_r: Any
    pb_s: Any
    pb_r: Any
    pc_s: Any
    pc_r: Any
    fx_s: Any
    fx_r: Any
    fz_s: Any
    fz_r: Any
    qx_s: Any
    qx_r: Any
    qz_s: Any
    qz_r: Any
    ox_s: Any
    ox_r: Any
    oz_s: Any
    oz_r: Any
    qa_s: Any
    qa_r: Any
    oa_s: Any
    oa_r: Any
    local_sem: Any


ROW_CHUNK = 16


def modulate_back(values, grad, scale_by):
    row_mean = jnp.mean(values, axis=-1, keepdims=True)
    centered = values - row_mean
    variance = jnp.mean(centered * centered, axis=-1, keepdims=True)
    inverse = lax.rsqrt(variance + 1e-06)
    normal = centered * inverse
    inner = grad * (1.0 + scale_by)
    back = inverse * (
        inner
        - jnp.mean(inner, axis=-1, keepdims=True)
        - normal * jnp.mean(inner * normal, axis=-1, keepdims=True)
    )
    return back, normal


def fold(values):
    total = values[:8]
    for start in range(8, values.shape[0], 8):
        total = total + values[start : start + 8]
    return total


def back_kernel(sizes, total_images, *refs):
    r = named(BackIn, BackOut, BackScratch, refs)
    bfloat, single = jnp.bfloat16, jnp.float32
    n_data, n_model = sizes
    d, m, z, x = device_parts()
    depth = n_data // NX
    rows = D // n_data
    heads = HEADS // n_model
    head_cols = heads * HDIM
    length = r.clean.shape[0]
    units = r.ff.shape[2]
    half = units // 2

    def at_dp(spot):
        return (spot, m)

    near_rank = m + 1 - 2 * lax.rem(m, 2)
    far_rank = lax.rem(m + 2, 4)

    def at_mlp(bit):
        return (d, near_rank if bit == 1 else far_rank)

    up = lax.rem(z + 1, depth) * NX + x
    down = lax.rem(z + depth - 1, depth) * NX + x
    side = z * NX + 1 - x
    barrier = pltpu.get_barrier_semaphore()
    everyone = n_data * n_model
    me = d * n_model + m

    def loop(first, last, body):
        def step_body(step, carry):
            body(step)
            return carry

        lax.fori_loop(first, last, step_body, 0)

    def anyone(step):
        peer = lax.rem(me + step, everyone)
        return peer, (lax.div(peer, n_model), lax.rem(peer, n_model))

    loop(
        1,
        everyone,
        lambda step: pl.semaphore_signal(
            barrier, inc=1, device_id=anyone(step)[1], device_id_type=MESH_IDS
        ),
    )
    pl.semaphore_wait(barrier, everyone - 1)

    def chunks(body, carry, amount=ROW_CHUNK, count=length):
        def step_body(step, held):
            return body(pl.ds(pl.multiple_of(step * amount, amount), amount), held)

        return lax.fori_loop(0, count // amount, step_body, carry)

    def kind_of(kind):
        return r.modulation[kind : kind + 1]

    def dot(left, right, dims):
        return lax.dot_general(left, right, (dims, ((), ())), preferred_element_type=single)

    zeros = jnp.zeros((8, D), single)

    def spread(send, buffer):
        return (
            send(0, buffer.at[0], buffer.at[1], at_mlp(1)),
            send(1, buffer.at[0], buffer.at[2], at_mlp(2)),
            send(2, buffer.at[2], buffer.at[3], at_mlp(1)),
        )

    def part_copies(*sems):
        send = Sender(*sems)
        return tuple(
            send(spot, r.parts_send.at[spot], r.parts_recv.at[spot], at_mlp(bit))
            for spot, bit in ((0, 1), (1, 2), (2, 1))
        )

    def add_far(copies):
        to_core, to_far, to_near = copies
        to_core.wait_recv()

        def body(at, held):
            r.parts_send[1, at] = (
                r.hold_far[at] + r.parts_recv[0, at].astype(single)
            ).astype(bfloat)
            return held

        chunks(body, 0)
        to_far.start()

    fx, fz = Sender(r.fx_s, r.fx_r), Sender(r.fz_s, r.fz_r)
    qx, qz = Sender(r.qx_s, r.qx_r), Sender(r.qz_s, r.qz_r)

    def block_rows(z_spot, x_spot):
        return pl.ds(pl.multiple_of((z_spot * NX + x_spot) * rows, 16), rows)

    def ff_aside(which, step):
        z_spot = lax.rem(z + step, depth)
        return fx(
            (which, step),
            r.g_ff.at[which, block_rows(z_spot, 1 - x)],
            r.x_ff.at[which, z_spot],
            at_dp(side),
        )

    def target_of(step, part):
        return lax.rem(z + (depth - 1 - step if part == 0 else 1 + step), depth)

    def ff_along(which, step, part):
        lanes = pl.ds(half * part, half)
        return fz(
            (which, step, part),
            r.g_ff.at[which, block_rows(target_of(step, part), x), lanes],
            r.z_ff.at[which, step, part],
            at_dp(up if part == 0 else down),
        )

    def ff_start(which):
        for step in range(depth):
            ff_aside(which, step).start()

    def ff_beside(which):
        for step in range(depth):
            ff_aside(which, step).wait_recv()

        def body(step, held):
            at = block_rows(step, x)
            r.g_ff[which, at] = (
                r.g_ff[which, at].astype(single) + r.x_ff[which, step].astype(single)
            ).astype(bfloat)
            return held

        lax.fori_loop(0, depth, body, 0)
        for part in range(2):
            ff_along(which, 0, part).start()

    def ff_service(which, step):
        for part in range(2):
            ff_along(which, step, part).wait_recv()
            lanes = pl.ds(half * part, half)
            at = block_rows(target_of(step + 1, part), x)
            running = r.z_ff[which, step, part].astype(single) + r.g_ff[
                which, at, lanes
            ].astype(single)
            if step < depth - 2:
                r.g_ff[which, at, lanes] = running.astype(bfloat)
                ff_along(which, step + 1, part).start()
            else:
                r.grad_ff[which, :, lanes] = running

    tops = (pl.ds(0, 80), pl.ds(80, rows - 80))

    def part_rows(z_spot, part):
        start = (z_spot * NX + x) * rows + 80 * part
        return pl.ds(pl.multiple_of(start, 16), 80 if part == 0 else rows - 80)

    def qkv_aside(step):
        z_spot = lax.rem(z + step, depth)
        return qx(
            step,
            r.g_qkv.at[block_rows(z_spot, 1 - x)],
            r.x_qkv.at[z_spot],
            at_dp(side),
        )

    def qkv_along(step, part):
        return qz(
            (step, part),
            r.g_qkv.at[part_rows(target_of(step, part), part)],
            r.z_qkv.at[step, tops[part]],
            at_dp(up if part == 0 else down),
        )

    def qkv_beside():
        for step in range(depth):
            qkv_aside(step).wait_recv()

        def body(step, held):
            at = block_rows(step, x)
            r.g_qkv[at] = (
                r.g_qkv[at].astype(single) + r.x_qkv[step].astype(single)
            ).astype(bfloat)
            return held

        lax.fori_loop(0, depth, body, 0)
        for part in range(2):
            qkv_along(0, part).start()

    def qkv_service(step):
        for part in range(2):
            qkv_along(step, part).wait_recv()
            at = part_rows(target_of(step + 1, part), part)
            running = (
                r.z_qkv[step, tops[part]].astype(single) + r.g_qkv[at].astype(single)
            ).astype(bfloat)
            if step < depth - 2:
                r.g_qkv[at] = running
                qkv_along(step + 1, part).start()
            else:
                r.grad_qkv[0, tops[part]] = running

    dm_near, dm_far, dm_on = spread(Sender(r.dm_s, r.dm_r), r.dm_rows)
    first_parts = part_copies(r.pa_s, r.pa_r)
    second_parts = part_copies(r.pb_s, r.pb_r)
    third_parts = part_copies(r.pc_s, r.pc_r)

    def swiglu(ff, two_rows, gates, ups, acts, d_gates, d_ups):
        load_ff = pltpu.make_async_copy(r.ff, ff, r.local_sem.at[0])
        load_two = pltpu.make_async_copy(r.two_rows, two_rows, r.local_sem.at[1])
        load_ff.start()
        load_two.start()
        load_two.wait()
        load_ff.wait()
        wide = 2 * length

        def rows_of(ref, which):
            return ref[2 * which : 2 * which + 2].reshape(wide, D)

        def inner(which):
            part = rows_of(two_rows, which)
            spot = pl.ds(which * wide, wide)
            gates[spot] = dot(part, ff[0], ((1,), (0,)))
            ups[spot] = dot(part, ff[1], ((1,), (0,)))

            def body(at, held):
                at = pl.ds(pl.multiple_of(at.start + which * wide, 32), 32)
                gate = gates[at]
                acts[at] = (gate * jax.nn.sigmoid(gate) * ups[at]).astype(bfloat)
                return held

            chunks(body, 0, 32, wide)

        def outer(image):
            return dot(acts[image * length : (image + 1) * length], ff[2], ((1,), (1,)))

        inner(1)
        r.parts_send[0] = outer(3).astype(bfloat)
        first_parts[0].start()
        r.hold_far[...] = outer(2)
        inner(0)
        add_far(first_parts)
        r.parts_send[2] = outer(1).astype(bfloat)
        first_parts[2].start()
        r.hold_near[...] = outer(0)
        first_parts[2].wait_recv()
        first_parts[1].wait_recv()

        def ending(at, held):
            mixed = (
                r.hold_near[at]
                + r.parts_recv[2, at].astype(single)
                + r.parts_recv[1, at].astype(single)
            )
            r.d_end[at] = mixed
            end = r.hidden_mid[at] + kind_of(5) * mixed
            r.normed_end[at] = modulate_rows(end, kind_of(6), kind_of(7)).astype(bfloat)
            return held

        chunks(ending, 0)

        eps_weight, var_weight = r.small_all[:, 32:48], r.small_all[:, 48:64]
        normed_end = r.normed_end[...]
        eps = dot(normed_end, eps_weight, ((1,), (0,))) + r.final_bias[0:1]
        var = dot(normed_end, var_weight, ((1,), (0,))) + r.final_bias[1:2]
        clean, noise, valid = r.clean[...], r.noise[...], r.valid[...]
        root_bar, root_rest, log_beta, post_log, coefficient = (
            r.consts[0:1, spot : spot + 1] for spot in range(5)
        )
        noisy = root_bar * clean + root_rest * noise
        fraction = (var + 1.0) * 0.5
        model_log = fraction * log_beta + (1.0 - fraction) * post_log
        start_est = (noisy - root_rest * eps) / root_bar
        gap = coefficient * (clean - start_est)
        ratio = jnp.exp(post_log - model_log)
        gap_part = gap * gap * jnp.exp(-model_log)
        scale_by = 0.5 / math.log(2.0)
        terms = (eps - noise) * (eps - noise) + scale_by * (
            -1.0 + model_log - post_log + ratio + gap_part
        )
        terms = jnp.where(valid > 0.0, terms, 0.0)
        r.loss[...] = jnp.sum(jnp.sum(terms, axis=1, keepdims=True), axis=0, keepdims=True)
        d_eps = 2.0 * (eps - noise) + 2.0 * scale_by * gap * jnp.exp(-model_log) * (
            coefficient * root_rest / root_bar
        )
        d_var = scale_by * (1.0 - ratio - gap_part) * (0.5 * (log_beta - post_log))
        share = 1.0 / total_images
        d_eps = jnp.where(valid > 0.0, d_eps * share, 0.0).astype(bfloat)
        d_var = jnp.where(valid > 0.0, d_var * share, 0.0).astype(bfloat)
        r.local[48:56] = zeros
        r.local[54:55, 0:CH] = jnp.sum(d_eps.astype(single), axis=0, keepdims=True)
        r.local[54:55, CH : 2 * CH] = jnp.sum(d_var.astype(single), axis=0, keepdims=True)
        r.local[CH : 2 * CH] = dot(d_eps, normed_end, ((0,), (0,)))
        r.local[2 * CH : 3 * CH] = dot(d_var, normed_end, ((0,), (0,)))
        r.hold_far[...] = dot(d_eps, eps_weight, ((1,), (1,))) + dot(
            d_var, var_weight, ((1,), (1,))
        )

        def end_back(at, held):
            shift_sum, scale_sum, gate_sum = held
            mixed, grad = r.d_end[at], r.hold_far[at]
            end = r.hidden_mid[at] + kind_of(5) * mixed
            back, normal = modulate_back(end, grad, kind_of(7))
            r.d_end[at] = back
            r.dm_rows[0, at] = (kind_of(5) * back).astype(bfloat)
            return (
                shift_sum + fold(grad),
                scale_sum + fold(grad * normal),
                gate_sum + fold(mixed * back),
            )

        shift_sum, scale_sum, gate_sum = chunks(end_back, (zeros, zeros, zeros))
        dm_far.start()
        dm_near.start()
        for kind, value in ((6, shift_sum), (7, scale_sum), (5, gate_sum)):
            r.d_modulation[kind : kind + 1] = jnp.sum(value, axis=0, keepdims=True)

        def inner_back(which):
            spot = pl.ds(which * wide, wide)
            gradient = dot(rows_of(r.dm_rows, which), ff[2], ((1,), (0,)))
            gate, up_val = gates[spot], ups[spot]
            sigma = jax.nn.sigmoid(gate)
            d_ups[spot] = (gradient * gate * sigma).astype(bfloat)
            d_gates[spot] = (gradient * up_val * (sigma * (1.0 + gate * (1.0 - sigma)))).astype(
                bfloat
            )

        def outer_back(image):
            spot = pl.ds(image * length, length)
            return dot(d_gates[spot], ff[0], ((1,), (1,))) + dot(d_ups[spot], ff[1], ((1,), (1,)))

        def ff_grad(which, left, right):
            for part in range(2):
                lanes = slice(half * part, half * part + half)
                r.g_ff[which, :, lanes] = dot(left, right[:, lanes], ((0,), (0,))).astype(bfloat)

        dm_near.wait_recv()
        inner_back(0)
        dm_far.wait_recv()
        dm_on.start()
        dm_on.wait_recv()
        inner_back(1)
        for copy in first_parts:
            copy.wait_send()
        r.parts_send[0] = outer_back(3).astype(bfloat)
        second_parts[0].start()
        r.hold_far[...] = outer_back(2)
        ff_grad(2, r.dm_rows[...].reshape(2 * wide, D), acts)
        ff_start(2)
        add_far(second_parts)
        r.parts_send[2] = outer_back(1).astype(bfloat)
        second_parts[2].start()
        r.hold_near[...] = outer_back(0)
        flat = two_rows[...].reshape(2 * wide, D)
        ff_grad(0, flat, d_gates)
        ff_start(0)
        ff_grad(1, flat, d_ups)
        ff_start(1)

    pl.run_scoped(
        swiglu,
        pltpu.VMEM((3, D, units), bfloat),
        pltpu.VMEM((n_model, length, D), bfloat),
        pltpu.VMEM((n_model * length, units), single),
        pltpu.VMEM((n_model * length, units), single),
        pltpu.VMEM((n_model * length, units), bfloat),
        pltpu.VMEM((n_model * length, units), bfloat),
        pltpu.VMEM((n_model * length, units), bfloat),
    )

    db_near, db_far, db_on = spread(Sender(r.db_s, r.db_r), r.db_rows)
    ox, oz = Sender(r.ox_s, r.ox_r), Sender(r.oz_s, r.oz_r)
    out_aside = ox(0, r.g_out.at[1 - x], r.x_out, at_dp(side))
    owner = z == m
    behind = lax.rem(z + depth - m, depth)
    out_along = oz(
        lax.rem(behind + depth - 1, depth),
        r.g_out.at[x],
        r.z_out.at[lax.rem(behind + depth - 1, depth)],
        at_dp(m * NX + x),
    )

    def attend(low, attended, trig, one_rows, qkv_weight, out_weight, d_attended, d_qkv):
        loads = []
        for spot, (source, target) in enumerate(
            (
                (r.out_weight, out_weight),
                (r.low, low),
                (r.trig_all, trig),
                (r.attended, attended),
                (r.one_rows, one_rows),
                (r.qkv_weight, qkv_weight),
            )
        ):
            load = pltpu.make_async_copy(source, target, r.local_sem.at[2 + spot])
            load.start()
            loads.append(load)
        second_parts[2].wait_recv()
        second_parts[1].wait_recv()

        def mid_back(at, held):
            shift_sum, scale_sum, gate_sum, branch_sum = held
            grad = (
                r.hold_near[at]
                + r.parts_recv[2, at].astype(single)
                + r.parts_recv[1, at].astype(single)
            )
            back, normal = modulate_back(r.hidden_mid[at], grad, kind_of(4))
            total = r.d_end[at] + back
            r.d_end[at] = total
            d_branch = (kind_of(2) * total).astype(bfloat)
            r.db_rows[0, at] = d_branch
            return (
                shift_sum + fold(grad),
                scale_sum + fold(grad * normal),
                gate_sum + fold(r.branch[at] * total),
                branch_sum + fold(d_branch.astype(single)),
            )

        sums = chunks(mid_back, (zeros, zeros, zeros, zeros))
        db_far.start()
        db_near.start()
        for kind, value in zip((3, 4, 2), sums):
            r.d_modulation[kind : kind + 1] = jnp.sum(value, axis=0, keepdims=True)
        r.local[49:50] = jnp.sum(sums[3], axis=0, keepdims=True)
        for load in loads:
            load.wait()

        def image_body(image, carry):
            d_attended[...] = dot(
                r.db_rows[image], out_weight[...], ((1,), (1,))
            ).astype(bfloat)
            rank = (
                2 * lax.rem(lax.div(m, 2) + lax.div(image, 2), 2)
                + lax.rem(lax.rem(m, 2) + lax.rem(image, 2), 2)
            )
            count = r.facts_all[d * n_model + rank, 2:3, 1:2]
            mask = lax.broadcasted_iota(jnp.int32, (1, length), 1).astype(single) < count
            cosine, sine = trig[image, 0], trig[image, 1]
            scale_by = 1.0 / math.sqrt(HDIM)
            for head in range(heads):
                start = head * HDIM

                def spot(which):
                    begin = which * head_cols + start
                    return slice(begin, begin + HDIM)

                query, key, value = (low[image, :, spot(which)] for which in range(3))
                grad = d_attended[:, start : start + HDIM]
                scores = dot(query, key, ((1,), (1,))) * scale_by
                scores = jnp.where(mask, scores, -1e30)
                probs = jnp.exp(scores - r.totals[image, :, head : head + 1])
                d_probs = dot(grad, value, ((1,), (1,)))
                row = jnp.sum(probs * d_probs, axis=-1, keepdims=True)
                d_scores = (probs * (d_probs - row)).astype(bfloat)
                d_query = dot(d_scores, key, ((1,), (0,))) * scale_by
                d_key = dot(d_scores, query, ((0,), (0,))) * scale_by
                d_value = dot(probs.astype(bfloat), grad, ((0,), (0,)))
                for which, turned in ((0, d_query), (1, d_key)):
                    back = turned * cosine + swapped(turned * sine)
                    d_qkv[image, :, spot(which)] = back.astype(bfloat)
                d_qkv[image, :, spot(2)] = d_value.astype(bfloat)
            return carry

        db_near.wait_recv()
        lax.fori_loop(0, 2, image_body, 0)
        db_far.wait_recv()
        db_on.start()
        ff_beside(2)
        db_on.wait_recv()
        lax.fori_loop(2, n_model, image_body, 0)

        def one_part(image):
            return dot(d_qkv[image], qkv_weight[...], ((1,), (1,)))

        for copy in second_parts:
            copy.wait_send()
        r.parts_send[0] = one_part(3).astype(bfloat)
        third_parts[0].start()
        r.hold_far[...] = one_part(2)
        ff_beside(0)
        ff_service(2, 0)
        add_far(third_parts)
        r.parts_send[2] = one_part(1).astype(bfloat)
        third_parts[2].start()
        r.hold_near[...] = one_part(0)
        flat_grad = d_qkv[...].reshape(n_model * length, 3 * head_cols)
        r.g_qkv[...] = dot(
            one_rows[...].reshape(n_model * length, D), flat_grad, ((0,), (0,))
        ).astype(bfloat)
        for step in range(depth):
            qkv_aside(step).start()
        r.g_out[...] = (
            dot(
                attended[...].reshape(n_model * length, head_cols),
                r.db_rows[...].reshape(n_model * length, D),
                ((0,), (0,)),
            )
            .astype(bfloat)
            .reshape(NX, rows, D)
        )
        out_aside.start()
        ones = jnp.ones((8, n_model * length), bfloat)
        qkv_sum = dot(ones, flat_grad, ((1,), (0,)))[0:1]
        for rank in range(n_model):
            r.local[50 + rank : 51 + rank, 0 : 3 * head_cols] = jnp.where(m == rank, qkv_sum, 0.0)

    pl.run_scoped(
        attend,
        pltpu.VMEM((n_model, length, 3 * head_cols), bfloat),
        pltpu.VMEM((n_model, length, head_cols), bfloat),
        pltpu.VMEM((n_model, 2, length, HDIM), single),
        pltpu.VMEM((n_model, length, D), bfloat),
        pltpu.VMEM((D, 3 * head_cols), bfloat),
        pltpu.VMEM((head_cols, D), bfloat),
        pltpu.VMEM((length, head_cols), bfloat),
        pltpu.VMEM((n_model, length, 3 * head_cols), bfloat),
    )
    ff_beside(1)
    ff_service(0, 0)
    ff_service(2, 1)
    third_parts[2].wait_recv()
    third_parts[1].wait_recv()

    def first_back(at, held):
        shift_sum, scale_sum, hidden_sum = held
        grad = (
            r.hold_near[at]
            + r.parts_recv[2, at].astype(single)
            + r.parts_recv[1, at].astype(single)
        )
        back, normal = modulate_back(r.hidden[at], grad, kind_of(1))
        d_hidden = (r.d_end[at] + back).astype(bfloat)
        r.normed_end[at] = d_hidden
        return (
            shift_sum + fold(grad),
            scale_sum + fold(grad * normal),
            hidden_sum + fold(d_hidden.astype(single)),
        )

    sums = chunks(first_back, (zeros, zeros, zeros))
    for kind in range(2):
        r.d_modulation[kind : kind + 1] = jnp.sum(sums[kind], axis=0, keepdims=True)
    r.local[48:49] = jnp.sum(sums[2], axis=0, keepdims=True)
    r.local[0:CH] = dot(r.noisy[...], r.normed_end[...], ((0,), (0,)))

    for kind in range(8):
        r.dmod_wide[2 * kind : 2 * kind + 1] = r.d_modulation[kind : kind + 1, 0 : D // 2]
        r.dmod_wide[2 * kind + 1 : 2 * kind + 2] = r.d_modulation[kind : kind + 1, D // 2 : D]
    r.dmod_row[...] = r.dmod_wide[...].astype(bfloat)
    r.dmod_all[me] = r.dmod_row[...]
    send_dmod = Sender(r.dl_s, r.dl_r)
    loop(
        1,
        everyone,
        lambda step: send_dmod(
            step - 1, r.dmod_row, r.dmod_all.at[me], anyone(step)[1]
        ).start(),
    )
    tiles = D // 128
    for top in range(7):
        for left in range(tiles):
            r.sums[top * tiles + left] = r.local[8 * top : 8 * top + 8, 128 * left : 128 * left + 128]
    r.sums[7 * tiles] = jnp.zeros((8, 128), single)
    send_sums = Sender(r.sm_s, r.sm_r)

    def sums_copy(step):
        peer, device = anyone(step)
        return send_sums(step - 1, r.sums.at[pl.ds(2 * peer, 2)], r.sums_recv.at[me], device)

    loop(1, everyone, lambda step: sums_copy(step).start())
    r.sums_recv[me] = r.sums[pl.ds(2 * me, 2)]
    ff_service(1, 0)
    ff_service(0, 1)
    ff_service(2, 2)

    time_pre, condition = r.time_pre[...], r.condition[...]
    sigma_time, sigma_cond = jax.nn.sigmoid(time_pre), jax.nn.sigmoid(condition)
    time_act = (time_pre * sigma_time).astype(bfloat)
    cond_act = (condition * sigma_cond).astype(bfloat)

    def gram(value, precision=None):
        return lax.dot_general(
            value,
            value,
            (((1,), (1,)), ((), ())),
            precision=precision,
            preferred_element_type=single,
        )

    send_dtime = Sender(r.dt_s, r.dt_r)

    def dtime_copy(step):
        return send_dtime(
            step - 1, r.dtime_mine, r.dtime_recv.at[d], at_dp(lax.rem(d + step, n_data))
        )

    def conditioning(mod_weight):
        load = pltpu.make_async_copy(r.mod_weight, mod_weight, r.local_sem.at[0])
        load.start()
        loop(
            1,
            everyone,
            lambda step: send_dmod(
                step - 1, r.dmod_row, r.dmod_all.at[me], anyone(step)[1]
            ).wait(),
        )
        gathered = r.dmod_all[...].astype(single)
        load.wait()
        d_cond = jnp.zeros((everyone, rows), single)
        mod_gram = jnp.zeros((everyone, everyone), single)
        bias_squares = jnp.zeros((1, 1), single)
        for kind in range(8):
            r.dtime_wide[:, 0 : D // 2] = gathered[:, 2 * kind]
            r.dtime_wide[:, D // 2 : D] = gathered[:, 2 * kind + 1]
            part = r.dtime_wide[...]
            column = jnp.sum(part, axis=0, keepdims=True)
            bias_squares = bias_squares + jnp.sum(column * column, axis=1, keepdims=True)
            part = part.astype(bfloat)
            r.dmod[kind] = part
            d_cond = d_cond + dot(
                part, mod_weight[:, kind * D : (kind + 1) * D], ((1,), (1,))
            )
            mod_gram = mod_gram + gram(part)
        d_condition = d_cond * (sigma_cond * (1.0 + condition * (1.0 - sigma_cond)))
        r.d_condition[...] = d_condition
        r.dtime_mine[...] = d_condition.astype(bfloat)
        loop(1, n_data, lambda step: dtime_copy(step).start())
        r.dtime_recv[d] = r.dtime_mine[...]
        r.pay[2] = jnp.zeros((8, 128), single)
        r.pay[2, 0:1, 0:1] = (
            jnp.sum(jnp.sum(mod_gram * gram(cond_act), axis=1, keepdims=True), axis=0, keepdims=True)
            / n_model
            + bias_squares / everyone
        )

    pl.run_scoped(conditioning, pltpu.VMEM((rows, 8 * D), bfloat))
    ff_service(1, 1)
    ff_service(0, 2)
    loop(1, n_data, lambda step: dtime_copy(step).wait())
    for spot in range(n_data):
        r.dtime_wide[:, spot * rows : (spot + 1) * rows] = r.dtime_recv[spot].astype(single)
    dtime = r.dtime_wide[...]
    column = jnp.sum(dtime, axis=0, keepdims=True)
    dtime = dtime.astype(bfloat)
    r.dtime[...] = dtime
    d_time_pre = dot(dtime, r.time_second[...], ((1,), (1,))) * (
        sigma_time * (1.0 + time_pre * (1.0 - sigma_time))
    )
    r.d_time_pre[...] = d_time_pre
    first_sum = jnp.sum(d_time_pre, axis=0, keepdims=True)
    facts = r.facts_all[...]
    sinus = jnp.concatenate([facts[:, 0], facts[:, 1]], axis=1).astype(bfloat)
    onehot = (
        facts[:, 2, 0:1]
        == lax.broadcasted_iota(jnp.int32, (everyone, CLASSES + 1), 1).astype(single)
    ).astype(bfloat)
    highest = lax.Precision.HIGHEST

    def total_of(value):
        return jnp.sum(jnp.sum(value, axis=1, keepdims=True), axis=0, keepdims=True)

    shared_squares = (
        total_of(gram(time_act) * gram(dtime))
        + total_of(gram(sinus) * gram(d_time_pre, highest))
        + total_of(gram(onehot) * gram(r.d_condition[...], highest))
        + total_of(first_sum * first_sum)
    ) / n_model + total_of(column * column) / everyone
    r.pay[3] = jnp.zeros((8, 128), single)
    r.pay[3, 0:1] = first_sum[:, 0:128]
    r.pay[3, 1:2, 0 : rows - 128] = first_sum[:, 128:rows]
    loop(1, everyone, lambda step: sums_copy(step).wait())

    def add_sums(step, held):
        return held + r.sums_recv[step]

    chunk = lax.fori_loop(0, everyone, add_sums, jnp.zeros((2, 8, 128), single))
    r.pay[0:2] = chunk
    own_squares = total_of(chunk[0] * chunk[0]) + total_of(chunk[1] * chunk[1])
    ff_service(1, 2)

    def ff_squares(at, held):
        return tuple(
            one + fold(r.grad_ff[which, at] * r.grad_ff[which, at])
            for which, one in enumerate(held)
        )

    block = jnp.zeros((8, units), single)
    for value in chunks(ff_squares, (block, block, block), 16, rows):
        own_squares = own_squares + total_of(value)
    qkv_beside()
    out_aside.wait()
    r.g_out[x] = (r.g_out[x].astype(single) + r.x_out[...].astype(single)).astype(bfloat)

    @pl.when(jnp.logical_not(owner))
    def _():
        out_along.start()

    for step in range(depth - 1):
        qkv_service(step)
    qkv_near, qkv_far, qkv_on = spread(Sender(r.qa_s, r.qa_r), r.grad_qkv)
    qkv_far.start()
    qkv_near.start()
    give = Sender(r.oa_s, r.oa_r)
    partners = [(d, near_rank), (d, far_rank), (d, lax.rem(near_rank + 2, 4))]
    gives = [
        give(spot, r.out_mine, r.out_mine, partner) for spot, partner in enumerate(partners)
    ]

    @pl.when(owner)
    def _():
        total = r.g_out[x].astype(single)
        for step in range(depth - 1):
            oz(step, r.g_out.at[x], r.z_out.at[step], at_dp(up)).wait_recv()
            total = total + r.z_out[step].astype(single)
        r.out_mine[...] = total.astype(bfloat)
        for copy in gives:
            copy.start()

    for spot, partner in enumerate(partners):

        @pl.when(z == partner[1])
        def _():
            gives[spot].wait_recv()

    qkv_far.wait_recv()
    qkv_on.start()
    r.grad_out[...] = r.out_mine[...]
    out_float, qkv_float = r.out_mine[...].astype(single), r.grad_qkv[0].astype(single)
    r.pay[2, 0:1, 0:1] = (
        r.pay[2, 0:1, 0:1]
        + shared_squares
        + own_squares
        + total_of(out_float * out_float) / n_model
        + total_of(qkv_float * qkv_float)
    )
    r.pay[2, 0:1, 1:2] = r.loss[...]
    send_late = Sender(r.lt_s, r.lt_r)

    def late_copy(step):
        return send_late(step - 1, r.pay, r.late.at[me], anyone(step)[1])

    loop(1, everyone, lambda step: late_copy(step).start())
    r.late[me] = r.pay[...]

    @pl.when(owner)
    def _():
        for copy in gives:
            copy.wait_send()

    @pl.when(jnp.logical_not(owner))
    def _():
        out_along.wait_send()

    qkv_near.wait()
    qkv_on.wait()
    qkv_far.wait_send()
    loop(1, everyone, lambda step: late_copy(step).wait())
    for copy in (dm_near, dm_far, dm_on, db_near, db_far, db_on, *third_parts):
        copy.wait_send()
    for step in range(depth):
        qkv_aside(step).wait_send()
        for which in range(3):
            ff_aside(which, step).wait_send()
    for step in range(depth - 1):
        for part in range(2):
            qkv_along(step, part).wait_send()
            for which in range(3):
                ff_along(which, step, part).wait_send()


def backward_all(values, sizes, total_images, collective):
    n_data, n_model = sizes
    bfloat, single = jnp.bfloat16, jnp.float32
    everyone = n_data * n_model
    rows = D // n_data
    heads = HEADS // n_model
    head_cols = heads * HDIM
    length = values.clean.shape[0]
    units = values.ff.shape[2]
    half = units // 2
    depth = n_data // NX
    shapes = dict(
        grad_ff=((3, rows, units), single),
        grad_qkv=((n_model, rows, 3 * head_cols), bfloat),
        grad_out=((rows, D), bfloat),
        late=((everyone, 4, 8, 128), single),
        dmod=((8, everyone, D), bfloat),
        dtime=((everyone, D), bfloat),
        d_condition=((everyone, rows), single),
        d_time_pre=((everyone, rows), single),
    )
    vmem, dma = pltpu.VMEM, pltpu.SemaphoreType.DMA
    scratch = dict(
        d_end=vmem((length, D), single),
        dm_rows=vmem((n_model, length, D), bfloat),
        db_rows=vmem((n_model, length, D), bfloat),
        hold_far=vmem((length, D), single),
        hold_near=vmem((length, D), single),
        parts_send=vmem((3, length, D), bfloat),
        parts_recv=vmem((3, length, D), bfloat),
        normed_end=vmem((length, D), bfloat),
        g_ff=vmem((3, D, units), bfloat),
        x_ff=vmem((3, depth, rows, units), bfloat),
        z_ff=vmem((3, depth - 1, 2, rows, half), bfloat),
        g_qkv=vmem((D, 3 * head_cols), bfloat),
        x_qkv=vmem((depth, rows, 3 * head_cols), bfloat),
        z_qkv=vmem((depth - 1, rows, 3 * head_cols), bfloat),
        g_out=vmem((NX, rows, D), bfloat),
        x_out=vmem((rows, D), bfloat),
        z_out=vmem((depth - 1, rows, D), bfloat),
        out_mine=vmem((rows, D), bfloat),
        d_modulation=vmem((8, D), single),
        local=vmem((56, D), single),
        sums=vmem((2 * everyone, 8, 128), single),
        sums_recv=vmem((everyone, 2, 8, 128), single),
        pay=vmem((4, 8, 128), single),
        dmod_row=vmem((16, D // 2), bfloat),
        dmod_all=vmem((everyone, 16, D // 2), bfloat),
        dmod_wide=vmem((16, D // 2), single),
        dtime_mine=vmem((everyone, rows), bfloat),
        dtime_recv=vmem((n_data, everyone, rows), bfloat),
        dtime_wide=vmem((everyone, D), single),
        loss=vmem((1, 1), single),
        local_sem=dma((8,)),
    )
    counts = dict(
        dm=(3,),
        db=(3,),
        pa=(3,),
        pb=(3,),
        pc=(3,),
        fx=(3, depth),
        fz=(3, depth - 1, 2),
        qx=(depth,),
        qz=(depth - 1, 2),
        ox=(1,),
        oz=(depth - 1,),
        qa=(3,),
        oa=(3,),
        sm=(everyone - 1,),
        dl=(everyone - 1,),
        dt=(n_data - 1,),
        lt=(everyone - 1,),
    )
    for name, count in counts.items():
        scratch[name + "_s"] = dma(count)
        scratch[name + "_r"] = dma(count)
    far = {
        "ff", "two_rows", "low", "trig_all", "attended", "one_rows", "qkv_weight", "out_weight",
        "mod_weight",
    }

    def space(name):
        return pl.BlockSpec(memory_space=pl.ANY if name in far else pltpu.VMEM)

    outs = pl.pallas_call(
        functools.partial(back_kernel, sizes, total_images),
        out_shape=[jax.ShapeDtypeStruct(*shapes[name]) for name in BackOut._fields],
        in_specs=[space(name) for name in BackIn._fields],
        out_specs=[space(name) for name in BackOut._fields],
        scratch_shapes=[scratch[name] for name in BackScratch._fields],
        compiler_params=pltpu.CompilerParams(
            collective_id=collective, has_side_effects=True, vmem_limit_bytes=60 * 2**20
        ),
    )(*values)
    return BackOut(*outs)


def forward_plain(clean_three, noise_three, patch_grid, labels, timesteps, matrices, embeddings, swiglu_weights, biases):
    bfloat = jnp.bfloat16
    single = jnp.float32
    images = labels.shape[0]
    length = clean_three.shape[1]
    n_model = lax.axis_size("mlp")
    n_data = lax.axis_size("dp")
    sizes = (n_data, n_model)
    total_images = images * n_data * n_model
    rows = D // n_data
    owned_start = lax.axis_index("dp") * rows
    data_index = lax.axis_index("dp")
    model_index = lax.axis_index("mlp")
    heads = HEADS // n_model
    head_cols = heads * HDIM
    qkv_shard = jnp.concatenate(
        [
            cut_columns(matrices, 9 * D + part * D + model_index * head_cols, head_cols)
            for part in range(3)
        ],
        axis=1,
    ).astype(bfloat)
    out_shard = matrices[:, 12 * D : 13 * D].astype(bfloat)
    swiglu_shard = swiglu_weights.astype(bfloat)
    qkv_weight = lax.all_gather(qkv_shard, "dp", axis=0, tiled=True)
    swiglu_use = lax.all_gather(swiglu_shard, "dp", axis=1, tiled=True)
    out_weight = gather_out(out_shard)

    time_second = matrices[:, :D].astype(bfloat)
    mod_weight = matrices[:, D : 9 * D].astype(bfloat)
    time_first = embeddings[CH : CH + FREQ].astype(bfloat)
    class_table = embeddings[CH + FREQ :].astype(bfloat)
    patch_bias = biases[:D]
    first_bias = biases[D : 2 * D]
    second_bias = biases[2 * D : 3 * D]
    mod_bias = biases[3 * D : 11 * D]
    qkv_bias = biases[11 * D : 14 * D]
    out_bias = biases[14 * D : 15 * D]
    final_bias = biases[15 * D :]

    facts = jnp.concatenate([timesteps[:, None], labels[:, None], patch_grid], axis=1)
    facts = jnp.pad(facts, ((0, 8 - images), (0, 124)))
    (facts_all,) = exchange([(facts, "all")], "both", sizes, 0)
    facts_all = facts_all[:, 0, :4]
    steps_all, labels_all, grid_all = facts_all[:, 0], facts_all[:, 1], facts_all[:, 2:4]
    sinus_all = sinusoid(steps_all).astype(bfloat)
    first_bias_own = lax.dynamic_slice_in_dim(first_bias, owned_start, rows)
    second_bias_own = lax.dynamic_slice_in_dim(second_bias, owned_start, rows)
    time_pre = jnp.dot(sinus_all, time_first, preferred_element_type=single) + first_bias_own
    time_act = jax.nn.silu(time_pre).astype(bfloat)
    time_part = jnp.dot(time_act, time_second, preferred_element_type=single)
    small_shard = jnp.concatenate(
        [embeddings[:CH], matrices[:, 13 * D :].T], axis=0
    ).astype(bfloat)
    time_parts, small_all = exchange(
        [
            (time_part.reshape(total_images, n_data, rows).transpose(1, 0, 2), "each"),
            (small_shard, "all"),
        ],
        "dp",
        sizes,
        1,
    )
    small_all = small_all.transpose(1, 0, 2).reshape(3 * CH, D)
    patch_weight = small_all[:CH]
    final_weight = small_all[CH:].T
    time_emb = jnp.sum(time_parts, axis=0) + second_bias_own
    onehot = (labels_all[:, None] == jnp.arange(CLASSES + 1, dtype=jnp.int32)[None, :]).astype(
        bfloat
    )
    condition = time_emb + jnp.dot(onehot, class_table, preferred_element_type=single)
    cond_act = jax.nn.silu(condition).astype(bfloat)
    cond_rank = lax.dynamic_index_in_dim(
        cond_act.reshape(n_data, n_model, rows), model_index, 1, keepdims=False
    )
    mod_part = jnp.dot(cond_rank, mod_weight, preferred_element_type=single)
    (mod_parts,) = exchange(
        [(mod_part.reshape(n_data, 8, D), "each")],
        "dp",
        sizes,
        2,
    )
    modulation = jnp.sum(mod_parts, axis=0).reshape(1, 8 * D) + mod_bias
    shift_one, scale_one, gate_one, shift_two, scale_two, gate_two, shift_end, scale_end = (
        jnp.split(modulation, 8, axis=1)
    )

    group_grid = lax.dynamic_slice_in_dim(grid_all, data_index * n_model, n_model, 0)
    group_grid = jnp.stack(
        [
            lax.dynamic_index_in_dim(group_grid, model_index ^ rank, 0, keepdims=False)
            for rank in range(n_model)
        ]
    )
    cosine, sine, mask = turn_tables(group_grid, length)
    noisy_low = noisy_input(clean_three, noise_three, timesteps).astype(bfloat)
    hidden = jnp.dot(noisy_low, patch_weight, preferred_element_type=single) + patch_bias
    normed_one = modulate(hidden, shift_one, scale_one).astype(bfloat)
    one_rows = jnp.concatenate(gather_rows(normed_one.reshape(length, D), n_model), axis=0)
    qkv_bias_own = jnp.concatenate(
        [
            lax.dynamic_slice_in_dim(qkv_bias, part * D + model_index * head_cols, head_cols)
            for part in range(3)
        ]
    )
    qkv = jnp.dot(one_rows, qkv_weight, preferred_element_type=single) + qkv_bias_own
    low, attended, log_total = attention(
        qkv.reshape(n_model, length, 3 * head_cols), cosine, sine, mask, heads
    )
    attended_rows = attended.reshape(n_model * length, head_cols)
    branch_part = jnp.dot(attended_rows, out_weight, preferred_element_type=single).astype(bfloat)
    branch_part = branch_part.reshape(n_model, length, D)
    branch = (
        scatter_rows(
            (branch_part[2], branch_part[3]), (branch_part[0], branch_part[1]), n_model
        )[None]
        + out_bias
    )
    hidden_mid = hidden + gate_one[:, None, :] * branch
    normed_two = modulate(hidden_mid, shift_two, scale_two).astype(bfloat)
    two_rows = gather_rows(normed_two.reshape(length, D), n_model)
    return SimpleNamespace(
        steps=sinus_all,
        onehot=onehot,
        time_pre=time_pre,
        condition=condition,
        modulation=modulation,
        hidden=hidden,
        one_rows=one_rows,
        qkv_weight=qkv_weight,
        out_weight=out_weight,
        swiglu=swiglu_use,
        low=low,
        attended=attended,
        totals=log_total,
        branch=branch,
        hidden_mid=hidden_mid,
        two_rows=two_rows,
        final_weight=final_weight,
        tables=(cosine, sine, mask),
    )


def forward_fused(clean_three, noise_three, patch_grid, labels, timesteps, matrices, embeddings, swiglu_weights, biases):
    bfloat = jnp.bfloat16
    single = jnp.float32
    length = clean_three.shape[1]
    n_model = lax.axis_size("mlp")
    n_data = lax.axis_size("dp")
    everyone = n_data * n_model
    rows = D // n_data
    owned_start = lax.axis_index("dp") * rows
    model_index = lax.axis_index("mlp")
    head_cols = HEADS // n_model * HDIM

    def own_bias(start, amount, offset):
        return lax.dynamic_slice_in_dim(biases, start + offset, amount)[None]

    sinus = sinusoid(timesteps).astype(bfloat).astype(single).reshape(2, 128)
    facts = jnp.concatenate(
        [labels, patch_grid[:, 0] * patch_grid[:, 1]]
    ).astype(single)
    facts = jnp.concatenate(
        [sinus, jnp.pad(facts[None], ((0, 0), (0, 126))), jnp.zeros((5, 128), single)], axis=0
    )
    cosine, sine, _ = turn_tables(patch_grid, length)
    small = jnp.concatenate(
        [
            embeddings[:CH].T,
            jnp.zeros((rows, CH), single),
            matrices[:, 13 * D :],
            jnp.zeros((rows, 64), single),
        ],
        axis=1,
    ).astype(bfloat)
    values = ForwardIn(
        facts=facts,
        trig=jnp.concatenate([cosine, sine], axis=0),
        small=small,
        time_first=embeddings[CH : CH + FREQ].astype(bfloat),
        first_bias=own_bias(D, rows, owned_start),
        second_bias=own_bias(2 * D, rows, owned_start),
        time_blocks=matrices[:, :D].astype(bfloat).reshape(rows, n_data, rows).transpose(1, 0, 2),
        class_table=embeddings[CH + FREQ :].astype(bfloat),
        mod_weight=matrices[:, D : 9 * D].astype(bfloat),
        mod_bias=biases[3 * D : 11 * D].reshape(8, D),
        noisy=noisy_input(clean_three, noise_three, timesteps).astype(bfloat)[0],
        patch_bias=biases[None, :D],
        qkv_shard=jnp.concatenate(
            [
                cut_columns(matrices, (9 + part) * D + model_index * head_cols, head_cols)
                for part in range(3)
            ],
            axis=1,
        ).astype(bfloat),
        out_shard=matrices[:, 12 * D : 13 * D].astype(bfloat),
        ff_shard=swiglu_weights.astype(bfloat),
        qkv_bias=jnp.concatenate(
            [
                own_bias((11 + part) * D, head_cols, model_index * head_cols)
                for part in range(3)
            ],
            axis=1,
        ),
        out_bias=biases[None, 14 * D : 15 * D],
    )
    out = forward_all(values, (n_data, n_model), 0)
    raw = {name: getattr(out, name) for name in BackIn._fields if name in ForwardOut._fields}
    facts_all = out.facts_all
    group = lax.dynamic_slice_in_dim(
        facts_all[:, 2, 1], lax.axis_index("dp") * n_model, n_model
    )
    spots = model_index ^ jnp.arange(n_model)
    counts = jnp.sum(
        jnp.where(spots[:, None] == jnp.arange(n_model)[None, :], group[None, :], 0.0), axis=1
    )
    mask = jnp.arange(length, dtype=jnp.int32)[None, None, :] < counts[:, None, None]
    return SimpleNamespace(
        raw=dict(
            raw,
            noisy=values.noisy,
            mod_weight=values.mod_weight,
            time_second=matrices[:, :D].astype(bfloat),
        ),
        steps=facts_all[:, :2].reshape(everyone, FREQ).astype(bfloat),
        onehot=(
            facts_all[:, 2, 0:1] == jnp.arange(CLASSES + 1, dtype=jnp.int32)[None].astype(single)
        ).astype(bfloat),
        time_pre=out.time_pre,
        condition=out.condition,
        modulation=out.modulation.reshape(1, 8 * D),
        hidden=out.hidden[None],
        one_rows=out.one_rows.reshape(n_model * length, D),
        qkv_weight=out.qkv_weight,
        out_weight=out.out_weight,
        swiglu=out.ff,
        low=out.low,
        attended=out.attended,
        totals=out.totals,
        branch=out.branch[None],
        hidden_mid=out.hidden_mid[None],
        two_rows=tuple(out.two_rows),
        final_weight=out.small_all[:, 2 * CH : 4 * CH],
        tables=(out.trig_all[:, 0], out.trig_all[:, 1], mask.astype(single)),
    )


def backward_plain(
    kept, clean_three, noise_three, patch_grid, timesteps, biases, total_images
):
    bfloat = jnp.bfloat16
    single = jnp.float32
    images, length = clean_three.shape[:2]
    n_model = lax.axis_size("mlp")
    n_data = lax.axis_size("dp")
    rows = D // n_data
    model_index = lax.axis_index("mlp")
    heads = HEADS // n_model
    head_cols = heads * HDIM
    valid_slot = valid_slots(patch_grid, length)
    final_bias = biases[15 * D :]
    noisy_low = noisy_input(clean_three, noise_three, timesteps).astype(bfloat)
    modulation, hidden, hidden_mid, branch = kept.modulation, kept.hidden, kept.hidden_mid, kept.branch
    shift_one, scale_one, gate_one, shift_two, scale_two, gate_two, shift_end, scale_end = (
        jnp.split(modulation, 8, axis=1)
    )
    qkv_weight, out_weight, swiglu_use = kept.qkv_weight, kept.out_weight, kept.swiglu
    final_weight, one_rows, two_rows = kept.final_weight, kept.one_rows, kept.two_rows
    low, log_total = kept.low, kept.totals
    attended_rows = kept.attended.reshape(n_model * length, head_cols)
    cosine, sine, mask = kept.tables
    two_halves = (
        jnp.concatenate(two_rows[:2], axis=0),
        jnp.concatenate(two_rows[2:], axis=0),
    )
    gates, ups, acts, parts = [], [], [], []
    for part in two_halves:
        gate_val = jnp.dot(part, swiglu_use[0], preferred_element_type=single)
        up_val = jnp.dot(part, swiglu_use[1], preferred_element_type=single)
        act = (jax.nn.silu(gate_val) * up_val).astype(bfloat)
        gates.append(gate_val)
        ups.append(up_val)
        acts.append(act)
        parts.append(backward_product(act, swiglu_use[2]).astype(bfloat).reshape(2, length, D))
    mixed = scatter_rows(parts[1], parts[0], n_model)[None]
    hidden_end = hidden_mid + gate_two[:, None, :] * mixed
    normed_end = modulate(hidden_end, shift_end, scale_end).astype(bfloat)
    output = jnp.dot(normed_end, final_weight, preferred_element_type=single) + final_bias
    local_loss, loss_pull = jax.vjp(
        lambda values_out: loss_terms(values_out, clean_three, noise_three, timesteps, valid_slot),
        output,
    )
    d_output = loss_pull(jnp.asarray(1.0 / total_images, single))[0].astype(bfloat)
    d_normed_end = backward_product(d_output, final_weight)
    unused, pull_end = jax.vjp(modulate, hidden_end, shift_end, scale_end)
    d_hidden_end, d_shift_end, d_scale_end = pull_end(d_normed_end)
    d_mixed = (gate_two[:, None, :] * d_hidden_end).astype(bfloat)
    d_gate_two = jnp.sum(mixed * d_hidden_end, axis=1)
    dmixed_rows = gather_rows(d_mixed.reshape(length, D), n_model)
    dmixed_halves = (
        jnp.concatenate(dmixed_rows[:2], axis=0),
        jnp.concatenate(dmixed_rows[2:], axis=0),
    )
    d_gates, d_ups, d_parts = [], [], []
    for part, gate_val, up_val in zip(dmixed_halves, gates, ups):
        d_inner = jnp.dot(part, swiglu_use[2], preferred_element_type=single)
        unused, pull_glu = jax.vjp(
            lambda gate_in, up_in: jax.nn.silu(gate_in) * up_in, gate_val, up_val
        )
        d_gate, d_up = pull_glu(d_inner)
        d_gate, d_up = d_gate.astype(bfloat), d_up.astype(bfloat)
        d_gates.append(d_gate)
        d_ups.append(d_up)
        d_parts.append(
            (backward_product(d_gate, swiglu_use[0]) + backward_product(d_up, swiglu_use[1]))
            .astype(bfloat)
            .reshape(2, length, D)
        )
    d_normed_two = scatter_rows(d_parts[1], d_parts[0], n_model)[None]
    rows_ready = jnp.concatenate(two_halves, axis=0)
    dmixed_ready = jnp.concatenate(dmixed_halves, axis=0)

    def owned(gradient):
        return reduce_dp(gradient.reshape(n_data, rows, -1))

    grad_swiglu = jnp.stack(
        [
            owned(weight_grad(rows_ready, jnp.concatenate(d_gates, axis=0))),
            owned(weight_grad(rows_ready, jnp.concatenate(d_ups, axis=0))),
            owned(weight_grad(dmixed_ready, jnp.concatenate(acts, axis=0))),
        ]
    )
    unused, pull_two = jax.vjp(modulate, hidden_mid, shift_two, scale_two)
    d_mid_part, d_shift_two, d_scale_two = pull_two(d_normed_two)
    d_hidden_mid = d_hidden_end + d_mid_part
    d_branch = (gate_one[:, None, :] * d_hidden_mid).astype(bfloat)
    d_gate_one = jnp.sum(branch * d_hidden_mid, axis=1)

    dbranch_rows = jnp.concatenate(gather_rows(d_branch.reshape(length, D), n_model), axis=0)
    d_attended = backward_product(dbranch_rows, out_weight).astype(bfloat)
    d_qkv = attention_back(
        low,
        log_total,
        d_attended.reshape(n_model, length, head_cols),
        cosine,
        sine,
        mask,
        heads,
    ).reshape(n_model * length, 3 * head_cols)
    grad_out = reduce_out(weight_grad(attended_rows, dbranch_rows))
    grad_qkv_own = owned(weight_grad(one_rows, d_qkv))
    d_one_part = backward_product(d_qkv, qkv_weight).astype(bfloat).reshape(n_model, length, D)
    d_normed_one = scatter_rows(
        (d_one_part[2], d_one_part[3]), (d_one_part[0], d_one_part[1]), n_model
    )[None]
    unused, pull_one = jax.vjp(modulate, hidden, shift_one, scale_one)
    d_hidden_part, d_shift_one, d_scale_one = pull_one(d_normed_one)
    d_hidden = (d_hidden_mid + d_hidden_part).astype(bfloat)

    return SimpleNamespace(
        d_modulation=jnp.concatenate(
            [
                d_shift_one,
                d_scale_one,
                d_gate_one,
                d_shift_two,
                d_scale_two,
                d_gate_two,
                d_shift_end,
                d_scale_end,
            ],
            axis=1,
        ),
        hidden_sum=column_sum(d_hidden),
        branch_sum=column_sum(d_branch),
        qkv_sum=column_sum(d_qkv),
        output_sum=column_sum(d_output),
        loss=local_loss.reshape(1),
        grad_patch=weight_grad(noisy_low, d_hidden),
        grad_final=weight_grad(normed_end, d_output).T,
        grad_swiglu=grad_swiglu,
        grad_out=grad_out,
        grad_qkv=jnp.stack(gather_rows(grad_qkv_own.astype(bfloat), n_model)).astype(single),
    )


def finish_fused(
    kept, clean_three, noise_three, patch_grid, timesteps, states, biases, total_images
):
    single = jnp.float32
    length = clean_three.shape[1]
    n_data, n_model = sizes = (lax.axis_size("dp"), lax.axis_size("mlp"))
    everyone = n_data * n_model
    rows = D // n_data
    head_cols = HEADS // n_model * HDIM
    owned_start = lax.axis_index("dp") * rows
    beta_now, bar_now, bar_prev = plan(timesteps)
    consts = jnp.stack(
        [
            jnp.sqrt(bar_now),
            jnp.sqrt(1.0 - bar_now),
            jnp.log(beta_now),
            jnp.log(beta_now * (1.0 - bar_prev) / (1.0 - bar_now)),
            beta_now * jnp.sqrt(bar_prev) / (1.0 - bar_now),
        ],
        axis=1,
    )
    values = BackIn(
        **kept.raw,
        final_bias=biases[15 * D :].reshape(2, CH),
        clean=clean_three[0],
        noise=noise_three[0],
        consts=jnp.pad(consts, ((0, 7), (0, 123))),
        valid=valid_slots(patch_grid, length).astype(single).reshape(length, 1),
    )
    out = backward_all(values, sizes, total_images, 1)
    grad_time_first = jnp.dot(
        kept.steps.astype(single).T,
        out.d_time_pre,
        precision=lax.Precision.HIGHEST,
        preferred_element_type=single,
    )
    grad_table = jnp.dot(
        kept.onehot.astype(single).T,
        out.d_condition,
        precision=lax.Precision.HIGHEST,
        preferred_element_type=single,
    )
    late = out.late
    grad_norm = jnp.sqrt(jnp.sum(late[:, 2, 0, 0]))
    factor = jnp.minimum(1.0, CLIP_LIMIT / grad_norm)
    tiles = D // 128
    sums = (
        late[:, :2]
        .reshape(2 * everyone, 8, 128)[: 7 * tiles]
        .reshape(7, tiles, 8, 128)
        .transpose(0, 2, 1, 3)
        .reshape(56, D)
    )
    first_bias_grad = late.reshape(n_data, n_model, 4, 1024)[:, 0, 3, :rows].reshape(D)
    qkv_sums = sums[50 : 50 + n_model, : 3 * head_cols].reshape(n_model, 3, head_cols)
    grad_bias = jnp.concatenate(
        [
            sums[48],
            first_bias_grad,
            column_sum(out.dtime),
            jnp.sum(out.dmod.astype(single), axis=1).reshape(-1),
            qkv_sums.transpose(1, 0, 2).reshape(-1),
            sums[49],
            sums[54, : 2 * CH],
        ]
    )
    own = cut_columns(sums[: 3 * CH], owned_start, rows)
    mats_out = adam_matrices(
        states,
        jax.nn.silu(kept.time_pre).astype(jnp.bfloat16),
        jax.nn.silu(kept.condition).astype(jnp.bfloat16),
        out.dtime,
        out.dmod,
        out.grad_qkv,
        out.grad_out,
        jnp.pad(own[CH:].T, ((0, 0), (0, 128 - 2 * CH))),
        factor.reshape(1, 1),
        n_model,
    )
    return SimpleNamespace(
        loss_sum=jnp.sum(late[:, 2, 0, 1]),
        grad_norm=grad_norm,
        factor=factor,
        grad_bias=grad_bias,
        grad_embed=jnp.concatenate([own[:CH], grad_time_first, grad_table], axis=0),
        grad_swiglu=out.grad_ff,
        mats_out=mats_out,
    )


def adam_matrices_kernel(
    n_model,
    weight_ref,
    first_ref,
    second_ref,
    average_ref,
    time_act_ref,
    cond_act_ref,
    dtime_ref,
    dmod_ref,
    qkv_ref,
    out_ref,
    final_ref,
    factor_ref,
    weight_out,
    first_out,
    second_out,
    average_out,
    grad_ref,
):
    single = jnp.float32
    block = pl.program_id(0)
    head_cols = HEADS // n_model * HDIM

    def outer(left, right):
        return lax.dot_general(left, right, (((0,), (0,)), ((), ())), preferred_element_type=single)

    @pl.when(block == 0)
    def _():
        grad_ref[...] = outer(time_act_ref[...], dtime_ref[...])

    @pl.when((block >= 1) & (block < 9))
    def _():
        grad_ref[...] = outer(cond_act_ref[...], dmod_ref[0])

    m = lax.axis_index("mlp")
    for part in range(3):

        @pl.when(block == 9 + part)
        def _():
            for rank in range(n_model):
                apart = (
                    2 * lax.rem(lax.div(m, 2) + rank // 2, 2)
                    + lax.rem(lax.rem(m, 2) + rank % 2, 2)
                )
                grad_ref[:, rank * head_cols : (rank + 1) * head_cols] = qkv_ref[
                    apart, :, part * head_cols : (part + 1) * head_cols
                ].astype(single)

    @pl.when(block == 12)
    def _():
        grad_ref[...] = out_ref[...].astype(single)

    @pl.when(block == 13)
    def _():
        grad_ref[:, 0:128] = final_ref[...]

    def body(step, carry):
        at = pl.ds(pl.multiple_of(step * 8, 8), 8)
        done = adam_step(
            weight_ref[at],
            first_ref[at],
            second_ref[at],
            grad_ref[at],
            average_ref[at],
            factor_ref[...],
            LEARN_RATE,
        )
        for place, value in zip((weight_out, first_out, second_out, average_out), done):
            place[at] = value
        return carry

    lax.fori_loop(0, weight_ref.shape[0] // 8, body, 0)


def adam_matrices(
    states, time_act, cond_act, dtime, dmod, grad_qkv, grad_out, grad_final, factor, n_model
):
    rows, width = states[0].shape
    whole = lambda array: pl.BlockSpec(array.shape, lambda i: (0,) * array.ndim)
    strip = pl.BlockSpec((rows, D), lambda i: (0, i))
    return pl.pallas_call(
        functools.partial(adam_matrices_kernel, n_model),
        grid=(pl.cdiv(width, D),),
        out_shape=[jax.ShapeDtypeStruct((rows, width), jnp.float32)] * 4,
        in_specs=[strip] * 4
        + [whole(time_act), whole(cond_act), whole(dtime)]
        + [pl.BlockSpec((1, *dmod.shape[1:]), lambda i: (jnp.clip(i - 1, 0, 7), 0, 0))]
        + [whole(grad_qkv), whole(grad_out), whole(grad_final), whole(factor)],
        out_specs=[strip] * 4,
        scratch_shapes=[pltpu.VMEM((rows, D), jnp.float32)],
        compiler_params=pltpu.CompilerParams(vmem_limit_bytes=KERNEL_VMEM),
    )(*states, time_act, cond_act, dtime, dmod, grad_qkv, grad_out, grad_final, factor)


def finish_plain(
    kept, clean_three, noise_three, patch_grid, timesteps, states, biases, total_images
):
    bfloat = jnp.bfloat16
    single = jnp.float32
    matrices, matrices_first, matrices_second, matrices_average = states
    n_data, n_model = sizes = (lax.axis_size("dp"), lax.axis_size("mlp"))
    rows = D // n_data
    owned_start = lax.axis_index("dp") * rows
    model_index = lax.axis_index("mlp")
    head_cols = HEADS // n_model * HDIM
    time_pre, condition = kept.time_pre, kept.condition
    onehot, sinus_all = kept.onehot, kept.steps
    time_act = jax.nn.silu(time_pre).astype(bfloat)
    cond_act = jax.nn.silu(condition).astype(bfloat)
    time_second = matrices[:, :D].astype(bfloat)
    mod_weight = matrices[:, D : 9 * D].astype(bfloat)

    grads = backward_plain(
        kept, clean_three, noise_three, patch_grid, timesteps, biases, total_images
    )
    grad_swiglu, grad_out = grads.grad_swiglu, grads.grad_out
    grad_qkv_own = grads.grad_qkv[0]
    qkv_stack = jnp.stack(
        [
            lax.dynamic_index_in_dim(grads.grad_qkv, model_index ^ rank, 0, keepdims=False)
            for rank in range(n_model)
        ]
    )
    grad_qkv = (
        qkv_stack.reshape(n_model, rows, 3, head_cols).transpose(1, 2, 0, 3).reshape(rows, 3 * D)
    )

    d_modulation = grads.d_modulation.astype(bfloat)
    (dmod_all,) = exchange(
        [(d_modulation.reshape(16, D // 2), "all")], "both", sizes, 3
    )
    dmod_all = dmod_all.reshape(total_images, 8 * D)
    d_cond_act = backward_product(dmod_all, mod_weight)
    unused, pull_cond = jax.vjp(jax.nn.silu, condition)
    d_condition = pull_cond(d_cond_act)[0]
    d_time_emb = d_condition.astype(bfloat)
    (dtime_parts,) = exchange([(d_time_emb, "all")], "dp", sizes, 4)
    dtime_all = dtime_parts.transpose(1, 0, 2).reshape(total_images, D)
    d_time_act = backward_product(dtime_all, time_second)
    unused, pull_time = jax.vjp(jax.nn.silu, time_pre)
    d_time_pre = pull_time(d_time_act)[0]
    grad_time_second = weight_grad(time_act, dtime_all)
    grad_mod = weight_grad(cond_act, dmod_all)
    grad_time_first = jnp.dot(
        sinus_all.astype(single).T,
        d_time_pre,
        precision=lax.Precision.HIGHEST,
        preferred_element_type=single,
    )
    grad_table = jnp.dot(
        onehot.astype(single).T,
        d_condition,
        precision=lax.Precision.HIGHEST,
        preferred_element_type=single,
    )

    qkv_sums = grads.qkv_sum.reshape(3, head_cols)
    qkv_bias_part = lax.dynamic_update_slice(
        jnp.zeros((3, D), single), qkv_sums, (0, model_index * head_cols)
    )
    local_sums = jnp.concatenate(
        [
            grads.hidden_sum,
            qkv_bias_part.reshape(-1),
            grads.branch_sum,
            grads.output_sum,
            grads.loss,
            jnp.zeros((95,), single),
            grads.grad_patch.reshape(-1),
            grads.grad_final.reshape(-1),
        ]
    )
    everyone = n_data * n_model
    chunk_rows = -(-local_sums.shape[0] // (everyone * 1024)) * 8
    local_sums = jnp.pad(local_sums, (0, everyone * chunk_rows * 128 - local_sums.shape[0]))
    (sum_parts,) = exchange(
        [(local_sums.reshape(everyone, chunk_rows, 128), "each")], "both", sizes, 5
    )
    chunk = jnp.sum(sum_parts, axis=0)
    local_squares = (
        jnp.sum(grad_time_second * grad_time_second)
        + jnp.sum(grad_mod * grad_mod)
        + jnp.sum(grad_out * grad_out)
        + jnp.sum(grad_time_first * grad_time_first)
        + jnp.sum(grad_table * grad_table)
    ) / n_model + jnp.sum(grad_swiglu * grad_swiglu) + jnp.sum(grad_qkv_own * grad_qkv_own)
    extra = jnp.concatenate([jnp.sum(d_time_pre, axis=0), local_squares.reshape(1)])
    extra = jnp.pad(extra, (0, 1024 - extra.shape[0])).reshape(8, 128)
    (late,) = exchange([(jnp.concatenate([chunk, extra], axis=0), "all")], "both", sizes, 6)
    sums = late[:, :chunk_rows].reshape(-1)
    extras = late[:, chunk_rows:].reshape(everyone, 1024)
    first_bias_grad = extras.reshape(n_data, n_model, 1024)[:, 0, :rows].reshape(D)
    squares = jnp.sum(extras[:, rows])
    ends = [D, 4 * D, 5 * D, 5 * D + 2 * CH, 5 * D + 2 * CH + 1]
    base = 5 * D + 128
    loss_sum = sums[5 * D + 2 * CH]
    grad_patch = sums[base : base + CH * D].reshape(CH, D)
    grad_final = sums[base + CH * D : base + 3 * CH * D].reshape(2 * CH, D)
    grad_patch = cut_columns(grad_patch, owned_start, rows)
    grad_final_own = cut_columns(grad_final, owned_start, rows).T
    grad_bias = jnp.concatenate(
        [
            sums[:D],
            first_bias_grad,
            column_sum(dtime_all),
            column_sum(dmod_all),
            sums[D : 4 * D],
            sums[4 * D : 5 * D],
            sums[5 * D : 5 * D + 2 * CH],
        ]
    )
    shared = sums[base : base + 3 * CH * D]
    squares = squares + jnp.sum(grad_bias * grad_bias) + jnp.sum(shared * shared)
    grad_norm = jnp.sqrt(squares)
    factor = jnp.minimum(1.0, CLIP_LIMIT / grad_norm)
    grad_mats = jnp.concatenate(
        [grad_time_second, grad_mod, grad_qkv, grad_out, grad_final_own], axis=1
    )
    grad_embed = jnp.concatenate([grad_patch, grad_time_first, grad_table], axis=0)
    mats_out = adam_step(
        matrices, matrices_first, matrices_second, grad_mats, matrices_average, factor, LEARN_RATE
    )
    return SimpleNamespace(
        loss_sum=loss_sum,
        grad_norm=grad_norm,
        factor=factor,
        grad_bias=grad_bias,
        grad_embed=grad_embed,
        grad_swiglu=grad_swiglu,
        mats_out=mats_out,
    )


def on_device(
    clean_patches,
    noise_patches,
    patch_grid,
    labels,
    timesteps,
    matrices,
    embeddings,
    swiglu_weights,
    biases,
    matrices_first,
    embeddings_first,
    swiglu_first,
    biases_first,
    matrices_second,
    embeddings_second,
    swiglu_second,
    biases_second,
    matrices_average,
    embeddings_average,
    swiglu_average,
    biases_average,
):
    images = labels.shape[0]
    length = clean_patches.shape[0] // images
    n_model = lax.axis_size("mlp")
    n_data = lax.axis_size("dp")
    total_images = images * n_data * n_model

    clean_three = clean_patches.reshape(images, length, CH)
    noise_three = noise_patches.reshape(images, length, CH)
    fused = (n_data, n_model, images) == (8, 4, 1)
    forward = forward_fused if fused else forward_plain
    kept = forward(
        clean_three,
        noise_three,
        patch_grid,
        labels,
        timesteps,
        matrices,
        embeddings,
        swiglu_weights,
        biases,
    )
    finish = finish_fused if fused else finish_plain
    done = finish(
        kept,
        clean_three,
        noise_three,
        patch_grid,
        timesteps,
        (matrices, matrices_first, matrices_second, matrices_average),
        biases,
        total_images,
    )
    loss_sum, grad_norm, factor = done.loss_sum, done.grad_norm, done.factor
    grad_embed, grad_swiglu, grad_bias = done.grad_embed, done.grad_swiglu, done.grad_bias
    mats_out = done.mats_out
    embed_out = adam_step(
        embeddings,
        embeddings_first,
        embeddings_second,
        grad_embed,
        embeddings_average,
        factor,
        TABLE_RATE,
    )
    swiglu_out = adam_step(
        swiglu_weights, swiglu_first, swiglu_second, grad_swiglu, swiglu_average, factor, LEARN_RATE
    )
    bias_out = adam_step(
        biases, biases_first, biases_second, grad_bias, biases_average, factor, TABLE_RATE
    )
    return (
        loss_sum,
        grad_norm,
        mats_out[0],
        embed_out[0],
        swiglu_out[0],
        bias_out[0],
        mats_out[1],
        embed_out[1],
        swiglu_out[1],
        bias_out[1],
        mats_out[2],
        embed_out[2],
        swiglu_out[2],
        bias_out[2],
        mats_out[3],
        embed_out[3],
        swiglu_out[3],
        bias_out[3],
        grad_bias * factor,
    )


def solution(mesh):
    placed = (
        P(("dp", "mlp"), None),
        P(("dp", "mlp"), None),
        P(("dp", "mlp"), None),
        P(("dp", "mlp")),
        P(("dp", "mlp")),
        P("dp", None),
        P(None, "dp"),
        P(None, "dp", "mlp"),
        P(),
        P("dp", None),
        P(None, "dp"),
        P(None, "dp", "mlp"),
        P(),
        P("dp", None),
        P(None, "dp"),
        P(None, "dp", "mlp"),
        P(),
        P("dp", None),
        P(None, "dp"),
        P(None, "dp", "mlp"),
        P(),
    )
    return jax.shard_map(
        on_device,
        mesh=mesh,
        in_specs=placed,
        out_specs=(
            P(),
            P(),
            P("dp", None),
            P(None, "dp"),
            P(None, "dp", "mlp"),
            P(),
            P("dp", None),
            P(None, "dp"),
            P(None, "dp", "mlp"),
            P(),
            P("dp", None),
            P(None, "dp"),
            P(None, "dp", "mlp"),
            P(),
            P("dp", None),
            P(None, "dp"),
            P(None, "dp", "mlp"),
            P(),
            P(),
        ),
        check_vma=False,
    )
```

```python
import functools
import math
from types import SimpleNamespace
from typing import Any, NamedTuple

import jax
import jax.numpy as jnp
from jax import lax
from jax.experimental import pallas as pl
from jax.experimental.pallas import tpu as pltpu
from jax.sharding import PartitionSpec as P

HEADS = 16
HDIM = 72
D = 1152
CH = 16
CLASSES = 1000
FREQ = 256
STEP = 10


CLIP_LIMIT = 1.0
LEARN_RATE = 0.03
TABLE_RATE = 0.4
FIRST_DECAY = 0.9
SECOND_DECAY = 0.999
ADAM_EPSILON = 1e-08
WEIGHT_DECAY = 0.01
AVERAGE_DECAY = 0.9999


def plan(steps_in):
    step_index = jnp.arange(1000, dtype=jnp.int32)
    beta_table = 0.0001 + (0.02 - 0.0001) * step_index.astype(jnp.float32) / 999.0
    logbar = jnp.cumsum(jnp.log1p(-beta_table))

    def lookup(values, wanted):
        return jnp.sum(
            jnp.where(wanted[:, None] == step_index[None, :], values[None, :], 0.0), axis=1
        )

    return (
        lookup(beta_table, steps_in),
        jnp.exp(lookup(logbar, steps_in)),
        jnp.exp(lookup(logbar, steps_in - 1)),
    )


def sinusoid(steps_in):
    halfway = FREQ // 2
    frequency = jnp.exp(-math.log(10000.0) * jnp.arange(halfway, dtype=jnp.float32) / halfway)
    angles = steps_in.astype(jnp.float32)[:, None] * frequency[None, :]
    return jnp.concatenate([jnp.cos(angles), jnp.sin(angles)], axis=1)


def modulate(hidden, shift_by, scale_by):
    row_mean = jnp.mean(hidden, axis=-1, keepdims=True)
    centered = hidden - row_mean
    variance = jnp.mean(centered * centered, axis=-1, keepdims=True)
    return (
        centered * lax.rsqrt(variance + 1e-06) * (1.0 + scale_by[:, None, :]) + shift_by[:, None, :]
    )


def noisy_input(clean_patches, noise_patches, steps_in):
    beta_now, bar_now, bar_prev = plan(steps_in)
    bar_now = bar_now[:, None, None]
    return jnp.sqrt(bar_now) * clean_patches + jnp.sqrt(1.0 - bar_now) * noise_patches


def loss_terms(output, clean_patches, noise_patches, steps_in, valid_slot):
    beta_now, bar_now, bar_prev = plan(steps_in)
    beta_now = beta_now[:, None, None]
    bar_now = bar_now[:, None, None]
    bar_prev = bar_prev[:, None, None]
    noisy = jnp.sqrt(bar_now) * clean_patches + jnp.sqrt(1.0 - bar_now) * noise_patches
    eps_pred = output[..., :CH]
    var_raw = output[..., CH:]
    squared = jnp.sum((eps_pred - noise_patches) ** 2, axis=-1)
    post_log = jnp.log(beta_now * (1.0 - bar_prev) / (1.0 - bar_now))
    fraction = (var_raw + 1.0) * 0.5
    model_log = fraction * jnp.log(beta_now) + (1.0 - fraction) * post_log
    coefficient = beta_now * jnp.sqrt(bar_prev) / (1.0 - bar_now)
    start_est = (noisy - jnp.sqrt(1.0 - bar_now) * eps_pred) / jnp.sqrt(bar_now)
    mean_gap = coefficient * (clean_patches - start_est)
    divergence = (
        0.5
        * (
            -1.0
            + model_log
            - post_log
            + jnp.exp(post_log - model_log)
            + mean_gap * mean_gap * jnp.exp(-model_log)
        )
        / math.log(2.0)
    )
    return jnp.sum(jnp.where(valid_slot, squared + jnp.sum(divergence, axis=-1), 0.0))


def adam_step(weight, first, second, gradient, average, factor, rate):
    average_decay = min(AVERAGE_DECAY, (1.0 + STEP) / (10.0 + STEP))
    clipped = gradient * factor
    first = FIRST_DECAY * first + (1.0 - FIRST_DECAY) * clipped
    second = SECOND_DECAY * second + (1.0 - SECOND_DECAY) * clipped * clipped
    ratio = (first * (1.0 / (1.0 - FIRST_DECAY**STEP))) / (
        jnp.sqrt(second * (1.0 / (1.0 - SECOND_DECAY**STEP))) + ADAM_EPSILON
    )
    weight = weight - rate * (ratio + WEIGHT_DECAY * weight)
    return (weight, first, second, average_decay * average + (1.0 - average_decay) * weight)


def backward_product(gradient, weight):
    return lax.dot_general(
        gradient,
        weight,
        (((gradient.ndim - 1,), (1,)), ((), ())),
        preferred_element_type=jnp.float32,
    )


def weight_grad(inputs, gradient):
    flat_in = inputs.reshape(-1, inputs.shape[-1])
    flat_grad = gradient.reshape(-1, gradient.shape[-1])
    return lax.dot_general(
        flat_in, flat_grad, (((0,), (0,)), ((), ())), preferred_element_type=jnp.float32
    )


def column_sum(gradient):
    return jnp.sum(gradient.astype(jnp.float32).reshape(-1, gradient.shape[-1]), axis=0)


def cut_columns(values, start, amount):
    return lax.dynamic_slice_in_dim(values, start, amount, 1)


MESH_IDS = pl.DeviceIdType.MESH
KERNEL_VMEM = 48 * 2**20


def exchange_kernel(axes, sizes, modes, *refs):
    count = len(modes)
    ins, outs = refs[:count], refs[count : 2 * count]
    send_sem, recv_sem = refs[2 * count :]
    if axes == "dp":
        total = sizes[0]
        me = lax.axis_index("dp")
    else:
        total = sizes[0] * sizes[1]
        me = lax.axis_index("dp") * sizes[1] + lax.axis_index("mlp")

    def device(spot):
        if axes == "dp":
            return (spot, lax.axis_index("mlp"))
        return (lax.div(spot, sizes[1]), lax.rem(spot, sizes[1]))

    barrier = pltpu.get_barrier_semaphore()

    def greet(step, carry):
        pl.semaphore_signal(
            barrier, inc=1, device_id=device(lax.rem(me + step, total)), device_id_type=MESH_IDS
        )
        return carry

    lax.fori_loop(1, total, greet, 0)
    pl.semaphore_wait(barrier, total - 1)

    def make(item, step):
        peer = lax.rem(me + step, total)
        source = ins[item].at[peer] if modes[item] == "each" else ins[item]
        return pltpu.make_async_remote_copy(
            src_ref=source,
            dst_ref=outs[item].at[me],
            send_sem=send_sem.at[item, step - 1],
            recv_sem=recv_sem.at[item, step - 1],
            device_id=device(peer),
            device_id_type=MESH_IDS,
        )

    def begin(step, carry):
        for item in range(count):
            make(item, step).start()
        return carry

    lax.fori_loop(1, total, begin, 0)
    for item in range(count):
        if modes[item] == "each":
            outs[item][me] = ins[item][me]
        else:
            outs[item][me] = ins[item][...]

    def finish(step, carry):
        for item in range(count):
            make(item, step).wait()
        return carry

    lax.fori_loop(1, total, finish, 0)


def exchange(items, axes, sizes, collective):
    total = sizes[0] if axes == "dp" else sizes[0] * sizes[1]
    modes = tuple(mode for _, mode in items)
    arrays = [array for array, _ in items]
    shapes = [
        jax.ShapeDtypeStruct(
            array.shape if mode == "each" else (total, *array.shape), array.dtype
        )
        for array, mode in items
    ]
    space = pl.BlockSpec(memory_space=pltpu.VMEM)
    return pl.pallas_call(
        functools.partial(exchange_kernel, axes, sizes, modes),
        out_shape=shapes,
        in_specs=[space] * len(items),
        out_specs=[space] * len(items),
        scratch_shapes=[
            pltpu.SemaphoreType.DMA((len(items), total - 1)),
            pltpu.SemaphoreType.DMA((len(items), total - 1)),
        ],
        compiler_params=pltpu.CompilerParams(
            collective_id=collective, has_side_effects=True, vmem_limit_bytes=KERNEL_VMEM
        ),
    )(*arrays)


NX = 2


def reduce_dp(value):
    return lax.psum_scatter(value.astype(jnp.bfloat16), "dp", scatter_dimension=0, tiled=True)[
        0
    ].astype(jnp.float32)


def flip(value, bit, count):
    return lax.ppermute(value, "mlp", [(spot, spot ^ bit) for spot in range(count)])


def gather_rows(own, count):
    far = flip(own, 2, count)
    near = flip(own, 1, count)
    return own, near, far, flip(far, 1, count)


def scatter_rows(far_parts, near_parts, count):
    single = jnp.float32
    got = flip(far_parts[1], 1, count)
    far = flip((far_parts[0].astype(single) + got.astype(single)).astype(jnp.bfloat16), 2, count)
    near = flip(near_parts[1], 1, count)
    return near_parts[0].astype(single) + near.astype(single) + far.astype(single)


def gather_out(shard):
    whole = lax.all_gather(shard, "dp", axis=0, tiled=True)
    height = D // lax.axis_size("mlp")
    return lax.dynamic_slice_in_dim(whole, lax.axis_index("mlp") * height, height, 0)


def reduce_out(value):
    whole = lax.dynamic_update_slice_in_dim(
        jnp.zeros((D, D), jnp.float32), value, lax.axis_index("mlp") * value.shape[0], 0
    )
    part = lax.psum_scatter(whole.astype(jnp.bfloat16), "dp", scatter_dimension=0, tiled=True)
    return lax.psum(part.astype(jnp.float32), "mlp")


def swapped(values):
    quarter = HDIM // 4
    return jnp.concatenate(
        [
            values[:, quarter : 2 * quarter],
            values[:, :quarter],
            values[:, 3 * quarter :],
            values[:, 2 * quarter : 3 * quarter],
        ],
        axis=1,
    )


def attention_kernel(heads, qkv_ref, cos_ref, sin_ref, mask_ref, low_ref, out_ref, total_ref):
    width = heads * HDIM
    cosine, sine, mask = cos_ref[0], sin_ref[0], mask_ref[0]
    totals = []
    for head in range(heads):
        start = head * HDIM

        def part(which):
            return qkv_ref[0, :, which * width + start : which * width + start + HDIM]

        raw_q, raw_k = part(0), part(1)
        query = (raw_q * cosine + swapped(raw_q) * sine).astype(jnp.bfloat16)
        key = (raw_k * cosine + swapped(raw_k) * sine).astype(jnp.bfloat16)
        value = part(2).astype(jnp.bfloat16)
        for which, kept in enumerate((query, key, value)):
            low_ref[0, :, which * width + start : which * width + start + HDIM] = kept
        scores = lax.dot_general(
            query, key, (((1,), (1,)), ((), ())), preferred_element_type=jnp.float32
        ) * (1.0 / math.sqrt(HDIM))
        scores = jnp.where(mask > 0.0, scores, -1e30)
        row_max = jnp.max(scores, axis=-1, keepdims=True)
        exponent = jnp.exp(scores - row_max)
        row_sum = jnp.sum(exponent, axis=-1, keepdims=True)
        probs = exponent / row_sum
        out_ref[0, :, start : start + HDIM] = jnp.dot(
            probs.astype(jnp.bfloat16), value, preferred_element_type=jnp.float32
        ).astype(jnp.bfloat16)
        totals.append(row_max + jnp.log(row_sum))
    total_ref[0] = jnp.concatenate(totals, axis=1)


def attention(qkv, cosine, sine, mask, heads):
    images, length, width = qkv.shape
    per_image = lambda *dims: pl.BlockSpec((1, *dims), lambda i: (i, 0, 0))
    return pl.pallas_call(
        functools.partial(attention_kernel, heads),
        grid=(images,),
        out_shape=[
            jax.ShapeDtypeStruct((images, length, width), jnp.bfloat16),
            jax.ShapeDtypeStruct((images, length, heads * HDIM), jnp.bfloat16),
            jax.ShapeDtypeStruct((images, length, heads), jnp.float32),
        ],
        in_specs=[
            per_image(length, width),
            per_image(length, HDIM),
            per_image(length, HDIM),
            per_image(1, length),
        ],
        out_specs=[
            per_image(length, width),
            per_image(length, heads * HDIM),
            per_image(length, heads),
        ],
        compiler_params=pltpu.CompilerParams(vmem_limit_bytes=KERNEL_VMEM),
    )(qkv, cosine, sine, mask)


def attention_back_kernel(
    heads, low_ref, total_ref, grad_ref, cos_ref, sin_ref, mask_ref, out_ref
):
    width = heads * HDIM
    scale_by = 1.0 / math.sqrt(HDIM)
    cosine, sine, mask = cos_ref[0], sin_ref[0], mask_ref[0]

    def contract(left, right, dims):
        return lax.dot_general(left, right, (dims, ((), ())), preferred_element_type=jnp.float32)

    for head in range(heads):
        start = head * HDIM

        def spot(which):
            return slice(which * width + start, which * width + start + HDIM)

        query, key, value = (low_ref[0, :, spot(which)] for which in range(3))
        grad = grad_ref[0, :, start : start + HDIM]
        scores = contract(query, key, ((1,), (1,))) * scale_by
        scores = jnp.where(mask > 0.0, scores, -1e30)
        probs = jnp.exp(scores - total_ref[0, :, head : head + 1])
        d_probs = contract(grad, value, ((1,), (1,)))
        row = jnp.sum(probs * d_probs, axis=-1, keepdims=True)
        d_scores = (probs * (d_probs - row)).astype(jnp.bfloat16)
        d_query = contract(d_scores, key, ((1,), (0,))) * scale_by
        d_key = contract(d_scores, query, ((0,), (0,))) * scale_by
        d_value = contract(probs.astype(jnp.bfloat16), grad, ((0,), (0,)))
        for which, turned in ((0, d_query), (1, d_key)):
            back = turned * cosine + swapped(turned * sine)
            out_ref[0, :, spot(which)] = back.astype(jnp.bfloat16)
        out_ref[0, :, spot(2)] = d_value.astype(jnp.bfloat16)


def attention_back(low, totals, grad, cosine, sine, mask, heads):
    images, length, width = low.shape
    per_image = lambda *dims: pl.BlockSpec((1, *dims), lambda i: (i, 0, 0))
    return pl.pallas_call(
        functools.partial(attention_back_kernel, heads),
        grid=(images,),
        out_shape=jax.ShapeDtypeStruct((images, length, width), jnp.bfloat16),
        in_specs=[
            per_image(length, width),
            per_image(length, heads),
            per_image(length, heads * HDIM),
            per_image(length, HDIM),
            per_image(length, HDIM),
            per_image(1, length),
        ],
        out_specs=per_image(length, width),
        compiler_params=pltpu.CompilerParams(vmem_limit_bytes=KERNEL_VMEM),
    )(low, totals, grad, cosine, sine, mask)


def turn_tables(patch_grid, length):
    slot_index = jnp.arange(length, dtype=jnp.int32)[None, :]
    grid_cols = patch_grid[:, 1:2]
    valid_slot = slot_index < patch_grid[:, 0:1] * grid_cols
    row_place = (slot_index // grid_cols).astype(jnp.float32)
    col_place = (slot_index % grid_cols).astype(jnp.float32)
    quarter = HDIM // 4
    frequency = jnp.exp(-math.log(10000.0) * jnp.arange(quarter, dtype=jnp.float32) / quarter)
    row_angle = row_place[..., None] * frequency
    col_angle = col_place[..., None] * frequency
    cos_row, sin_row = jnp.cos(row_angle), jnp.sin(row_angle)
    cos_col, sin_col = jnp.cos(col_angle), jnp.sin(col_angle)
    return (
        jnp.concatenate([cos_row, cos_row, cos_col, cos_col], axis=-1),
        jnp.concatenate([-sin_row, sin_row, -sin_col, sin_col], axis=-1),
        valid_slot.astype(jnp.float32)[:, None, :],
    )


def valid_slots(patch_grid, length):
    return jnp.arange(length, dtype=jnp.int32)[None, :] < patch_grid[:, 0:1] * patch_grid[:, 1:2]


def device_parts():
    d, m = lax.axis_index("dp"), lax.axis_index("mlp")
    return d, m, lax.div(d, NX), lax.rem(d, NX)


class Sender:
    def __init__(self, send_sem, recv_sem):
        self.send_sem, self.recv_sem = send_sem, recv_sem

    def __call__(self, spot, source, target, device):
        spot = spot if isinstance(spot, tuple) else (spot,)
        return pltpu.make_async_remote_copy(
            src_ref=source,
            dst_ref=target,
            send_sem=self.send_sem.at[spot],
            recv_sem=self.recv_sem.at[spot],
            device_id=device,
            device_id_type=MESH_IDS,
        )


def modulate_rows(values, shift_by, scale_by):
    row_mean = jnp.mean(values, axis=-1, keepdims=True)
    centered = values - row_mean
    variance = jnp.mean(centered * centered, axis=-1, keepdims=True)
    return centered * lax.rsqrt(variance + 1e-06) * (1.0 + scale_by) + shift_by


def named(inputs, outputs, scratch, refs):
    ends = len(inputs._fields), len(inputs._fields) + len(outputs._fields)
    parts = inputs(*refs[: ends[0]]), outputs(*refs[ends[0] : ends[1]]), scratch(*refs[ends[1] :])
    return SimpleNamespace(**{k: v for part in parts for k, v in part._asdict().items()})


class ForwardIn(NamedTuple):
    facts: Any
    trig: Any
    small: Any
    time_first: Any
    first_bias: Any
    second_bias: Any
    class_table: Any
    matrices: Any
    mod_bias: Any
    noisy: Any
    patch_bias: Any
    qkv_shard: Any
    ff_shard: Any
    qkv_bias: Any
    out_bias: Any


class ForwardOut(NamedTuple):
    facts_all: Any
    trig_all: Any
    small_all: Any
    time_pre: Any
    condition: Any
    modulation: Any
    hidden: Any
    one_rows: Any
    qkv_weight: Any
    out_weight: Any
    ff: Any
    low: Any
    attended: Any
    totals: Any
    branch: Any
    hidden_mid: Any
    two_rows: Any


class ForwardScratch(NamedTuple):
    time_low: Any
    out_low: Any
    time_send: Any
    time_recv: Any
    mod_send: Any
    mod_recv: Any
    mod_low: Any
    qkv: Any
    parts_send: Any
    parts_recv: Any
    facts_s: Any
    facts_r: Any
    small_s: Any
    small_r: Any
    time_s: Any
    time_r: Any
    mods_s: Any
    mods_r: Any
    trig_s: Any
    trig_r: Any
    noisy_s: Any
    noisy_r: Any
    kinds_s: Any
    kinds_r: Any
    noisy_all: Any
    kinds_all: Any
    two_s: Any
    two_r: Any
    part_s: Any
    part_r: Any
    qz_s: Any
    qz_r: Any
    qx_s: Any
    qx_r: Any
    oz_s: Any
    oz_r: Any
    ox_s: Any
    ox_r: Any
    fz_s: Any
    fz_r: Any
    fx_s: Any
    fx_r: Any
    local_sem: Any


def forward_kernel(sizes, *refs):
    r = named(ForwardIn, ForwardOut, ForwardScratch, refs)
    bfloat, single = jnp.bfloat16, jnp.float32
    n_data, n_model = sizes
    everyone = n_data * n_model
    d, m, z, x = device_parts()
    me = d * n_model + m
    depth = n_data // NX
    rows = D // n_data
    heads = HEADS // n_model
    head_cols = heads * HDIM
    length = r.noisy.shape[0]
    units = r.ff_shard.shape[2]
    half = units // 2

    def at_dp(spot):
        return (spot, m)

    def at_mlp(bit):
        flipped = m + 1 - 2 * lax.rem(m, 2) if bit == 1 else lax.rem(m + 2, 4)
        return (d, flipped)

    up = lax.rem(z + 1, depth) * NX + x
    down = lax.rem(z + depth - 1, depth) * NX + x
    side = z * NX + 1 - x

    barrier = pltpu.get_barrier_semaphore()

    def greet(step, carry):
        peer = lax.rem(me + step, everyone)
        pl.semaphore_signal(
            barrier,
            inc=1,
            device_id=(lax.div(peer, n_model), lax.rem(peer, n_model)),
            device_id_type=MESH_IDS,
        )
        return carry

    lax.fori_loop(1, everyone, greet, 0)

    load_out = pltpu.make_async_copy(
        r.matrices.at[:, pl.ds(12 * D, D)], r.out_low, r.local_sem.at[2]
    )
    load_out.start()
    load_time = pltpu.make_async_copy(
        r.matrices.at[:, pl.ds(0, D)], r.time_low, r.local_sem.at[3]
    )
    load_time.start()
    load_mod = pltpu.make_async_copy(
        r.matrices.at[:, pl.ds(D, 8 * D)], r.mod_low, r.local_sem.at[0]
    )
    load_mod.start()
    own_ff = pltpu.make_async_copy(
        r.ff_shard,
        r.ff.at[:, pl.ds(pl.multiple_of(d * rows, 16), rows)],
        r.local_sem.at[1],
    )
    own_ff.start()
    pl.semaphore_wait(barrier, everyone - 1)

    send_facts = Sender(r.facts_s, r.facts_r)

    def facts_copy(step):
        peer = lax.rem(me + step, everyone)
        return send_facts(
            step - 1,
            r.facts,
            r.facts_all.at[me],
            (lax.div(peer, n_model), lax.rem(peer, n_model)),
        )

    def loop(first, last, body):
        def step_body(step, carry):
            body(step)
            return carry

        lax.fori_loop(first, last, step_body, 0)

    loop(1, everyone, lambda step: facts_copy(step).start())
    r.facts_all[me] = r.facts[...]

    def qkv_rows(spot, part):
        if part == 0:
            return r.qkv_weight.at[pl.ds(pl.multiple_of(spot * rows, 16), 80)]
        return r.qkv_weight.at[pl.ds(pl.multiple_of(spot * rows + 80, 16), rows - 80)]

    def ff_block(spot, part, which):
        return r.ff.at[
            which,
            pl.ds(pl.multiple_of(spot * rows, 16), rows),
            pl.ds(half * part, half),
        ]

    def origin(step, part):
        return lax.rem(z + (depth - step if part == 0 else step), depth) * NX + x

    qz, qx = Sender(r.qz_s, r.qz_r), Sender(r.qx_s, r.qx_r)
    fz, fx = Sender(r.fz_s, r.fz_r), Sender(r.fx_s, r.fx_r)

    def qkv_along(step, part):
        block = qkv_rows(origin(step - 1, part), part)
        return qz((part, step - 1), block, block, at_dp(up if part == 0 else down))

    def qkv_aside(step, part):
        block = qkv_rows(origin(step, part), part)
        return qx((part, step), block, block, at_dp(side))

    def ff_along(step, part, which):
        block = ff_block(origin(step - 1, part), part, which)
        return fz((part, step - 1, which), block, block, at_dp(up if part == 0 else down))

    def ff_aside(step, part, which):
        block = ff_block(origin(step, part), part, which)
        return fx((part, step, which), block, block, at_dp(side))

    own_rows = pl.ds(pl.multiple_of(d * rows, 16), rows)
    r.qkv_weight[own_rows] = r.qkv_shard[...]
    for part in range(2):
        qkv_along(1, part).start()
        qkv_aside(0, part).start()

    send_small = Sender(r.small_s, r.small_r)

    def small_copy(step):
        return send_small(
            step - 1,
            r.small,
            r.small_all.at[own_rows],
            at_dp(lax.rem(d + step, n_data)),
        )

    loop(1, n_data, lambda step: small_copy(step).start())
    r.small_all[own_rows] = r.small[...]
    r.trig_all[0] = r.trig[...]

    def spread(send, buffer):
        return (
            send(0, buffer.at[0], buffer.at[1], at_mlp(1)),
            send(1, buffer.at[0], buffer.at[2], at_mlp(2)),
            send(2, buffer.at[2], buffer.at[3], at_mlp(1)),
        )

    trig_near, trig_far, trig_on = spread(Sender(r.trig_s, r.trig_r), r.trig_all)
    trig_near.start()
    trig_far.start()
    near_rank = m + 1 - 2 * lax.rem(m, 2)
    partners = ((d, near_rank), (d, lax.rem(m + 2, 4)), (d, lax.rem(near_rank + 2, 4)))
    send_noisy, send_kinds = Sender(r.noisy_s, r.noisy_r), Sender(r.kinds_s, r.kinds_r)
    noisy_copies = [
        send_noisy(spot, r.noisy, r.noisy_all.at[spot + 1], partner)
        for spot, partner in enumerate(partners)
    ]
    kinds_copies = [
        send_kinds(spot, r.modulation, r.kinds_all.at[spot + 1], partner)
        for spot, partner in enumerate(partners)
    ]
    for copy in noisy_copies:
        copy.start()
    r.noisy_all[0] = r.noisy[...]

    oz, ox = Sender(r.oz_s, r.oz_r), Sender(r.ox_s, r.ox_r)
    out_place = r.out_weight.at[pl.ds(pl.multiple_of(x * rows, 16), rows)]
    owner = z == m
    load_out.wait()

    def out_along(step):
        return oz(step - 1, out_place, out_place, at_dp(lax.rem(z + step, depth) * NX + x))

    out_aside = ox(0, out_place, out_place, at_dp(side))

    @pl.when(owner)
    def _():
        r.out_weight[pl.ds(pl.multiple_of(x * rows, 16), rows)] = r.out_low[...].astype(bfloat)
        for step in range(1, depth):
            out_along(step).start()
        out_aside.start()


    for part in range(2):
        for which in range(3):
            own = r.ff_shard.at[which, :, pl.ds(half * part, half)]
            fz(
                (part, 0, which),
                own,
                ff_block(d, part, which),
                at_dp(up if part == 0 else down),
            ).start()
            fx((part, 0, which), own, ff_block(d, part, which), at_dp(side)).start()

    loop(1, everyone, lambda step: facts_copy(step).wait())
    facts_all = r.facts_all[...]
    sinus = jnp.concatenate([facts_all[:, 0], facts_all[:, 1]], axis=1).astype(bfloat)
    labels = facts_all[:, 2, 0:1]
    time_pre = (
        jnp.dot(sinus, r.time_first[...], preferred_element_type=single) + r.first_bias[...]
    )
    r.time_pre[...] = time_pre
    time_act = (time_pre * jax.nn.sigmoid(time_pre)).astype(bfloat)
    send_time = Sender(r.time_s, r.time_r)

    def time_copy(step):
        peer = lax.rem(d + step, n_data)
        return send_time(
            step - 1, r.time_send.at[peer], r.time_recv.at[d], at_dp(peer)
        )

    load_time.wait()
    time_part = jnp.dot(time_act, r.time_low[...].astype(bfloat), preferred_element_type=single)
    for spot in range(n_data):
        r.time_send[spot] = time_part[:, spot * rows : (spot + 1) * rows]
    loop(1, n_data, lambda step: time_copy(step).start())
    r.time_recv[d] = r.time_send[d]

    def qkv_service(step):
        for part in range(2):
            qkv_along(step, part).wait_recv()
            if step < depth - 1:
                qkv_along(step + 1, part).start()
            qkv_aside(step, part).start()

    qkv_service(1)
    onehot = (
        labels == lax.broadcasted_iota(jnp.int32, (everyone, CLASSES + 1), 1).astype(single)
    ).astype(bfloat)
    picked = jnp.dot(onehot, r.class_table[...], preferred_element_type=single)
    load_mod.wait()

    loop(1, n_data, lambda step: time_copy(step).wait())
    condition = jnp.sum(r.time_recv[...], axis=0) + r.second_bias[...] + picked
    r.condition[...] = condition
    cond_act = (condition * jax.nn.sigmoid(condition)).astype(bfloat)
    pick = (
        lax.broadcasted_iota(jnp.int32, (n_data, everyone), 1)
        == lax.broadcasted_iota(jnp.int32, (n_data, everyone), 0) * n_model + m
    ).astype(bfloat)
    cond_rank = jnp.dot(pick, cond_act, preferred_element_type=single).astype(bfloat)
    for kind in range(8):
        block = jnp.dot(
            cond_rank,
            r.mod_low[:, kind * D : (kind + 1) * D].astype(bfloat),
            preferred_element_type=single,
        )
        for spot in range(n_data):
            r.mod_send[spot, kind : kind + 1] = block[spot : spot + 1]
    send_mods = Sender(r.mods_s, r.mods_r)

    def mods_copy(step):
        peer = lax.rem(d + step, n_data)
        return send_mods(step - 1, r.mod_send.at[peer], r.mod_recv.at[d], at_dp(peer))

    loop(1, n_data, lambda step: mods_copy(step).start())
    r.mod_recv[d] = r.mod_send[d]
    def ff_service(step, which):
        for part in range(2):
            ff_along(step, part, which).wait_recv()
            if step < depth - 1:
                ff_along(step + 1, part, which).start()
            ff_aside(step, part, which).start()

    qkv_service(2)
    ff_service(1, 0)
    loop(1, n_data, lambda step: small_copy(step).wait())
    trig_far.wait_recv()
    trig_on.start()
    hidden = (
        lax.dot_general(
            r.noisy[...],
            r.small_all[:, 0:CH],
            (((1,), (1,)), ((), ())),
            preferred_element_type=single,
        )
        + r.patch_bias[...]
    )
    r.hidden[...] = hidden
    loop(1, n_data, lambda step: mods_copy(step).wait())
    modulation = jnp.sum(r.mod_recv[...], axis=0) + r.mod_bias[...]
    r.modulation[...] = modulation

    def kind_of(kind):
        return r.modulation[kind : kind + 1]

    for copy in kinds_copies:
        copy.start()
    r.kinds_all[0] = modulation
    qkv_service(3)
    ff_service(1, 1)
    ff_service(1, 2)

    @pl.when(jnp.logical_not(owner))
    def _():
        oz(
            lax.rem(z + depth - m, depth) - 1, out_place, out_place, at_dp(up)
        ).wait_recv()
        out_aside.start()

    for part in range(2):
        for step in range(depth):
            qkv_aside(step, part).wait_recv()
    for copy in noisy_copies + kinds_copies:
        copy.wait_recv()
    trig_near.wait_recv()
    trig_on.wait_recv()

    def image_body(step, carry):
        image = n_model - 1 - step
        start_rows = (
            lax.dot_general(
                r.noisy_all[image],
                r.small_all[:, 0:CH],
                (((1,), (1,)), ((), ())),
                preferred_element_type=single,
            )
            + r.patch_bias[...]
        )
        r.one_rows[image] = modulate_rows(
            start_rows, r.kinds_all[image, 0:1], r.kinds_all[image, 1:2]
        ).astype(bfloat)
        r.qkv[...] = (
            jnp.dot(r.one_rows[image], r.qkv_weight[...], preferred_element_type=single)
            + r.qkv_bias[...]
        )
        rank = (
            2 * lax.rem(lax.div(m, 2) + lax.div(image, 2), 2)
            + lax.rem(lax.rem(m, 2) + lax.rem(image, 2), 2)
        )
        count = r.facts_all[d * n_model + rank, 2:3, 1:2]
        mask = lax.broadcasted_iota(jnp.int32, (1, length), 1).astype(single) < count
        cosine, sine = r.trig_all[image, 0], r.trig_all[image, 1]
        totals = []
        for head in range(heads):
            start = head * HDIM

            def part(which):
                return r.qkv[:, which * head_cols + start : which * head_cols + start + HDIM]

            raw_q, raw_k = part(0), part(1)
            query = (raw_q * cosine + swapped(raw_q) * sine).astype(bfloat)
            key = (raw_k * cosine + swapped(raw_k) * sine).astype(bfloat)
            value = part(2).astype(bfloat)
            for which, kept in enumerate((query, key, value)):
                low = which * head_cols + start
                r.low[image, :, low : low + HDIM] = kept
            scores = lax.dot_general(
                query, key, (((1,), (1,)), ((), ())), preferred_element_type=single
            ) * (1.0 / math.sqrt(HDIM))
            scores = jnp.where(mask, scores, -1e30)
            row_max = jnp.max(scores, axis=-1, keepdims=True)
            exponent = jnp.exp(scores - row_max)
            row_sum = jnp.sum(exponent, axis=-1, keepdims=True)
            probs = exponent / row_sum
            r.attended[image, :, start : start + HDIM] = jnp.dot(
                probs.astype(bfloat), value, preferred_element_type=single
            ).astype(bfloat)
            totals.append(row_max + jnp.log(row_sum))
        r.totals[image] = jnp.concatenate(totals, axis=1)
        return carry

    lax.fori_loop(0, 2, image_body, 0)

    @pl.when(owner)
    def _():
        for step in range(1, depth):
            out_along(step).wait_send()

    out_aside.wait()

    def partial(image):
        return jnp.dot(r.attended[image], r.out_weight[...], preferred_element_type=single)

    send_part = Sender(r.part_s, r.part_r)
    to_core = send_part(0, r.parts_send.at[0], r.parts_recv.at[0], at_mlp(1))
    to_far = send_part(1, r.parts_send.at[1], r.parts_recv.at[1], at_mlp(2))
    to_near = send_part(2, r.parts_send.at[2], r.parts_recv.at[2], at_mlp(1))
    r.parts_send[0] = partial(3).astype(bfloat)
    to_core.start()
    r.branch[...] = partial(2)
    to_core.wait_recv()
    r.parts_send[1] = (r.branch[...] + r.parts_recv[0].astype(single)).astype(bfloat)
    to_far.start()
    for which in range(3):
        ff_service(2, which)
    lax.fori_loop(2, n_model, image_body, 0)
    r.parts_send[2] = partial(1).astype(bfloat)
    to_near.start()
    own_part = partial(0) + r.out_bias[...]
    ff_service(3, 0)
    to_near.wait_recv()
    to_far.wait_recv()
    branch = own_part + r.parts_recv[2].astype(single) + r.parts_recv[1].astype(single)
    r.branch[...] = branch
    hidden_mid = r.hidden[...] + kind_of(2) * branch
    r.hidden_mid[...] = hidden_mid
    r.two_rows[0] = modulate_rows(hidden_mid, kind_of(3), kind_of(4)).astype(bfloat)
    two_near, two_far, two_on = spread(Sender(r.two_s, r.two_r), r.two_rows)
    two_far.start()
    two_near.start()
    ff_service(3, 1)
    ff_service(3, 2)
    two_far.wait_recv()
    two_on.start()

    own_ff.wait()
    for part in range(2):
        for step in range(depth):
            for which in range(3):
                ff_aside(step, part, which).wait()
            qkv_aside(step, part).wait_send()
            if step:
                for which in range(3):
                    ff_along(step, part, which).wait_send()
                qkv_along(step, part).wait_send()
    for copy in (two_near, two_on):
        copy.wait()
    two_far.wait_send()
    for copy in (trig_near, trig_far, trig_on, to_core, to_far, to_near):
        copy.wait_send()
    for copy in noisy_copies + kinds_copies:
        copy.wait_send()


def forward_all(values, sizes, collective):
    n_data, n_model = sizes
    bfloat, single = jnp.bfloat16, jnp.float32
    everyone = n_data * n_model
    rows = D // n_data
    heads = HEADS // n_model
    head_cols = heads * HDIM
    length = values.noisy.shape[0]
    units = values.ff_shard.shape[2]
    depth = n_data // NX
    shapes = dict(
        facts_all=((everyone, 8, 128), single),
        trig_all=((n_model, 2, length, HDIM), single),
        small_all=((D, 128), bfloat),
        time_pre=((everyone, rows), single),
        condition=((everyone, rows), single),
        modulation=((8, D), single),
        hidden=((length, D), single),
        one_rows=((n_model, length, D), bfloat),
        qkv_weight=((D, 3 * head_cols), bfloat),
        out_weight=((head_cols, D), bfloat),
        ff=((3, D, units), bfloat),
        low=((n_model, length, 3 * head_cols), bfloat),
        attended=((n_model, length, head_cols), bfloat),
        totals=((n_model, length, heads), single),
        branch=((length, D), single),
        hidden_mid=((length, D), single),
        two_rows=((n_model, length, D), bfloat),
    )
    dma = pltpu.SemaphoreType.DMA
    scratch = dict(
        time_send=pltpu.VMEM((n_data, everyone, rows), single),
        time_recv=pltpu.VMEM((n_data, everyone, rows), single),
        mod_send=pltpu.VMEM((n_data, 8, D), single),
        mod_recv=pltpu.VMEM((n_data, 8, D), single),
        mod_low=pltpu.VMEM((rows, 8 * D), single),
        time_low=pltpu.VMEM((rows, D), single),
        out_low=pltpu.VMEM((rows, D), single),
        qkv=pltpu.VMEM((length, 3 * head_cols), single),
        noisy_all=pltpu.VMEM((n_model, length, CH), bfloat),
        kinds_all=pltpu.VMEM((n_model, 8, D), single),
        parts_send=pltpu.VMEM((3, length, D), bfloat),
        parts_recv=pltpu.VMEM((3, length, D), bfloat),
        local_sem=dma((4,)),
    )
    counts = dict(
        facts=(everyone - 1,),
        small=(n_data - 1,),
        time=(n_data - 1,),
        mods=(n_data - 1,),
        trig=(3,),
        noisy=(3,),
        kinds=(3,),
        two=(3,),
        part=(3,),
        qz=(2, depth - 1),
        qx=(2, depth),
        oz=(depth - 1,),
        ox=(1,),
        fz=(2, depth - 1, 3),
        fx=(2, depth, 3),
    )
    for name, count in counts.items():
        scratch[name + "_s"] = dma(count)
        scratch[name + "_r"] = dma(count)
    far = {"matrices", "ff_shard", "ff"}

    def space(name):
        return pl.BlockSpec(memory_space=pl.ANY if name in far else pltpu.VMEM)

    outs = pl.pallas_call(
        functools.partial(forward_kernel, sizes),
        out_shape=[jax.ShapeDtypeStruct(*shapes[name]) for name in ForwardOut._fields],
        in_specs=[space(name) for name in ForwardIn._fields],
        out_specs=[space(name) for name in ForwardOut._fields],
        scratch_shapes=[scratch[name] for name in ForwardScratch._fields],
        compiler_params=pltpu.CompilerParams(
            collective_id=collective, has_side_effects=True, vmem_limit_bytes=56 * 2**20
        ),
    )(*values)
    return ForwardOut(*outs)


class BackIn(NamedTuple):
    ff: Any
    two_rows: Any
    hidden_mid: Any
    hidden: Any
    branch: Any
    modulation: Any
    small_all: Any
    final_bias: Any
    clean: Any
    noise: Any
    consts: Any
    valid: Any
    noisy: Any
    low: Any
    totals: Any
    trig_all: Any
    facts_all: Any
    attended: Any
    one_rows: Any
    qkv_weight: Any
    out_weight: Any
    matrices: Any
    time_pre: Any
    condition: Any


class BackOut(NamedTuple):
    bias_rows: Any
    own: Any
    stats: Any
    dmod: Any
    dtime: Any
    d_condition: Any
    d_time_pre: Any
    grad_ff: Any
    grad_qkv: Any
    grad_out: Any


class BackScratch(NamedTuple):
    time_low: Any
    late: Any
    d_modulation: Any
    local: Any
    sums: Any
    sums_recv: Any
    pay: Any
    dmod_row: Any
    dmod_all: Any
    dmod_wide: Any
    dtime_mine: Any
    dtime_recv: Any
    dtime_wide: Any
    loss: Any
    sm_s: Any
    sm_r: Any
    dl_s: Any
    dl_r: Any
    dt_s: Any
    dt_r: Any
    lt_s: Any
    lt_r: Any
    d_end: Any
    dm_rows: Any
    db_rows: Any
    hold_far: Any
    hold_near: Any
    parts_send: Any
    parts_recv: Any
    normed_end: Any
    g_ff: Any
    x_ff: Any
    z_ff: Any
    g_qkv: Any
    x_qkv: Any
    z_qkv: Any
    g_out: Any
    x_out: Any
    z_out: Any
    out_mine: Any
    dm_s: Any
    dm_r: Any
    db_s: Any
    db_r: Any
    pa_s: Any
    pa_r: Any
    pb_s: Any
    pb_r: Any
    pc_s: Any
    pc_r: Any
    fx_s: Any
    fx_r: Any
    fz_s: Any
    fz_r: Any
    qx_s: Any
    qx_r: Any
    qz_s: Any
    qz_r: Any
    ox_s: Any
    ox_r: Any
    oz_s: Any
    oz_r: Any
    qa_s: Any
    qa_r: Any
    oa_s: Any
    oa_r: Any
    local_sem: Any


ROW_CHUNK = 64


def modulate_back(values, grad, scale_by):
    row_mean = jnp.mean(values, axis=-1, keepdims=True)
    centered = values - row_mean
    variance = jnp.mean(centered * centered, axis=-1, keepdims=True)
    inverse = lax.rsqrt(variance + 1e-06)
    normal = centered * inverse
    inner = grad * (1.0 + scale_by)
    back = inverse * (
        inner
        - jnp.mean(inner, axis=-1, keepdims=True)
        - normal * jnp.mean(inner * normal, axis=-1, keepdims=True)
    )
    return back, normal


def fold(values):
    total = values[:8]
    for start in range(8, values.shape[0], 8):
        total = total + values[start : start + 8]
    return total


def back_kernel(sizes, total_images, *refs):
    r = named(BackIn, BackOut, BackScratch, refs)
    bfloat, single = jnp.bfloat16, jnp.float32
    n_data, n_model = sizes
    d, m, z, x = device_parts()
    depth = n_data // NX
    rows = D // n_data
    heads = HEADS // n_model
    head_cols = heads * HDIM
    length = r.clean.shape[0]
    units = r.ff.shape[2]
    half = units // 2

    def at_dp(spot):
        return (spot, m)

    near_rank = m + 1 - 2 * lax.rem(m, 2)
    far_rank = lax.rem(m + 2, 4)

    def at_mlp(bit):
        return (d, near_rank if bit == 1 else far_rank)

    up = lax.rem(z + 1, depth) * NX + x
    down = lax.rem(z + depth - 1, depth) * NX + x
    side = z * NX + 1 - x
    barrier = pltpu.get_barrier_semaphore()
    everyone = n_data * n_model
    me = d * n_model + m

    def loop(first, last, body):
        def step_body(step, carry):
            body(step)
            return carry

        lax.fori_loop(first, last, step_body, 0)

    def anyone(step):
        peer = lax.rem(me + step, everyone)
        return peer, (lax.div(peer, n_model), lax.rem(peer, n_model))

    loop(
        1,
        everyone,
        lambda step: pl.semaphore_signal(
            barrier, inc=1, device_id=anyone(step)[1], device_id_type=MESH_IDS
        ),
    )
    pl.semaphore_wait(barrier, everyone - 1)

    def chunks(body, carry, amount=ROW_CHUNK, count=length):
        def step_body(step, held):
            return body(pl.ds(pl.multiple_of(step * amount, amount), amount), held)

        return lax.fori_loop(0, count // amount, step_body, carry)

    def kind_of(kind):
        return r.modulation[kind : kind + 1]

    def dot(left, right, dims):
        return lax.dot_general(left, right, (dims, ((), ())), preferred_element_type=single)

    zeros = jnp.zeros((8, D), single)

    def spread(send, buffer):
        return (
            send(0, buffer.at[0], buffer.at[1], at_mlp(1)),
            send(1, buffer.at[0], buffer.at[2], at_mlp(2)),
            send(2, buffer.at[2], buffer.at[3], at_mlp(1)),
        )

    def part_copies(*sems):
        send = Sender(*sems)
        return tuple(
            send(spot, r.parts_send.at[spot], r.parts_recv.at[spot], at_mlp(bit))
            for spot, bit in ((0, 1), (1, 2), (2, 1))
        )

    def add_far(copies):
        to_core, to_far, to_near = copies
        to_core.wait_recv()

        def body(at, held):
            r.parts_send[1, at] = (
                r.hold_far[at] + r.parts_recv[0, at].astype(single)
            ).astype(bfloat)
            return held

        chunks(body, 0)
        to_far.start()

    fx, fz = Sender(r.fx_s, r.fx_r), Sender(r.fz_s, r.fz_r)
    qx, qz = Sender(r.qx_s, r.qx_r), Sender(r.qz_s, r.qz_r)

    def block_rows(z_spot, x_spot):
        return pl.ds(pl.multiple_of((z_spot * NX + x_spot) * rows, 16), rows)

    def ff_aside(which, step):
        z_spot = lax.rem(z + step, depth)
        return fx(
            (which, step),
            r.g_ff.at[which, block_rows(z_spot, 1 - x)],
            r.x_ff.at[which, z_spot],
            at_dp(side),
        )

    def target_of(step, part):
        return lax.rem(z + (depth - 1 - step if part == 0 else 1 + step), depth)

    def ff_along(which, step, part):
        lanes = pl.ds(half * part, half)
        return fz(
            (which, step, part),
            r.g_ff.at[which, block_rows(target_of(step, part), x), lanes],
            r.z_ff.at[which, step, part],
            at_dp(up if part == 0 else down),
        )

    def ff_start(which):
        for step in (3, 1, 2, 0):
            ff_aside(which, step).start()

    def ff_absorb(which, step):
        ff_aside(which, step).wait_recv()
        z_spot = lax.rem(z + step, depth)
        at = block_rows(z_spot, x)
        r.g_ff[which, at] = (
            r.g_ff[which, at].astype(single) + r.x_ff[which, z_spot].astype(single)
        ).astype(bfloat)

    def ff_beside(which):
        ff_absorb(which, 3)
        ff_absorb(which, 1)
        for part in range(2):
            ff_along(which, 0, part).start()

    def ff_service(which, step):
        if step != 1:
            ff_absorb(which, 2 - step)
        for part in range(2):
            ff_along(which, step, part).wait_recv()
            lanes = pl.ds(half * part, half)
            at = block_rows(target_of(step + 1, part), x)
            running = r.z_ff[which, step, part].astype(single) + r.g_ff[
                which, at, lanes
            ].astype(single)
            if step < depth - 2:
                r.g_ff[which, at, lanes] = running.astype(bfloat)
                ff_along(which, step + 1, part).start()
            else:
                r.grad_ff[which, :, lanes] = running

    tops = (pl.ds(0, 80), pl.ds(80, rows - 80))

    def part_rows(z_spot, part):
        start = (z_spot * NX + x) * rows + 80 * part
        return pl.ds(pl.multiple_of(start, 16), 80 if part == 0 else rows - 80)

    def qkv_aside(step):
        z_spot = lax.rem(z + step, depth)
        return qx(
            step,
            r.g_qkv.at[block_rows(z_spot, 1 - x)],
            r.x_qkv.at[z_spot],
            at_dp(side),
        )

    def qkv_along(step, part):
        return qz(
            (step, part),
            r.g_qkv.at[part_rows(target_of(step, part), part)],
            r.z_qkv.at[step, tops[part]],
            at_dp(up if part == 0 else down),
        )

    def qkv_absorb(step):
        qkv_aside(step).wait_recv()
        z_spot = lax.rem(z + step, depth)
        at = block_rows(z_spot, x)
        r.g_qkv[at] = (r.g_qkv[at].astype(single) + r.x_qkv[z_spot].astype(single)).astype(bfloat)

    def qkv_beside():
        qkv_absorb(3)
        qkv_absorb(1)
        for part in range(2):
            qkv_along(0, part).start()

    def qkv_service(step):
        if step != 1:
            qkv_absorb(2 - step)
        for part in range(2):
            qkv_along(step, part).wait_recv()
            at = part_rows(target_of(step + 1, part), part)
            running = (
                r.z_qkv[step, tops[part]].astype(single) + r.g_qkv[at].astype(single)
            ).astype(bfloat)
            if step < depth - 2:
                r.g_qkv[at] = running
                qkv_along(step + 1, part).start()
            else:
                r.grad_qkv[0, tops[part]] = running

    dm_near, dm_far, dm_on = spread(Sender(r.dm_s, r.dm_r), r.dm_rows)
    first_parts = part_copies(r.pa_s, r.pa_r)
    second_parts = part_copies(r.pb_s, r.pb_r)
    third_parts = part_copies(r.pc_s, r.pc_r)

    def swiglu(ff, two_rows, gates, ups, acts, d_gates, d_ups):
        load_ff = pltpu.make_async_copy(r.ff, ff, r.local_sem.at[0])
        load_two = pltpu.make_async_copy(r.two_rows, two_rows, r.local_sem.at[1])
        load_ff.start()
        load_two.start()
        load_two.wait()
        load_ff.wait()
        wide = 2 * length

        def rows_of(ref, which):
            return ref[2 * which : 2 * which + 2].reshape(wide, D)

        def inner(which):
            part = rows_of(two_rows, which)
            spot = pl.ds(which * wide, wide)
            gates[spot] = dot(part, ff[0], ((1,), (0,)))
            ups[spot] = dot(part, ff[1], ((1,), (0,)))

            def body(at, held):
                at = pl.ds(pl.multiple_of(at.start + which * wide, 32), 32)
                gate = gates[at]
                acts[at] = (gate * jax.nn.sigmoid(gate) * ups[at]).astype(bfloat)
                return held

            chunks(body, 0, 32, wide)

        def outer(image):
            return dot(acts[image * length : (image + 1) * length], ff[2], ((1,), (1,)))

        inner(1)
        r.parts_send[0] = outer(3).astype(bfloat)
        first_parts[0].start()
        r.hold_far[...] = outer(2)
        add_far(first_parts)
        inner(0)
        r.parts_send[2] = outer(1).astype(bfloat)
        first_parts[2].start()
        r.hold_near[...] = outer(0)
        first_parts[2].wait_recv()
        first_parts[1].wait_recv()

        def ending(at, held):
            mixed = (
                r.hold_near[at]
                + r.parts_recv[2, at].astype(single)
                + r.parts_recv[1, at].astype(single)
            )
            r.d_end[at] = mixed
            end = r.hidden_mid[at] + kind_of(5) * mixed
            r.normed_end[at] = modulate_rows(end, kind_of(6), kind_of(7)).astype(bfloat)
            return held

        chunks(ending, 0)

        eps_weight, var_weight = r.small_all[:, 32:48], r.small_all[:, 48:64]
        normed_end = r.normed_end[...]
        eps = dot(normed_end, eps_weight, ((1,), (0,))) + r.final_bias[0:1]
        var = dot(normed_end, var_weight, ((1,), (0,))) + r.final_bias[1:2]
        clean, noise, valid = r.clean[...], r.noise[...], r.valid[...]
        root_bar, root_rest, log_beta, post_log, coefficient = (
            r.consts[0:1, spot : spot + 1] for spot in range(5)
        )
        noisy = root_bar * clean + root_rest * noise
        fraction = (var + 1.0) * 0.5
        model_log = fraction * log_beta + (1.0 - fraction) * post_log
        start_est = (noisy - root_rest * eps) / root_bar
        gap = coefficient * (clean - start_est)
        ratio = jnp.exp(post_log - model_log)
        gap_part = gap * gap * jnp.exp(-model_log)
        scale_by = 0.5 / math.log(2.0)
        terms = (eps - noise) * (eps - noise) + scale_by * (
            -1.0 + model_log - post_log + ratio + gap_part
        )
        terms = jnp.where(valid > 0.0, terms, 0.0)
        r.loss[...] = jnp.sum(jnp.sum(terms, axis=1, keepdims=True), axis=0, keepdims=True)
        d_eps = 2.0 * (eps - noise) + 2.0 * scale_by * gap * jnp.exp(-model_log) * (
            coefficient * root_rest / root_bar
        )
        d_var = scale_by * (1.0 - ratio - gap_part) * (0.5 * (log_beta - post_log))
        share = 1.0 / total_images
        d_eps = jnp.where(valid > 0.0, d_eps * share, 0.0).astype(bfloat)
        d_var = jnp.where(valid > 0.0, d_var * share, 0.0).astype(bfloat)
        r.local[48:56] = zeros
        r.local[54:55, 0:CH] = jnp.sum(d_eps.astype(single), axis=0, keepdims=True)
        r.local[54:55, CH : 2 * CH] = jnp.sum(d_var.astype(single), axis=0, keepdims=True)
        r.local[CH : 2 * CH] = dot(d_eps, normed_end, ((0,), (0,)))
        r.local[2 * CH : 3 * CH] = dot(d_var, normed_end, ((0,), (0,)))
        r.hold_far[...] = dot(d_eps, eps_weight, ((1,), (1,))) + dot(
            d_var, var_weight, ((1,), (1,))
        )

        def end_back(at, held):
            shift_sum, scale_sum, gate_sum = held
            mixed, grad = r.d_end[at], r.hold_far[at]
            end = r.hidden_mid[at] + kind_of(5) * mixed
            back, normal = modulate_back(end, grad, kind_of(7))
            r.d_end[at] = back
            r.dm_rows[0, at] = (kind_of(5) * back).astype(bfloat)
            return (
                shift_sum + fold(grad),
                scale_sum + fold(grad * normal),
                gate_sum + fold(mixed * back),
            )

        shift_sum, scale_sum, gate_sum = chunks(end_back, (zeros, zeros, zeros))
        dm_far.start()
        dm_near.start()
        for kind, value in ((6, shift_sum), (7, scale_sum), (5, gate_sum)):
            r.d_modulation[kind : kind + 1] = jnp.sum(value, axis=0, keepdims=True)

        def inner_back(which):
            spot = pl.ds(which * wide, wide)
            gradient = dot(rows_of(r.dm_rows, which), ff[2], ((1,), (0,)))
            gate, up_val = gates[spot], ups[spot]
            sigma = jax.nn.sigmoid(gate)
            d_ups[spot] = (gradient * gate * sigma).astype(bfloat)
            d_gates[spot] = (gradient * up_val * (sigma * (1.0 + gate * (1.0 - sigma)))).astype(
                bfloat
            )

        def outer_back(image):
            spot = pl.ds(image * length, length)
            return dot(d_gates[spot], ff[0], ((1,), (1,))) + dot(d_ups[spot], ff[1], ((1,), (1,)))

        def ff_grad(which, left, right):
            for part in range(2):
                lanes = slice(half * part, half * part + half)
                r.g_ff[which, :, lanes] = dot(left, right[:, lanes], ((0,), (0,))).astype(bfloat)

        dm_near.wait_recv()
        inner_back(0)
        dm_far.wait_recv()
        dm_on.start()
        dm_on.wait_recv()
        inner_back(1)
        for copy in first_parts:
            copy.wait_send()
        r.parts_send[0] = outer_back(3).astype(bfloat)
        second_parts[0].start()
        r.hold_far[...] = outer_back(2)
        add_far(second_parts)
        ff_grad(2, r.dm_rows[...].reshape(2 * wide, D), acts)
        ff_start(2)
        r.parts_send[2] = outer_back(1).astype(bfloat)
        second_parts[2].start()
        r.hold_near[...] = outer_back(0)
        flat = two_rows[...].reshape(2 * wide, D)
        ff_grad(0, flat, d_gates)
        ff_start(0)
        ff_grad(1, flat, d_ups)
        ff_start(1)

    pl.run_scoped(
        swiglu,
        pltpu.VMEM((3, D, units), bfloat),
        pltpu.VMEM((n_model, length, D), bfloat),
        pltpu.VMEM((n_model * length, units), single),
        pltpu.VMEM((n_model * length, units), single),
        pltpu.VMEM((n_model * length, units), bfloat),
        pltpu.VMEM((n_model * length, units), bfloat),
        pltpu.VMEM((n_model * length, units), bfloat),
    )

    db_near, db_far, db_on = spread(Sender(r.db_s, r.db_r), r.db_rows)
    ox, oz = Sender(r.ox_s, r.ox_r), Sender(r.oz_s, r.oz_r)
    out_aside = ox(0, r.g_out.at[1 - x], r.x_out, at_dp(side))
    owner = z == m
    behind = lax.rem(z + depth - m, depth)
    out_along = oz(
        lax.rem(behind + depth - 1, depth),
        r.g_out.at[x],
        r.z_out.at[lax.rem(behind + depth - 1, depth)],
        at_dp(m * NX + x),
    )

    def attend(low, attended, trig, one_rows, qkv_weight, out_weight, d_attended, d_qkv):
        loads = []
        for spot, (source, target) in enumerate(
            (
                (r.out_weight, out_weight),
                (r.low, low),
                (r.trig_all, trig),
                (r.attended, attended),
                (r.one_rows, one_rows),
                (r.qkv_weight, qkv_weight),
            )
        ):
            load = pltpu.make_async_copy(source, target, r.local_sem.at[2 + spot])
            load.start()
            loads.append(load)
        second_parts[2].wait_recv()
        second_parts[1].wait_recv()

        def mid_back(at, held):
            shift_sum, scale_sum, gate_sum, branch_sum = held
            grad = (
                r.hold_near[at]
                + r.parts_recv[2, at].astype(single)
                + r.parts_recv[1, at].astype(single)
            )
            back, normal = modulate_back(r.hidden_mid[at], grad, kind_of(4))
            total = r.d_end[at] + back
            r.d_end[at] = total
            d_branch = (kind_of(2) * total).astype(bfloat)
            r.db_rows[0, at] = d_branch
            return (
                shift_sum + fold(grad),
                scale_sum + fold(grad * normal),
                gate_sum + fold(r.branch[at] * total),
                branch_sum + fold(d_branch.astype(single)),
            )

        sums = chunks(mid_back, (zeros, zeros, zeros, zeros))
        db_far.start()
        db_near.start()
        for kind, value in zip((3, 4, 2), sums):
            r.d_modulation[kind : kind + 1] = jnp.sum(value, axis=0, keepdims=True)
        r.local[49:50] = jnp.sum(sums[3], axis=0, keepdims=True)
        for load in loads:
            load.wait()

        def image_body(image, carry):
            d_attended[...] = dot(
                r.db_rows[image], out_weight[...], ((1,), (1,))
            ).astype(bfloat)
            rank = (
                2 * lax.rem(lax.div(m, 2) + lax.div(image, 2), 2)
                + lax.rem(lax.rem(m, 2) + lax.rem(image, 2), 2)
            )
            count = r.facts_all[d * n_model + rank, 2:3, 1:2]
            mask = lax.broadcasted_iota(jnp.int32, (1, length), 1).astype(single) < count
            cosine, sine = trig[image, 0], trig[image, 1]
            scale_by = 1.0 / math.sqrt(HDIM)
            for head in range(heads):
                start = head * HDIM

                def spot(which):
                    begin = which * head_cols + start
                    return slice(begin, begin + HDIM)

                query, key, value = (low[image, :, spot(which)] for which in range(3))
                grad = d_attended[:, start : start + HDIM]
                scores = dot(query, key, ((1,), (1,))) * scale_by
                scores = jnp.where(mask, scores, -1e30)
                probs = jnp.exp(scores - r.totals[image, :, head : head + 1])
                d_probs = dot(grad, value, ((1,), (1,)))
                row = jnp.sum(probs * d_probs, axis=-1, keepdims=True)
                d_scores = (probs * (d_probs - row)).astype(bfloat)
                d_query = dot(d_scores, key, ((1,), (0,))) * scale_by
                d_key = dot(d_scores, query, ((0,), (0,))) * scale_by
                d_value = dot(probs.astype(bfloat), grad, ((0,), (0,)))
                for which, turned in ((0, d_query), (1, d_key)):
                    back = turned * cosine + swapped(turned * sine)
                    d_qkv[image, :, spot(which)] = back.astype(bfloat)
                d_qkv[image, :, spot(2)] = d_value.astype(bfloat)
            return carry

        db_near.wait_recv()
        lax.fori_loop(0, 2, image_body, 0)
        db_far.wait_recv()
        db_on.start()
        ff_beside(2)
        db_on.wait_recv()
        lax.fori_loop(2, n_model, image_body, 0)

        def one_part(image):
            return dot(d_qkv[image], qkv_weight[...], ((1,), (1,)))

        for copy in second_parts:
            copy.wait_send()
        r.parts_send[0] = one_part(3).astype(bfloat)
        third_parts[0].start()
        r.hold_far[...] = one_part(2)
        add_far(third_parts)
        ff_beside(0)
        ff_service(2, 0)
        r.parts_send[2] = one_part(1).astype(bfloat)
        third_parts[2].start()
        r.hold_near[...] = one_part(0)
        flat_grad = d_qkv[...].reshape(n_model * length, 3 * head_cols)
        r.g_qkv[...] = dot(
            one_rows[...].reshape(n_model * length, D), flat_grad, ((0,), (0,))
        ).astype(bfloat)
        for step in (3, 1, 2, 0):
            qkv_aside(step).start()
        r.g_out[...] = (
            dot(
                attended[...].reshape(n_model * length, head_cols),
                r.db_rows[...].reshape(n_model * length, D),
                ((0,), (0,)),
            )
            .astype(bfloat)
            .reshape(NX, rows, D)
        )
        out_aside.start()
        ones = jnp.ones((8, n_model * length), bfloat)
        qkv_sum = dot(ones, flat_grad, ((1,), (0,)))[0:1]
        for rank in range(n_model):
            r.local[50 + rank : 51 + rank, 0 : 3 * head_cols] = jnp.where(m == rank, qkv_sum, 0.0)

    pl.run_scoped(
        attend,
        pltpu.VMEM((n_model, length, 3 * head_cols), bfloat),
        pltpu.VMEM((n_model, length, head_cols), bfloat),
        pltpu.VMEM((n_model, 2, length, HDIM), single),
        pltpu.VMEM((n_model, length, D), bfloat),
        pltpu.VMEM((D, 3 * head_cols), bfloat),
        pltpu.VMEM((head_cols, D), bfloat),
        pltpu.VMEM((length, head_cols), bfloat),
        pltpu.VMEM((n_model, length, 3 * head_cols), bfloat),
    )
    ff_beside(1)
    ff_service(0, 0)
    ff_service(2, 1)
    third_parts[2].wait_recv()
    third_parts[1].wait_recv()

    def first_back(at, held):
        shift_sum, scale_sum, hidden_sum = held
        grad = (
            r.hold_near[at]
            + r.parts_recv[2, at].astype(single)
            + r.parts_recv[1, at].astype(single)
        )
        back, normal = modulate_back(r.hidden[at], grad, kind_of(1))
        d_hidden = (r.d_end[at] + back).astype(bfloat)
        r.normed_end[at] = d_hidden
        return (
            shift_sum + fold(grad),
            scale_sum + fold(grad * normal),
            hidden_sum + fold(d_hidden.astype(single)),
        )

    sums = chunks(first_back, (zeros, zeros, zeros))
    for kind in range(2):
        r.d_modulation[kind : kind + 1] = jnp.sum(sums[kind], axis=0, keepdims=True)
    r.local[48:49] = jnp.sum(sums[2], axis=0, keepdims=True)
    r.local[0:CH] = dot(r.noisy[...], r.normed_end[...], ((0,), (0,)))

    for kind in range(8):
        r.dmod_wide[2 * kind : 2 * kind + 1] = r.d_modulation[kind : kind + 1, 0 : D // 2]
        r.dmod_wide[2 * kind + 1 : 2 * kind + 2] = r.d_modulation[kind : kind + 1, D // 2 : D]
    r.dmod_row[...] = r.dmod_wide[...].astype(bfloat)
    r.dmod_all[me] = r.dmod_row[...]
    send_dmod = Sender(r.dl_s, r.dl_r)
    loop(
        1,
        everyone,
        lambda step: send_dmod(
            step - 1, r.dmod_row, r.dmod_all.at[me], anyone(step)[1]
        ).start(),
    )
    tiles = D // 128
    for top in range(7):
        for left in range(tiles):
            r.sums[top * tiles + left] = r.local[8 * top : 8 * top + 8, 128 * left : 128 * left + 128]
    r.sums[7 * tiles] = jnp.zeros((8, 128), single)
    send_sums = Sender(r.sm_s, r.sm_r)

    def sums_copy(step):
        peer, device = anyone(step)
        return send_sums(step - 1, r.sums.at[pl.ds(2 * peer, 2)], r.sums_recv.at[me], device)

    loop(1, everyone, lambda step: sums_copy(step).start())
    r.sums_recv[me] = r.sums[pl.ds(2 * me, 2)]
    ff_service(1, 0)
    ff_service(0, 1)
    ff_service(2, 2)
    qkv_beside()
    out_aside.wait()
    r.g_out[x] = (r.g_out[x].astype(single) + r.x_out[...].astype(single)).astype(bfloat)

    @pl.when(jnp.logical_not(owner))
    def _():
        out_along.start()


    time_pre, condition = r.time_pre[...], r.condition[...]
    sigma_time, sigma_cond = jax.nn.sigmoid(time_pre), jax.nn.sigmoid(condition)
    time_act = (time_pre * sigma_time).astype(bfloat)
    cond_act = (condition * sigma_cond).astype(bfloat)

    def gram(value, precision=None):
        return lax.dot_general(
            value,
            value,
            (((1,), (1,)), ((), ())),
            precision=precision,
            preferred_element_type=single,
        )

    send_dtime = Sender(r.dt_s, r.dt_r)

    def dtime_copy(step):
        return send_dtime(
            step - 1, r.dtime_mine, r.dtime_recv.at[d], at_dp(lax.rem(d + step, n_data))
        )

    def conditioning(mod_weight):
        load = pltpu.make_async_copy(
            r.matrices.at[:, pl.ds(D, 8 * D)], mod_weight, r.local_sem.at[0]
        )
        load.start()
        load_time = pltpu.make_async_copy(
            r.matrices.at[:, pl.ds(0, D)], r.time_low, r.local_sem.at[1]
        )
        load_time.start()
        loop(
            1,
            everyone,
            lambda step: send_dmod(
                step - 1, r.dmod_row, r.dmod_all.at[me], anyone(step)[1]
            ).wait(),
        )
        gathered = r.dmod_all[...].astype(single)
        load.wait()
        load_time.wait()
        d_cond = jnp.zeros((everyone, rows), single)
        mod_gram = jnp.zeros((everyone, everyone), single)
        bias_squares = jnp.zeros((1, 1), single)
        for kind in range(8):
            r.dtime_wide[:, 0 : D // 2] = gathered[:, 2 * kind]
            r.dtime_wide[:, D // 2 : D] = gathered[:, 2 * kind + 1]
            part = r.dtime_wide[...]
            column = jnp.sum(part, axis=0, keepdims=True)
            bias_squares = bias_squares + jnp.sum(column * column, axis=1, keepdims=True)
            r.bias_rows[3 + kind : 4 + kind] = column
            part = part.astype(bfloat)
            r.dmod[kind] = part
            d_cond = d_cond + dot(
                part, mod_weight[:, kind * D : (kind + 1) * D].astype(bfloat), ((1,), (1,))
            )
            mod_gram = mod_gram + gram(part)
        d_condition = d_cond * (sigma_cond * (1.0 + condition * (1.0 - sigma_cond)))
        r.d_condition[...] = d_condition
        r.dtime_mine[...] = d_condition.astype(bfloat)
        loop(1, n_data, lambda step: dtime_copy(step).start())
        r.dtime_recv[d] = r.dtime_mine[...]
        r.pay[2] = jnp.zeros((8, 128), single)
        r.pay[2, 0:1, 0:1] = (
            jnp.sum(jnp.sum(mod_gram * gram(cond_act), axis=1, keepdims=True), axis=0, keepdims=True)
            / n_model
            + bias_squares / everyone
        )

    pl.run_scoped(conditioning, pltpu.VMEM((rows, 8 * D), single))
    qkv_service(0)
    ff_service(1, 1)
    ff_service(0, 2)
    qkv_service(1)
    loop(1, n_data, lambda step: dtime_copy(step).wait())
    for spot in range(n_data):
        r.dtime_wide[:, spot * rows : (spot + 1) * rows] = r.dtime_recv[spot].astype(single)
    dtime = r.dtime_wide[...]
    column = jnp.sum(dtime, axis=0, keepdims=True)
    r.bias_rows[2:3] = column
    dtime = dtime.astype(bfloat)
    r.dtime[...] = dtime
    d_time_pre = dot(dtime, r.time_low[...].astype(bfloat), ((1,), (1,))) * (
        sigma_time * (1.0 + time_pre * (1.0 - sigma_time))
    )
    r.d_time_pre[...] = d_time_pre
    first_sum = jnp.sum(d_time_pre, axis=0, keepdims=True)
    facts = r.facts_all[...]
    sinus = jnp.concatenate([facts[:, 0], facts[:, 1]], axis=1).astype(bfloat)
    onehot = (
        facts[:, 2, 0:1]
        == lax.broadcasted_iota(jnp.int32, (everyone, CLASSES + 1), 1).astype(single)
    ).astype(bfloat)
    highest = lax.Precision.HIGHEST

    def total_of(value):
        return jnp.sum(jnp.sum(value, axis=1, keepdims=True), axis=0, keepdims=True)

    shared_squares = (
        total_of(gram(time_act) * gram(dtime))
        + total_of(gram(sinus) * gram(d_time_pre, highest))
        + total_of(gram(onehot) * gram(r.d_condition[...], highest))
        + total_of(first_sum * first_sum)
    ) / n_model + total_of(column * column) / everyone
    r.pay[3] = jnp.zeros((8, 128), single)
    r.pay[3, 0:1] = first_sum[:, 0:128]
    r.pay[3, 1:2, 0 : rows - 128] = first_sum[:, 128:rows]
    ff_service(1, 2)
    qkv_service(2)
    qkv_near, qkv_far, qkv_on = spread(Sender(r.qa_s, r.qa_r), r.grad_qkv)
    qkv_far.start()
    qkv_near.start()
    give = Sender(r.oa_s, r.oa_r)
    partners = [(d, near_rank), (d, far_rank), (d, lax.rem(near_rank + 2, 4))]
    gives = [
        give(spot, r.out_mine, r.out_mine, partner) for spot, partner in enumerate(partners)
    ]

    @pl.when(owner)
    def _():
        total = r.g_out[x].astype(single)
        for step in range(depth - 1):
            oz(step, r.g_out.at[x], r.z_out.at[step], at_dp(up)).wait_recv()
            total = total + r.z_out[step].astype(single)
        total = total.astype(bfloat)
        r.out_mine[...] = total
        total = total.astype(single)
        r.pay[2, 0:1, 2:3] = total_of(total * total)
        for copy in gives:
            copy.start()

    loop(1, everyone, lambda step: sums_copy(step).wait())

    def add_sums(step, held):
        return held + r.sums_recv[step]

    chunk = lax.fori_loop(0, everyone, add_sums, jnp.zeros((2, 8, 128), single))
    r.pay[0:2] = chunk
    own_squares = total_of(chunk[0] * chunk[0]) + total_of(chunk[1] * chunk[1])

    def ff_squares(at, held):
        return tuple(
            one + fold(r.grad_ff[which, at] * r.grad_ff[which, at])
            for which, one in enumerate(held)
        )

    block = jnp.zeros((8, units), single)
    for value in chunks(ff_squares, (block, block, block), 16, rows):
        own_squares = own_squares + total_of(value)
    qkv_float = r.grad_qkv[0].astype(single)
    r.pay[2, 0:1, 0:1] = (
        r.pay[2, 0:1, 0:1]
        + shared_squares
        + own_squares
        + r.pay[2, 0:1, 2:3]
        + total_of(qkv_float * qkv_float)
    )
    r.pay[2, 0:1, 1:2] = r.loss[...]
    send_late = Sender(r.lt_s, r.lt_r)

    def late_copy(step):
        return send_late(step - 1, r.pay, r.late.at[me], anyone(step)[1])

    loop(1, everyone, lambda step: late_copy(step).start())
    r.late[me] = r.pay[...]

    for spot, partner in enumerate(partners):

        @pl.when(z == partner[1])
        def _():
            gives[spot].wait_recv()

    qkv_far.wait_recv()
    qkv_on.start()
    r.grad_out[...] = r.out_mine[...]

    @pl.when(owner)
    def _():
        for copy in gives:
            copy.wait_send()

    @pl.when(jnp.logical_not(owner))
    def _():
        out_along.wait_send()

    qkv_near.wait()
    qkv_on.wait()
    qkv_far.wait_send()
    loop(1, everyone, lambda step: late_copy(step).wait())
    for top in range(7):
        for left in range(tiles):
            spot = top * tiles + left
            r.local[8 * top : 8 * top + 8, 128 * left : 128 * left + 128] = r.late[
                spot // 2, spot % 2
            ]
    r.bias_rows[0:1] = r.local[48:49]
    r.bias_rows[14:15] = r.local[49:50]
    r.bias_rows[15:16] = r.local[54:55]
    for spot in range(n_data):
        first = r.late[spot * n_model, 3]
        r.bias_rows[1:2, spot * rows : spot * rows + 128] = first[0:1]
        r.bias_rows[1:2, spot * rows + 128 : (spot + 1) * rows] = first[1:2, 0 : rows - 128]
    for rank in range(n_model):
        for part in range(3):
            r.bias_rows[11 + part : 12 + part, rank * head_cols : (rank + 1) * head_cols] = r.local[
                50 + rank : 51 + rank, part * head_cols : (part + 1) * head_cols
            ]
    for spot in range(n_data):

        @pl.when(d == spot)
        def _():
            r.own[...] = r.local[0 : 3 * CH, spot * rows : (spot + 1) * rows]

    totals = lax.fori_loop(
        0, everyone, lambda step, held: held + r.late[step, 2, 0:1], jnp.zeros((1, 128), single)
    )
    norm = jnp.sqrt(totals[:, 0:1])
    r.stats[...] = jnp.zeros((1, 128), single)
    r.stats[0:1, 0:1] = norm
    r.stats[0:1, 1:2] = jnp.minimum(1.0, CLIP_LIMIT / norm)
    r.stats[0:1, 2:3] = totals[:, 1:2]
    for copy in (dm_near, dm_far, dm_on, db_near, db_far, db_on, *third_parts):
        copy.wait_send()
    for step in range(depth):
        qkv_aside(step).wait_send()
        for which in range(3):
            ff_aside(which, step).wait_send()
    for step in range(depth - 1):
        for part in range(2):
            qkv_along(step, part).wait_send()
            for which in range(3):
                ff_along(which, step, part).wait_send()


def backward_all(values, sizes, total_images, collective):
    n_data, n_model = sizes
    bfloat, single = jnp.bfloat16, jnp.float32
    everyone = n_data * n_model
    rows = D // n_data
    heads = HEADS // n_model
    head_cols = heads * HDIM
    length = values.clean.shape[0]
    units = values.ff.shape[2]
    half = units // 2
    depth = n_data // NX
    shapes = dict(
        grad_ff=((3, rows, units), single),
        grad_qkv=((n_model, rows, 3 * head_cols), bfloat),
        grad_out=((rows, D), bfloat),
        bias_rows=((16, D), single),
        own=((3 * CH, rows), single),
        stats=((1, 128), single),
        dmod=((8, everyone, D), bfloat),
        dtime=((everyone, D), bfloat),
        d_condition=((everyone, rows), single),
        d_time_pre=((everyone, rows), single),
    )
    vmem, dma = pltpu.VMEM, pltpu.SemaphoreType.DMA
    scratch = dict(
        d_end=vmem((length, D), single),
        dm_rows=vmem((n_model, length, D), bfloat),
        db_rows=vmem((n_model, length, D), bfloat),
        hold_far=vmem((length, D), single),
        hold_near=vmem((length, D), single),
        parts_send=vmem((3, length, D), bfloat),
        parts_recv=vmem((3, length, D), bfloat),
        normed_end=vmem((length, D), bfloat),
        g_ff=vmem((3, D, units), bfloat),
        x_ff=vmem((3, depth, rows, units), bfloat),
        z_ff=vmem((3, depth - 1, 2, rows, half), bfloat),
        g_qkv=vmem((D, 3 * head_cols), bfloat),
        x_qkv=vmem((depth, rows, 3 * head_cols), bfloat),
        z_qkv=vmem((depth - 1, rows, 3 * head_cols), bfloat),
        g_out=vmem((NX, rows, D), bfloat),
        x_out=vmem((rows, D), bfloat),
        z_out=vmem((depth - 1, rows, D), bfloat),
        out_mine=vmem((rows, D), bfloat),
        late=vmem((everyone, 4, 8, 128), single),
        d_modulation=vmem((8, D), single),
        local=vmem((56, D), single),
        sums=vmem((2 * everyone, 8, 128), single),
        sums_recv=vmem((everyone, 2, 8, 128), single),
        pay=vmem((4, 8, 128), single),
        dmod_row=vmem((16, D // 2), bfloat),
        dmod_all=vmem((everyone, 16, D // 2), bfloat),
        dmod_wide=vmem((16, D // 2), single),
        dtime_mine=vmem((everyone, rows), bfloat),
        dtime_recv=vmem((n_data, everyone, rows), bfloat),
        dtime_wide=vmem((everyone, D), single),
        loss=vmem((1, 1), single),
        time_low=vmem((rows, D), single),
        local_sem=dma((8,)),
    )
    counts = dict(
        dm=(3,),
        db=(3,),
        pa=(3,),
        pb=(3,),
        pc=(3,),
        fx=(3, depth),
        fz=(3, depth - 1, 2),
        qx=(depth,),
        qz=(depth - 1, 2),
        ox=(1,),
        oz=(depth - 1,),
        qa=(3,),
        oa=(3,),
        sm=(everyone - 1,),
        dl=(everyone - 1,),
        dt=(n_data - 1,),
        lt=(everyone - 1,),
    )
    for name, count in counts.items():
        scratch[name + "_s"] = dma(count)
        scratch[name + "_r"] = dma(count)
    far = {
        "ff", "two_rows", "low", "trig_all", "attended", "one_rows", "qkv_weight", "out_weight",
        "matrices",
    }

    def space(name):
        return pl.BlockSpec(memory_space=pl.ANY if name in far else pltpu.VMEM)

    outs = pl.pallas_call(
        functools.partial(back_kernel, sizes, total_images),
        out_shape=[jax.ShapeDtypeStruct(*shapes[name]) for name in BackOut._fields],
        in_specs=[space(name) for name in BackIn._fields],
        out_specs=[space(name) for name in BackOut._fields],
        scratch_shapes=[scratch[name] for name in BackScratch._fields],
        compiler_params=pltpu.CompilerParams(
            collective_id=collective, has_side_effects=True, vmem_limit_bytes=62 * 2**20
        ),
    )(*values)
    return BackOut(*outs)


def forward_plain(clean_three, noise_three, patch_grid, labels, timesteps, matrices, embeddings, swiglu_weights, biases):
    bfloat = jnp.bfloat16
    single = jnp.float32
    images = labels.shape[0]
    length = clean_three.shape[1]
    n_model = lax.axis_size("mlp")
    n_data = lax.axis_size("dp")
    sizes = (n_data, n_model)
    total_images = images * n_data * n_model
    rows = D // n_data
    owned_start = lax.axis_index("dp") * rows
    data_index = lax.axis_index("dp")
    model_index = lax.axis_index("mlp")
    heads = HEADS // n_model
    head_cols = heads * HDIM
    qkv_shard = jnp.concatenate(
        [
            cut_columns(matrices, 9 * D + part * D + model_index * head_cols, head_cols)
            for part in range(3)
        ],
        axis=1,
    ).astype(bfloat)
    out_shard = matrices[:, 12 * D : 13 * D].astype(bfloat)
    swiglu_shard = swiglu_weights.astype(bfloat)
    qkv_weight = lax.all_gather(qkv_shard, "dp", axis=0, tiled=True)
    swiglu_use = lax.all_gather(swiglu_shard, "dp", axis=1, tiled=True)
    out_weight = gather_out(out_shard)

    time_second = matrices[:, :D].astype(bfloat)
    mod_weight = matrices[:, D : 9 * D].astype(bfloat)
    time_first = embeddings[CH : CH + FREQ].astype(bfloat)
    class_table = embeddings[CH + FREQ :].astype(bfloat)
    patch_bias = biases[:D]
    first_bias = biases[D : 2 * D]
    second_bias = biases[2 * D : 3 * D]
    mod_bias = biases[3 * D : 11 * D]
    qkv_bias = biases[11 * D : 14 * D]
    out_bias = biases[14 * D : 15 * D]
    final_bias = biases[15 * D :]

    facts = jnp.concatenate([timesteps[:, None], labels[:, None], patch_grid], axis=1)
    facts = jnp.pad(facts, ((0, 8 - images), (0, 124)))
    (facts_all,) = exchange([(facts, "all")], "both", sizes, 0)
    facts_all = facts_all[:, 0, :4]
    steps_all, labels_all, grid_all = facts_all[:, 0], facts_all[:, 1], facts_all[:, 2:4]
    sinus_all = sinusoid(steps_all).astype(bfloat)
    first_bias_own = lax.dynamic_slice_in_dim(first_bias, owned_start, rows)
    second_bias_own = lax.dynamic_slice_in_dim(second_bias, owned_start, rows)
    time_pre = jnp.dot(sinus_all, time_first, preferred_element_type=single) + first_bias_own
    time_act = jax.nn.silu(time_pre).astype(bfloat)
    time_part = jnp.dot(time_act, time_second, preferred_element_type=single)
    small_shard = jnp.concatenate(
        [embeddings[:CH], matrices[:, 13 * D :].T], axis=0
    ).astype(bfloat)
    time_parts, small_all = exchange(
        [
            (time_part.reshape(total_images, n_data, rows).transpose(1, 0, 2), "each"),
            (small_shard, "all"),
        ],
        "dp",
        sizes,
        1,
    )
    small_all = small_all.transpose(1, 0, 2).reshape(3 * CH, D)
    patch_weight = small_all[:CH]
    final_weight = small_all[CH:].T
    time_emb = jnp.sum(time_parts, axis=0) + second_bias_own
    onehot = (labels_all[:, None] == jnp.arange(CLASSES + 1, dtype=jnp.int32)[None, :]).astype(
        bfloat
    )
    condition = time_emb + jnp.dot(onehot, class_table, preferred_element_type=single)
    cond_act = jax.nn.silu(condition).astype(bfloat)
    cond_rank = lax.dynamic_index_in_dim(
        cond_act.reshape(n_data, n_model, rows), model_index, 1, keepdims=False
    )
    mod_part = jnp.dot(cond_rank, mod_weight, preferred_element_type=single)
    (mod_parts,) = exchange(
        [(mod_part.reshape(n_data, 8, D), "each")],
        "dp",
        sizes,
        2,
    )
    modulation = jnp.sum(mod_parts, axis=0).reshape(1, 8 * D) + mod_bias
    shift_one, scale_one, gate_one, shift_two, scale_two, gate_two, shift_end, scale_end = (
        jnp.split(modulation, 8, axis=1)
    )

    group_grid = lax.dynamic_slice_in_dim(grid_all, data_index * n_model, n_model, 0)
    group_grid = jnp.stack(
        [
            lax.dynamic_index_in_dim(group_grid, model_index ^ rank, 0, keepdims=False)
            for rank in range(n_model)
        ]
    )
    cosine, sine, mask = turn_tables(group_grid, length)
    noisy_low = noisy_input(clean_three, noise_three, timesteps).astype(bfloat)
    hidden = jnp.dot(noisy_low, patch_weight, preferred_element_type=single) + patch_bias
    normed_one = modulate(hidden, shift_one, scale_one).astype(bfloat)
    one_rows = jnp.concatenate(gather_rows(normed_one.reshape(length, D), n_model), axis=0)
    qkv_bias_own = jnp.concatenate(
        [
            lax.dynamic_slice_in_dim(qkv_bias, part * D + model_index * head_cols, head_cols)
            for part in range(3)
        ]
    )
    qkv = jnp.dot(one_rows, qkv_weight, preferred_element_type=single) + qkv_bias_own
    low, attended, log_total = attention(
        qkv.reshape(n_model, length, 3 * head_cols), cosine, sine, mask, heads
    )
    attended_rows = attended.reshape(n_model * length, head_cols)
    branch_part = jnp.dot(attended_rows, out_weight, preferred_element_type=single).astype(bfloat)
    branch_part = branch_part.reshape(n_model, length, D)
    branch = (
        scatter_rows(
            (branch_part[2], branch_part[3]), (branch_part[0], branch_part[1]), n_model
        )[None]
        + out_bias
    )
    hidden_mid = hidden + gate_one[:, None, :] * branch
    normed_two = modulate(hidden_mid, shift_two, scale_two).astype(bfloat)
    two_rows = gather_rows(normed_two.reshape(length, D), n_model)
    return SimpleNamespace(
        steps=sinus_all,
        onehot=onehot,
        time_pre=time_pre,
        condition=condition,
        modulation=modulation,
        hidden=hidden,
        one_rows=one_rows,
        qkv_weight=qkv_weight,
        out_weight=out_weight,
        swiglu=swiglu_use,
        low=low,
        attended=attended,
        totals=log_total,
        branch=branch,
        hidden_mid=hidden_mid,
        two_rows=two_rows,
        final_weight=final_weight,
        tables=(cosine, sine, mask),
    )


def forward_fused(clean_three, noise_three, patch_grid, labels, timesteps, matrices, embeddings, swiglu_weights, biases):
    bfloat = jnp.bfloat16
    single = jnp.float32
    length = clean_three.shape[1]
    n_model = lax.axis_size("mlp")
    n_data = lax.axis_size("dp")
    everyone = n_data * n_model
    rows = D // n_data
    owned_start = lax.axis_index("dp") * rows
    model_index = lax.axis_index("mlp")
    head_cols = HEADS // n_model * HDIM

    def own_bias(start, amount, offset):
        return lax.dynamic_slice_in_dim(biases, start + offset, amount)[None]

    sinus = sinusoid(timesteps).astype(bfloat).astype(single).reshape(2, 128)
    facts = jnp.concatenate(
        [labels, patch_grid[:, 0] * patch_grid[:, 1]]
    ).astype(single)
    facts = jnp.concatenate(
        [sinus, jnp.pad(facts[None], ((0, 0), (0, 126))), jnp.zeros((5, 128), single)], axis=0
    )
    cosine, sine, _ = turn_tables(patch_grid, length)
    small = jnp.concatenate(
        [
            embeddings[:CH].T,
            jnp.zeros((rows, CH), single),
            matrices[:, 13 * D :],
            jnp.zeros((rows, 64), single),
        ],
        axis=1,
    ).astype(bfloat)
    values = ForwardIn(
        facts=facts,
        trig=jnp.concatenate([cosine, sine], axis=0),
        small=small,
        time_first=embeddings[CH : CH + FREQ].astype(bfloat),
        first_bias=own_bias(D, rows, owned_start),
        second_bias=own_bias(2 * D, rows, owned_start),
        class_table=embeddings[CH + FREQ :].astype(bfloat),
        matrices=matrices,
        mod_bias=biases[3 * D : 11 * D].reshape(8, D),
        noisy=noisy_input(clean_three, noise_three, timesteps).astype(bfloat)[0],
        patch_bias=biases[None, :D],
        qkv_shard=jnp.concatenate(
            [
                cut_columns(matrices, (9 + part) * D + model_index * head_cols, head_cols)
                for part in range(3)
            ],
            axis=1,
        ).astype(bfloat),
        ff_shard=swiglu_weights.astype(bfloat),
        qkv_bias=jnp.concatenate(
            [
                own_bias((11 + part) * D, head_cols, model_index * head_cols)
                for part in range(3)
            ],
            axis=1,
        ),
        out_bias=biases[None, 14 * D : 15 * D],
    )
    out = forward_all(values, (n_data, n_model), 0)
    raw = {name: getattr(out, name) for name in BackIn._fields if name in ForwardOut._fields}
    facts_all = out.facts_all
    group = lax.dynamic_slice_in_dim(
        facts_all[:, 2, 1], lax.axis_index("dp") * n_model, n_model
    )
    spots = model_index ^ jnp.arange(n_model)
    counts = jnp.sum(
        jnp.where(spots[:, None] == jnp.arange(n_model)[None, :], group[None, :], 0.0), axis=1
    )
    mask = jnp.arange(length, dtype=jnp.int32)[None, None, :] < counts[:, None, None]
    return SimpleNamespace(
        raw=dict(
            raw,
            noisy=values.noisy,
            matrices=matrices,
        ),
        steps=facts_all[:, :2].reshape(everyone, FREQ).astype(bfloat),
        onehot=(
            facts_all[:, 2, 0:1] == jnp.arange(CLASSES + 1, dtype=jnp.int32)[None].astype(single)
        ).astype(bfloat),
        time_pre=out.time_pre,
        condition=out.condition,
        modulation=out.modulation.reshape(1, 8 * D),
        hidden=out.hidden[None],
        one_rows=out.one_rows.reshape(n_model * length, D),
        qkv_weight=out.qkv_weight,
        out_weight=out.out_weight,
        swiglu=out.ff,
        low=out.low,
        attended=out.attended,
        totals=out.totals,
        branch=out.branch[None],
        hidden_mid=out.hidden_mid[None],
        two_rows=tuple(out.two_rows),
        final_weight=out.small_all[:, 2 * CH : 4 * CH],
        tables=(out.trig_all[:, 0], out.trig_all[:, 1], mask.astype(single)),
    )


def backward_plain(
    kept, clean_three, noise_three, patch_grid, timesteps, biases, total_images
):
    bfloat = jnp.bfloat16
    single = jnp.float32
    images, length = clean_three.shape[:2]
    n_model = lax.axis_size("mlp")
    n_data = lax.axis_size("dp")
    rows = D // n_data
    model_index = lax.axis_index("mlp")
    heads = HEADS // n_model
    head_cols = heads * HDIM
    valid_slot = valid_slots(patch_grid, length)
    final_bias = biases[15 * D :]
    noisy_low = noisy_input(clean_three, noise_three, timesteps).astype(bfloat)
    modulation, hidden, hidden_mid, branch = kept.modulation, kept.hidden, kept.hidden_mid, kept.branch
    shift_one, scale_one, gate_one, shift_two, scale_two, gate_two, shift_end, scale_end = (
        jnp.split(modulation, 8, axis=1)
    )
    qkv_weight, out_weight, swiglu_use = kept.qkv_weight, kept.out_weight, kept.swiglu
    final_weight, one_rows, two_rows = kept.final_weight, kept.one_rows, kept.two_rows
    low, log_total = kept.low, kept.totals
    attended_rows = kept.attended.reshape(n_model * length, head_cols)
    cosine, sine, mask = kept.tables
    two_halves = (
        jnp.concatenate(two_rows[:2], axis=0),
        jnp.concatenate(two_rows[2:], axis=0),
    )
    gates, ups, acts, parts = [], [], [], []
    for part in two_halves:
        gate_val = jnp.dot(part, swiglu_use[0], preferred_element_type=single)
        up_val = jnp.dot(part, swiglu_use[1], preferred_element_type=single)
        act = (jax.nn.silu(gate_val) * up_val).astype(bfloat)
        gates.append(gate_val)
        ups.append(up_val)
        acts.append(act)
        parts.append(backward_product(act, swiglu_use[2]).astype(bfloat).reshape(2, length, D))
    mixed = scatter_rows(parts[1], parts[0], n_model)[None]
    hidden_end = hidden_mid + gate_two[:, None, :] * mixed
    normed_end = modulate(hidden_end, shift_end, scale_end).astype(bfloat)
    output = jnp.dot(normed_end, final_weight, preferred_element_type=single) + final_bias
    local_loss, loss_pull = jax.vjp(
        lambda values_out: loss_terms(values_out, clean_three, noise_three, timesteps, valid_slot),
        output,
    )
    d_output = loss_pull(jnp.asarray(1.0 / total_images, single))[0].astype(bfloat)
    d_normed_end = backward_product(d_output, final_weight)
    unused, pull_end = jax.vjp(modulate, hidden_end, shift_end, scale_end)
    d_hidden_end, d_shift_end, d_scale_end = pull_end(d_normed_end)
    d_mixed = (gate_two[:, None, :] * d_hidden_end).astype(bfloat)
    d_gate_two = jnp.sum(mixed * d_hidden_end, axis=1)
    dmixed_rows = gather_rows(d_mixed.reshape(length, D), n_model)
    dmixed_halves = (
        jnp.concatenate(dmixed_rows[:2], axis=0),
        jnp.concatenate(dmixed_rows[2:], axis=0),
    )
    d_gates, d_ups, d_parts = [], [], []
    for part, gate_val, up_val in zip(dmixed_halves, gates, ups):
        d_inner = jnp.dot(part, swiglu_use[2], preferred_element_type=single)
        unused, pull_glu = jax.vjp(
            lambda gate_in, up_in: jax.nn.silu(gate_in) * up_in, gate_val, up_val
        )
        d_gate, d_up = pull_glu(d_inner)
        d_gate, d_up = d_gate.astype(bfloat), d_up.astype(bfloat)
        d_gates.append(d_gate)
        d_ups.append(d_up)
        d_parts.append(
            (backward_product(d_gate, swiglu_use[0]) + backward_product(d_up, swiglu_use[1]))
            .astype(bfloat)
            .reshape(2, length, D)
        )
    d_normed_two = scatter_rows(d_parts[1], d_parts[0], n_model)[None]
    rows_ready = jnp.concatenate(two_halves, axis=0)
    dmixed_ready = jnp.concatenate(dmixed_halves, axis=0)

    def owned(gradient):
        return reduce_dp(gradient.reshape(n_data, rows, -1))

    grad_swiglu = jnp.stack(
        [
            owned(weight_grad(rows_ready, jnp.concatenate(d_gates, axis=0))),
            owned(weight_grad(rows_ready, jnp.concatenate(d_ups, axis=0))),
            owned(weight_grad(dmixed_ready, jnp.concatenate(acts, axis=0))),
        ]
    )
    unused, pull_two = jax.vjp(modulate, hidden_mid, shift_two, scale_two)
    d_mid_part, d_shift_two, d_scale_two = pull_two(d_normed_two)
    d_hidden_mid = d_hidden_end + d_mid_part
    d_branch = (gate_one[:, None, :] * d_hidden_mid).astype(bfloat)
    d_gate_one = jnp.sum(branch * d_hidden_mid, axis=1)

    dbranch_rows = jnp.concatenate(gather_rows(d_branch.reshape(length, D), n_model), axis=0)
    d_attended = backward_product(dbranch_rows, out_weight).astype(bfloat)
    d_qkv = attention_back(
        low,
        log_total,
        d_attended.reshape(n_model, length, head_cols),
        cosine,
        sine,
        mask,
        heads,
    ).reshape(n_model * length, 3 * head_cols)
    grad_out = reduce_out(weight_grad(attended_rows, dbranch_rows))
    grad_qkv_own = owned(weight_grad(one_rows, d_qkv))
    d_one_part = backward_product(d_qkv, qkv_weight).astype(bfloat).reshape(n_model, length, D)
    d_normed_one = scatter_rows(
        (d_one_part[2], d_one_part[3]), (d_one_part[0], d_one_part[1]), n_model
    )[None]
    unused, pull_one = jax.vjp(modulate, hidden, shift_one, scale_one)
    d_hidden_part, d_shift_one, d_scale_one = pull_one(d_normed_one)
    d_hidden = (d_hidden_mid + d_hidden_part).astype(bfloat)

    return SimpleNamespace(
        d_modulation=jnp.concatenate(
            [
                d_shift_one,
                d_scale_one,
                d_gate_one,
                d_shift_two,
                d_scale_two,
                d_gate_two,
                d_shift_end,
                d_scale_end,
            ],
            axis=1,
        ),
        hidden_sum=column_sum(d_hidden),
        branch_sum=column_sum(d_branch),
        qkv_sum=column_sum(d_qkv),
        output_sum=column_sum(d_output),
        loss=local_loss.reshape(1),
        grad_patch=weight_grad(noisy_low, d_hidden),
        grad_final=weight_grad(normed_end, d_output).T,
        grad_swiglu=grad_swiglu,
        grad_out=grad_out,
        grad_qkv=jnp.stack(gather_rows(grad_qkv_own.astype(bfloat), n_model)).astype(single),
    )


def finish_fused(
    kept, clean_three, noise_three, patch_grid, timesteps, states, biases, total_images
):
    single = jnp.float32
    length = clean_three.shape[1]
    n_data, n_model = sizes = (lax.axis_size("dp"), lax.axis_size("mlp"))
    beta_now, bar_now, bar_prev = plan(timesteps)
    consts = jnp.stack(
        [
            jnp.sqrt(bar_now),
            jnp.sqrt(1.0 - bar_now),
            jnp.log(beta_now),
            jnp.log(beta_now * (1.0 - bar_prev) / (1.0 - bar_now)),
            beta_now * jnp.sqrt(bar_prev) / (1.0 - bar_now),
        ],
        axis=1,
    )
    values = BackIn(
        **kept.raw,
        final_bias=biases[15 * D :].reshape(2, CH),
        clean=clean_three[0],
        noise=noise_three[0],
        consts=jnp.pad(consts, ((0, 7), (0, 123))),
        valid=valid_slots(patch_grid, length).astype(single).reshape(length, 1),
    )
    out = backward_all(values, sizes, total_images, 1)
    grad_time_first = jnp.dot(
        kept.steps.astype(single).T,
        out.d_time_pre,
        precision=lax.Precision.HIGHEST,
        preferred_element_type=single,
    )
    grad_table = jnp.dot(
        kept.onehot.astype(single).T,
        out.d_condition,
        precision=lax.Precision.HIGHEST,
        preferred_element_type=single,
    )
    grad_norm, factor, loss_sum = (out.stats[0, spot] for spot in range(3))
    grad_bias = jnp.concatenate([out.bias_rows[:15].reshape(-1), out.bias_rows[15, : 2 * CH]])
    mats_out = adam_matrices(
        states,
        jax.nn.silu(kept.time_pre).astype(jnp.bfloat16),
        jax.nn.silu(kept.condition).astype(jnp.bfloat16),
        out.dtime,
        out.dmod,
        out.grad_qkv,
        out.grad_out,
        jnp.pad(out.own[CH:].T, ((0, 0), (0, 128 - 2 * CH))),
        out.stats,
        n_model,
    )
    return SimpleNamespace(
        loss_sum=loss_sum,
        grad_norm=grad_norm,
        factor=factor,
        grad_bias=grad_bias,
        grad_embed=jnp.concatenate([out.own[:CH], grad_time_first, grad_table], axis=0),
        grad_swiglu=out.grad_ff,
        mats_out=mats_out,
    )


def adam_matrices_kernel(
    n_model,
    weight_ref,
    first_ref,
    second_ref,
    average_ref,
    time_act_ref,
    cond_act_ref,
    dtime_ref,
    dmod_ref,
    qkv_ref,
    out_ref,
    final_ref,
    factor_ref,
    weight_out,
    first_out,
    second_out,
    average_out,
    grad_ref,
):
    single = jnp.float32
    head_cols = HEADS // n_model * HDIM
    m = lax.axis_index("mlp")

    def outer(left, right):
        return lax.dot_general(left, right, (((0,), (0,)), ((), ())), preferred_element_type=single)

    for side in range(2):
        section = 2 * pl.program_id(0) + side
        base = side * D
        lanes = slice(base, base + D)

        @pl.when((section >= 1) & (section < 9))
        def _():
            grad_ref[:, lanes] = outer(cond_act_ref[...], dmod_ref[jnp.clip(section - 1, 0, 7)])

        if side == 0:

            @pl.when(section == 0)
            def _():
                grad_ref[:, lanes] = outer(time_act_ref[...], dtime_ref[...])

            @pl.when(section == 12)
            def _():
                grad_ref[:, lanes] = out_ref[...].astype(single)

        else:

            @pl.when(section == 13)
            def _():
                grad_ref[:, base : base + 128] = final_ref[...]

        for part in range(3):
            if (9 + part) % 2 == side:

                @pl.when(section == 9 + part)
                def _():
                    for rank in range(n_model):
                        apart = (
                            2 * lax.rem(lax.div(m, 2) + rank // 2, 2)
                            + lax.rem(lax.rem(m, 2) + rank % 2, 2)
                        )
                        start = base + rank * head_cols
                        grad_ref[:, start : start + head_cols] = qkv_ref[
                            apart, :, part * head_cols : (part + 1) * head_cols
                        ].astype(single)

    def body(step, carry):
        at = pl.ds(pl.multiple_of(step * 24, 24), 24)
        done = adam_step(
            weight_ref[at],
            first_ref[at],
            second_ref[at],
            grad_ref[at],
            average_ref[at],
            factor_ref[0:1, 1:2],
            LEARN_RATE,
        )
        for place, value in zip((weight_out, first_out, second_out, average_out), done):
            place[at] = value
        return carry

    lax.fori_loop(0, weight_ref.shape[0] // 24, body, 0)


def adam_matrices(
    states, time_act, cond_act, dtime, dmod, grad_qkv, grad_out, grad_final, stats, n_model
):
    rows, width = states[0].shape
    whole = lambda array: pl.BlockSpec(array.shape, lambda i: (0,) * array.ndim)
    strip = pl.BlockSpec((rows, 2 * D), lambda i: (0, i))
    gradients = (time_act, cond_act, dtime, dmod, grad_qkv, grad_out, grad_final, stats)
    return pl.pallas_call(
        functools.partial(adam_matrices_kernel, n_model),
        grid=(pl.cdiv(width, 2 * D),),
        out_shape=[jax.ShapeDtypeStruct((rows, width), jnp.float32)] * 4,
        in_specs=[strip] * 4 + [whole(array) for array in gradients],
        out_specs=[strip] * 4,
        scratch_shapes=[pltpu.VMEM((rows, 2 * D), jnp.float32)],
        compiler_params=pltpu.CompilerParams(vmem_limit_bytes=KERNEL_VMEM),
    )(*states, *gradients)


def finish_plain(
    kept, clean_three, noise_three, patch_grid, timesteps, states, biases, total_images
):
    bfloat = jnp.bfloat16
    single = jnp.float32
    matrices, matrices_first, matrices_second, matrices_average = states
    n_data, n_model = sizes = (lax.axis_size("dp"), lax.axis_size("mlp"))
    rows = D // n_data
    owned_start = lax.axis_index("dp") * rows
    model_index = lax.axis_index("mlp")
    head_cols = HEADS // n_model * HDIM
    time_pre, condition = kept.time_pre, kept.condition
    onehot, sinus_all = kept.onehot, kept.steps
    time_act = jax.nn.silu(time_pre).astype(bfloat)
    cond_act = jax.nn.silu(condition).astype(bfloat)
    time_second = matrices[:, :D].astype(bfloat)
    mod_weight = matrices[:, D : 9 * D].astype(bfloat)

    grads = backward_plain(
        kept, clean_three, noise_three, patch_grid, timesteps, biases, total_images
    )
    grad_swiglu, grad_out = grads.grad_swiglu, grads.grad_out
    grad_qkv_own = grads.grad_qkv[0]
    qkv_stack = jnp.stack(
        [
            lax.dynamic_index_in_dim(grads.grad_qkv, model_index ^ rank, 0, keepdims=False)
            for rank in range(n_model)
        ]
    )
    grad_qkv = (
        qkv_stack.reshape(n_model, rows, 3, head_cols).transpose(1, 2, 0, 3).reshape(rows, 3 * D)
    )

    d_modulation = grads.d_modulation.astype(bfloat)
    (dmod_all,) = exchange(
        [(d_modulation.reshape(16, D // 2), "all")], "both", sizes, 3
    )
    dmod_all = dmod_all.reshape(total_images, 8 * D)
    d_cond_act = backward_product(dmod_all, mod_weight)
    unused, pull_cond = jax.vjp(jax.nn.silu, condition)
    d_condition = pull_cond(d_cond_act)[0]
    d_time_emb = d_condition.astype(bfloat)
    (dtime_parts,) = exchange([(d_time_emb, "all")], "dp", sizes, 4)
    dtime_all = dtime_parts.transpose(1, 0, 2).reshape(total_images, D)
    d_time_act = backward_product(dtime_all, time_second)
    unused, pull_time = jax.vjp(jax.nn.silu, time_pre)
    d_time_pre = pull_time(d_time_act)[0]
    grad_time_second = weight_grad(time_act, dtime_all)
    grad_mod = weight_grad(cond_act, dmod_all)
    grad_time_first = jnp.dot(
        sinus_all.astype(single).T,
        d_time_pre,
        precision=lax.Precision.HIGHEST,
        preferred_element_type=single,
    )
    grad_table = jnp.dot(
        onehot.astype(single).T,
        d_condition,
        precision=lax.Precision.HIGHEST,
        preferred_element_type=single,
    )

    qkv_sums = grads.qkv_sum.reshape(3, head_cols)
    qkv_bias_part = lax.dynamic_update_slice(
        jnp.zeros((3, D), single), qkv_sums, (0, model_index * head_cols)
    )
    local_sums = jnp.concatenate(
        [
            grads.hidden_sum,
            qkv_bias_part.reshape(-1),
            grads.branch_sum,
            grads.output_sum,
            grads.loss,
            jnp.zeros((95,), single),
            grads.grad_patch.reshape(-1),
            grads.grad_final.reshape(-1),
        ]
    )
    everyone = n_data * n_model
    chunk_rows = -(-local_sums.shape[0] // (everyone * 1024)) * 8
    local_sums = jnp.pad(local_sums, (0, everyone * chunk_rows * 128 - local_sums.shape[0]))
    (sum_parts,) = exchange(
        [(local_sums.reshape(everyone, chunk_rows, 128), "each")], "both", sizes, 5
    )
    chunk = jnp.sum(sum_parts, axis=0)
    local_squares = (
        jnp.sum(grad_time_second * grad_time_second)
        + jnp.sum(grad_mod * grad_mod)
        + jnp.sum(grad_out * grad_out)
        + jnp.sum(grad_time_first * grad_time_first)
        + jnp.sum(grad_table * grad_table)
    ) / n_model + jnp.sum(grad_swiglu * grad_swiglu) + jnp.sum(grad_qkv_own * grad_qkv_own)
    extra = jnp.concatenate([jnp.sum(d_time_pre, axis=0), local_squares.reshape(1)])
    extra = jnp.pad(extra, (0, 1024 - extra.shape[0])).reshape(8, 128)
    (late,) = exchange([(jnp.concatenate([chunk, extra], axis=0), "all")], "both", sizes, 6)
    sums = late[:, :chunk_rows].reshape(-1)
    extras = late[:, chunk_rows:].reshape(everyone, 1024)
    first_bias_grad = extras.reshape(n_data, n_model, 1024)[:, 0, :rows].reshape(D)
    squares = jnp.sum(extras[:, rows])
    ends = [D, 4 * D, 5 * D, 5 * D + 2 * CH, 5 * D + 2 * CH + 1]
    base = 5 * D + 128
    loss_sum = sums[5 * D + 2 * CH]
    grad_patch = sums[base : base + CH * D].reshape(CH, D)
    grad_final = sums[base + CH * D : base + 3 * CH * D].reshape(2 * CH, D)
    grad_patch = cut_columns(grad_patch, owned_start, rows)
    grad_final_own = cut_columns(grad_final, owned_start, rows).T
    grad_bias = jnp.concatenate(
        [
            sums[:D],
            first_bias_grad,
            column_sum(dtime_all),
            column_sum(dmod_all),
            sums[D : 4 * D],
            sums[4 * D : 5 * D],
            sums[5 * D : 5 * D + 2 * CH],
        ]
    )
    shared = sums[base : base + 3 * CH * D]
    squares = squares + jnp.sum(grad_bias * grad_bias) + jnp.sum(shared * shared)
    grad_norm = jnp.sqrt(squares)
    factor = jnp.minimum(1.0, CLIP_LIMIT / grad_norm)
    grad_mats = jnp.concatenate(
        [grad_time_second, grad_mod, grad_qkv, grad_out, grad_final_own], axis=1
    )
    grad_embed = jnp.concatenate([grad_patch, grad_time_first, grad_table], axis=0)
    mats_out = adam_step(
        matrices, matrices_first, matrices_second, grad_mats, matrices_average, factor, LEARN_RATE
    )
    return SimpleNamespace(
        loss_sum=loss_sum,
        grad_norm=grad_norm,
        factor=factor,
        grad_bias=grad_bias,
        grad_embed=grad_embed,
        grad_swiglu=grad_swiglu,
        mats_out=mats_out,
    )


def on_device(
    clean_patches,
    noise_patches,
    patch_grid,
    labels,
    timesteps,
    matrices,
    embeddings,
    swiglu_weights,
    biases,
    matrices_first,
    embeddings_first,
    swiglu_first,
    biases_first,
    matrices_second,
    embeddings_second,
    swiglu_second,
    biases_second,
    matrices_average,
    embeddings_average,
    swiglu_average,
    biases_average,
):
    images = labels.shape[0]
    length = clean_patches.shape[0] // images
    n_model = lax.axis_size("mlp")
    n_data = lax.axis_size("dp")
    total_images = images * n_data * n_model

    clean_three = clean_patches.reshape(images, length, CH)
    noise_three = noise_patches.reshape(images, length, CH)
    fused = (n_data, n_model, images) == (8, 4, 1)
    forward = forward_fused if fused else forward_plain
    kept = forward(
        clean_three,
        noise_three,
        patch_grid,
        labels,
        timesteps,
        matrices,
        embeddings,
        swiglu_weights,
        biases,
    )
    finish = finish_fused if fused else finish_plain
    done = finish(
        kept,
        clean_three,
        noise_three,
        patch_grid,
        timesteps,
        (matrices, matrices_first, matrices_second, matrices_average),
        biases,
        total_images,
    )
    loss_sum, grad_norm, factor = done.loss_sum, done.grad_norm, done.factor
    grad_embed, grad_swiglu, grad_bias = done.grad_embed, done.grad_swiglu, done.grad_bias
    mats_out = done.mats_out
    embed_out = adam_step(
        embeddings,
        embeddings_first,
        embeddings_second,
        grad_embed,
        embeddings_average,
        factor,
        TABLE_RATE,
    )
    swiglu_out = adam_step(
        swiglu_weights, swiglu_first, swiglu_second, grad_swiglu, swiglu_average, factor, LEARN_RATE
    )
    bias_out = adam_step(
        biases, biases_first, biases_second, grad_bias, biases_average, factor, TABLE_RATE
    )
    return (
        loss_sum,
        grad_norm,
        mats_out[0],
        embed_out[0],
        swiglu_out[0],
        bias_out[0],
        mats_out[1],
        embed_out[1],
        swiglu_out[1],
        bias_out[1],
        mats_out[2],
        embed_out[2],
        swiglu_out[2],
        bias_out[2],
        mats_out[3],
        embed_out[3],
        swiglu_out[3],
        bias_out[3],
        grad_bias * factor,
    )


def solution(mesh):
    placed = (
        P(("dp", "mlp"), None),
        P(("dp", "mlp"), None),
        P(("dp", "mlp"), None),
        P(("dp", "mlp")),
        P(("dp", "mlp")),
        P("dp", None),
        P(None, "dp"),
        P(None, "dp", "mlp"),
        P(),
        P("dp", None),
        P(None, "dp"),
        P(None, "dp", "mlp"),
        P(),
        P("dp", None),
        P(None, "dp"),
        P(None, "dp", "mlp"),
        P(),
        P("dp", None),
        P(None, "dp"),
        P(None, "dp", "mlp"),
        P(),
    )
    return jax.shard_map(
        on_device,
        mesh=mesh,
        in_specs=placed,
        out_specs=(
            P(),
            P(),
            P("dp", None),
            P(None, "dp"),
            P(None, "dp", "mlp"),
            P(),
            P("dp", None),
            P(None, "dp"),
            P(None, "dp", "mlp"),
            P(),
            P("dp", None),
            P(None, "dp"),
            P(None, "dp", "mlp"),
            P(),
            P("dp", None),
            P(None, "dp"),
            P(None, "dp", "mlp"),
            P(),
            P(),
        ),
        check_vma=False,
    )
```

```python
import functools
import math
from types import SimpleNamespace
from typing import Any, NamedTuple

import jax
import jax.numpy as jnp
import numpy as np
from jax import lax
from jax.experimental import pallas as pl
from jax.experimental.pallas import tpu as pltpu
from jax.sharding import PartitionSpec as P

HEADS = 16
HDIM = 72
D = 1152
CH = 16
CLASSES = 1000
FREQ = 256
STEP = 10


CLIP_LIMIT = 1.0
LEARN_RATE = 0.03
TABLE_RATE = 0.4
FIRST_DECAY = 0.9
SECOND_DECAY = 0.999
ADAM_EPSILON = 1e-08
WEIGHT_DECAY = 0.01
AVERAGE_DECAY = 0.9999


def plan(steps_in):
    step_index = jnp.arange(1000, dtype=jnp.int32)
    betas = 0.0001 + (0.02 - 0.0001) * np.arange(1000) / 999.0
    beta_table = jnp.asarray(betas, jnp.float32)
    logbar = jnp.asarray(np.cumsum(np.log1p(-betas)), jnp.float32)

    def lookup(values, wanted):
        return jnp.sum(
            jnp.where(wanted[:, None] == step_index[None, :], values[None, :], 0.0), axis=1
        )

    return (
        lookup(beta_table, steps_in),
        jnp.exp(lookup(logbar, steps_in)),
        jnp.exp(lookup(logbar, steps_in - 1)),
    )


def sinusoid(steps_in):
    halfway = FREQ // 2
    frequency = jnp.exp(-math.log(10000.0) * jnp.arange(halfway, dtype=jnp.float32) / halfway)
    angles = steps_in.astype(jnp.float32)[:, None] * frequency[None, :]
    return jnp.concatenate([jnp.cos(angles), jnp.sin(angles)], axis=1)


def modulate(hidden, shift_by, scale_by):
    row_mean = jnp.mean(hidden, axis=-1, keepdims=True)
    centered = hidden - row_mean
    variance = jnp.mean(centered * centered, axis=-1, keepdims=True)
    return (
        centered * lax.rsqrt(variance + 1e-06) * (1.0 + scale_by[:, None, :]) + shift_by[:, None, :]
    )


def noisy_input(clean_patches, noise_patches, steps_in):
    beta_now, bar_now, bar_prev = plan(steps_in)
    bar_now = bar_now[:, None, None]
    return jnp.sqrt(bar_now) * clean_patches + jnp.sqrt(1.0 - bar_now) * noise_patches


def loss_terms(output, clean_patches, noise_patches, steps_in, valid_slot):
    beta_now, bar_now, bar_prev = plan(steps_in)
    beta_now = beta_now[:, None, None]
    bar_now = bar_now[:, None, None]
    bar_prev = bar_prev[:, None, None]
    noisy = jnp.sqrt(bar_now) * clean_patches + jnp.sqrt(1.0 - bar_now) * noise_patches
    eps_pred = output[..., :CH]
    var_raw = output[..., CH:]
    squared = jnp.sum((eps_pred - noise_patches) ** 2, axis=-1)
    post_log = jnp.log(beta_now * (1.0 - bar_prev) / (1.0 - bar_now))
    fraction = (var_raw + 1.0) * 0.5
    model_log = fraction * jnp.log(beta_now) + (1.0 - fraction) * post_log
    coefficient = beta_now * jnp.sqrt(bar_prev) / (1.0 - bar_now)
    start_est = (noisy - jnp.sqrt(1.0 - bar_now) * eps_pred) / jnp.sqrt(bar_now)
    mean_gap = coefficient * (clean_patches - start_est)
    divergence = (
        0.5
        * (
            -1.0
            + model_log
            - post_log
            + jnp.exp(post_log - model_log)
            + mean_gap * mean_gap * jnp.exp(-model_log)
        )
        / math.log(2.0)
    )
    return jnp.sum(jnp.where(valid_slot, squared + jnp.sum(divergence, axis=-1), 0.0))


def adam_step(weight, first, second, gradient, average, factor, rate):
    average_decay = min(AVERAGE_DECAY, (1.0 + STEP) / (10.0 + STEP))
    clipped = gradient * factor
    first = FIRST_DECAY * first + (1.0 - FIRST_DECAY) * clipped
    second = SECOND_DECAY * second + (1.0 - SECOND_DECAY) * clipped * clipped
    ratio = (first * (1.0 / (1.0 - FIRST_DECAY**STEP))) / (
        jnp.sqrt(second * (1.0 / (1.0 - SECOND_DECAY**STEP))) + ADAM_EPSILON
    )
    weight = weight - rate * (ratio + WEIGHT_DECAY * weight)
    return (weight, first, second, average_decay * average + (1.0 - average_decay) * weight)


def backward_product(gradient, weight):
    return lax.dot_general(
        gradient,
        weight,
        (((gradient.ndim - 1,), (1,)), ((), ())),
        preferred_element_type=jnp.float32,
    )


def weight_grad(inputs, gradient):
    flat_in = inputs.reshape(-1, inputs.shape[-1])
    flat_grad = gradient.reshape(-1, gradient.shape[-1])
    return lax.dot_general(
        flat_in, flat_grad, (((0,), (0,)), ((), ())), preferred_element_type=jnp.float32
    )


def column_sum(gradient):
    return jnp.sum(gradient.astype(jnp.float32).reshape(-1, gradient.shape[-1]), axis=0)


def cut_columns(values, start, amount):
    return lax.dynamic_slice_in_dim(values, start, amount, 1)


MESH_IDS = pl.DeviceIdType.MESH
KERNEL_VMEM = 48 * 2**20


def exchange_kernel(axes, sizes, modes, *refs):
    count = len(modes)
    ins, outs = refs[:count], refs[count : 2 * count]
    send_sem, recv_sem = refs[2 * count :]
    if axes == "dp":
        total = sizes[0]
        me = lax.axis_index("dp")
    else:
        total = sizes[0] * sizes[1]
        me = lax.axis_index("dp") * sizes[1] + lax.axis_index("mlp")

    def device(spot):
        if axes == "dp":
            return (spot, lax.axis_index("mlp"))
        return (lax.div(spot, sizes[1]), lax.rem(spot, sizes[1]))

    barrier = pltpu.get_barrier_semaphore()

    def greet(step, carry):
        pl.semaphore_signal(
            barrier, inc=1, device_id=device(lax.rem(me + step, total)), device_id_type=MESH_IDS
        )
        return carry

    lax.fori_loop(1, total, greet, 0)
    pl.semaphore_wait(barrier, total - 1)

    def make(item, step):
        peer = lax.rem(me + step, total)
        source = ins[item].at[peer] if modes[item] == "each" else ins[item]
        return pltpu.make_async_remote_copy(
            src_ref=source,
            dst_ref=outs[item].at[me],
            send_sem=send_sem.at[item, step - 1],
            recv_sem=recv_sem.at[item, step - 1],
            device_id=device(peer),
            device_id_type=MESH_IDS,
        )

    def begin(step, carry):
        for item in range(count):
            make(item, step).start()
        return carry

    lax.fori_loop(1, total, begin, 0)
    for item in range(count):
        if modes[item] == "each":
            outs[item][me] = ins[item][me]
        else:
            outs[item][me] = ins[item][...]

    def finish(step, carry):
        for item in range(count):
            make(item, step).wait()
        return carry

    lax.fori_loop(1, total, finish, 0)


def exchange(items, axes, sizes, collective):
    total = sizes[0] if axes == "dp" else sizes[0] * sizes[1]
    modes = tuple(mode for _, mode in items)
    arrays = [array for array, _ in items]
    shapes = [
        jax.ShapeDtypeStruct(
            array.shape if mode == "each" else (total, *array.shape), array.dtype
        )
        for array, mode in items
    ]
    space = pl.BlockSpec(memory_space=pltpu.VMEM)
    return pl.pallas_call(
        functools.partial(exchange_kernel, axes, sizes, modes),
        out_shape=shapes,
        in_specs=[space] * len(items),
        out_specs=[space] * len(items),
        scratch_shapes=[
            pltpu.SemaphoreType.DMA((len(items), total - 1)),
            pltpu.SemaphoreType.DMA((len(items), total - 1)),
        ],
        compiler_params=pltpu.CompilerParams(
            collective_id=collective, has_side_effects=True, vmem_limit_bytes=KERNEL_VMEM
        ),
    )(*arrays)


NX = 2


def reduce_dp(value):
    return lax.psum_scatter(value.astype(jnp.bfloat16), "dp", scatter_dimension=0, tiled=True)[
        0
    ].astype(jnp.float32)


def flip(value, bit, count):
    return lax.ppermute(value, "mlp", [(spot, spot ^ bit) for spot in range(count)])


def gather_rows(own, count):
    far = flip(own, 2, count)
    near = flip(own, 1, count)
    return own, near, far, flip(far, 1, count)


def scatter_rows(far_parts, near_parts, count):
    single = jnp.float32
    got = flip(far_parts[1], 1, count)
    far = flip((far_parts[0].astype(single) + got.astype(single)).astype(jnp.bfloat16), 2, count)
    near = flip(near_parts[1], 1, count)
    return near_parts[0].astype(single) + near.astype(single) + far.astype(single)


def gather_out(shard):
    whole = lax.all_gather(shard, "dp", axis=0, tiled=True)
    height = D // lax.axis_size("mlp")
    return lax.dynamic_slice_in_dim(whole, lax.axis_index("mlp") * height, height, 0)


def reduce_out(value):
    whole = lax.dynamic_update_slice_in_dim(
        jnp.zeros((D, D), jnp.float32), value, lax.axis_index("mlp") * value.shape[0], 0
    )
    part = lax.psum_scatter(whole.astype(jnp.bfloat16), "dp", scatter_dimension=0, tiled=True)
    return lax.psum(part.astype(jnp.float32), "mlp")


def swapped(values):
    quarter = HDIM // 4
    return jnp.concatenate(
        [
            values[:, quarter : 2 * quarter],
            values[:, :quarter],
            values[:, 3 * quarter :],
            values[:, 2 * quarter : 3 * quarter],
        ],
        axis=1,
    )


def attention_kernel(heads, qkv_ref, cos_ref, sin_ref, mask_ref, low_ref, out_ref, total_ref):
    width = heads * HDIM
    cosine, sine, mask = cos_ref[0], sin_ref[0], mask_ref[0]
    totals = []
    for head in range(heads):
        start = head * HDIM

        def part(which):
            return qkv_ref[0, :, which * width + start : which * width + start + HDIM]

        raw_q, raw_k = part(0), part(1)
        query = (raw_q * cosine + swapped(raw_q) * sine).astype(jnp.bfloat16)
        key = (raw_k * cosine + swapped(raw_k) * sine).astype(jnp.bfloat16)
        value = part(2).astype(jnp.bfloat16)
        for which, kept in enumerate((query, key, value)):
            low_ref[0, :, which * width + start : which * width + start + HDIM] = kept
        scores = lax.dot_general(
            query, key, (((1,), (1,)), ((), ())), preferred_element_type=jnp.float32
        ) * (1.0 / math.sqrt(HDIM))
        scores = jnp.where(mask > 0.0, scores, -1e30)
        row_max = jnp.max(scores, axis=-1, keepdims=True)
        exponent = jnp.exp(scores - row_max)
        row_sum = jnp.sum(exponent, axis=-1, keepdims=True)
        probs = exponent / row_sum
        out_ref[0, :, start : start + HDIM] = jnp.dot(
            probs.astype(jnp.bfloat16), value, preferred_element_type=jnp.float32
        ).astype(jnp.bfloat16)
        totals.append(row_max + jnp.log(row_sum))
    total_ref[0] = jnp.concatenate(totals, axis=1)


def attention(qkv, cosine, sine, mask, heads):
    images, length, width = qkv.shape
    per_image = lambda *dims: pl.BlockSpec((1, *dims), lambda i: (i, 0, 0))
    return pl.pallas_call(
        functools.partial(attention_kernel, heads),
        grid=(images,),
        out_shape=[
            jax.ShapeDtypeStruct((images, length, width), jnp.bfloat16),
            jax.ShapeDtypeStruct((images, length, heads * HDIM), jnp.bfloat16),
            jax.ShapeDtypeStruct((images, length, heads), jnp.float32),
        ],
        in_specs=[
            per_image(length, width),
            per_image(length, HDIM),
            per_image(length, HDIM),
            per_image(1, length),
        ],
        out_specs=[
            per_image(length, width),
            per_image(length, heads * HDIM),
            per_image(length, heads),
        ],
        compiler_params=pltpu.CompilerParams(vmem_limit_bytes=KERNEL_VMEM),
    )(qkv, cosine, sine, mask)


def attention_back_kernel(
    heads, low_ref, total_ref, grad_ref, cos_ref, sin_ref, mask_ref, out_ref
):
    width = heads * HDIM
    scale_by = 1.0 / math.sqrt(HDIM)
    cosine, sine, mask = cos_ref[0], sin_ref[0], mask_ref[0]

    def contract(left, right, dims):
        return lax.dot_general(left, right, (dims, ((), ())), preferred_element_type=jnp.float32)

    for head in range(heads):
        start = head * HDIM

        def spot(which):
            return slice(which * width + start, which * width + start + HDIM)

        query, key, value = (low_ref[0, :, spot(which)] for which in range(3))
        grad = grad_ref[0, :, start : start + HDIM]
        scores = contract(query, key, ((1,), (1,))) * scale_by
        scores = jnp.where(mask > 0.0, scores, -1e30)
        probs = jnp.exp(scores - total_ref[0, :, head : head + 1])
        d_probs = contract(grad, value, ((1,), (1,)))
        row = jnp.sum(probs * d_probs, axis=-1, keepdims=True)
        d_scores = (probs * (d_probs - row)).astype(jnp.bfloat16)
        d_query = contract(d_scores, key, ((1,), (0,))) * scale_by
        d_key = contract(d_scores, query, ((0,), (0,))) * scale_by
        d_value = contract(probs.astype(jnp.bfloat16), grad, ((0,), (0,)))
        for which, turned in ((0, d_query), (1, d_key)):
            back = turned * cosine + swapped(turned * sine)
            out_ref[0, :, spot(which)] = back.astype(jnp.bfloat16)
        out_ref[0, :, spot(2)] = d_value.astype(jnp.bfloat16)


def attention_back(low, totals, grad, cosine, sine, mask, heads):
    images, length, width = low.shape
    per_image = lambda *dims: pl.BlockSpec((1, *dims), lambda i: (i, 0, 0))
    return pl.pallas_call(
        functools.partial(attention_back_kernel, heads),
        grid=(images,),
        out_shape=jax.ShapeDtypeStruct((images, length, width), jnp.bfloat16),
        in_specs=[
            per_image(length, width),
            per_image(length, heads),
            per_image(length, heads * HDIM),
            per_image(length, HDIM),
            per_image(length, HDIM),
            per_image(1, length),
        ],
        out_specs=per_image(length, width),
        compiler_params=pltpu.CompilerParams(vmem_limit_bytes=KERNEL_VMEM),
    )(low, totals, grad, cosine, sine, mask)


def turn_tables(patch_grid, length):
    slot_index = jnp.arange(length, dtype=jnp.int32)[None, :]
    grid_cols = patch_grid[:, 1:2]
    valid_slot = slot_index < patch_grid[:, 0:1] * grid_cols
    row_place = (slot_index // grid_cols).astype(jnp.float32)
    col_place = (slot_index % grid_cols).astype(jnp.float32)
    quarter = HDIM // 4
    frequency = jnp.exp(-math.log(10000.0) * jnp.arange(quarter, dtype=jnp.float32) / quarter)
    row_angle = row_place[..., None] * frequency
    col_angle = col_place[..., None] * frequency
    cos_row, sin_row = jnp.cos(row_angle), jnp.sin(row_angle)
    cos_col, sin_col = jnp.cos(col_angle), jnp.sin(col_angle)
    return (
        jnp.concatenate([cos_row, cos_row, cos_col, cos_col], axis=-1),
        jnp.concatenate([-sin_row, sin_row, -sin_col, sin_col], axis=-1),
        valid_slot.astype(jnp.float32)[:, None, :],
    )


def valid_slots(patch_grid, length):
    return jnp.arange(length, dtype=jnp.int32)[None, :] < patch_grid[:, 0:1] * patch_grid[:, 1:2]


def device_parts():
    d, m = lax.axis_index("dp"), lax.axis_index("mlp")
    return d, m, lax.div(d, NX), lax.rem(d, NX)


class Sender:
    def __init__(self, send_sem, recv_sem):
        self.send_sem, self.recv_sem = send_sem, recv_sem

    def __call__(self, spot, source, target, device):
        spot = spot if isinstance(spot, tuple) else (spot,)
        return pltpu.make_async_remote_copy(
            src_ref=source,
            dst_ref=target,
            send_sem=self.send_sem.at[spot],
            recv_sem=self.recv_sem.at[spot],
            device_id=device,
            device_id_type=MESH_IDS,
        )


def modulate_rows(values, shift_by, scale_by):
    row_mean = jnp.mean(values, axis=-1, keepdims=True)
    centered = values - row_mean
    variance = jnp.mean(centered * centered, axis=-1, keepdims=True)
    return centered * lax.rsqrt(variance + 1e-06) * (1.0 + scale_by) + shift_by


def named(inputs, outputs, scratch, refs):
    ends = len(inputs._fields), len(inputs._fields) + len(outputs._fields)
    parts = inputs(*refs[: ends[0]]), outputs(*refs[ends[0] : ends[1]]), scratch(*refs[ends[1] :])
    return SimpleNamespace(**{k: v for part in parts for k, v in part._asdict().items()})


class ForwardIn(NamedTuple):
    facts: Any
    trig: Any
    small: Any
    time_first: Any
    first_bias: Any
    second_bias: Any
    class_table: Any
    matrices: Any
    mod_bias: Any
    noisy: Any
    patch_bias: Any
    qkv_shard: Any
    ff_shard: Any
    qkv_bias: Any
    out_bias: Any


class ForwardOut(NamedTuple):
    facts_all: Any
    trig_all_out: Any
    small_all: Any
    time_pre: Any
    condition: Any
    modulation: Any
    hidden: Any
    one_rows_out: Any
    qkv_weight_out: Any
    out_weight_out: Any
    ff: Any
    low_out: Any
    attended_out: Any
    totals: Any
    branch: Any
    hidden_mid: Any
    two_rows: Any


class ForwardScratch(NamedTuple):
    one_rows: Any
    qkv_weight: Any
    out_weight: Any
    low: Any
    attended: Any
    trig_all: Any
    leave_sem: Any
    time_low: Any
    out_low: Any
    time_send: Any
    time_recv: Any
    mod_send: Any
    mod_recv: Any
    mod_low: Any
    qkv: Any
    parts_send: Any
    parts_recv: Any
    facts_s: Any
    facts_r: Any
    small_s: Any
    small_r: Any
    time_s: Any
    time_r: Any
    mods_s: Any
    mods_r: Any
    trig_s: Any
    trig_r: Any
    noisy_s: Any
    noisy_r: Any
    kinds_s: Any
    kinds_r: Any
    noisy_all: Any
    kinds_all: Any
    two_s: Any
    two_r: Any
    part_s: Any
    part_r: Any
    qz_s: Any
    qz_r: Any
    qx_s: Any
    qx_r: Any
    oz_s: Any
    oz_r: Any
    ox_s: Any
    ox_r: Any
    fz_s: Any
    fz_r: Any
    fx_s: Any
    fx_r: Any
    local_sem: Any


def forward_kernel(sizes, *refs):
    r = named(ForwardIn, ForwardOut, ForwardScratch, refs)
    bfloat, single = jnp.bfloat16, jnp.float32
    n_data, n_model = sizes
    everyone = n_data * n_model
    d, m, z, x = device_parts()
    me = d * n_model + m
    depth = n_data // NX
    rows = D // n_data
    heads = HEADS // n_model
    head_cols = heads * HDIM
    length = r.noisy.shape[0]
    units = r.ff_shard.shape[2]
    half = units // 2

    def at_dp(spot):
        return (spot, m)

    def at_mlp(bit):
        flipped = m + 1 - 2 * lax.rem(m, 2) if bit == 1 else lax.rem(m + 2, 4)
        return (d, flipped)

    up = lax.rem(z + 1, depth) * NX + x
    down = lax.rem(z + depth - 1, depth) * NX + x
    side = z * NX + 1 - x

    barrier = pltpu.get_barrier_semaphore()

    def greet(step, carry):
        peer = lax.rem(me + step, everyone)
        pl.semaphore_signal(
            barrier,
            inc=1,
            device_id=(lax.div(peer, n_model), lax.rem(peer, n_model)),
            device_id_type=MESH_IDS,
        )
        return carry

    lax.fori_loop(1, everyone, greet, 0)

    load_out = pltpu.make_async_copy(
        r.matrices.at[:, pl.ds(12 * D, D)], r.out_low, r.local_sem.at[2]
    )
    load_out.start()
    load_time = pltpu.make_async_copy(
        r.matrices.at[:, pl.ds(0, D)], r.time_low, r.local_sem.at[3]
    )
    load_time.start()
    load_mod = pltpu.make_async_copy(
        r.matrices.at[:, pl.ds(D, 8 * D)], r.mod_low, r.local_sem.at[0]
    )
    load_mod.start()
    own_ff = pltpu.make_async_copy(
        r.ff_shard,
        r.ff.at[:, pl.ds(pl.multiple_of(d * rows, 16), rows)],
        r.local_sem.at[1],
    )
    own_ff.start()
    pl.semaphore_wait(barrier, everyone - 1)

    send_facts = Sender(r.facts_s, r.facts_r)

    def facts_copy(step):
        peer = lax.rem(me + step, everyone)
        return send_facts(
            step - 1,
            r.facts,
            r.facts_all.at[me],
            (lax.div(peer, n_model), lax.rem(peer, n_model)),
        )

    def loop(first, last, body):
        def step_body(step, carry):
            body(step)
            return carry

        lax.fori_loop(first, last, step_body, 0)

    loop(1, everyone, lambda step: facts_copy(step).start())
    r.facts_all[me] = r.facts[...]

    def qkv_rows(spot, part):
        if part == 0:
            return r.qkv_weight.at[pl.ds(pl.multiple_of(spot * rows, 16), 80)]
        return r.qkv_weight.at[pl.ds(pl.multiple_of(spot * rows + 80, 16), rows - 80)]

    def ff_block(spot, part, which):
        return r.ff.at[
            which,
            pl.ds(pl.multiple_of(spot * rows, 16), rows),
            pl.ds(half * part, half),
        ]

    def origin(step, part):
        return lax.rem(z + (depth - step if part == 0 else step), depth) * NX + x

    qz, qx = Sender(r.qz_s, r.qz_r), Sender(r.qx_s, r.qx_r)
    fz, fx = Sender(r.fz_s, r.fz_r), Sender(r.fx_s, r.fx_r)

    def qkv_along(step, part):
        block = qkv_rows(origin(step - 1, part), part)
        return qz((part, step - 1), block, block, at_dp(up if part == 0 else down))

    def qkv_aside(step, part):
        block = qkv_rows(origin(step, part), part)
        return qx((part, step), block, block, at_dp(side))

    def ff_along(step, part, which):
        block = ff_block(origin(step - 1, part), part, which)
        return fz((part, step - 1, which), block, block, at_dp(up if part == 0 else down))

    def ff_aside(step, part, which):
        block = ff_block(origin(step, part), part, which)
        return fx((part, step, which), block, block, at_dp(side))

    own_rows = pl.ds(pl.multiple_of(d * rows, 16), rows)
    r.qkv_weight[own_rows] = r.qkv_shard[...]
    for part in range(2):
        qkv_along(1, part).start()
        qkv_aside(0, part).start()

    send_small = Sender(r.small_s, r.small_r)

    def small_copy(step):
        return send_small(
            step - 1,
            r.small,
            r.small_all.at[own_rows],
            at_dp(lax.rem(d + step, n_data)),
        )

    loop(1, n_data, lambda step: small_copy(step).start())
    r.small_all[own_rows] = r.small[...]
    r.trig_all[0] = r.trig[...]

    def spread(send, buffer):
        return (
            send(0, buffer.at[0], buffer.at[1], at_mlp(1)),
            send(1, buffer.at[0], buffer.at[2], at_mlp(2)),
            send(2, buffer.at[2], buffer.at[3], at_mlp(1)),
        )

    trig_near, trig_far, trig_on = spread(Sender(r.trig_s, r.trig_r), r.trig_all)
    trig_near.start()
    trig_far.start()
    near_rank = m + 1 - 2 * lax.rem(m, 2)
    partners = ((d, near_rank), (d, lax.rem(m + 2, 4)), (d, lax.rem(near_rank + 2, 4)))
    send_noisy, send_kinds = Sender(r.noisy_s, r.noisy_r), Sender(r.kinds_s, r.kinds_r)
    noisy_copies = [
        send_noisy(spot, r.noisy, r.noisy_all.at[spot + 1], partner)
        for spot, partner in enumerate(partners)
    ]
    kinds_copies = [
        send_kinds(spot, r.modulation, r.kinds_all.at[spot + 1], partner)
        for spot, partner in enumerate(partners)
    ]
    for copy in noisy_copies:
        copy.start()
    r.noisy_all[0] = r.noisy[...]

    oz, ox = Sender(r.oz_s, r.oz_r), Sender(r.ox_s, r.ox_r)
    out_place = r.out_weight.at[pl.ds(pl.multiple_of(x * rows, 16), rows)]
    owner = z == m
    load_out.wait()

    def out_along(step):
        return oz(step - 1, out_place, out_place, at_dp(lax.rem(z + step, depth) * NX + x))

    out_aside = ox(0, out_place, out_place, at_dp(side))

    @pl.when(owner)
    def _():
        r.out_weight[pl.ds(pl.multiple_of(x * rows, 16), rows)] = r.out_low[...].astype(bfloat)
        for step in range(1, depth):
            out_along(step).start()
        out_aside.start()


    for part in range(2):
        for which in range(3):
            own = r.ff_shard.at[which, :, pl.ds(half * part, half)]
            fz(
                (part, 0, which),
                own,
                ff_block(d, part, which),
                at_dp(up if part == 0 else down),
            ).start()
            fx((part, 0, which), own, ff_block(d, part, which), at_dp(side)).start()

    loop(1, everyone, lambda step: facts_copy(step).wait())
    facts_all = r.facts_all[...]
    sinus = jnp.concatenate([facts_all[:, 0], facts_all[:, 1]], axis=1).astype(bfloat)
    labels = facts_all[:, 2, 0:1]
    time_pre = (
        jnp.dot(sinus, r.time_first[...], preferred_element_type=single) + r.first_bias[...]
    )
    r.time_pre[...] = time_pre
    time_act = (time_pre * jax.nn.sigmoid(time_pre)).astype(bfloat)
    send_time = Sender(r.time_s, r.time_r)

    def time_copy(step):
        peer = lax.rem(d + step, n_data)
        return send_time(
            step - 1, r.time_send.at[peer], r.time_recv.at[d], at_dp(peer)
        )

    load_time.wait()
    time_part = jnp.dot(time_act, r.time_low[...].astype(bfloat), preferred_element_type=single)
    for spot in range(n_data):
        r.time_send[spot] = time_part[:, spot * rows : (spot + 1) * rows]
    loop(1, n_data, lambda step: time_copy(step).start())
    r.time_recv[d] = r.time_send[d]

    def qkv_service(step):
        for part in range(2):
            qkv_along(step, part).wait_recv()
            if step < depth - 1:
                qkv_along(step + 1, part).start()
            qkv_aside(step, part).start()

    qkv_service(1)
    onehot = (
        labels == lax.broadcasted_iota(jnp.int32, (everyone, CLASSES + 1), 1).astype(single)
    ).astype(bfloat)
    picked = jnp.dot(onehot, r.class_table[...], preferred_element_type=single)
    load_mod.wait()

    loop(1, n_data, lambda step: time_copy(step).wait())
    condition = jnp.sum(r.time_recv[...], axis=0) + r.second_bias[...] + picked
    r.condition[...] = condition
    cond_act = (condition * jax.nn.sigmoid(condition)).astype(bfloat)
    pick = (
        lax.broadcasted_iota(jnp.int32, (n_data, everyone), 1)
        == lax.broadcasted_iota(jnp.int32, (n_data, everyone), 0) * n_model + m
    ).astype(bfloat)
    cond_rank = jnp.dot(pick, cond_act, preferred_element_type=single).astype(bfloat)
    for kind in range(8):
        block = jnp.dot(
            cond_rank,
            r.mod_low[:, kind * D : (kind + 1) * D].astype(bfloat),
            preferred_element_type=single,
        )
        for spot in range(n_data):
            r.mod_send[spot, kind : kind + 1] = block[spot : spot + 1]
    send_mods = Sender(r.mods_s, r.mods_r)

    def mods_copy(step):
        peer = lax.rem(d + step, n_data)
        return send_mods(step - 1, r.mod_send.at[peer], r.mod_recv.at[d], at_dp(peer))

    loop(1, n_data, lambda step: mods_copy(step).start())
    r.mod_recv[d] = r.mod_send[d]
    def ff_service(step, which):
        for part in range(2):
            ff_along(step, part, which).wait_recv()
            if step < depth - 1:
                ff_along(step + 1, part, which).start()
            ff_aside(step, part, which).start()

    qkv_service(2)
    ff_service(1, 0)
    loop(1, n_data, lambda step: small_copy(step).wait())
    trig_far.wait_recv()
    trig_on.start()
    hidden = (
        lax.dot_general(
            r.noisy[...],
            r.small_all[:, 0:CH],
            (((1,), (1,)), ((), ())),
            preferred_element_type=single,
        )
        + r.patch_bias[...]
    )
    r.hidden[...] = hidden
    loop(1, n_data, lambda step: mods_copy(step).wait())
    modulation = jnp.sum(r.mod_recv[...], axis=0) + r.mod_bias[...]
    r.modulation[...] = modulation

    def kind_of(kind):
        return r.modulation[kind : kind + 1]

    for copy in kinds_copies:
        copy.start()
    r.kinds_all[0] = modulation
    qkv_service(3)
    ff_service(1, 1)
    ff_service(1, 2)

    @pl.when(jnp.logical_not(owner))
    def _():
        oz(
            lax.rem(z + depth - m, depth) - 1, out_place, out_place, at_dp(up)
        ).wait_recv()
        out_aside.start()

    for part in range(2):
        for step in range(depth):
            qkv_aside(step, part).wait_recv()
    for copy in noisy_copies + kinds_copies:
        copy.wait_recv()
    trig_near.wait_recv()
    trig_on.wait_recv()

    def image_body(step, carry):
        image = n_model - 1 - step
        start_rows = (
            lax.dot_general(
                r.noisy_all[image],
                r.small_all[:, 0:CH],
                (((1,), (1,)), ((), ())),
                preferred_element_type=single,
            )
            + r.patch_bias[...]
        )
        r.one_rows[image] = modulate_rows(
            start_rows, r.kinds_all[image, 0:1], r.kinds_all[image, 1:2]
        ).astype(bfloat)
        r.qkv[...] = (
            jnp.dot(r.one_rows[image], r.qkv_weight[...], preferred_element_type=single)
            + r.qkv_bias[...]
        )
        rank = (
            2 * lax.rem(lax.div(m, 2) + lax.div(image, 2), 2)
            + lax.rem(lax.rem(m, 2) + lax.rem(image, 2), 2)
        )
        count = r.facts_all[d * n_model + rank, 2:3, 1:2]
        mask = lax.broadcasted_iota(jnp.int32, (1, length), 1).astype(single) < count
        cosine, sine = r.trig_all[image, 0], r.trig_all[image, 1]
        totals = []
        for head in range(heads):
            start = head * HDIM

            def part(which):
                return r.qkv[:, which * head_cols + start : which * head_cols + start + HDIM]

            raw_q, raw_k = part(0), part(1)
            query = (raw_q * cosine + swapped(raw_q) * sine).astype(bfloat)
            key = (raw_k * cosine + swapped(raw_k) * sine).astype(bfloat)
            value = part(2).astype(bfloat)
            for which, kept in enumerate((query, key, value)):
                low = which * head_cols + start
                r.low[image, :, low : low + HDIM] = kept
            scores = lax.dot_general(
                query, key, (((1,), (1,)), ((), ())), preferred_element_type=single
            ) * (1.0 / math.sqrt(HDIM))
            scores = jnp.where(mask, scores, -1e30)
            row_max = jnp.max(scores, axis=-1, keepdims=True)
            exponent = jnp.exp(scores - row_max)
            row_sum = jnp.sum(exponent, axis=-1, keepdims=True)
            probs = exponent / row_sum
            r.attended[image, :, start : start + HDIM] = jnp.dot(
                probs.astype(bfloat), value, preferred_element_type=single
            ).astype(bfloat)
            totals.append(row_max + jnp.log(row_sum))
        r.totals[image] = jnp.concatenate(totals, axis=1)
        return carry

    lax.fori_loop(0, 2, image_body, 0)

    @pl.when(owner)
    def _():
        for step in range(1, depth):
            out_along(step).wait_send()

    out_aside.wait()

    def partial(image):
        return jnp.dot(r.attended[image], r.out_weight[...], preferred_element_type=single)

    send_part = Sender(r.part_s, r.part_r)
    to_core = send_part(0, r.parts_send.at[0], r.parts_recv.at[0], at_mlp(1))
    to_far = send_part(1, r.parts_send.at[1], r.parts_recv.at[1], at_mlp(2))
    to_near = send_part(2, r.parts_send.at[2], r.parts_recv.at[2], at_mlp(1))
    r.parts_send[0] = partial(3).astype(bfloat)
    to_core.start()
    r.branch[...] = partial(2)
    to_core.wait_recv()
    r.parts_send[1] = (r.branch[...] + r.parts_recv[0].astype(single)).astype(bfloat)
    to_far.start()
    for which in range(3):
        ff_service(2, which)
    lax.fori_loop(2, n_model, image_body, 0)
    leaves = [
        pltpu.make_async_copy(source, target, r.leave_sem.at[spot])
        for spot, (source, target) in enumerate(
            (
                (r.one_rows, r.one_rows_out),
                (r.qkv_weight, r.qkv_weight_out),
                (r.out_weight, r.out_weight_out),
                (r.low, r.low_out),
                (r.attended, r.attended_out),
                (r.trig_all, r.trig_all_out),
            )
        )
    ]
    for leave in leaves:
        leave.start()
    r.parts_send[2] = partial(1).astype(bfloat)
    to_near.start()
    own_part = partial(0) + r.out_bias[...]
    ff_service(3, 0)
    to_near.wait_recv()
    to_far.wait_recv()
    branch = own_part + r.parts_recv[2].astype(single) + r.parts_recv[1].astype(single)
    r.branch[...] = branch
    hidden_mid = r.hidden[...] + kind_of(2) * branch
    r.hidden_mid[...] = hidden_mid
    r.two_rows[0] = modulate_rows(hidden_mid, kind_of(3), kind_of(4)).astype(bfloat)
    two_near, two_far, two_on = spread(Sender(r.two_s, r.two_r), r.two_rows)
    two_far.start()
    two_near.start()
    ff_service(3, 1)
    ff_service(3, 2)
    two_far.wait_recv()
    two_on.start()

    own_ff.wait()
    for leave in leaves:
        leave.wait()
    for part in range(2):
        for step in range(depth):
            for which in range(3):
                ff_aside(step, part, which).wait()
            qkv_aside(step, part).wait_send()
            if step:
                for which in range(3):
                    ff_along(step, part, which).wait_send()
                qkv_along(step, part).wait_send()
    for copy in (two_near, two_on):
        copy.wait()
    two_far.wait_send()
    for copy in (trig_near, trig_far, trig_on, to_core, to_far, to_near):
        copy.wait_send()
    for copy in noisy_copies + kinds_copies:
        copy.wait_send()


def forward_all(values, sizes, collective):
    n_data, n_model = sizes
    bfloat, single = jnp.bfloat16, jnp.float32
    everyone = n_data * n_model
    rows = D // n_data
    heads = HEADS // n_model
    head_cols = heads * HDIM
    length = values.noisy.shape[0]
    units = values.ff_shard.shape[2]
    depth = n_data // NX
    shapes = dict(
        facts_all=((everyone, 8, 128), single),
        trig_all_out=((n_model, 2, length, HDIM), single),
        small_all=((D, 128), bfloat),
        time_pre=((everyone, rows), single),
        condition=((everyone, rows), single),
        modulation=((8, D), single),
        hidden=((length, D), single),
        one_rows_out=((n_model, length, D), bfloat),
        qkv_weight_out=((D, 3 * head_cols), bfloat),
        out_weight_out=((head_cols, D), bfloat),
        ff=((3, D, units), bfloat),
        low_out=((n_model, length, 3 * head_cols), bfloat),
        attended_out=((n_model, length, head_cols), bfloat),
        totals=((n_model, length, heads), single),
        branch=((length, D), single),
        hidden_mid=((length, D), single),
        two_rows=((n_model, length, D), bfloat),
    )
    dma = pltpu.SemaphoreType.DMA
    scratch = dict(
        time_send=pltpu.VMEM((n_data, everyone, rows), single),
        time_recv=pltpu.VMEM((n_data, everyone, rows), single),
        mod_send=pltpu.VMEM((n_data, 8, D), single),
        mod_recv=pltpu.VMEM((n_data, 8, D), single),
        mod_low=pltpu.VMEM((rows, 8 * D), single),
        time_low=pltpu.VMEM((rows, D), single),
        out_low=pltpu.VMEM((rows, D), single),
        qkv=pltpu.VMEM((length, 3 * head_cols), single),
        noisy_all=pltpu.VMEM((n_model, length, CH), bfloat),
        kinds_all=pltpu.VMEM((n_model, 8, D), single),
        parts_send=pltpu.VMEM((3, length, D), bfloat),
        parts_recv=pltpu.VMEM((3, length, D), bfloat),
        local_sem=dma((4,)),
        leave_sem=dma((6,)),
    )
    counts = dict(
        facts=(everyone - 1,),
        small=(n_data - 1,),
        time=(n_data - 1,),
        mods=(n_data - 1,),
        trig=(3,),
        noisy=(3,),
        kinds=(3,),
        two=(3,),
        part=(3,),
        qz=(2, depth - 1),
        qx=(2, depth),
        oz=(depth - 1,),
        ox=(1,),
        fz=(2, depth - 1, 3),
        fx=(2, depth, 3),
    )
    for name, count in counts.items():
        scratch[name + "_s"] = dma(count)
        scratch[name + "_r"] = dma(count)
    for name in ForwardOut._fields:
        if name.endswith("_out"):
            scratch[name[:-4]] = pltpu.VMEM(*shapes[name])
    far = {"matrices", "ff_shard", "ff"}

    def space(name):
        outside = name in far or name.endswith("_out")
        return pl.BlockSpec(memory_space=pl.ANY if outside else pltpu.VMEM)

    outs = pl.pallas_call(
        functools.partial(forward_kernel, sizes),
        out_shape=[jax.ShapeDtypeStruct(*shapes[name]) for name in ForwardOut._fields],
        in_specs=[space(name) for name in ForwardIn._fields],
        out_specs=[space(name) for name in ForwardOut._fields],
        scratch_shapes=[scratch[name] for name in ForwardScratch._fields],
        compiler_params=pltpu.CompilerParams(
            collective_id=collective, has_side_effects=True, vmem_limit_bytes=56 * 2**20
        ),
    )(*values)
    return ForwardOut(*outs)


class BackIn(NamedTuple):
    ff: Any
    two_rows: Any
    hidden_mid: Any
    hidden: Any
    branch: Any
    modulation: Any
    small_all: Any
    final_bias: Any
    clean: Any
    noise: Any
    consts: Any
    valid: Any
    noisy: Any
    low: Any
    totals: Any
    trig_all: Any
    facts_all: Any
    attended: Any
    one_rows: Any
    qkv_weight: Any
    out_weight: Any
    matrices: Any
    time_pre: Any
    condition: Any


class BackOut(NamedTuple):
    bias_rows: Any
    own: Any
    norm: Any
    factor: Any
    loss_sum: Any
    dmod: Any
    dtime: Any
    d_condition: Any
    d_time_pre: Any
    grad_ff: Any
    grad_qkv: Any
    grad_out: Any


class BackScratch(NamedTuple):
    time_low: Any
    late: Any
    d_modulation: Any
    local: Any
    sums: Any
    sums_recv: Any
    pay: Any
    dmod_row: Any
    dmod_all: Any
    dmod_wide: Any
    dtime_mine: Any
    dtime_recv: Any
    dtime_wide: Any
    loss: Any
    sm_s: Any
    sm_r: Any
    dl_s: Any
    dl_r: Any
    dt_s: Any
    dt_r: Any
    lt_s: Any
    lt_r: Any
    d_end: Any
    dm_rows: Any
    db_rows: Any
    hold_far: Any
    hold_near: Any
    parts_send: Any
    parts_recv: Any
    normed_end: Any
    g_ff: Any
    x_ff: Any
    z_ff: Any
    g_qkv: Any
    x_qkv: Any
    z_qkv: Any
    g_out: Any
    x_out: Any
    z_out: Any
    out_mine: Any
    dm_s: Any
    dm_r: Any
    db_s: Any
    db_r: Any
    pa_s: Any
    pa_r: Any
    pb_s: Any
    pb_r: Any
    pc_s: Any
    pc_r: Any
    fx_s: Any
    fx_r: Any
    fz_s: Any
    fz_r: Any
    qx_s: Any
    qx_r: Any
    qz_s: Any
    qz_r: Any
    ox_s: Any
    ox_r: Any
    oz_s: Any
    oz_r: Any
    qa_s: Any
    qa_r: Any
    oa_s: Any
    oa_r: Any
    local_sem: Any


ROW_CHUNK = 64


def modulate_back(values, grad, scale_by):
    row_mean = jnp.mean(values, axis=-1, keepdims=True)
    centered = values - row_mean
    variance = jnp.mean(centered * centered, axis=-1, keepdims=True)
    inverse = lax.rsqrt(variance + 1e-06)
    normal = centered * inverse
    inner = grad * (1.0 + scale_by)
    back = inverse * (
        inner
        - jnp.mean(inner, axis=-1, keepdims=True)
        - normal * jnp.mean(inner * normal, axis=-1, keepdims=True)
    )
    return back, normal


def fold(values):
    total = values[:8]
    for start in range(8, values.shape[0], 8):
        total = total + values[start : start + 8]
    return total


def back_kernel(sizes, total_images, *refs):
    r = named(BackIn, BackOut, BackScratch, refs)
    bfloat, single = jnp.bfloat16, jnp.float32
    n_data, n_model = sizes
    d, m, z, x = device_parts()
    depth = n_data // NX
    rows = D // n_data
    heads = HEADS // n_model
    head_cols = heads * HDIM
    length = r.clean.shape[0]
    units = r.ff.shape[2]
    half = units // 2

    def at_dp(spot):
        return (spot, m)

    near_rank = m + 1 - 2 * lax.rem(m, 2)
    far_rank = lax.rem(m + 2, 4)

    def at_mlp(bit):
        return (d, near_rank if bit == 1 else far_rank)

    up = lax.rem(z + 1, depth) * NX + x
    down = lax.rem(z + depth - 1, depth) * NX + x
    side = z * NX + 1 - x
    barrier = pltpu.get_barrier_semaphore()
    everyone = n_data * n_model
    me = d * n_model + m

    def loop(first, last, body):
        def step_body(step, carry):
            body(step)
            return carry

        lax.fori_loop(first, last, step_body, 0)

    def anyone(step):
        peer = lax.rem(me + step, everyone)
        return peer, (lax.div(peer, n_model), lax.rem(peer, n_model))

    loop(
        1,
        everyone,
        lambda step: pl.semaphore_signal(
            barrier, inc=1, device_id=anyone(step)[1], device_id_type=MESH_IDS
        ),
    )
    pl.semaphore_wait(barrier, everyone - 1)

    def chunks(body, carry, amount=ROW_CHUNK, count=length):
        def step_body(step, held):
            return body(pl.ds(pl.multiple_of(step * amount, amount), amount), held)

        return lax.fori_loop(0, count // amount, step_body, carry)

    def kind_of(kind):
        return r.modulation[kind : kind + 1]

    def dot(left, right, dims):
        return lax.dot_general(left, right, (dims, ((), ())), preferred_element_type=single)

    zeros = jnp.zeros((8, D), single)

    def spread(send, buffer):
        return (
            send(0, buffer.at[0], buffer.at[1], at_mlp(1)),
            send(1, buffer.at[0], buffer.at[2], at_mlp(2)),
            send(2, buffer.at[2], buffer.at[3], at_mlp(1)),
        )

    def part_copies(*sems):
        send = Sender(*sems)
        return tuple(
            send(spot, r.parts_send.at[spot], r.parts_recv.at[spot], at_mlp(bit))
            for spot, bit in ((0, 1), (1, 2), (2, 1))
        )

    def add_far(copies):
        to_core, to_far, to_near = copies
        to_core.wait_recv()

        def body(at, held):
            r.parts_send[1, at] = (
                r.hold_far[at] + r.parts_recv[0, at].astype(single)
            ).astype(bfloat)
            return held

        chunks(body, 0)
        to_far.start()

    fx, fz = Sender(r.fx_s, r.fx_r), Sender(r.fz_s, r.fz_r)
    qx, qz = Sender(r.qx_s, r.qx_r), Sender(r.qz_s, r.qz_r)

    def block_rows(z_spot, x_spot):
        return pl.ds(pl.multiple_of((z_spot * NX + x_spot) * rows, 16), rows)

    def ff_aside(which, step):
        z_spot = lax.rem(z + step, depth)
        return fx(
            (which, step),
            r.g_ff.at[which, block_rows(z_spot, 1 - x)],
            r.x_ff.at[which, z_spot],
            at_dp(side),
        )

    def target_of(step, part):
        return lax.rem(z + (depth - 1 - step if part == 0 else 1 + step), depth)

    def ff_along(which, step, part):
        lanes = pl.ds(half * part, half)
        return fz(
            (which, step, part),
            r.g_ff.at[which, block_rows(target_of(step, part), x), lanes],
            r.z_ff.at[which, step, part],
            at_dp(up if part == 0 else down),
        )

    def ff_start(which):
        for step in (3, 1, 2, 0):
            ff_aside(which, step).start()

    def ff_absorb(which, step):
        ff_aside(which, step).wait_recv()
        z_spot = lax.rem(z + step, depth)
        at = block_rows(z_spot, x)
        r.g_ff[which, at] = (
            r.g_ff[which, at].astype(single) + r.x_ff[which, z_spot].astype(single)
        ).astype(bfloat)

    def ff_beside(which):
        ff_absorb(which, 3)
        ff_absorb(which, 1)
        for part in range(2):
            ff_along(which, 0, part).start()

    def ff_service(which, step):
        if step != 1:
            ff_absorb(which, 2 - step)
        for part in range(2):
            ff_along(which, step, part).wait_recv()
            lanes = pl.ds(half * part, half)
            at = block_rows(target_of(step + 1, part), x)
            running = r.z_ff[which, step, part].astype(single) + r.g_ff[
                which, at, lanes
            ].astype(single)
            if step < depth - 2:
                r.g_ff[which, at, lanes] = running.astype(bfloat)
                ff_along(which, step + 1, part).start()
            else:
                r.grad_ff[which, :, lanes] = running

    tops = (pl.ds(0, 80), pl.ds(80, rows - 80))

    def part_rows(z_spot, part):
        start = (z_spot * NX + x) * rows + 80 * part
        return pl.ds(pl.multiple_of(start, 16), 80 if part == 0 else rows - 80)

    def qkv_aside(step):
        z_spot = lax.rem(z + step, depth)
        return qx(
            step,
            r.g_qkv.at[block_rows(z_spot, 1 - x)],
            r.x_qkv.at[z_spot],
            at_dp(side),
        )

    def qkv_along(step, part):
        return qz(
            (step, part),
            r.g_qkv.at[part_rows(target_of(step, part), part)],
            r.z_qkv.at[step, tops[part]],
            at_dp(up if part == 0 else down),
        )

    def qkv_absorb(step):
        qkv_aside(step).wait_recv()
        z_spot = lax.rem(z + step, depth)
        at = block_rows(z_spot, x)
        r.g_qkv[at] = (r.g_qkv[at].astype(single) + r.x_qkv[z_spot].astype(single)).astype(bfloat)

    def qkv_beside():
        qkv_absorb(3)
        qkv_absorb(1)
        for part in range(2):
            qkv_along(0, part).start()

    def qkv_service(step):
        if step != 1:
            qkv_absorb(2 - step)
        for part in range(2):
            qkv_along(step, part).wait_recv()
            at = part_rows(target_of(step + 1, part), part)
            running = (
                r.z_qkv[step, tops[part]].astype(single) + r.g_qkv[at].astype(single)
            ).astype(bfloat)
            if step < depth - 2:
                r.g_qkv[at] = running
                qkv_along(step + 1, part).start()
            else:
                r.grad_qkv[0, tops[part]] = running

    dm_near, dm_far, dm_on = spread(Sender(r.dm_s, r.dm_r), r.dm_rows)
    first_parts = part_copies(r.pa_s, r.pa_r)
    second_parts = part_copies(r.pb_s, r.pb_r)
    third_parts = part_copies(r.pc_s, r.pc_r)

    def swiglu(ff, two_rows, gates, ups, acts, d_gates, d_ups):
        load_ff = pltpu.make_async_copy(r.ff, ff, r.local_sem.at[0])
        load_two = pltpu.make_async_copy(r.two_rows, two_rows, r.local_sem.at[1])
        load_ff.start()
        load_two.start()
        load_two.wait()
        load_ff.wait()
        wide = 2 * length

        def rows_of(ref, which):
            return ref[2 * which : 2 * which + 2].reshape(wide, D)

        def inner(which):
            part = rows_of(two_rows, which)
            spot = pl.ds(which * wide, wide)
            gates[spot] = dot(part, ff[0], ((1,), (0,)))
            ups[spot] = dot(part, ff[1], ((1,), (0,)))

            def body(at, held):
                at = pl.ds(pl.multiple_of(at.start + which * wide, 32), 32)
                gate = gates[at]
                acts[at] = (gate * jax.nn.sigmoid(gate) * ups[at]).astype(bfloat)
                return held

            chunks(body, 0, 32, wide)

        def outer(image):
            return dot(acts[image * length : (image + 1) * length], ff[2], ((1,), (1,)))

        inner(1)
        r.parts_send[0] = outer(3).astype(bfloat)
        first_parts[0].start()
        r.hold_far[...] = outer(2)
        add_far(first_parts)
        inner(0)
        r.parts_send[2] = outer(1).astype(bfloat)
        first_parts[2].start()
        r.hold_near[...] = outer(0)
        first_parts[2].wait_recv()
        first_parts[1].wait_recv()

        def ending(at, held):
            mixed = (
                r.hold_near[at]
                + r.parts_recv[2, at].astype(single)
                + r.parts_recv[1, at].astype(single)
            )
            r.d_end[at] = mixed
            end = r.hidden_mid[at] + kind_of(5) * mixed
            r.normed_end[at] = modulate_rows(end, kind_of(6), kind_of(7)).astype(bfloat)
            return held

        chunks(ending, 0)

        eps_weight, var_weight = r.small_all[:, 32:48], r.small_all[:, 48:64]
        normed_end = r.normed_end[...]
        eps = dot(normed_end, eps_weight, ((1,), (0,))) + r.final_bias[0:1]
        var = dot(normed_end, var_weight, ((1,), (0,))) + r.final_bias[1:2]
        clean, noise, valid = r.clean[...], r.noise[...], r.valid[...]
        root_bar, root_rest, log_beta, post_log, coefficient = (
            r.consts[0:1, spot : spot + 1] for spot in range(5)
        )
        noisy = root_bar * clean + root_rest * noise
        fraction = (var + 1.0) * 0.5
        model_log = fraction * log_beta + (1.0 - fraction) * post_log
        start_est = (noisy - root_rest * eps) / root_bar
        gap = coefficient * (clean - start_est)
        ratio = jnp.exp(post_log - model_log)
        gap_part = gap * gap * jnp.exp(-model_log)
        scale_by = 0.5 / math.log(2.0)
        terms = (eps - noise) * (eps - noise) + scale_by * (
            -1.0 + model_log - post_log + ratio + gap_part
        )
        terms = jnp.where(valid > 0.0, terms, 0.0)
        r.loss[...] = jnp.sum(jnp.sum(terms, axis=1, keepdims=True), axis=0, keepdims=True)
        d_eps = 2.0 * (eps - noise) + 2.0 * scale_by * gap * jnp.exp(-model_log) * (
            coefficient * root_rest / root_bar
        )
        d_var = scale_by * (1.0 - ratio - gap_part) * (0.5 * (log_beta - post_log))
        share = 1.0 / total_images
        d_eps = jnp.where(valid > 0.0, d_eps * share, 0.0).astype(bfloat)
        d_var = jnp.where(valid > 0.0, d_var * share, 0.0).astype(bfloat)
        r.local[48:56] = zeros
        r.local[54:55, 0:CH] = jnp.sum(d_eps.astype(single), axis=0, keepdims=True)
        r.local[54:55, CH : 2 * CH] = jnp.sum(d_var.astype(single), axis=0, keepdims=True)
        r.local[CH : 2 * CH] = dot(d_eps, normed_end, ((0,), (0,)))
        r.local[2 * CH : 3 * CH] = dot(d_var, normed_end, ((0,), (0,)))
        r.hold_far[...] = dot(d_eps, eps_weight, ((1,), (1,))) + dot(
            d_var, var_weight, ((1,), (1,))
        )

        def end_back(at, held):
            shift_sum, scale_sum, gate_sum = held
            mixed, grad = r.d_end[at], r.hold_far[at]
            end = r.hidden_mid[at] + kind_of(5) * mixed
            back, normal = modulate_back(end, grad, kind_of(7))
            r.d_end[at] = back
            r.dm_rows[0, at] = (kind_of(5) * back).astype(bfloat)
            return (
                shift_sum + fold(grad),
                scale_sum + fold(grad * normal),
                gate_sum + fold(mixed * back),
            )

        shift_sum, scale_sum, gate_sum = chunks(end_back, (zeros, zeros, zeros))
        dm_far.start()
        dm_near.start()
        for kind, value in ((6, shift_sum), (7, scale_sum), (5, gate_sum)):
            r.d_modulation[kind : kind + 1] = jnp.sum(value, axis=0, keepdims=True)

        def inner_back(which):
            spot = pl.ds(which * wide, wide)
            gradient = dot(rows_of(r.dm_rows, which), ff[2], ((1,), (0,)))
            gate, up_val = gates[spot], ups[spot]
            sigma = jax.nn.sigmoid(gate)
            d_ups[spot] = (gradient * gate * sigma).astype(bfloat)
            d_gates[spot] = (gradient * up_val * (sigma * (1.0 + gate * (1.0 - sigma)))).astype(
                bfloat
            )

        def outer_back(image):
            spot = pl.ds(image * length, length)
            return dot(d_gates[spot], ff[0], ((1,), (1,))) + dot(d_ups[spot], ff[1], ((1,), (1,)))

        def ff_grad(which, left, right):
            for part in range(2):
                lanes = slice(half * part, half * part + half)
                r.g_ff[which, :, lanes] = dot(left, right[:, lanes], ((0,), (0,))).astype(bfloat)

        dm_near.wait_recv()
        inner_back(0)
        dm_far.wait_recv()
        dm_on.start()
        dm_on.wait_recv()
        inner_back(1)
        for copy in first_parts:
            copy.wait_send()
        r.parts_send[0] = outer_back(3).astype(bfloat)
        second_parts[0].start()
        r.hold_far[...] = outer_back(2)
        add_far(second_parts)
        ff_grad(2, r.dm_rows[...].reshape(2 * wide, D), acts)
        ff_start(2)
        r.parts_send[2] = outer_back(1).astype(bfloat)
        second_parts[2].start()
        r.hold_near[...] = outer_back(0)
        flat = two_rows[...].reshape(2 * wide, D)
        ff_grad(0, flat, d_gates)
        ff_start(0)
        ff_grad(1, flat, d_ups)
        ff_start(1)

    pl.run_scoped(
        swiglu,
        pltpu.VMEM((3, D, units), bfloat),
        pltpu.VMEM((n_model, length, D), bfloat),
        pltpu.VMEM((n_model * length, units), single),
        pltpu.VMEM((n_model * length, units), single),
        pltpu.VMEM((n_model * length, units), bfloat),
        pltpu.VMEM((n_model * length, units), bfloat),
        pltpu.VMEM((n_model * length, units), bfloat),
    )

    db_near, db_far, db_on = spread(Sender(r.db_s, r.db_r), r.db_rows)
    ox, oz = Sender(r.ox_s, r.ox_r), Sender(r.oz_s, r.oz_r)
    out_aside = ox(0, r.g_out.at[1 - x], r.x_out, at_dp(side))
    owner = z == m
    behind = lax.rem(z + depth - m, depth)
    out_along = oz(
        lax.rem(behind + depth - 1, depth),
        r.g_out.at[x],
        r.z_out.at[lax.rem(behind + depth - 1, depth)],
        at_dp(m * NX + x),
    )

    def attend(low, attended, trig, one_rows, qkv_weight, out_weight, d_attended, d_qkv):
        loads = []
        for spot, (source, target) in enumerate(
            (
                (r.out_weight, out_weight),
                (r.low, low),
                (r.trig_all, trig),
                (r.attended, attended),
                (r.one_rows, one_rows),
                (r.qkv_weight, qkv_weight),
            )
        ):
            load = pltpu.make_async_copy(source, target, r.local_sem.at[2 + spot])
            load.start()
            loads.append(load)
        second_parts[2].wait_recv()
        second_parts[1].wait_recv()

        def mid_back(at, held):
            shift_sum, scale_sum, gate_sum, branch_sum = held
            grad = (
                r.hold_near[at]
                + r.parts_recv[2, at].astype(single)
                + r.parts_recv[1, at].astype(single)
            )
            back, normal = modulate_back(r.hidden_mid[at], grad, kind_of(4))
            total = r.d_end[at] + back
            r.d_end[at] = total
            d_branch = (kind_of(2) * total).astype(bfloat)
            r.db_rows[0, at] = d_branch
            return (
                shift_sum + fold(grad),
                scale_sum + fold(grad * normal),
                gate_sum + fold(r.branch[at] * total),
                branch_sum + fold(d_branch.astype(single)),
            )

        sums = chunks(mid_back, (zeros, zeros, zeros, zeros))
        db_far.start()
        db_near.start()
        for kind, value in zip((3, 4, 2), sums):
            r.d_modulation[kind : kind + 1] = jnp.sum(value, axis=0, keepdims=True)
        r.local[49:50] = jnp.sum(sums[3], axis=0, keepdims=True)
        for load in loads:
            load.wait()

        def image_body(image, carry):
            d_attended[...] = dot(
                r.db_rows[image], out_weight[...], ((1,), (1,))
            ).astype(bfloat)
            rank = (
                2 * lax.rem(lax.div(m, 2) + lax.div(image, 2), 2)
                + lax.rem(lax.rem(m, 2) + lax.rem(image, 2), 2)
            )
            count = r.facts_all[d * n_model + rank, 2:3, 1:2]
            mask = lax.broadcasted_iota(jnp.int32, (1, length), 1).astype(single) < count
            cosine, sine = trig[image, 0], trig[image, 1]
            scale_by = 1.0 / math.sqrt(HDIM)
            for head in range(heads):
                start = head * HDIM

                def spot(which):
                    begin = which * head_cols + start
                    return slice(begin, begin + HDIM)

                query, key, value = (low[image, :, spot(which)] for which in range(3))
                grad = d_attended[:, start : start + HDIM]
                scores = dot(query, key, ((1,), (1,))) * scale_by
                scores = jnp.where(mask, scores, -1e30)
                probs = jnp.exp(scores - r.totals[image, :, head : head + 1])
                d_probs = dot(grad, value, ((1,), (1,)))
                row = jnp.sum(probs * d_probs, axis=-1, keepdims=True)
                d_scores = (probs * (d_probs - row)).astype(bfloat)
                d_query = dot(d_scores, key, ((1,), (0,))) * scale_by
                d_key = dot(d_scores, query, ((0,), (0,))) * scale_by
                d_value = dot(probs.astype(bfloat), grad, ((0,), (0,)))
                for which, turned in ((0, d_query), (1, d_key)):
                    back = turned * cosine + swapped(turned * sine)
                    d_qkv[image, :, spot(which)] = back.astype(bfloat)
                d_qkv[image, :, spot(2)] = d_value.astype(bfloat)
            return carry

        db_near.wait_recv()
        lax.fori_loop(0, 2, image_body, 0)
        db_far.wait_recv()
        db_on.start()
        ff_beside(2)
        db_on.wait_recv()
        lax.fori_loop(2, n_model, image_body, 0)

        def one_part(image):
            return dot(d_qkv[image], qkv_weight[...], ((1,), (1,)))

        for copy in second_parts:
            copy.wait_send()
        r.parts_send[0] = one_part(3).astype(bfloat)
        third_parts[0].start()
        r.hold_far[...] = one_part(2)
        add_far(third_parts)
        ff_beside(0)
        ff_service(2, 0)
        r.parts_send[2] = one_part(1).astype(bfloat)
        third_parts[2].start()
        r.hold_near[...] = one_part(0)
        flat_grad = d_qkv[...].reshape(n_model * length, 3 * head_cols)
        r.g_qkv[...] = dot(
            one_rows[...].reshape(n_model * length, D), flat_grad, ((0,), (0,))
        ).astype(bfloat)
        for step in (3, 1, 2, 0):
            qkv_aside(step).start()
        r.g_out[...] = (
            dot(
                attended[...].reshape(n_model * length, head_cols),
                r.db_rows[...].reshape(n_model * length, D),
                ((0,), (0,)),
            )
            .astype(bfloat)
            .reshape(NX, rows, D)
        )
        out_aside.start()
        ones = jnp.ones((8, n_model * length), bfloat)
        qkv_sum = dot(ones, flat_grad, ((1,), (0,)))[0:1]
        for rank in range(n_model):
            r.local[50 + rank : 51 + rank, 0 : 3 * head_cols] = jnp.where(m == rank, qkv_sum, 0.0)

    pl.run_scoped(
        attend,
        pltpu.VMEM((n_model, length, 3 * head_cols), bfloat),
        pltpu.VMEM((n_model, length, head_cols), bfloat),
        pltpu.VMEM((n_model, 2, length, HDIM), single),
        pltpu.VMEM((n_model, length, D), bfloat),
        pltpu.VMEM((D, 3 * head_cols), bfloat),
        pltpu.VMEM((head_cols, D), bfloat),
        pltpu.VMEM((length, head_cols), bfloat),
        pltpu.VMEM((n_model, length, 3 * head_cols), bfloat),
    )
    ff_beside(1)
    ff_service(0, 0)
    ff_service(2, 1)
    third_parts[2].wait_recv()
    third_parts[1].wait_recv()

    def first_back(at, held):
        shift_sum, scale_sum, hidden_sum = held
        grad = (
            r.hold_near[at]
            + r.parts_recv[2, at].astype(single)
            + r.parts_recv[1, at].astype(single)
        )
        back, normal = modulate_back(r.hidden[at], grad, kind_of(1))
        d_hidden = (r.d_end[at] + back).astype(bfloat)
        r.normed_end[at] = d_hidden
        return (
            shift_sum + fold(grad),
            scale_sum + fold(grad * normal),
            hidden_sum + fold(d_hidden.astype(single)),
        )

    sums = chunks(first_back, (zeros, zeros, zeros))
    for kind in range(2):
        r.d_modulation[kind : kind + 1] = jnp.sum(sums[kind], axis=0, keepdims=True)
    r.local[48:49] = jnp.sum(sums[2], axis=0, keepdims=True)
    r.local[0:CH] = dot(r.noisy[...], r.normed_end[...], ((0,), (0,)))

    for kind in range(8):
        r.dmod_wide[2 * kind : 2 * kind + 1] = r.d_modulation[kind : kind + 1, 0 : D // 2]
        r.dmod_wide[2 * kind + 1 : 2 * kind + 2] = r.d_modulation[kind : kind + 1, D // 2 : D]
    r.dmod_row[...] = r.dmod_wide[...].astype(bfloat)
    r.dmod_all[me] = r.dmod_row[...]
    send_dmod = Sender(r.dl_s, r.dl_r)
    loop(
        1,
        everyone,
        lambda step: send_dmod(
            step - 1, r.dmod_row, r.dmod_all.at[me], anyone(step)[1]
        ).start(),
    )
    tiles = D // 128
    for top in range(7):
        for left in range(tiles):
            r.sums[top * tiles + left] = r.local[8 * top : 8 * top + 8, 128 * left : 128 * left + 128]
    r.sums[7 * tiles] = jnp.zeros((8, 128), single)
    send_sums = Sender(r.sm_s, r.sm_r)

    def sums_copy(step):
        peer, device = anyone(step)
        return send_sums(step - 1, r.sums.at[pl.ds(2 * peer, 2)], r.sums_recv.at[me], device)

    loop(1, everyone, lambda step: sums_copy(step).start())
    r.sums_recv[me] = r.sums[pl.ds(2 * me, 2)]
    ff_service(1, 0)
    qkv_beside()
    out_aside.wait()
    r.g_out[x] = (r.g_out[x].astype(single) + r.x_out[...].astype(single)).astype(bfloat)

    @pl.when(jnp.logical_not(owner))
    def _():
        out_along.start()


    time_pre, condition = r.time_pre[...], r.condition[...]
    sigma_time, sigma_cond = jax.nn.sigmoid(time_pre), jax.nn.sigmoid(condition)
    time_act = (time_pre * sigma_time).astype(bfloat)
    cond_act = (condition * sigma_cond).astype(bfloat)

    def gram(value, precision=None):
        return lax.dot_general(
            value,
            value,
            (((1,), (1,)), ((), ())),
            precision=precision,
            preferred_element_type=single,
        )

    send_dtime = Sender(r.dt_s, r.dt_r)

    def dtime_copy(step):
        return send_dtime(
            step - 1, r.dtime_mine, r.dtime_recv.at[d], at_dp(lax.rem(d + step, n_data))
        )

    def conditioning(mod_weight):
        load = pltpu.make_async_copy(
            r.matrices.at[:, pl.ds(D, 8 * D)], mod_weight, r.local_sem.at[0]
        )
        load.start()
        load_time = pltpu.make_async_copy(
            r.matrices.at[:, pl.ds(0, D)], r.time_low, r.local_sem.at[1]
        )
        load_time.start()
        loop(
            1,
            everyone,
            lambda step: send_dmod(
                step - 1, r.dmod_row, r.dmod_all.at[me], anyone(step)[1]
            ).wait(),
        )
        gathered = r.dmod_all[...].astype(single)
        load.wait()
        load_time.wait()
        d_cond = jnp.zeros((everyone, rows), single)
        mod_gram = jnp.zeros((everyone, everyone), single)
        bias_squares = jnp.zeros((1, 1), single)
        for kind in range(8):
            r.dtime_wide[:, 0 : D // 2] = gathered[:, 2 * kind]
            r.dtime_wide[:, D // 2 : D] = gathered[:, 2 * kind + 1]
            part = r.dtime_wide[...]
            column = jnp.sum(part, axis=0, keepdims=True)
            bias_squares = bias_squares + jnp.sum(column * column, axis=1, keepdims=True)
            r.bias_rows[3 + kind : 4 + kind] = column
            part = part.astype(bfloat)
            r.dmod[kind] = part
            d_cond = d_cond + dot(
                part, mod_weight[:, kind * D : (kind + 1) * D].astype(bfloat), ((1,), (1,))
            )
            mod_gram = mod_gram + gram(part)
        d_condition = d_cond * (sigma_cond * (1.0 + condition * (1.0 - sigma_cond)))
        r.d_condition[...] = d_condition
        r.dtime_mine[...] = d_condition.astype(bfloat)
        loop(1, n_data, lambda step: dtime_copy(step).start())
        r.dtime_recv[d] = r.dtime_mine[...]
        r.pay[2] = jnp.zeros((8, 128), single)
        r.pay[2, 0:1, 0:1] = (
            jnp.sum(jnp.sum(mod_gram * gram(cond_act), axis=1, keepdims=True), axis=0, keepdims=True)
            / n_model
            + bias_squares / everyone
        )

    pl.run_scoped(conditioning, pltpu.VMEM((rows, 8 * D), single))
    ff_service(0, 1)
    ff_service(2, 2)
    qkv_service(0)
    ff_service(1, 1)
    ff_service(0, 2)
    qkv_service(1)
    loop(1, n_data, lambda step: dtime_copy(step).wait())
    for spot in range(n_data):
        r.dtime_wide[:, spot * rows : (spot + 1) * rows] = r.dtime_recv[spot].astype(single)
    dtime = r.dtime_wide[...]
    column = jnp.sum(dtime, axis=0, keepdims=True)
    r.bias_rows[2:3] = column
    dtime = dtime.astype(bfloat)
    r.dtime[...] = dtime
    d_time_pre = dot(dtime, r.time_low[...].astype(bfloat), ((1,), (1,))) * (
        sigma_time * (1.0 + time_pre * (1.0 - sigma_time))
    )
    r.d_time_pre[...] = d_time_pre
    first_sum = jnp.sum(d_time_pre, axis=0, keepdims=True)
    facts = r.facts_all[...]
    sinus = jnp.concatenate([facts[:, 0], facts[:, 1]], axis=1).astype(bfloat)
    onehot = (
        facts[:, 2, 0:1]
        == lax.broadcasted_iota(jnp.int32, (everyone, CLASSES + 1), 1).astype(single)
    ).astype(bfloat)
    highest = lax.Precision.HIGHEST

    def total_of(value):
        return jnp.sum(jnp.sum(value, axis=1, keepdims=True), axis=0, keepdims=True)

    shared_squares = (
        total_of(gram(time_act) * gram(dtime))
        + total_of(gram(sinus) * gram(d_time_pre, highest))
        + total_of(gram(onehot) * gram(r.d_condition[...], highest))
        + total_of(first_sum * first_sum)
    ) / n_model + total_of(column * column) / everyone
    r.pay[3] = jnp.zeros((8, 128), single)
    r.pay[3, 0:1] = first_sum[:, 0:128]
    r.pay[3, 1:2, 0 : rows - 128] = first_sum[:, 128:rows]
    ff_service(1, 2)
    qkv_service(2)
    qkv_near, qkv_far, qkv_on = spread(Sender(r.qa_s, r.qa_r), r.grad_qkv)
    qkv_far.start()
    qkv_near.start()
    give = Sender(r.oa_s, r.oa_r)
    partners = [(d, near_rank), (d, far_rank), (d, lax.rem(near_rank + 2, 4))]
    gives = [
        give(spot, r.out_mine, r.out_mine, partner) for spot, partner in enumerate(partners)
    ]

    @pl.when(owner)
    def _():
        total = r.g_out[x].astype(single)
        for step in range(depth - 1):
            oz(step, r.g_out.at[x], r.z_out.at[step], at_dp(up)).wait_recv()
            total = total + r.z_out[step].astype(single)
        total = total.astype(bfloat)
        r.out_mine[...] = total
        total = total.astype(single)
        r.pay[2, 0:1, 2:3] = total_of(total * total)
        for copy in gives:
            copy.start()

    loop(1, everyone, lambda step: sums_copy(step).wait())

    def add_sums(step, held):
        return held + r.sums_recv[step]

    chunk = lax.fori_loop(0, everyone, add_sums, jnp.zeros((2, 8, 128), single))
    r.pay[0:2] = chunk
    own_squares = total_of(chunk[0] * chunk[0]) + total_of(chunk[1] * chunk[1])

    def ff_squares(at, held):
        return tuple(
            one + fold(r.grad_ff[which, at] * r.grad_ff[which, at])
            for which, one in enumerate(held)
        )

    block = jnp.zeros((8, units), single)
    for value in chunks(ff_squares, (block, block, block), 16, rows):
        own_squares = own_squares + total_of(value)
    qkv_float = r.grad_qkv[0].astype(single)
    r.pay[2, 0:1, 0:1] = (
        r.pay[2, 0:1, 0:1]
        + shared_squares
        + own_squares
        + r.pay[2, 0:1, 2:3]
        + total_of(qkv_float * qkv_float)
    )
    r.pay[2, 0:1, 1:2] = r.loss[...]
    send_late = Sender(r.lt_s, r.lt_r)

    def late_copy(step):
        return send_late(step - 1, r.pay, r.late.at[me], anyone(step)[1])

    loop(1, everyone, lambda step: late_copy(step).start())
    r.late[me] = r.pay[...]

    for spot, partner in enumerate(partners):

        @pl.when(z == partner[1])
        def _():
            gives[spot].wait_recv()

    qkv_far.wait_recv()
    qkv_on.start()
    r.grad_out[...] = r.out_mine[...]

    @pl.when(owner)
    def _():
        for copy in gives:
            copy.wait_send()

    @pl.when(jnp.logical_not(owner))
    def _():
        out_along.wait_send()

    qkv_near.wait()
    qkv_on.wait()
    qkv_far.wait_send()
    loop(1, everyone, lambda step: late_copy(step).wait())
    for top in range(7):
        for left in range(tiles):
            spot = top * tiles + left
            r.local[8 * top : 8 * top + 8, 128 * left : 128 * left + 128] = r.late[
                spot // 2, spot % 2
            ]
    r.bias_rows[0:1] = r.local[48:49]
    r.bias_rows[14:15] = r.local[49:50]
    r.bias_rows[15:16] = r.local[54:55]
    for spot in range(n_data):
        first = r.late[spot * n_model, 3]
        r.bias_rows[1:2, spot * rows : spot * rows + 128] = first[0:1]
        r.bias_rows[1:2, spot * rows + 128 : (spot + 1) * rows] = first[1:2, 0 : rows - 128]
    for rank in range(n_model):
        for part in range(3):
            r.bias_rows[11 + part : 12 + part, rank * head_cols : (rank + 1) * head_cols] = r.local[
                50 + rank : 51 + rank, part * head_cols : (part + 1) * head_cols
            ]
    for spot in range(n_data):

        @pl.when(d == spot)
        def _():
            r.own[...] = r.local[0 : 3 * CH, spot * rows : (spot + 1) * rows]

    totals = lax.fori_loop(
        0, everyone, lambda step, held: held + r.late[step, 2, 0:1], jnp.zeros((1, 128), single)
    )
    norm = jnp.sqrt(totals[:, 0:1])
    r.norm[...] = norm
    r.factor[...] = jnp.minimum(1.0, CLIP_LIMIT / norm)
    r.loss_sum[...] = totals[:, 1:2]
    for copy in (dm_near, dm_far, dm_on, db_near, db_far, db_on, *third_parts):
        copy.wait_send()
    for step in range(depth):
        qkv_aside(step).wait_send()
        for which in range(3):
            ff_aside(which, step).wait_send()
    for step in range(depth - 1):
        for part in range(2):
            qkv_along(step, part).wait_send()
            for which in range(3):
                ff_along(which, step, part).wait_send()


def backward_all(values, sizes, total_images, collective):
    n_data, n_model = sizes
    bfloat, single = jnp.bfloat16, jnp.float32
    everyone = n_data * n_model
    rows = D // n_data
    heads = HEADS // n_model
    head_cols = heads * HDIM
    length = values.clean.shape[0]
    units = values.ff.shape[2]
    half = units // 2
    depth = n_data // NX
    shapes = dict(
        grad_ff=((3, rows, units), single),
        grad_qkv=((n_model, rows, 3 * head_cols), bfloat),
        grad_out=((rows, D), bfloat),
        bias_rows=((16, D), single),
        own=((3 * CH, rows), single),
        norm=((1, 1), single),
        factor=((1, 1), single),
        loss_sum=((1, 1), single),
        dmod=((8, everyone, D), bfloat),
        dtime=((everyone, D), bfloat),
        d_condition=((everyone, rows), single),
        d_time_pre=((everyone, rows), single),
    )
    vmem, dma = pltpu.VMEM, pltpu.SemaphoreType.DMA
    scratch = dict(
        d_end=vmem((length, D), single),
        dm_rows=vmem((n_model, length, D), bfloat),
        db_rows=vmem((n_model, length, D), bfloat),
        hold_far=vmem((length, D), single),
        hold_near=vmem((length, D), single),
        parts_send=vmem((3, length, D), bfloat),
        parts_recv=vmem((3, length, D), bfloat),
        normed_end=vmem((length, D), bfloat),
        g_ff=vmem((3, D, units), bfloat),
        x_ff=vmem((3, depth, rows, units), bfloat),
        z_ff=vmem((3, depth - 1, 2, rows, half), bfloat),
        g_qkv=vmem((D, 3 * head_cols), bfloat),
        x_qkv=vmem((depth, rows, 3 * head_cols), bfloat),
        z_qkv=vmem((depth - 1, rows, 3 * head_cols), bfloat),
        g_out=vmem((NX, rows, D), bfloat),
        x_out=vmem((rows, D), bfloat),
        z_out=vmem((depth - 1, rows, D), bfloat),
        out_mine=vmem((rows, D), bfloat),
        late=vmem((everyone, 4, 8, 128), single),
        d_modulation=vmem((8, D), single),
        local=vmem((56, D), single),
        sums=vmem((2 * everyone, 8, 128), single),
        sums_recv=vmem((everyone, 2, 8, 128), single),
        pay=vmem((4, 8, 128), single),
        dmod_row=vmem((16, D // 2), bfloat),
        dmod_all=vmem((everyone, 16, D // 2), bfloat),
        dmod_wide=vmem((16, D // 2), single),
        dtime_mine=vmem((everyone, rows), bfloat),
        dtime_recv=vmem((n_data, everyone, rows), bfloat),
        dtime_wide=vmem((everyone, D), single),
        loss=vmem((1, 1), single),
        time_low=vmem((rows, D), single),
        local_sem=dma((8,)),
    )
    counts = dict(
        dm=(3,),
        db=(3,),
        pa=(3,),
        pb=(3,),
        pc=(3,),
        fx=(3, depth),
        fz=(3, depth - 1, 2),
        qx=(depth,),
        qz=(depth - 1, 2),
        ox=(1,),
        oz=(depth - 1,),
        qa=(3,),
        oa=(3,),
        sm=(everyone - 1,),
        dl=(everyone - 1,),
        dt=(n_data - 1,),
        lt=(everyone - 1,),
    )
    for name, count in counts.items():
        scratch[name + "_s"] = dma(count)
        scratch[name + "_r"] = dma(count)
    far = {
        "ff", "two_rows", "low", "trig_all", "attended", "one_rows", "qkv_weight", "out_weight",
        "matrices",
    }

    def space(name):
        return pl.BlockSpec(memory_space=pl.ANY if name in far else pltpu.VMEM)

    outs = pl.pallas_call(
        functools.partial(back_kernel, sizes, total_images),
        out_shape=[jax.ShapeDtypeStruct(*shapes[name]) for name in BackOut._fields],
        in_specs=[space(name) for name in BackIn._fields],
        out_specs=[space(name) for name in BackOut._fields],
        scratch_shapes=[scratch[name] for name in BackScratch._fields],
        compiler_params=pltpu.CompilerParams(
            collective_id=collective, has_side_effects=True, vmem_limit_bytes=62 * 2**20
        ),
    )(*values)
    return BackOut(*outs)


def forward_plain(clean_three, noise_three, patch_grid, labels, timesteps, matrices, embeddings, swiglu_weights, biases):
    bfloat = jnp.bfloat16
    single = jnp.float32
    images = labels.shape[0]
    length = clean_three.shape[1]
    n_model = lax.axis_size("mlp")
    n_data = lax.axis_size("dp")
    sizes = (n_data, n_model)
    total_images = images * n_data * n_model
    rows = D // n_data
    owned_start = lax.axis_index("dp") * rows
    data_index = lax.axis_index("dp")
    model_index = lax.axis_index("mlp")
    heads = HEADS // n_model
    head_cols = heads * HDIM
    qkv_shard = jnp.concatenate(
        [
            cut_columns(matrices, 9 * D + part * D + model_index * head_cols, head_cols)
            for part in range(3)
        ],
        axis=1,
    ).astype(bfloat)
    out_shard = matrices[:, 12 * D : 13 * D].astype(bfloat)
    swiglu_shard = swiglu_weights.astype(bfloat)
    qkv_weight = lax.all_gather(qkv_shard, "dp", axis=0, tiled=True)
    swiglu_use = lax.all_gather(swiglu_shard, "dp", axis=1, tiled=True)
    out_weight = gather_out(out_shard)

    time_second = matrices[:, :D].astype(bfloat)
    mod_weight = matrices[:, D : 9 * D].astype(bfloat)
    time_first = embeddings[CH : CH + FREQ].astype(bfloat)
    class_table = embeddings[CH + FREQ :].astype(bfloat)
    patch_bias = biases[:D]
    first_bias = biases[D : 2 * D]
    second_bias = biases[2 * D : 3 * D]
    mod_bias = biases[3 * D : 11 * D]
    qkv_bias = biases[11 * D : 14 * D]
    out_bias = biases[14 * D : 15 * D]
    final_bias = biases[15 * D :]

    facts = jnp.concatenate([timesteps[:, None], labels[:, None], patch_grid], axis=1)
    facts = jnp.pad(facts, ((0, 8 - images), (0, 124)))
    (facts_all,) = exchange([(facts, "all")], "both", sizes, 0)
    facts_all = facts_all[:, 0, :4]
    steps_all, labels_all, grid_all = facts_all[:, 0], facts_all[:, 1], facts_all[:, 2:4]
    sinus_all = sinusoid(steps_all).astype(bfloat)
    first_bias_own = lax.dynamic_slice_in_dim(first_bias, owned_start, rows)
    second_bias_own = lax.dynamic_slice_in_dim(second_bias, owned_start, rows)
    time_pre = jnp.dot(sinus_all, time_first, preferred_element_type=single) + first_bias_own
    time_act = jax.nn.silu(time_pre).astype(bfloat)
    time_part = jnp.dot(time_act, time_second, preferred_element_type=single)
    small_shard = jnp.concatenate(
        [embeddings[:CH], matrices[:, 13 * D :].T], axis=0
    ).astype(bfloat)
    time_parts, small_all = exchange(
        [
            (time_part.reshape(total_images, n_data, rows).transpose(1, 0, 2), "each"),
            (small_shard, "all"),
        ],
        "dp",
        sizes,
        1,
    )
    small_all = small_all.transpose(1, 0, 2).reshape(3 * CH, D)
    patch_weight = small_all[:CH]
    final_weight = small_all[CH:].T
    time_emb = jnp.sum(time_parts, axis=0) + second_bias_own
    onehot = (labels_all[:, None] == jnp.arange(CLASSES + 1, dtype=jnp.int32)[None, :]).astype(
        bfloat
    )
    condition = time_emb + jnp.dot(onehot, class_table, preferred_element_type=single)
    cond_act = jax.nn.silu(condition).astype(bfloat)
    cond_rank = lax.dynamic_index_in_dim(
        cond_act.reshape(n_data, n_model, rows), model_index, 1, keepdims=False
    )
    mod_part = jnp.dot(cond_rank, mod_weight, preferred_element_type=single)
    (mod_parts,) = exchange(
        [(mod_part.reshape(n_data, 8, D), "each")],
        "dp",
        sizes,
        2,
    )
    modulation = jnp.sum(mod_parts, axis=0).reshape(1, 8 * D) + mod_bias
    shift_one, scale_one, gate_one, shift_two, scale_two, gate_two, shift_end, scale_end = (
        jnp.split(modulation, 8, axis=1)
    )

    group_grid = lax.dynamic_slice_in_dim(grid_all, data_index * n_model, n_model, 0)
    group_grid = jnp.stack(
        [
            lax.dynamic_index_in_dim(group_grid, model_index ^ rank, 0, keepdims=False)
            for rank in range(n_model)
        ]
    )
    cosine, sine, mask = turn_tables(group_grid, length)
    noisy_low = noisy_input(clean_three, noise_three, timesteps).astype(bfloat)
    hidden = jnp.dot(noisy_low, patch_weight, preferred_element_type=single) + patch_bias
    normed_one = modulate(hidden, shift_one, scale_one).astype(bfloat)
    one_rows = jnp.concatenate(gather_rows(normed_one.reshape(length, D), n_model), axis=0)
    qkv_bias_own = jnp.concatenate(
        [
            lax.dynamic_slice_in_dim(qkv_bias, part * D + model_index * head_cols, head_cols)
            for part in range(3)
        ]
    )
    qkv = jnp.dot(one_rows, qkv_weight, preferred_element_type=single) + qkv_bias_own
    low, attended, log_total = attention(
        qkv.reshape(n_model, length, 3 * head_cols), cosine, sine, mask, heads
    )
    attended_rows = attended.reshape(n_model * length, head_cols)
    branch_part = jnp.dot(attended_rows, out_weight, preferred_element_type=single).astype(bfloat)
    branch_part = branch_part.reshape(n_model, length, D)
    branch = (
        scatter_rows(
            (branch_part[2], branch_part[3]), (branch_part[0], branch_part[1]), n_model
        )[None]
        + out_bias
    )
    hidden_mid = hidden + gate_one[:, None, :] * branch
    normed_two = modulate(hidden_mid, shift_two, scale_two).astype(bfloat)
    two_rows = gather_rows(normed_two.reshape(length, D), n_model)
    return SimpleNamespace(
        steps=sinus_all,
        onehot=onehot,
        time_pre=time_pre,
        condition=condition,
        modulation=modulation,
        hidden=hidden,
        one_rows=one_rows,
        qkv_weight=qkv_weight,
        out_weight=out_weight,
        swiglu=swiglu_use,
        low=low,
        attended=attended,
        totals=log_total,
        branch=branch,
        hidden_mid=hidden_mid,
        two_rows=two_rows,
        final_weight=final_weight,
        tables=(cosine, sine, mask),
    )


def forward_fused(clean_three, noise_three, patch_grid, labels, timesteps, matrices, embeddings, swiglu_weights, biases):
    bfloat = jnp.bfloat16
    single = jnp.float32
    length = clean_three.shape[1]
    n_model = lax.axis_size("mlp")
    n_data = lax.axis_size("dp")
    everyone = n_data * n_model
    rows = D // n_data
    owned_start = lax.axis_index("dp") * rows
    model_index = lax.axis_index("mlp")
    head_cols = HEADS // n_model * HDIM

    def own_bias(start, amount, offset):
        return lax.dynamic_slice_in_dim(biases, start + offset, amount)[None]

    sinus = sinusoid(timesteps).astype(bfloat).astype(single).reshape(2, 128)
    facts = jnp.concatenate(
        [labels, patch_grid[:, 0] * patch_grid[:, 1]]
    ).astype(single)
    facts = jnp.concatenate(
        [sinus, jnp.pad(facts[None], ((0, 0), (0, 126))), jnp.zeros((5, 128), single)], axis=0
    )
    cosine, sine, _ = turn_tables(patch_grid, length)
    small = jnp.concatenate(
        [
            embeddings[:CH].T,
            jnp.zeros((rows, CH), single),
            matrices[:, 13 * D :],
            jnp.zeros((rows, 64), single),
        ],
        axis=1,
    ).astype(bfloat)
    values = ForwardIn(
        facts=facts,
        trig=jnp.concatenate([cosine, sine], axis=0),
        small=small,
        time_first=embeddings[CH : CH + FREQ].astype(bfloat),
        first_bias=own_bias(D, rows, owned_start),
        second_bias=own_bias(2 * D, rows, owned_start),
        class_table=embeddings[CH + FREQ :].astype(bfloat),
        matrices=matrices,
        mod_bias=biases[3 * D : 11 * D].reshape(8, D),
        noisy=noisy_input(clean_three, noise_three, timesteps).astype(bfloat)[0],
        patch_bias=biases[None, :D],
        qkv_shard=jnp.concatenate(
            [
                cut_columns(matrices, (9 + part) * D + model_index * head_cols, head_cols)
                for part in range(3)
            ],
            axis=1,
        ).astype(bfloat),
        ff_shard=swiglu_weights.astype(bfloat),
        qkv_bias=jnp.concatenate(
            [
                own_bias((11 + part) * D, head_cols, model_index * head_cols)
                for part in range(3)
            ],
            axis=1,
        ),
        out_bias=biases[None, 14 * D : 15 * D],
    )
    out = forward_all(values, (n_data, n_model), 0)
    found = {name.removesuffix("_out"): value for name, value in out._asdict().items()}
    raw = {name: found[name] for name in BackIn._fields if name in found}
    facts_all = out.facts_all
    group = lax.dynamic_slice_in_dim(
        facts_all[:, 2, 1], lax.axis_index("dp") * n_model, n_model
    )
    spots = model_index ^ jnp.arange(n_model)
    counts = jnp.sum(
        jnp.where(spots[:, None] == jnp.arange(n_model)[None, :], group[None, :], 0.0), axis=1
    )
    mask = jnp.arange(length, dtype=jnp.int32)[None, None, :] < counts[:, None, None]
    return SimpleNamespace(
        raw=dict(
            raw,
            noisy=values.noisy,
            matrices=matrices,
        ),
        steps=facts_all[:, :2].reshape(everyone, FREQ).astype(bfloat),
        onehot=(
            facts_all[:, 2, 0:1] == jnp.arange(CLASSES + 1, dtype=jnp.int32)[None].astype(single)
        ).astype(bfloat),
        time_pre=out.time_pre,
        condition=out.condition,
        modulation=out.modulation.reshape(1, 8 * D),
        hidden=out.hidden[None],
        one_rows=out.one_rows_out.reshape(n_model * length, D),
        qkv_weight=out.qkv_weight_out,
        out_weight=out.out_weight_out,
        swiglu=out.ff,
        low=out.low_out,
        attended=out.attended_out,
        totals=out.totals,
        branch=out.branch[None],
        hidden_mid=out.hidden_mid[None],
        two_rows=tuple(out.two_rows),
        final_weight=out.small_all[:, 2 * CH : 4 * CH],
        tables=(out.trig_all_out[:, 0], out.trig_all_out[:, 1], mask.astype(single)),
    )


def backward_plain(
    kept, clean_three, noise_three, patch_grid, timesteps, biases, total_images
):
    bfloat = jnp.bfloat16
    single = jnp.float32
    images, length = clean_three.shape[:2]
    n_model = lax.axis_size("mlp")
    n_data = lax.axis_size("dp")
    rows = D // n_data
    model_index = lax.axis_index("mlp")
    heads = HEADS // n_model
    head_cols = heads * HDIM
    valid_slot = valid_slots(patch_grid, length)
    final_bias = biases[15 * D :]
    noisy_low = noisy_input(clean_three, noise_three, timesteps).astype(bfloat)
    modulation, hidden, hidden_mid, branch = kept.modulation, kept.hidden, kept.hidden_mid, kept.branch
    shift_one, scale_one, gate_one, shift_two, scale_two, gate_two, shift_end, scale_end = (
        jnp.split(modulation, 8, axis=1)
    )
    qkv_weight, out_weight, swiglu_use = kept.qkv_weight, kept.out_weight, kept.swiglu
    final_weight, one_rows, two_rows = kept.final_weight, kept.one_rows, kept.two_rows
    low, log_total = kept.low, kept.totals
    attended_rows = kept.attended.reshape(n_model * length, head_cols)
    cosine, sine, mask = kept.tables
    two_halves = (
        jnp.concatenate(two_rows[:2], axis=0),
        jnp.concatenate(two_rows[2:], axis=0),
    )
    gates, ups, acts, parts = [], [], [], []
    for part in two_halves:
        gate_val = jnp.dot(part, swiglu_use[0], preferred_element_type=single)
        up_val = jnp.dot(part, swiglu_use[1], preferred_element_type=single)
        act = (jax.nn.silu(gate_val) * up_val).astype(bfloat)
        gates.append(gate_val)
        ups.append(up_val)
        acts.append(act)
        parts.append(backward_product(act, swiglu_use[2]).astype(bfloat).reshape(2, length, D))
    mixed = scatter_rows(parts[1], parts[0], n_model)[None]
    hidden_end = hidden_mid + gate_two[:, None, :] * mixed
    normed_end = modulate(hidden_end, shift_end, scale_end).astype(bfloat)
    output = jnp.dot(normed_end, final_weight, preferred_element_type=single) + final_bias
    local_loss, loss_pull = jax.vjp(
        lambda values_out: loss_terms(values_out, clean_three, noise_three, timesteps, valid_slot),
        output,
    )
    d_output = loss_pull(jnp.asarray(1.0 / total_images, single))[0].astype(bfloat)
    d_normed_end = backward_product(d_output, final_weight)
    unused, pull_end = jax.vjp(modulate, hidden_end, shift_end, scale_end)
    d_hidden_end, d_shift_end, d_scale_end = pull_end(d_normed_end)
    d_mixed = (gate_two[:, None, :] * d_hidden_end).astype(bfloat)
    d_gate_two = jnp.sum(mixed * d_hidden_end, axis=1)
    dmixed_rows = gather_rows(d_mixed.reshape(length, D), n_model)
    dmixed_halves = (
        jnp.concatenate(dmixed_rows[:2], axis=0),
        jnp.concatenate(dmixed_rows[2:], axis=0),
    )
    d_gates, d_ups, d_parts = [], [], []
    for part, gate_val, up_val in zip(dmixed_halves, gates, ups):
        d_inner = jnp.dot(part, swiglu_use[2], preferred_element_type=single)
        unused, pull_glu = jax.vjp(
            lambda gate_in, up_in: jax.nn.silu(gate_in) * up_in, gate_val, up_val
        )
        d_gate, d_up = pull_glu(d_inner)
        d_gate, d_up = d_gate.astype(bfloat), d_up.astype(bfloat)
        d_gates.append(d_gate)
        d_ups.append(d_up)
        d_parts.append(
            (backward_product(d_gate, swiglu_use[0]) + backward_product(d_up, swiglu_use[1]))
            .astype(bfloat)
            .reshape(2, length, D)
        )
    d_normed_two = scatter_rows(d_parts[1], d_parts[0], n_model)[None]
    rows_ready = jnp.concatenate(two_halves, axis=0)
    dmixed_ready = jnp.concatenate(dmixed_halves, axis=0)

    def owned(gradient):
        return reduce_dp(gradient.reshape(n_data, rows, -1))

    grad_swiglu = jnp.stack(
        [
            owned(weight_grad(rows_ready, jnp.concatenate(d_gates, axis=0))),
            owned(weight_grad(rows_ready, jnp.concatenate(d_ups, axis=0))),
            owned(weight_grad(dmixed_ready, jnp.concatenate(acts, axis=0))),
        ]
    )
    unused, pull_two = jax.vjp(modulate, hidden_mid, shift_two, scale_two)
    d_mid_part, d_shift_two, d_scale_two = pull_two(d_normed_two)
    d_hidden_mid = d_hidden_end + d_mid_part
    d_branch = (gate_one[:, None, :] * d_hidden_mid).astype(bfloat)
    d_gate_one = jnp.sum(branch * d_hidden_mid, axis=1)

    dbranch_rows = jnp.concatenate(gather_rows(d_branch.reshape(length, D), n_model), axis=0)
    d_attended = backward_product(dbranch_rows, out_weight).astype(bfloat)
    d_qkv = attention_back(
        low,
        log_total,
        d_attended.reshape(n_model, length, head_cols),
        cosine,
        sine,
        mask,
        heads,
    ).reshape(n_model * length, 3 * head_cols)
    grad_out = reduce_out(weight_grad(attended_rows, dbranch_rows))
    grad_qkv_own = owned(weight_grad(one_rows, d_qkv))
    d_one_part = backward_product(d_qkv, qkv_weight).astype(bfloat).reshape(n_model, length, D)
    d_normed_one = scatter_rows(
        (d_one_part[2], d_one_part[3]), (d_one_part[0], d_one_part[1]), n_model
    )[None]
    unused, pull_one = jax.vjp(modulate, hidden, shift_one, scale_one)
    d_hidden_part, d_shift_one, d_scale_one = pull_one(d_normed_one)
    d_hidden = (d_hidden_mid + d_hidden_part).astype(bfloat)

    return SimpleNamespace(
        d_modulation=jnp.concatenate(
            [
                d_shift_one,
                d_scale_one,
                d_gate_one,
                d_shift_two,
                d_scale_two,
                d_gate_two,
                d_shift_end,
                d_scale_end,
            ],
            axis=1,
        ),
        hidden_sum=column_sum(d_hidden),
        branch_sum=column_sum(d_branch),
        qkv_sum=column_sum(d_qkv),
        output_sum=column_sum(d_output),
        loss=local_loss.reshape(1),
        grad_patch=weight_grad(noisy_low, d_hidden),
        grad_final=weight_grad(normed_end, d_output).T,
        grad_swiglu=grad_swiglu,
        grad_out=grad_out,
        grad_qkv=jnp.stack(gather_rows(grad_qkv_own.astype(bfloat), n_model)).astype(single),
    )


def finish_fused(
    kept, clean_three, noise_three, patch_grid, timesteps, states, biases, total_images
):
    single = jnp.float32
    length = clean_three.shape[1]
    n_data, n_model = sizes = (lax.axis_size("dp"), lax.axis_size("mlp"))
    beta_now, bar_now, bar_prev = plan(timesteps)
    consts = jnp.stack(
        [
            jnp.sqrt(bar_now),
            jnp.sqrt(1.0 - bar_now),
            jnp.log(beta_now),
            jnp.log(beta_now * (1.0 - bar_prev) / (1.0 - bar_now)),
            beta_now * jnp.sqrt(bar_prev) / (1.0 - bar_now),
        ],
        axis=1,
    )
    values = BackIn(
        **kept.raw,
        final_bias=biases[15 * D :].reshape(2, CH),
        clean=clean_three[0],
        noise=noise_three[0],
        consts=jnp.pad(consts, ((0, 7), (0, 123))),
        valid=valid_slots(patch_grid, length).astype(single).reshape(length, 1),
    )
    out = backward_all(values, sizes, total_images, 1)
    grad_time_first = jnp.dot(
        kept.steps.astype(single).T,
        out.d_time_pre,
        precision=lax.Precision.HIGHEST,
        preferred_element_type=single,
    )
    grad_table = jnp.dot(
        kept.onehot.astype(single).T,
        out.d_condition,
        precision=lax.Precision.HIGHEST,
        preferred_element_type=single,
    )
    grad_norm, factor, loss_sum = (one.reshape(()) for one in (out.norm, out.factor, out.loss_sum))
    grad_bias = jnp.concatenate([out.bias_rows[:15].reshape(-1), out.bias_rows[15, : 2 * CH]])
    mats_out = adam_matrices(
        states,
        jax.nn.silu(kept.time_pre).astype(jnp.bfloat16),
        jax.nn.silu(kept.condition).astype(jnp.bfloat16),
        out.dtime,
        out.dmod,
        out.grad_qkv,
        out.grad_out,
        jnp.pad(out.own[CH:].T, ((0, 0), (0, 128 - 2 * CH))),
        out.factor,
        n_model,
    )
    return SimpleNamespace(
        loss_sum=loss_sum,
        grad_norm=grad_norm,
        factor=factor,
        grad_bias=grad_bias,
        grad_embed=jnp.concatenate([out.own[:CH], grad_time_first, grad_table], axis=0),
        grad_swiglu=out.grad_ff,
        mats_out=mats_out,
    )


def adam_matrices_kernel(
    n_model,
    weight_ref,
    first_ref,
    second_ref,
    average_ref,
    time_act_ref,
    cond_act_ref,
    dtime_ref,
    dmod_ref,
    qkv_ref,
    out_ref,
    final_ref,
    factor_ref,
    weight_out,
    first_out,
    second_out,
    average_out,
    grad_ref,
):
    single = jnp.float32
    head_cols = HEADS // n_model * HDIM
    m = lax.axis_index("mlp")

    def outer(left, right):
        return lax.dot_general(left, right, (((0,), (0,)), ((), ())), preferred_element_type=single)

    for side in range(2):
        section = 2 * pl.program_id(0) + side
        base = side * D
        lanes = slice(base, base + D)

        @pl.when((section >= 1) & (section < 9))
        def _():
            grad_ref[:, lanes] = outer(cond_act_ref[...], dmod_ref[jnp.clip(section - 1, 0, 7)])

        if side == 0:

            @pl.when(section == 0)
            def _():
                grad_ref[:, lanes] = outer(time_act_ref[...], dtime_ref[...])

            @pl.when(section == 12)
            def _():
                grad_ref[:, lanes] = out_ref[...].astype(single)

        else:

            @pl.when(section == 13)
            def _():
                grad_ref[:, base : base + 128] = final_ref[...]

        for part in range(3):
            if (9 + part) % 2 == side:

                @pl.when(section == 9 + part)
                def _():
                    for rank in range(n_model):
                        apart = (
                            2 * lax.rem(lax.div(m, 2) + rank // 2, 2)
                            + lax.rem(lax.rem(m, 2) + rank % 2, 2)
                        )
                        start = base + rank * head_cols
                        grad_ref[:, start : start + head_cols] = qkv_ref[
                            apart, :, part * head_cols : (part + 1) * head_cols
                        ].astype(single)

    def body(step, carry):
        at = pl.ds(pl.multiple_of(step * 24, 24), 24)
        done = adam_step(
            weight_ref[at],
            first_ref[at],
            second_ref[at],
            grad_ref[at],
            average_ref[at],
            factor_ref[...],
            LEARN_RATE,
        )
        for place, value in zip((weight_out, first_out, second_out, average_out), done):
            place[at] = value
        return carry

    lax.fori_loop(0, weight_ref.shape[0] // 24, body, 0)


def adam_matrices(
    states, time_act, cond_act, dtime, dmod, grad_qkv, grad_out, grad_final, factor, n_model
):
    rows, width = states[0].shape
    whole = lambda array: pl.BlockSpec(array.shape, lambda i: (0,) * array.ndim)
    strip = pl.BlockSpec((rows, 2 * D), lambda i: (0, i))
    gradients = (time_act, cond_act, dtime, dmod, grad_qkv, grad_out, grad_final, factor)
    return pl.pallas_call(
        functools.partial(adam_matrices_kernel, n_model),
        grid=(pl.cdiv(width, 2 * D),),
        out_shape=[jax.ShapeDtypeStruct((rows, width), jnp.float32)] * 4,
        in_specs=[strip] * 4 + [whole(array) for array in gradients],
        out_specs=[strip] * 4,
        scratch_shapes=[pltpu.VMEM((rows, 2 * D), jnp.float32)],
        compiler_params=pltpu.CompilerParams(vmem_limit_bytes=62 * 2**20),
    )(*states, *gradients)


def finish_plain(
    kept, clean_three, noise_three, patch_grid, timesteps, states, biases, total_images
):
    bfloat = jnp.bfloat16
    single = jnp.float32
    matrices, matrices_first, matrices_second, matrices_average = states
    n_data, n_model = sizes = (lax.axis_size("dp"), lax.axis_size("mlp"))
    rows = D // n_data
    owned_start = lax.axis_index("dp") * rows
    model_index = lax.axis_index("mlp")
    head_cols = HEADS // n_model * HDIM
    time_pre, condition = kept.time_pre, kept.condition
    onehot, sinus_all = kept.onehot, kept.steps
    time_act = jax.nn.silu(time_pre).astype(bfloat)
    cond_act = jax.nn.silu(condition).astype(bfloat)
    time_second = matrices[:, :D].astype(bfloat)
    mod_weight = matrices[:, D : 9 * D].astype(bfloat)

    grads = backward_plain(
        kept, clean_three, noise_three, patch_grid, timesteps, biases, total_images
    )
    grad_swiglu, grad_out = grads.grad_swiglu, grads.grad_out
    grad_qkv_own = grads.grad_qkv[0]
    qkv_stack = jnp.stack(
        [
            lax.dynamic_index_in_dim(grads.grad_qkv, model_index ^ rank, 0, keepdims=False)
            for rank in range(n_model)
        ]
    )
    grad_qkv = (
        qkv_stack.reshape(n_model, rows, 3, head_cols).transpose(1, 2, 0, 3).reshape(rows, 3 * D)
    )

    d_modulation = grads.d_modulation.astype(bfloat)
    (dmod_all,) = exchange(
        [(d_modulation.reshape(16, D // 2), "all")], "both", sizes, 3
    )
    dmod_all = dmod_all.reshape(total_images, 8 * D)
    d_cond_act = backward_product(dmod_all, mod_weight)
    unused, pull_cond = jax.vjp(jax.nn.silu, condition)
    d_condition = pull_cond(d_cond_act)[0]
    d_time_emb = d_condition.astype(bfloat)
    (dtime_parts,) = exchange([(d_time_emb, "all")], "dp", sizes, 4)
    dtime_all = dtime_parts.transpose(1, 0, 2).reshape(total_images, D)
    d_time_act = backward_product(dtime_all, time_second)
    unused, pull_time = jax.vjp(jax.nn.silu, time_pre)
    d_time_pre = pull_time(d_time_act)[0]
    grad_time_second = weight_grad(time_act, dtime_all)
    grad_mod = weight_grad(cond_act, dmod_all)
    grad_time_first = jnp.dot(
        sinus_all.astype(single).T,
        d_time_pre,
        precision=lax.Precision.HIGHEST,
        preferred_element_type=single,
    )
    grad_table = jnp.dot(
        onehot.astype(single).T,
        d_condition,
        precision=lax.Precision.HIGHEST,
        preferred_element_type=single,
    )

    qkv_sums = grads.qkv_sum.reshape(3, head_cols)
    qkv_bias_part = lax.dynamic_update_slice(
        jnp.zeros((3, D), single), qkv_sums, (0, model_index * head_cols)
    )
    local_sums = jnp.concatenate(
        [
            grads.hidden_sum,
            qkv_bias_part.reshape(-1),
            grads.branch_sum,
            grads.output_sum,
            grads.loss,
            jnp.zeros((95,), single),
            grads.grad_patch.reshape(-1),
            grads.grad_final.reshape(-1),
        ]
    )
    everyone = n_data * n_model
    chunk_rows = -(-local_sums.shape[0] // (everyone * 1024)) * 8
    local_sums = jnp.pad(local_sums, (0, everyone * chunk_rows * 128 - local_sums.shape[0]))
    (sum_parts,) = exchange(
        [(local_sums.reshape(everyone, chunk_rows, 128), "each")], "both", sizes, 5
    )
    chunk = jnp.sum(sum_parts, axis=0)
    local_squares = (
        jnp.sum(grad_time_second * grad_time_second)
        + jnp.sum(grad_mod * grad_mod)
        + jnp.sum(grad_out * grad_out)
        + jnp.sum(grad_time_first * grad_time_first)
        + jnp.sum(grad_table * grad_table)
    ) / n_model + jnp.sum(grad_swiglu * grad_swiglu) + jnp.sum(grad_qkv_own * grad_qkv_own)
    extra = jnp.concatenate([jnp.sum(d_time_pre, axis=0), local_squares.reshape(1)])
    extra = jnp.pad(extra, (0, 1024 - extra.shape[0])).reshape(8, 128)
    (late,) = exchange([(jnp.concatenate([chunk, extra], axis=0), "all")], "both", sizes, 6)
    sums = late[:, :chunk_rows].reshape(-1)
    extras = late[:, chunk_rows:].reshape(everyone, 1024)
    first_bias_grad = extras.reshape(n_data, n_model, 1024)[:, 0, :rows].reshape(D)
    squares = jnp.sum(extras[:, rows])
    ends = [D, 4 * D, 5 * D, 5 * D + 2 * CH, 5 * D + 2 * CH + 1]
    base = 5 * D + 128
    loss_sum = sums[5 * D + 2 * CH]
    grad_patch = sums[base : base + CH * D].reshape(CH, D)
    grad_final = sums[base + CH * D : base + 3 * CH * D].reshape(2 * CH, D)
    grad_patch = cut_columns(grad_patch, owned_start, rows)
    grad_final_own = cut_columns(grad_final, owned_start, rows).T
    grad_bias = jnp.concatenate(
        [
            sums[:D],
            first_bias_grad,
            column_sum(dtime_all),
            column_sum(dmod_all),
            sums[D : 4 * D],
            sums[4 * D : 5 * D],
            sums[5 * D : 5 * D + 2 * CH],
        ]
    )
    shared = sums[base : base + 3 * CH * D]
    squares = squares + jnp.sum(grad_bias * grad_bias) + jnp.sum(shared * shared)
    grad_norm = jnp.sqrt(squares)
    factor = jnp.minimum(1.0, CLIP_LIMIT / grad_norm)
    grad_mats = jnp.concatenate(
        [grad_time_second, grad_mod, grad_qkv, grad_out, grad_final_own], axis=1
    )
    grad_embed = jnp.concatenate([grad_patch, grad_time_first, grad_table], axis=0)
    mats_out = adam_step(
        matrices, matrices_first, matrices_second, grad_mats, matrices_average, factor, LEARN_RATE
    )
    return SimpleNamespace(
        loss_sum=loss_sum,
        grad_norm=grad_norm,
        factor=factor,
        grad_bias=grad_bias,
        grad_embed=grad_embed,
        grad_swiglu=grad_swiglu,
        mats_out=mats_out,
    )


def on_device(
    clean_patches,
    noise_patches,
    patch_grid,
    labels,
    timesteps,
    matrices,
    embeddings,
    swiglu_weights,
    biases,
    matrices_first,
    embeddings_first,
    swiglu_first,
    biases_first,
    matrices_second,
    embeddings_second,
    swiglu_second,
    biases_second,
    matrices_average,
    embeddings_average,
    swiglu_average,
    biases_average,
):
    images = labels.shape[0]
    length = clean_patches.shape[0] // images
    n_model = lax.axis_size("mlp")
    n_data = lax.axis_size("dp")
    total_images = images * n_data * n_model

    clean_three = clean_patches.reshape(images, length, CH)
    noise_three = noise_patches.reshape(images, length, CH)
    fused = (n_data, n_model, images) == (8, 4, 1)
    forward = forward_fused if fused else forward_plain
    kept = forward(
        clean_three,
        noise_three,
        patch_grid,
        labels,
        timesteps,
        matrices,
        embeddings,
        swiglu_weights,
        biases,
    )
    finish = finish_fused if fused else finish_plain
    done = finish(
        kept,
        clean_three,
        noise_three,
        patch_grid,
        timesteps,
        (matrices, matrices_first, matrices_second, matrices_average),
        biases,
        total_images,
    )
    loss_sum, grad_norm, factor = done.loss_sum, done.grad_norm, done.factor
    grad_embed, grad_swiglu, grad_bias = done.grad_embed, done.grad_swiglu, done.grad_bias
    mats_out = done.mats_out
    embed_out = adam_step(
        embeddings,
        embeddings_first,
        embeddings_second,
        grad_embed,
        embeddings_average,
        factor,
        TABLE_RATE,
    )
    swiglu_out = adam_step(
        swiglu_weights, swiglu_first, swiglu_second, grad_swiglu, swiglu_average, factor, LEARN_RATE
    )
    bias_out = adam_step(
        biases, biases_first, biases_second, grad_bias, biases_average, factor, TABLE_RATE
    )
    return (
        loss_sum,
        grad_norm,
        mats_out[0],
        embed_out[0],
        swiglu_out[0],
        bias_out[0],
        mats_out[1],
        embed_out[1],
        swiglu_out[1],
        bias_out[1],
        mats_out[2],
        embed_out[2],
        swiglu_out[2],
        bias_out[2],
        mats_out[3],
        embed_out[3],
        swiglu_out[3],
        bias_out[3],
        grad_bias * factor,
    )


def solution(mesh):
    placed = (
        P(("dp", "mlp"), None),
        P(("dp", "mlp"), None),
        P(("dp", "mlp"), None),
        P(("dp", "mlp")),
        P(("dp", "mlp")),
        P("dp", None),
        P(None, "dp"),
        P(None, "dp", "mlp"),
        P(),
        P("dp", None),
        P(None, "dp"),
        P(None, "dp", "mlp"),
        P(),
        P("dp", None),
        P(None, "dp"),
        P(None, "dp", "mlp"),
        P(),
        P("dp", None),
        P(None, "dp"),
        P(None, "dp", "mlp"),
        P(),
    )
    return jax.shard_map(
        on_device,
        mesh=mesh,
        in_specs=placed,
        out_specs=(
            P(),
            P(),
            P("dp", None),
            P(None, "dp"),
            P(None, "dp", "mlp"),
            P(),
            P("dp", None),
            P(None, "dp"),
            P(None, "dp", "mlp"),
            P(),
            P("dp", None),
            P(None, "dp"),
            P(None, "dp", "mlp"),
            P(),
            P("dp", None),
            P(None, "dp"),
            P(None, "dp", "mlp"),
            P(),
            P(),
        ),
        check_vma=False,
    )
```

```python
import functools
import math
from types import SimpleNamespace
from typing import Any, NamedTuple

import jax
import jax.numpy as jnp
import numpy as np
from jax import lax
from jax.experimental import pallas as pl
from jax.experimental.pallas import tpu as pltpu
from jax.sharding import PartitionSpec as P

HEADS = 16
HDIM = 72
D = 1152
CH = 16
CLASSES = 1000
FREQ = 256
STEP = 10


CLIP_LIMIT = 1.0
LEARN_RATE = 0.03
TABLE_RATE = 0.4
FIRST_DECAY = 0.9
SECOND_DECAY = 0.999
ADAM_EPSILON = 1e-08
WEIGHT_DECAY = 0.01
AVERAGE_DECAY = 0.9999


def plan(steps_in):
    step_index = jnp.arange(1000, dtype=jnp.int32)
    betas = 0.0001 + (0.02 - 0.0001) * np.arange(1000) / 999.0
    beta_table = jnp.asarray(betas, jnp.float32)
    logbar = jnp.asarray(np.cumsum(np.log1p(-betas)), jnp.float32)

    def lookup(values, wanted):
        return jnp.sum(
            jnp.where(wanted[:, None] == step_index[None, :], values[None, :], 0.0), axis=1
        )

    return (
        lookup(beta_table, steps_in),
        jnp.exp(lookup(logbar, steps_in)),
        jnp.exp(lookup(logbar, steps_in - 1)),
    )


def sinusoid(steps_in):
    halfway = FREQ // 2
    frequency = jnp.exp(-math.log(10000.0) * jnp.arange(halfway, dtype=jnp.float32) / halfway)
    angles = steps_in.astype(jnp.float32)[:, None] * frequency[None, :]
    return jnp.concatenate([jnp.cos(angles), jnp.sin(angles)], axis=1)


def modulate(hidden, shift_by, scale_by):
    row_mean = jnp.mean(hidden, axis=-1, keepdims=True)
    centered = hidden - row_mean
    variance = jnp.mean(centered * centered, axis=-1, keepdims=True)
    return (
        centered * lax.rsqrt(variance + 1e-06) * (1.0 + scale_by[:, None, :]) + shift_by[:, None, :]
    )


def noisy_input(clean_patches, noise_patches, steps_in):
    beta_now, bar_now, bar_prev = plan(steps_in)
    bar_now = bar_now[:, None, None]
    return jnp.sqrt(bar_now) * clean_patches + jnp.sqrt(1.0 - bar_now) * noise_patches


def loss_terms(output, clean_patches, noise_patches, steps_in, valid_slot):
    beta_now, bar_now, bar_prev = plan(steps_in)
    beta_now = beta_now[:, None, None]
    bar_now = bar_now[:, None, None]
    bar_prev = bar_prev[:, None, None]
    noisy = jnp.sqrt(bar_now) * clean_patches + jnp.sqrt(1.0 - bar_now) * noise_patches
    eps_pred = output[..., :CH]
    var_raw = output[..., CH:]
    squared = jnp.sum((eps_pred - noise_patches) ** 2, axis=-1)
    post_log = jnp.log(beta_now * (1.0 - bar_prev) / (1.0 - bar_now))
    fraction = (var_raw + 1.0) * 0.5
    model_log = fraction * jnp.log(beta_now) + (1.0 - fraction) * post_log
    coefficient = beta_now * jnp.sqrt(bar_prev) / (1.0 - bar_now)
    start_est = (noisy - jnp.sqrt(1.0 - bar_now) * eps_pred) / jnp.sqrt(bar_now)
    mean_gap = coefficient * (clean_patches - start_est)
    divergence = (
        0.5
        * (
            -1.0
            + model_log
            - post_log
            + jnp.exp(post_log - model_log)
            + mean_gap * mean_gap * jnp.exp(-model_log)
        )
        / math.log(2.0)
    )
    return jnp.sum(jnp.where(valid_slot, squared + jnp.sum(divergence, axis=-1), 0.0))


def adam_step(weight, first, second, gradient, average, factor, rate):
    average_decay = min(AVERAGE_DECAY, (1.0 + STEP) / (10.0 + STEP))
    clipped = gradient * factor
    first = FIRST_DECAY * first + (1.0 - FIRST_DECAY) * clipped
    second = SECOND_DECAY * second + (1.0 - SECOND_DECAY) * clipped * clipped
    ratio = (first * (1.0 / (1.0 - FIRST_DECAY**STEP))) / (
        jnp.sqrt(second * (1.0 / (1.0 - SECOND_DECAY**STEP))) + ADAM_EPSILON
    )
    weight = weight - rate * (ratio + WEIGHT_DECAY * weight)
    return (weight, first, second, average_decay * average + (1.0 - average_decay) * weight)


def backward_product(gradient, weight):
    return lax.dot_general(
        gradient,
        weight,
        (((gradient.ndim - 1,), (1,)), ((), ())),
        preferred_element_type=jnp.float32,
    )


def weight_grad(inputs, gradient):
    flat_in = inputs.reshape(-1, inputs.shape[-1])
    flat_grad = gradient.reshape(-1, gradient.shape[-1])
    return lax.dot_general(
        flat_in, flat_grad, (((0,), (0,)), ((), ())), preferred_element_type=jnp.float32
    )


def column_sum(gradient):
    return jnp.sum(gradient.astype(jnp.float32).reshape(-1, gradient.shape[-1]), axis=0)


def cut_columns(values, start, amount):
    return lax.dynamic_slice_in_dim(values, start, amount, 1)


MESH_IDS = pl.DeviceIdType.MESH
KERNEL_VMEM = 48 * 2**20


def exchange_kernel(axes, sizes, modes, *refs):
    count = len(modes)
    ins, outs = refs[:count], refs[count : 2 * count]
    send_sem, recv_sem = refs[2 * count :]
    if axes == "dp":
        total = sizes[0]
        me = lax.axis_index("dp")
    else:
        total = sizes[0] * sizes[1]
        me = lax.axis_index("dp") * sizes[1] + lax.axis_index("mlp")

    def device(spot):
        if axes == "dp":
            return (spot, lax.axis_index("mlp"))
        return (lax.div(spot, sizes[1]), lax.rem(spot, sizes[1]))

    barrier = pltpu.get_barrier_semaphore()

    def greet(step, carry):
        pl.semaphore_signal(
            barrier, inc=1, device_id=device(lax.rem(me + step, total)), device_id_type=MESH_IDS
        )
        return carry

    lax.fori_loop(1, total, greet, 0)
    pl.semaphore_wait(barrier, total - 1)

    def make(item, step):
        peer = lax.rem(me + step, total)
        source = ins[item].at[peer] if modes[item] == "each" else ins[item]
        return pltpu.make_async_remote_copy(
            src_ref=source,
            dst_ref=outs[item].at[me],
            send_sem=send_sem.at[item, step - 1],
            recv_sem=recv_sem.at[item, step - 1],
            device_id=device(peer),
            device_id_type=MESH_IDS,
        )

    def begin(step, carry):
        for item in range(count):
            make(item, step).start()
        return carry

    lax.fori_loop(1, total, begin, 0)
    for item in range(count):
        if modes[item] == "each":
            outs[item][me] = ins[item][me]
        else:
            outs[item][me] = ins[item][...]

    def finish(step, carry):
        for item in range(count):
            make(item, step).wait()
        return carry

    lax.fori_loop(1, total, finish, 0)


def exchange(items, axes, sizes, collective):
    total = sizes[0] if axes == "dp" else sizes[0] * sizes[1]
    modes = tuple(mode for _, mode in items)
    arrays = [array for array, _ in items]
    shapes = [
        jax.ShapeDtypeStruct(
            array.shape if mode == "each" else (total, *array.shape), array.dtype
        )
        for array, mode in items
    ]
    space = pl.BlockSpec(memory_space=pltpu.VMEM)
    return pl.pallas_call(
        functools.partial(exchange_kernel, axes, sizes, modes),
        out_shape=shapes,
        in_specs=[space] * len(items),
        out_specs=[space] * len(items),
        scratch_shapes=[
            pltpu.SemaphoreType.DMA((len(items), total - 1)),
            pltpu.SemaphoreType.DMA((len(items), total - 1)),
        ],
        compiler_params=pltpu.CompilerParams(
            collective_id=collective, has_side_effects=True, vmem_limit_bytes=KERNEL_VMEM
        ),
    )(*arrays)


NX = 2


def reduce_dp(value):
    return lax.psum_scatter(value.astype(jnp.bfloat16), "dp", scatter_dimension=0, tiled=True)[
        0
    ].astype(jnp.float32)


def flip(value, bit, count):
    return lax.ppermute(value, "mlp", [(spot, spot ^ bit) for spot in range(count)])


def gather_rows(own, count):
    far = flip(own, 2, count)
    near = flip(own, 1, count)
    return own, near, far, flip(far, 1, count)


def scatter_rows(far_parts, near_parts, count):
    single = jnp.float32
    got = flip(far_parts[1], 1, count)
    far = flip((far_parts[0].astype(single) + got.astype(single)).astype(jnp.bfloat16), 2, count)
    near = flip(near_parts[1], 1, count)
    return near_parts[0].astype(single) + near.astype(single) + far.astype(single)


def gather_out(shard):
    whole = lax.all_gather(shard, "dp", axis=0, tiled=True)
    height = D // lax.axis_size("mlp")
    return lax.dynamic_slice_in_dim(whole, lax.axis_index("mlp") * height, height, 0)


def reduce_out(value):
    whole = lax.dynamic_update_slice_in_dim(
        jnp.zeros((D, D), jnp.float32), value, lax.axis_index("mlp") * value.shape[0], 0
    )
    part = lax.psum_scatter(whole.astype(jnp.bfloat16), "dp", scatter_dimension=0, tiled=True)
    return lax.psum(part.astype(jnp.float32), "mlp")


def swapped(values):
    quarter = HDIM // 4
    return jnp.concatenate(
        [
            values[:, quarter : 2 * quarter],
            values[:, :quarter],
            values[:, 3 * quarter :],
            values[:, 2 * quarter : 3 * quarter],
        ],
        axis=1,
    )


def attention_kernel(heads, qkv_ref, cos_ref, sin_ref, mask_ref, low_ref, out_ref, total_ref):
    width = heads * HDIM
    cosine, sine, mask = cos_ref[0], sin_ref[0], mask_ref[0]
    totals = []
    for head in range(heads):
        start = head * HDIM

        def part(which):
            return qkv_ref[0, :, which * width + start : which * width + start + HDIM]

        raw_q, raw_k = part(0), part(1)
        query = (raw_q * cosine + swapped(raw_q) * sine).astype(jnp.bfloat16)
        key = (raw_k * cosine + swapped(raw_k) * sine).astype(jnp.bfloat16)
        value = part(2).astype(jnp.bfloat16)
        for which, kept in enumerate((query, key, value)):
            low_ref[0, :, which * width + start : which * width + start + HDIM] = kept
        scores = lax.dot_general(
            query, key, (((1,), (1,)), ((), ())), preferred_element_type=jnp.float32
        ) * (1.0 / math.sqrt(HDIM))
        scores = jnp.where(mask > 0.0, scores, -1e30)
        row_max = jnp.max(scores, axis=-1, keepdims=True)
        exponent = jnp.exp(scores - row_max)
        row_sum = jnp.sum(exponent, axis=-1, keepdims=True)
        probs = exponent / row_sum
        out_ref[0, :, start : start + HDIM] = jnp.dot(
            probs.astype(jnp.bfloat16), value, preferred_element_type=jnp.float32
        ).astype(jnp.bfloat16)
        totals.append(row_max + jnp.log(row_sum))
    total_ref[0] = jnp.concatenate(totals, axis=1)


def attention(qkv, cosine, sine, mask, heads):
    images, length, width = qkv.shape
    per_image = lambda *dims: pl.BlockSpec((1, *dims), lambda i: (i, 0, 0))
    return pl.pallas_call(
        functools.partial(attention_kernel, heads),
        grid=(images,),
        out_shape=[
            jax.ShapeDtypeStruct((images, length, width), jnp.bfloat16),
            jax.ShapeDtypeStruct((images, length, heads * HDIM), jnp.bfloat16),
            jax.ShapeDtypeStruct((images, length, heads), jnp.float32),
        ],
        in_specs=[
            per_image(length, width),
            per_image(length, HDIM),
            per_image(length, HDIM),
            per_image(1, length),
        ],
        out_specs=[
            per_image(length, width),
            per_image(length, heads * HDIM),
            per_image(length, heads),
        ],
        compiler_params=pltpu.CompilerParams(vmem_limit_bytes=KERNEL_VMEM),
    )(qkv, cosine, sine, mask)


def attention_back_kernel(
    heads, low_ref, total_ref, grad_ref, cos_ref, sin_ref, mask_ref, out_ref
):
    width = heads * HDIM
    scale_by = 1.0 / math.sqrt(HDIM)
    cosine, sine, mask = cos_ref[0], sin_ref[0], mask_ref[0]

    def contract(left, right, dims):
        return lax.dot_general(left, right, (dims, ((), ())), preferred_element_type=jnp.float32)

    for head in range(heads):
        start = head * HDIM

        def spot(which):
            return slice(which * width + start, which * width + start + HDIM)

        query, key, value = (low_ref[0, :, spot(which)] for which in range(3))
        grad = grad_ref[0, :, start : start + HDIM]
        scores = contract(query, key, ((1,), (1,))) * scale_by
        scores = jnp.where(mask > 0.0, scores, -1e30)
        probs = jnp.exp(scores - total_ref[0, :, head : head + 1])
        d_probs = contract(grad, value, ((1,), (1,)))
        row = jnp.sum(probs * d_probs, axis=-1, keepdims=True)
        d_scores = (probs * (d_probs - row)).astype(jnp.bfloat16)
        d_query = contract(d_scores, key, ((1,), (0,))) * scale_by
        d_key = contract(d_scores, query, ((0,), (0,))) * scale_by
        d_value = contract(probs.astype(jnp.bfloat16), grad, ((0,), (0,)))
        for which, turned in ((0, d_query), (1, d_key)):
            back = turned * cosine + swapped(turned * sine)
            out_ref[0, :, spot(which)] = back.astype(jnp.bfloat16)
        out_ref[0, :, spot(2)] = d_value.astype(jnp.bfloat16)


def attention_back(low, totals, grad, cosine, sine, mask, heads):
    images, length, width = low.shape
    per_image = lambda *dims: pl.BlockSpec((1, *dims), lambda i: (i, 0, 0))
    return pl.pallas_call(
        functools.partial(attention_back_kernel, heads),
        grid=(images,),
        out_shape=jax.ShapeDtypeStruct((images, length, width), jnp.bfloat16),
        in_specs=[
            per_image(length, width),
            per_image(length, heads),
            per_image(length, heads * HDIM),
            per_image(length, HDIM),
            per_image(length, HDIM),
            per_image(1, length),
        ],
        out_specs=per_image(length, width),
        compiler_params=pltpu.CompilerParams(vmem_limit_bytes=KERNEL_VMEM),
    )(low, totals, grad, cosine, sine, mask)


def turn_tables(patch_grid, length):
    slot_index = jnp.arange(length, dtype=jnp.int32)[None, :]
    grid_cols = patch_grid[:, 1:2]
    valid_slot = slot_index < patch_grid[:, 0:1] * grid_cols
    row_place = (slot_index // grid_cols).astype(jnp.float32)
    col_place = (slot_index % grid_cols).astype(jnp.float32)
    quarter = HDIM // 4
    frequency = jnp.exp(-math.log(10000.0) * jnp.arange(quarter, dtype=jnp.float32) / quarter)
    row_angle = row_place[..., None] * frequency
    col_angle = col_place[..., None] * frequency
    cos_row, sin_row = jnp.cos(row_angle), jnp.sin(row_angle)
    cos_col, sin_col = jnp.cos(col_angle), jnp.sin(col_angle)
    return (
        jnp.concatenate([cos_row, cos_row, cos_col, cos_col], axis=-1),
        jnp.concatenate([-sin_row, sin_row, -sin_col, sin_col], axis=-1),
        valid_slot.astype(jnp.float32)[:, None, :],
    )


def valid_slots(patch_grid, length):
    return jnp.arange(length, dtype=jnp.int32)[None, :] < patch_grid[:, 0:1] * patch_grid[:, 1:2]


def device_parts():
    d, m = lax.axis_index("dp"), lax.axis_index("mlp")
    return d, m, lax.div(d, NX), lax.rem(d, NX)


class Sender:
    def __init__(self, send_sem, recv_sem):
        self.send_sem, self.recv_sem = send_sem, recv_sem

    def __call__(self, spot, source, target, device):
        spot = spot if isinstance(spot, tuple) else (spot,)
        return pltpu.make_async_remote_copy(
            src_ref=source,
            dst_ref=target,
            send_sem=self.send_sem.at[spot],
            recv_sem=self.recv_sem.at[spot],
            device_id=device,
            device_id_type=MESH_IDS,
        )


def modulate_rows(values, shift_by, scale_by):
    row_mean = jnp.mean(values, axis=-1, keepdims=True)
    centered = values - row_mean
    variance = jnp.mean(centered * centered, axis=-1, keepdims=True)
    return centered * lax.rsqrt(variance + 1e-06) * (1.0 + scale_by) + shift_by


def named(inputs, outputs, scratch, refs):
    ends = len(inputs._fields), len(inputs._fields) + len(outputs._fields)
    parts = inputs(*refs[: ends[0]]), outputs(*refs[ends[0] : ends[1]]), scratch(*refs[ends[1] :])
    return SimpleNamespace(**{k: v for part in parts for k, v in part._asdict().items()})


class ForwardIn(NamedTuple):
    facts: Any
    trig: Any
    small: Any
    time_first: Any
    first_bias: Any
    second_bias: Any
    class_table: Any
    matrices: Any
    mod_bias: Any
    noisy: Any
    patch_bias: Any
    qkv_shard: Any
    ff_shard: Any
    qkv_bias: Any
    out_bias: Any


class ForwardOut(NamedTuple):
    facts_all: Any
    trig_all_out: Any
    small_all: Any
    time_pre: Any
    condition: Any
    modulation: Any
    hidden: Any
    one_rows_out: Any
    qkv_weight_out: Any
    out_weight_out: Any
    ff: Any
    low_out: Any
    attended_out: Any
    totals: Any
    branch: Any
    hidden_mid: Any
    two_rows: Any


class ForwardScratch(NamedTuple):
    one_rows: Any
    qkv_weight: Any
    out_weight: Any
    low: Any
    attended: Any
    trig_all: Any
    leave_sem: Any
    time_low: Any
    out_low: Any
    time_send: Any
    time_recv: Any
    mod_send: Any
    mod_recv: Any
    mod_low: Any
    qkv: Any
    parts_send: Any
    parts_recv: Any
    facts_s: Any
    facts_r: Any
    small_s: Any
    small_r: Any
    time_s: Any
    time_r: Any
    mods_s: Any
    mods_r: Any
    trig_s: Any
    trig_r: Any
    noisy_s: Any
    noisy_r: Any
    kinds_s: Any
    kinds_r: Any
    noisy_all: Any
    kinds_all: Any
    two_s: Any
    two_r: Any
    part_s: Any
    part_r: Any
    qz_s: Any
    qz_r: Any
    qx_s: Any
    qx_r: Any
    oz_s: Any
    oz_r: Any
    ox_s: Any
    ox_r: Any
    fz_s: Any
    fz_r: Any
    fx_s: Any
    fx_r: Any
    local_sem: Any


def forward_kernel(sizes, *refs):
    r = named(ForwardIn, ForwardOut, ForwardScratch, refs)
    bfloat, single = jnp.bfloat16, jnp.float32
    n_data, n_model = sizes
    everyone = n_data * n_model
    d, m, z, x = device_parts()
    me = d * n_model + m
    depth = n_data // NX
    rows = D // n_data
    heads = HEADS // n_model
    head_cols = heads * HDIM
    length = r.noisy.shape[0]
    units = r.ff_shard.shape[2]
    half = units // 2

    def at_dp(spot):
        return (spot, m)

    def at_mlp(bit):
        flipped = m + 1 - 2 * lax.rem(m, 2) if bit == 1 else lax.rem(m + 2, 4)
        return (d, flipped)

    up = lax.rem(z + 1, depth) * NX + x
    down = lax.rem(z + depth - 1, depth) * NX + x
    side = z * NX + 1 - x

    barrier = pltpu.get_barrier_semaphore()

    def greet(step, carry):
        peer = lax.rem(me + step, everyone)
        pl.semaphore_signal(
            barrier,
            inc=1,
            device_id=(lax.div(peer, n_model), lax.rem(peer, n_model)),
            device_id_type=MESH_IDS,
        )
        return carry

    lax.fori_loop(1, everyone, greet, 0)

    load_out = pltpu.make_async_copy(
        r.matrices.at[:, pl.ds(12 * D, D)], r.out_low, r.local_sem.at[2]
    )
    load_out.start()
    load_time = pltpu.make_async_copy(
        r.matrices.at[:, pl.ds(0, D)], r.time_low, r.local_sem.at[3]
    )
    load_time.start()
    load_mod = pltpu.make_async_copy(
        r.matrices.at[:, pl.ds(D, 8 * D)], r.mod_low, r.local_sem.at[0]
    )
    load_mod.start()
    own_ff = pltpu.make_async_copy(
        r.ff_shard,
        r.ff.at[:, pl.ds(pl.multiple_of(d * rows, 16), rows)],
        r.local_sem.at[1],
    )
    own_ff.start()
    pl.semaphore_wait(barrier, everyone - 1)

    send_facts = Sender(r.facts_s, r.facts_r)

    def facts_copy(step):
        peer = lax.rem(me + step, everyone)
        return send_facts(
            step - 1,
            r.facts,
            r.facts_all.at[me],
            (lax.div(peer, n_model), lax.rem(peer, n_model)),
        )

    def loop(first, last, body):
        def step_body(step, carry):
            body(step)
            return carry

        lax.fori_loop(first, last, step_body, 0)

    loop(1, everyone, lambda step: facts_copy(step).start())
    r.facts_all[me] = r.facts[...]

    def qkv_rows(spot, part):
        if part == 0:
            return r.qkv_weight.at[pl.ds(pl.multiple_of(spot * rows, 16), 80)]
        return r.qkv_weight.at[pl.ds(pl.multiple_of(spot * rows + 80, 16), rows - 80)]

    def ff_block(spot, part, which):
        return r.ff.at[
            which,
            pl.ds(pl.multiple_of(spot * rows, 16), rows),
            pl.ds(half * part, half),
        ]

    def origin(step, part):
        return lax.rem(z + (depth - step if part == 0 else step), depth) * NX + x

    qz, qx = Sender(r.qz_s, r.qz_r), Sender(r.qx_s, r.qx_r)
    fz, fx = Sender(r.fz_s, r.fz_r), Sender(r.fx_s, r.fx_r)

    def qkv_along(step, part):
        block = qkv_rows(origin(step - 1, part), part)
        return qz((part, step - 1), block, block, at_dp(up if part == 0 else down))

    def qkv_aside(step, part):
        block = qkv_rows(origin(step, part), part)
        return qx((part, step), block, block, at_dp(side))

    def ff_along(step, part, which):
        block = ff_block(origin(step - 1, part), part, which)
        return fz((part, step - 1, which), block, block, at_dp(up if part == 0 else down))

    def ff_aside(step, part, which):
        block = ff_block(origin(step, part), part, which)
        return fx((part, step, which), block, block, at_dp(side))

    own_rows = pl.ds(pl.multiple_of(d * rows, 16), rows)
    r.qkv_weight[own_rows] = r.qkv_shard[...]
    for part in range(2):
        qkv_along(1, part).start()
        qkv_aside(0, part).start()

    send_small = Sender(r.small_s, r.small_r)

    def small_copy(step):
        return send_small(
            step - 1,
            r.small,
            r.small_all.at[own_rows],
            at_dp(lax.rem(d + step, n_data)),
        )

    loop(1, n_data, lambda step: small_copy(step).start())
    r.small_all[own_rows] = r.small[...]
    r.trig_all[0] = r.trig[...]

    def spread(send, buffer):
        return (
            send(0, buffer.at[0], buffer.at[1], at_mlp(1)),
            send(1, buffer.at[0], buffer.at[2], at_mlp(2)),
            send(2, buffer.at[2], buffer.at[3], at_mlp(1)),
        )

    trig_near, trig_far, trig_on = spread(Sender(r.trig_s, r.trig_r), r.trig_all)
    trig_near.start()
    trig_far.start()
    near_rank = m + 1 - 2 * lax.rem(m, 2)
    partners = ((d, near_rank), (d, lax.rem(m + 2, 4)), (d, lax.rem(near_rank + 2, 4)))
    send_noisy, send_kinds = Sender(r.noisy_s, r.noisy_r), Sender(r.kinds_s, r.kinds_r)
    noisy_copies = [
        send_noisy(spot, r.noisy, r.noisy_all.at[spot + 1], partner)
        for spot, partner in enumerate(partners)
    ]
    kinds_copies = [
        send_kinds(spot, r.modulation, r.kinds_all.at[spot + 1], partner)
        for spot, partner in enumerate(partners)
    ]
    for copy in noisy_copies:
        copy.start()
    r.noisy_all[0] = r.noisy[...]

    oz, ox = Sender(r.oz_s, r.oz_r), Sender(r.ox_s, r.ox_r)
    out_place = r.out_weight.at[pl.ds(pl.multiple_of(x * rows, 16), rows)]
    owner = z == m
    load_out.wait()

    def out_along(step):
        return oz(step - 1, out_place, out_place, at_dp(lax.rem(z + step, depth) * NX + x))

    out_aside = ox(0, out_place, out_place, at_dp(side))

    @pl.when(owner)
    def _():
        r.out_weight[pl.ds(pl.multiple_of(x * rows, 16), rows)] = r.out_low[...].astype(bfloat)
        for step in range(1, depth):
            out_along(step).start()
        out_aside.start()


    for part in range(2):
        for which in range(3):
            own = r.ff_shard.at[which, :, pl.ds(half * part, half)]
            fz(
                (part, 0, which),
                own,
                ff_block(d, part, which),
                at_dp(up if part == 0 else down),
            ).start()
            fx((part, 0, which), own, ff_block(d, part, which), at_dp(side)).start()

    loop(1, everyone, lambda step: facts_copy(step).wait())
    facts_all = r.facts_all[...]
    sinus = jnp.concatenate([facts_all[:, 0], facts_all[:, 1]], axis=1).astype(bfloat)
    labels = facts_all[:, 2, 0:1]
    time_pre = (
        jnp.dot(sinus, r.time_first[...], preferred_element_type=single) + r.first_bias[...]
    )
    r.time_pre[...] = time_pre
    time_act = (time_pre * jax.nn.sigmoid(time_pre)).astype(bfloat)
    send_time = Sender(r.time_s, r.time_r)

    def time_copy(step):
        peer = lax.rem(d + step, n_data)
        return send_time(
            step - 1, r.time_send.at[peer], r.time_recv.at[d], at_dp(peer)
        )

    load_time.wait()
    time_part = jnp.dot(time_act, r.time_low[...].astype(bfloat), preferred_element_type=single)
    for spot in range(n_data):
        r.time_send[spot] = time_part[:, spot * rows : (spot + 1) * rows]
    loop(1, n_data, lambda step: time_copy(step).start())
    r.time_recv[d] = r.time_send[d]

    def qkv_service(step):
        for part in range(2):
            qkv_along(step, part).wait_recv()
            if step < depth - 1:
                qkv_along(step + 1, part).start()
            qkv_aside(step, part).start()

    qkv_service(1)
    onehot = (
        labels == lax.broadcasted_iota(jnp.int32, (everyone, CLASSES + 1), 1).astype(single)
    ).astype(bfloat)
    picked = jnp.dot(onehot, r.class_table[...], preferred_element_type=single)
    load_mod.wait()

    loop(1, n_data, lambda step: time_copy(step).wait())
    condition = jnp.sum(r.time_recv[...], axis=0) + r.second_bias[...] + picked
    r.condition[...] = condition
    cond_act = (condition * jax.nn.sigmoid(condition)).astype(bfloat)
    pick = (
        lax.broadcasted_iota(jnp.int32, (n_data, everyone), 1)
        == lax.broadcasted_iota(jnp.int32, (n_data, everyone), 0) * n_model + m
    ).astype(bfloat)
    cond_rank = jnp.dot(pick, cond_act, preferred_element_type=single).astype(bfloat)
    for kind in range(8):
        block = jnp.dot(
            cond_rank,
            r.mod_low[:, kind * D : (kind + 1) * D].astype(bfloat),
            preferred_element_type=single,
        )
        for spot in range(n_data):
            r.mod_send[spot, kind : kind + 1] = block[spot : spot + 1]
    send_mods = Sender(r.mods_s, r.mods_r)

    def mods_copy(step):
        peer = lax.rem(d + step, n_data)
        return send_mods(step - 1, r.mod_send.at[peer], r.mod_recv.at[d], at_dp(peer))

    loop(1, n_data, lambda step: mods_copy(step).start())
    r.mod_recv[d] = r.mod_send[d]
    def ff_service(step, which):
        for part in range(2):
            ff_along(step, part, which).wait_recv()
            if step < depth - 1:
                ff_along(step + 1, part, which).start()
            ff_aside(step, part, which).start()

    qkv_service(2)
    ff_service(1, 0)
    loop(1, n_data, lambda step: small_copy(step).wait())
    trig_far.wait_recv()
    trig_on.start()
    hidden = (
        lax.dot_general(
            r.noisy[...],
            r.small_all[:, 0:CH],
            (((1,), (1,)), ((), ())),
            preferred_element_type=single,
        )
        + r.patch_bias[...]
    )
    r.hidden[...] = hidden
    loop(1, n_data, lambda step: mods_copy(step).wait())
    modulation = jnp.sum(r.mod_recv[...], axis=0) + r.mod_bias[...]
    r.modulation[...] = modulation

    def kind_of(kind):
        return r.modulation[kind : kind + 1]

    for copy in kinds_copies:
        copy.start()
    r.kinds_all[0] = modulation
    qkv_service(3)
    ff_service(1, 1)
    ff_service(1, 2)

    @pl.when(jnp.logical_not(owner))
    def _():
        oz(
            lax.rem(z + depth - m, depth) - 1, out_place, out_place, at_dp(up)
        ).wait_recv()
        out_aside.start()

    for part in range(2):
        for step in range(depth):
            qkv_aside(step, part).wait_recv()
    for copy in noisy_copies + kinds_copies:
        copy.wait_recv()
    trig_near.wait_recv()
    trig_on.wait_recv()

    def image_body(step, carry):
        image = n_model - 1 - step
        start_rows = (
            lax.dot_general(
                r.noisy_all[image],
                r.small_all[:, 0:CH],
                (((1,), (1,)), ((), ())),
                preferred_element_type=single,
            )
            + r.patch_bias[...]
        )
        r.one_rows[image] = modulate_rows(
            start_rows, r.kinds_all[image, 0:1], r.kinds_all[image, 1:2]
        ).astype(bfloat)
        r.qkv[...] = (
            jnp.dot(r.one_rows[image], r.qkv_weight[...], preferred_element_type=single)
            + r.qkv_bias[...]
        )
        rank = (
            2 * lax.rem(lax.div(m, 2) + lax.div(image, 2), 2)
            + lax.rem(lax.rem(m, 2) + lax.rem(image, 2), 2)
        )
        count = r.facts_all[d * n_model + rank, 2:3, 1:2]
        mask = lax.broadcasted_iota(jnp.int32, (1, length), 1).astype(single) < count
        cosine, sine = r.trig_all[image, 0], r.trig_all[image, 1]
        totals = []
        for head in range(heads):
            start = head * HDIM

            def part(which):
                return r.qkv[:, which * head_cols + start : which * head_cols + start + HDIM]

            raw_q, raw_k = part(0), part(1)
            query = (raw_q * cosine + swapped(raw_q) * sine).astype(bfloat)
            key = (raw_k * cosine + swapped(raw_k) * sine).astype(bfloat)
            value = part(2).astype(bfloat)
            for which, kept in enumerate((query, key, value)):
                low = which * head_cols + start
                r.low[image, :, low : low + HDIM] = kept
            scores = lax.dot_general(
                query, key, (((1,), (1,)), ((), ())), preferred_element_type=single
            ) * (1.0 / math.sqrt(HDIM))
            scores = jnp.where(mask, scores, -1e30)
            row_max = jnp.max(scores, axis=-1, keepdims=True)
            exponent = jnp.exp(scores - row_max)
            row_sum = jnp.sum(exponent, axis=-1, keepdims=True)
            probs = exponent / row_sum
            r.attended[image, :, start : start + HDIM] = jnp.dot(
                probs.astype(bfloat), value, preferred_element_type=single
            ).astype(bfloat)
            totals.append(row_max + jnp.log(row_sum))
        r.totals[image] = jnp.concatenate(totals, axis=1)
        return carry

    lax.fori_loop(0, 2, image_body, 0)

    @pl.when(owner)
    def _():
        for step in range(1, depth):
            out_along(step).wait_send()

    out_aside.wait()

    def partial(image):
        return jnp.dot(r.attended[image], r.out_weight[...], preferred_element_type=single)

    send_part = Sender(r.part_s, r.part_r)
    to_core = send_part(0, r.parts_send.at[0], r.parts_recv.at[0], at_mlp(1))
    to_far = send_part(1, r.parts_send.at[1], r.parts_recv.at[1], at_mlp(2))
    to_near = send_part(2, r.parts_send.at[2], r.parts_recv.at[2], at_mlp(1))
    r.parts_send[0] = partial(3).astype(bfloat)
    to_core.start()
    r.branch[...] = partial(2)
    to_core.wait_recv()
    r.parts_send[1] = (r.branch[...] + r.parts_recv[0].astype(single)).astype(bfloat)
    to_far.start()
    for which in range(3):
        ff_service(2, which)
    lax.fori_loop(2, n_model, image_body, 0)
    leaves = [
        pltpu.make_async_copy(source, target, r.leave_sem.at[spot])
        for spot, (source, target) in enumerate(
            (
                (r.one_rows, r.one_rows_out),
                (r.qkv_weight, r.qkv_weight_out),
                (r.out_weight, r.out_weight_out),
                (r.low, r.low_out),
                (r.attended, r.attended_out),
                (r.trig_all, r.trig_all_out),
            )
        )
    ]
    for leave in leaves:
        leave.start()
    r.parts_send[2] = partial(1).astype(bfloat)
    to_near.start()
    own_part = partial(0) + r.out_bias[...]
    ff_service(3, 0)
    to_near.wait_recv()
    to_far.wait_recv()
    branch = own_part + r.parts_recv[2].astype(single) + r.parts_recv[1].astype(single)
    r.branch[...] = branch
    hidden_mid = r.hidden[...] + kind_of(2) * branch
    r.hidden_mid[...] = hidden_mid
    r.two_rows[0] = modulate_rows(hidden_mid, kind_of(3), kind_of(4)).astype(bfloat)
    two_near, two_far, two_on = spread(Sender(r.two_s, r.two_r), r.two_rows)
    two_far.start()
    two_near.start()
    ff_service(3, 1)
    ff_service(3, 2)
    two_far.wait_recv()
    two_on.start()

    own_ff.wait()
    for leave in leaves:
        leave.wait()
    for part in range(2):
        for step in range(depth):
            for which in range(3):
                ff_aside(step, part, which).wait()
            qkv_aside(step, part).wait_send()
            if step:
                for which in range(3):
                    ff_along(step, part, which).wait_send()
                qkv_along(step, part).wait_send()
    for copy in (two_near, two_on):
        copy.wait()
    two_far.wait_send()
    for copy in (trig_near, trig_far, trig_on, to_core, to_far, to_near):
        copy.wait_send()
    for copy in noisy_copies + kinds_copies:
        copy.wait_send()


def forward_all(values, sizes, collective):
    n_data, n_model = sizes
    bfloat, single = jnp.bfloat16, jnp.float32
    everyone = n_data * n_model
    rows = D // n_data
    heads = HEADS // n_model
    head_cols = heads * HDIM
    length = values.noisy.shape[0]
    units = values.ff_shard.shape[2]
    depth = n_data // NX
    shapes = dict(
        facts_all=((everyone, 8, 128), single),
        trig_all_out=((n_model, 2, length, HDIM), single),
        small_all=((D, 128), bfloat),
        time_pre=((everyone, rows), single),
        condition=((everyone, rows), single),
        modulation=((8, D), single),
        hidden=((length, D), single),
        one_rows_out=((n_model, length, D), bfloat),
        qkv_weight_out=((D, 3 * head_cols), bfloat),
        out_weight_out=((head_cols, D), bfloat),
        ff=((3, D, units), bfloat),
        low_out=((n_model, length, 3 * head_cols), bfloat),
        attended_out=((n_model, length, head_cols), bfloat),
        totals=((n_model, length, heads), single),
        branch=((length, D), single),
        hidden_mid=((length, D), single),
        two_rows=((n_model, length, D), bfloat),
    )
    dma = pltpu.SemaphoreType.DMA
    scratch = dict(
        time_send=pltpu.VMEM((n_data, everyone, rows), single),
        time_recv=pltpu.VMEM((n_data, everyone, rows), single),
        mod_send=pltpu.VMEM((n_data, 8, D), single),
        mod_recv=pltpu.VMEM((n_data, 8, D), single),
        mod_low=pltpu.VMEM((rows, 8 * D), single),
        time_low=pltpu.VMEM((rows, D), single),
        out_low=pltpu.VMEM((rows, D), single),
        qkv=pltpu.VMEM((length, 3 * head_cols), single),
        noisy_all=pltpu.VMEM((n_model, length, CH), bfloat),
        kinds_all=pltpu.VMEM((n_model, 8, D), single),
        parts_send=pltpu.VMEM((3, length, D), bfloat),
        parts_recv=pltpu.VMEM((3, length, D), bfloat),
        local_sem=dma((4,)),
        leave_sem=dma((6,)),
    )
    counts = dict(
        facts=(everyone - 1,),
        small=(n_data - 1,),
        time=(n_data - 1,),
        mods=(n_data - 1,),
        trig=(3,),
        noisy=(3,),
        kinds=(3,),
        two=(3,),
        part=(3,),
        qz=(2, depth - 1),
        qx=(2, depth),
        oz=(depth - 1,),
        ox=(1,),
        fz=(2, depth - 1, 3),
        fx=(2, depth, 3),
    )
    for name, count in counts.items():
        scratch[name + "_s"] = dma(count)
        scratch[name + "_r"] = dma(count)
    for name in ForwardOut._fields:
        if name.endswith("_out"):
            scratch[name[:-4]] = pltpu.VMEM(*shapes[name])
    far = {"matrices", "ff_shard", "ff"}

    def space(name):
        outside = name in far or name.endswith("_out")
        return pl.BlockSpec(memory_space=pl.ANY if outside else pltpu.VMEM)

    outs = pl.pallas_call(
        functools.partial(forward_kernel, sizes),
        out_shape=[jax.ShapeDtypeStruct(*shapes[name]) for name in ForwardOut._fields],
        in_specs=[space(name) for name in ForwardIn._fields],
        out_specs=[space(name) for name in ForwardOut._fields],
        scratch_shapes=[scratch[name] for name in ForwardScratch._fields],
        compiler_params=pltpu.CompilerParams(
            collective_id=collective, has_side_effects=True, vmem_limit_bytes=56 * 2**20
        ),
    )(*values)
    return ForwardOut(*outs)


class BackIn(NamedTuple):
    ff: Any
    two_rows: Any
    hidden_mid: Any
    hidden: Any
    branch: Any
    modulation: Any
    small_all: Any
    final_bias: Any
    clean: Any
    noise: Any
    consts: Any
    valid: Any
    noisy: Any
    low: Any
    totals: Any
    trig_all: Any
    facts_all: Any
    attended: Any
    one_rows: Any
    qkv_weight: Any
    out_weight: Any
    matrices: Any
    time_pre: Any
    condition: Any


class BackOut(NamedTuple):
    bias_rows: Any
    own: Any
    norm: Any
    factor: Any
    loss_sum: Any
    dmod: Any
    dtime: Any
    d_condition: Any
    d_time_pre: Any
    grad_ff: Any
    grad_qkv: Any
    grad_out: Any


class BackScratch(NamedTuple):
    time_low: Any
    late: Any
    d_modulation: Any
    local: Any
    sums: Any
    sums_recv: Any
    pay: Any
    dmod_row: Any
    dmod_all: Any
    dmod_wide: Any
    dtime_mine: Any
    dtime_recv: Any
    dtime_wide: Any
    loss: Any
    sm_s: Any
    sm_r: Any
    dl_s: Any
    dl_r: Any
    dt_s: Any
    dt_r: Any
    lt_s: Any
    lt_r: Any
    d_end: Any
    dm_rows: Any
    db_rows: Any
    hold_far: Any
    hold_near: Any
    parts_send: Any
    parts_recv: Any
    normed_end: Any
    g_ff: Any
    x_ff: Any
    z_ff: Any
    g_qkv: Any
    x_qkv: Any
    z_qkv: Any
    g_out: Any
    x_out: Any
    z_out: Any
    out_mine: Any
    dm_s: Any
    dm_r: Any
    db_s: Any
    db_r: Any
    pa_s: Any
    pa_r: Any
    pb_s: Any
    pb_r: Any
    pc_s: Any
    pc_r: Any
    fx_s: Any
    fx_r: Any
    fz_s: Any
    fz_r: Any
    qx_s: Any
    qx_r: Any
    qz_s: Any
    qz_r: Any
    ox_s: Any
    ox_r: Any
    oz_s: Any
    oz_r: Any
    qa_s: Any
    qa_r: Any
    oa_s: Any
    oa_r: Any
    local_sem: Any


ROW_CHUNK = 64


def modulate_back(values, grad, scale_by):
    row_mean = jnp.mean(values, axis=-1, keepdims=True)
    centered = values - row_mean
    variance = jnp.mean(centered * centered, axis=-1, keepdims=True)
    inverse = lax.rsqrt(variance + 1e-06)
    normal = centered * inverse
    inner = grad * (1.0 + scale_by)
    back = inverse * (
        inner
        - jnp.mean(inner, axis=-1, keepdims=True)
        - normal * jnp.mean(inner * normal, axis=-1, keepdims=True)
    )
    return back, normal


def fold(values):
    total = values[:8]
    for start in range(8, values.shape[0], 8):
        total = total + values[start : start + 8]
    return total


def back_kernel(sizes, total_images, *refs):
    r = named(BackIn, BackOut, BackScratch, refs)
    bfloat, single = jnp.bfloat16, jnp.float32
    n_data, n_model = sizes
    d, m, z, x = device_parts()
    depth = n_data // NX
    rows = D // n_data
    heads = HEADS // n_model
    head_cols = heads * HDIM
    length = r.clean.shape[0]
    units = r.ff.shape[2]
    half = units // 2

    def at_dp(spot):
        return (spot, m)

    near_rank = m + 1 - 2 * lax.rem(m, 2)
    far_rank = lax.rem(m + 2, 4)

    def at_mlp(bit):
        return (d, near_rank if bit == 1 else far_rank)

    up = lax.rem(z + 1, depth) * NX + x
    down = lax.rem(z + depth - 1, depth) * NX + x
    side = z * NX + 1 - x
    barrier = pltpu.get_barrier_semaphore()
    everyone = n_data * n_model
    me = d * n_model + m

    def loop(first, last, body):
        def step_body(step, carry):
            body(step)
            return carry

        lax.fori_loop(first, last, step_body, 0)

    def anyone(step):
        peer = lax.rem(me + step, everyone)
        return peer, (lax.div(peer, n_model), lax.rem(peer, n_model))

    loop(
        1,
        everyone,
        lambda step: pl.semaphore_signal(
            barrier, inc=1, device_id=anyone(step)[1], device_id_type=MESH_IDS
        ),
    )
    pl.semaphore_wait(barrier, everyone - 1)

    def chunks(body, carry, amount=ROW_CHUNK, count=length):
        def step_body(step, held):
            return body(pl.ds(pl.multiple_of(step * amount, amount), amount), held)

        return lax.fori_loop(0, count // amount, step_body, carry)

    def kind_of(kind):
        return r.modulation[kind : kind + 1]

    def dot(left, right, dims):
        return lax.dot_general(left, right, (dims, ((), ())), preferred_element_type=single)

    zeros = jnp.zeros((8, D), single)

    def spread(send, buffer):
        return (
            send(0, buffer.at[0], buffer.at[1], at_mlp(1)),
            send(1, buffer.at[0], buffer.at[2], at_mlp(2)),
            send(2, buffer.at[2], buffer.at[3], at_mlp(1)),
        )

    def part_copies(*sems):
        send = Sender(*sems)
        return tuple(
            send(spot, r.parts_send.at[spot], r.parts_recv.at[spot], at_mlp(bit))
            for spot, bit in ((0, 1), (1, 2), (2, 1))
        )

    def add_far(copies):
        to_core, to_far, to_near = copies
        to_core.wait_recv()

        def body(at, held):
            r.parts_send[1, at] = (
                r.hold_far[at] + r.parts_recv[0, at].astype(single)
            ).astype(bfloat)
            return held

        chunks(body, 0)
        to_far.start()

    fx, fz = Sender(r.fx_s, r.fx_r), Sender(r.fz_s, r.fz_r)
    qx, qz = Sender(r.qx_s, r.qx_r), Sender(r.qz_s, r.qz_r)

    def block_rows(z_spot, x_spot):
        return pl.ds(pl.multiple_of((z_spot * NX + x_spot) * rows, 16), rows)

    def ff_aside(which, step):
        z_spot = lax.rem(z + step, depth)
        return fx(
            (which, step),
            r.g_ff.at[which, block_rows(z_spot, 1 - x)],
            r.x_ff.at[which, z_spot],
            at_dp(side),
        )

    def target_of(step, part):
        return lax.rem(z + (depth - 1 - step if part == 0 else 1 + step), depth)

    def ff_along(which, step, part):
        lanes = pl.ds(half * part, half)
        return fz(
            (which, step, part),
            r.g_ff.at[which, block_rows(target_of(step, part), x), lanes],
            r.z_ff.at[which, step, part],
            at_dp(up if part == 0 else down),
        )

    def ff_start(which):
        for step in (3, 1, 2, 0):
            ff_aside(which, step).start()

    def ff_absorb(which, step):
        ff_aside(which, step).wait_recv()
        z_spot = lax.rem(z + step, depth)
        at = block_rows(z_spot, x)
        r.g_ff[which, at] = (
            r.g_ff[which, at].astype(single) + r.x_ff[which, z_spot].astype(single)
        ).astype(bfloat)

    def ff_beside(which):
        ff_absorb(which, 3)
        ff_absorb(which, 1)
        for part in range(2):
            ff_along(which, 0, part).start()

    def ff_service(which, step):
        if step != 1:
            ff_absorb(which, 2 - step)
        for part in range(2):
            ff_along(which, step, part).wait_recv()
            lanes = pl.ds(half * part, half)
            at = block_rows(target_of(step + 1, part), x)
            running = r.z_ff[which, step, part].astype(single) + r.g_ff[
                which, at, lanes
            ].astype(single)
            if step < depth - 2:
                r.g_ff[which, at, lanes] = running.astype(bfloat)
                ff_along(which, step + 1, part).start()
            else:
                r.grad_ff[which, :, lanes] = running

    tops = (pl.ds(0, 80), pl.ds(80, rows - 80))

    def part_rows(z_spot, part):
        start = (z_spot * NX + x) * rows + 80 * part
        return pl.ds(pl.multiple_of(start, 16), 80 if part == 0 else rows - 80)

    def qkv_aside(step):
        z_spot = lax.rem(z + step, depth)
        return qx(
            step,
            r.g_qkv.at[block_rows(z_spot, 1 - x)],
            r.x_qkv.at[z_spot],
            at_dp(side),
        )

    def qkv_along(step, part):
        return qz(
            (step, part),
            r.g_qkv.at[part_rows(target_of(step, part), part)],
            r.z_qkv.at[step, tops[part]],
            at_dp(up if part == 0 else down),
        )

    def qkv_absorb(step):
        qkv_aside(step).wait_recv()
        z_spot = lax.rem(z + step, depth)
        at = block_rows(z_spot, x)
        r.g_qkv[at] = (r.g_qkv[at].astype(single) + r.x_qkv[z_spot].astype(single)).astype(bfloat)

    def qkv_beside():
        qkv_absorb(3)
        qkv_absorb(1)
        for part in range(2):
            qkv_along(0, part).start()

    def qkv_service(step):
        if step != 1:
            qkv_absorb(2 - step)
        for part in range(2):
            qkv_along(step, part).wait_recv()
            at = part_rows(target_of(step + 1, part), part)
            running = (
                r.z_qkv[step, tops[part]].astype(single) + r.g_qkv[at].astype(single)
            ).astype(bfloat)
            if step < depth - 2:
                r.g_qkv[at] = running
                qkv_along(step + 1, part).start()
            else:
                r.grad_qkv[0, tops[part]] = running

    dm_near, dm_far, dm_on = spread(Sender(r.dm_s, r.dm_r), r.dm_rows)
    first_parts = part_copies(r.pa_s, r.pa_r)
    second_parts = part_copies(r.pb_s, r.pb_r)
    third_parts = part_copies(r.pc_s, r.pc_r)

    def swiglu(ff, two_rows, gates, ups, acts, d_gates, d_ups):
        load_ff = pltpu.make_async_copy(r.ff, ff, r.local_sem.at[0])
        load_two = pltpu.make_async_copy(r.two_rows, two_rows, r.local_sem.at[1])
        load_ff.start()
        load_two.start()
        load_two.wait()
        load_ff.wait()
        wide = 2 * length

        def rows_of(ref, which):
            return ref[2 * which : 2 * which + 2].reshape(wide, D)

        def inner(which):
            part = rows_of(two_rows, which)
            spot = pl.ds(which * wide, wide)
            gates[spot] = dot(part, ff[0], ((1,), (0,)))
            ups[spot] = dot(part, ff[1], ((1,), (0,)))

            def body(at, held):
                at = pl.ds(pl.multiple_of(at.start + which * wide, 64), 64)
                gate = gates[at]
                acts[at] = (gate * jax.nn.sigmoid(gate) * ups[at]).astype(bfloat)
                return held

            chunks(body, 0, 64, wide)

        def outer(image):
            return dot(acts[image * length : (image + 1) * length], ff[2], ((1,), (1,)))

        inner(1)
        r.parts_send[0] = outer(3).astype(bfloat)
        first_parts[0].start()
        r.hold_far[...] = outer(2)
        add_far(first_parts)
        inner(0)
        r.parts_send[2] = outer(1).astype(bfloat)
        first_parts[2].start()
        r.hold_near[...] = outer(0)
        first_parts[2].wait_recv()
        first_parts[1].wait_recv()

        def ending(at, held):
            mixed = (
                r.hold_near[at]
                + r.parts_recv[2, at].astype(single)
                + r.parts_recv[1, at].astype(single)
            )
            r.d_end[at] = mixed
            end = r.hidden_mid[at] + kind_of(5) * mixed
            r.normed_end[at] = modulate_rows(end, kind_of(6), kind_of(7)).astype(bfloat)
            return held

        chunks(ending, 0)

        eps_weight, var_weight = r.small_all[:, 32:48], r.small_all[:, 48:64]
        normed_end = r.normed_end[...]
        eps = dot(normed_end, eps_weight, ((1,), (0,))) + r.final_bias[0:1]
        var = dot(normed_end, var_weight, ((1,), (0,))) + r.final_bias[1:2]
        clean, noise, valid = r.clean[...], r.noise[...], r.valid[...]
        root_bar, root_rest, log_beta, post_log, coefficient = (
            r.consts[0:1, spot : spot + 1] for spot in range(5)
        )
        noisy = root_bar * clean + root_rest * noise
        fraction = (var + 1.0) * 0.5
        model_log = fraction * log_beta + (1.0 - fraction) * post_log
        start_est = (noisy - root_rest * eps) / root_bar
        gap = coefficient * (clean - start_est)
        ratio = jnp.exp(post_log - model_log)
        gap_part = gap * gap * jnp.exp(-model_log)
        scale_by = 0.5 / math.log(2.0)
        terms = (eps - noise) * (eps - noise) + scale_by * (
            -1.0 + model_log - post_log + ratio + gap_part
        )
        terms = jnp.where(valid > 0.0, terms, 0.0)
        r.loss[...] = jnp.sum(jnp.sum(terms, axis=1, keepdims=True), axis=0, keepdims=True)
        d_eps = 2.0 * (eps - noise) + 2.0 * scale_by * gap * jnp.exp(-model_log) * (
            coefficient * root_rest / root_bar
        )
        d_var = scale_by * (1.0 - ratio - gap_part) * (0.5 * (log_beta - post_log))
        share = 1.0 / total_images
        d_eps = jnp.where(valid > 0.0, d_eps * share, 0.0).astype(bfloat)
        d_var = jnp.where(valid > 0.0, d_var * share, 0.0).astype(bfloat)
        r.local[48:56] = zeros
        r.local[54:55, 0:CH] = jnp.sum(d_eps.astype(single), axis=0, keepdims=True)
        r.local[54:55, CH : 2 * CH] = jnp.sum(d_var.astype(single), axis=0, keepdims=True)
        r.local[CH : 2 * CH] = dot(d_eps, normed_end, ((0,), (0,)))
        r.local[2 * CH : 3 * CH] = dot(d_var, normed_end, ((0,), (0,)))
        r.hold_far[...] = dot(d_eps, eps_weight, ((1,), (1,))) + dot(
            d_var, var_weight, ((1,), (1,))
        )

        def end_back(at, held):
            shift_sum, scale_sum, gate_sum = held
            mixed, grad = r.d_end[at], r.hold_far[at]
            end = r.hidden_mid[at] + kind_of(5) * mixed
            back, normal = modulate_back(end, grad, kind_of(7))
            r.d_end[at] = back
            r.dm_rows[0, at] = (kind_of(5) * back).astype(bfloat)
            return (
                shift_sum + fold(grad),
                scale_sum + fold(grad * normal),
                gate_sum + fold(mixed * back),
            )

        shift_sum, scale_sum, gate_sum = chunks(end_back, (zeros, zeros, zeros))
        dm_far.start()
        dm_near.start()
        for kind, value in ((6, shift_sum), (7, scale_sum), (5, gate_sum)):
            r.d_modulation[kind : kind + 1] = jnp.sum(value, axis=0, keepdims=True)

        def inner_back(which):
            spot = pl.ds(which * wide, wide)
            gradient = dot(rows_of(r.dm_rows, which), ff[2], ((1,), (0,)))
            gate, up_val = gates[spot], ups[spot]
            sigma = jax.nn.sigmoid(gate)
            d_ups[spot] = (gradient * gate * sigma).astype(bfloat)
            d_gates[spot] = (gradient * up_val * (sigma * (1.0 + gate * (1.0 - sigma)))).astype(
                bfloat
            )

        def outer_back(image):
            spot = pl.ds(image * length, length)
            return dot(d_gates[spot], ff[0], ((1,), (1,))) + dot(d_ups[spot], ff[1], ((1,), (1,)))

        def ff_grad(which, left, right):
            for part in range(2):
                lanes = slice(half * part, half * part + half)
                r.g_ff[which, :, lanes] = dot(left, right[:, lanes], ((0,), (0,))).astype(bfloat)

        dm_near.wait_recv()
        inner_back(0)
        dm_far.wait_recv()
        dm_on.start()
        dm_on.wait_recv()
        inner_back(1)
        for copy in first_parts:
            copy.wait_send()
        r.parts_send[0] = outer_back(3).astype(bfloat)
        second_parts[0].start()
        r.hold_far[...] = outer_back(2)
        add_far(second_parts)
        ff_grad(2, r.dm_rows[...].reshape(2 * wide, D), acts)
        ff_start(2)
        r.parts_send[2] = outer_back(1).astype(bfloat)
        second_parts[2].start()
        r.hold_near[...] = outer_back(0)
        flat = two_rows[...].reshape(2 * wide, D)
        ff_grad(0, flat, d_gates)
        ff_start(0)
        ff_grad(1, flat, d_ups)
        ff_start(1)

    pl.run_scoped(
        swiglu,
        pltpu.VMEM((3, D, units), bfloat),
        pltpu.VMEM((n_model, length, D), bfloat),
        pltpu.VMEM((n_model * length, units), single),
        pltpu.VMEM((n_model * length, units), single),
        pltpu.VMEM((n_model * length, units), bfloat),
        pltpu.VMEM((n_model * length, units), bfloat),
        pltpu.VMEM((n_model * length, units), bfloat),
    )

    db_near, db_far, db_on = spread(Sender(r.db_s, r.db_r), r.db_rows)
    ox, oz = Sender(r.ox_s, r.ox_r), Sender(r.oz_s, r.oz_r)
    out_aside = ox(0, r.g_out.at[1 - x], r.x_out, at_dp(side))
    owner = z == m
    behind = lax.rem(z + depth - m, depth)
    out_along = oz(
        lax.rem(behind + depth - 1, depth),
        r.g_out.at[x],
        r.z_out.at[lax.rem(behind + depth - 1, depth)],
        at_dp(m * NX + x),
    )

    def attend(low, attended, trig, one_rows, qkv_weight, out_weight, d_attended, d_qkv):
        loads = []
        for spot, (source, target) in enumerate(
            (
                (r.out_weight, out_weight),
                (r.low, low),
                (r.trig_all, trig),
                (r.attended, attended),
                (r.one_rows, one_rows),
                (r.qkv_weight, qkv_weight),
            )
        ):
            load = pltpu.make_async_copy(source, target, r.local_sem.at[2 + spot])
            load.start()
            loads.append(load)
        second_parts[2].wait_recv()
        second_parts[1].wait_recv()

        def mid_back(at, held):
            shift_sum, scale_sum, gate_sum, branch_sum = held
            grad = (
                r.hold_near[at]
                + r.parts_recv[2, at].astype(single)
                + r.parts_recv[1, at].astype(single)
            )
            back, normal = modulate_back(r.hidden_mid[at], grad, kind_of(4))
            total = r.d_end[at] + back
            r.d_end[at] = total
            d_branch = (kind_of(2) * total).astype(bfloat)
            r.db_rows[0, at] = d_branch
            return (
                shift_sum + fold(grad),
                scale_sum + fold(grad * normal),
                gate_sum + fold(r.branch[at] * total),
                branch_sum + fold(d_branch.astype(single)),
            )

        sums = chunks(mid_back, (zeros, zeros, zeros, zeros))
        db_far.start()
        db_near.start()
        for kind, value in zip((3, 4, 2), sums):
            r.d_modulation[kind : kind + 1] = jnp.sum(value, axis=0, keepdims=True)
        r.local[49:50] = jnp.sum(sums[3], axis=0, keepdims=True)
        for load in loads:
            load.wait()

        def image_body(image, carry):
            d_attended[...] = dot(
                r.db_rows[image], out_weight[...], ((1,), (1,))
            ).astype(bfloat)
            rank = (
                2 * lax.rem(lax.div(m, 2) + lax.div(image, 2), 2)
                + lax.rem(lax.rem(m, 2) + lax.rem(image, 2), 2)
            )
            count = r.facts_all[d * n_model + rank, 2:3, 1:2]
            mask = lax.broadcasted_iota(jnp.int32, (1, length), 1).astype(single) < count
            cosine, sine = trig[image, 0], trig[image, 1]
            scale_by = 1.0 / math.sqrt(HDIM)
            for head in range(heads):
                start = head * HDIM

                def spot(which):
                    begin = which * head_cols + start
                    return slice(begin, begin + HDIM)

                query, key, value = (low[image, :, spot(which)] for which in range(3))
                grad = d_attended[:, start : start + HDIM]
                scores = dot(query, key, ((1,), (1,))) * scale_by
                scores = jnp.where(mask, scores, -1e30)
                probs = jnp.exp(scores - r.totals[image, :, head : head + 1])
                d_probs = dot(grad, value, ((1,), (1,)))
                row = jnp.sum(probs * d_probs, axis=-1, keepdims=True)
                d_scores = (probs * (d_probs - row)).astype(bfloat)
                d_query = dot(d_scores, key, ((1,), (0,))) * scale_by
                d_key = dot(d_scores, query, ((0,), (0,))) * scale_by
                d_value = dot(probs.astype(bfloat), grad, ((0,), (0,)))
                for which, turned in ((0, d_query), (1, d_key)):
                    back = turned * cosine + swapped(turned * sine)
                    d_qkv[image, :, spot(which)] = back.astype(bfloat)
                d_qkv[image, :, spot(2)] = d_value.astype(bfloat)
            return carry

        db_near.wait_recv()
        lax.fori_loop(0, 2, image_body, 0)
        db_far.wait_recv()
        db_on.start()
        ff_beside(2)
        db_on.wait_recv()
        lax.fori_loop(2, n_model, image_body, 0)

        def one_part(image):
            return dot(d_qkv[image], qkv_weight[...], ((1,), (1,)))

        for copy in second_parts:
            copy.wait_send()
        r.parts_send[0] = one_part(3).astype(bfloat)
        third_parts[0].start()
        r.hold_far[...] = one_part(2)
        add_far(third_parts)
        ff_beside(0)
        ff_service(2, 0)
        r.parts_send[2] = one_part(1).astype(bfloat)
        third_parts[2].start()
        r.hold_near[...] = one_part(0)
        flat_grad = d_qkv[...].reshape(n_model * length, 3 * head_cols)
        r.g_qkv[...] = dot(
            one_rows[...].reshape(n_model * length, D), flat_grad, ((0,), (0,))
        ).astype(bfloat)
        for step in (3, 1, 2, 0):
            qkv_aside(step).start()
        r.g_out[...] = (
            dot(
                attended[...].reshape(n_model * length, head_cols),
                r.db_rows[...].reshape(n_model * length, D),
                ((0,), (0,)),
            )
            .astype(bfloat)
            .reshape(NX, rows, D)
        )
        out_aside.start()
        ones = jnp.ones((8, n_model * length), bfloat)
        qkv_sum = dot(ones, flat_grad, ((1,), (0,)))[0:1]
        for rank in range(n_model):
            r.local[50 + rank : 51 + rank, 0 : 3 * head_cols] = jnp.where(m == rank, qkv_sum, 0.0)

    pl.run_scoped(
        attend,
        pltpu.VMEM((n_model, length, 3 * head_cols), bfloat),
        pltpu.VMEM((n_model, length, head_cols), bfloat),
        pltpu.VMEM((n_model, 2, length, HDIM), single),
        pltpu.VMEM((n_model, length, D), bfloat),
        pltpu.VMEM((D, 3 * head_cols), bfloat),
        pltpu.VMEM((head_cols, D), bfloat),
        pltpu.VMEM((length, head_cols), bfloat),
        pltpu.VMEM((n_model, length, 3 * head_cols), bfloat),
    )
    ff_beside(1)
    ff_service(0, 0)
    ff_service(2, 1)
    third_parts[2].wait_recv()
    third_parts[1].wait_recv()

    def first_back(at, held):
        shift_sum, scale_sum, hidden_sum = held
        grad = (
            r.hold_near[at]
            + r.parts_recv[2, at].astype(single)
            + r.parts_recv[1, at].astype(single)
        )
        back, normal = modulate_back(r.hidden[at], grad, kind_of(1))
        d_hidden = (r.d_end[at] + back).astype(bfloat)
        r.normed_end[at] = d_hidden
        return (
            shift_sum + fold(grad),
            scale_sum + fold(grad * normal),
            hidden_sum + fold(d_hidden.astype(single)),
        )

    sums = chunks(first_back, (zeros, zeros, zeros))
    for kind in range(2):
        r.d_modulation[kind : kind + 1] = jnp.sum(sums[kind], axis=0, keepdims=True)
    r.local[48:49] = jnp.sum(sums[2], axis=0, keepdims=True)
    r.local[0:CH] = dot(r.noisy[...], r.normed_end[...], ((0,), (0,)))

    for kind in range(8):
        r.dmod_wide[2 * kind : 2 * kind + 1] = r.d_modulation[kind : kind + 1, 0 : D // 2]
        r.dmod_wide[2 * kind + 1 : 2 * kind + 2] = r.d_modulation[kind : kind + 1, D // 2 : D]
    r.dmod_row[...] = r.dmod_wide[...].astype(bfloat)
    r.dmod_all[me] = r.dmod_row[...]
    send_dmod = Sender(r.dl_s, r.dl_r)
    loop(
        1,
        everyone,
        lambda step: send_dmod(
            step - 1, r.dmod_row, r.dmod_all.at[me], anyone(step)[1]
        ).start(),
    )
    tiles = D // 128
    for top in range(7):
        for left in range(tiles):
            r.sums[top * tiles + left] = r.local[8 * top : 8 * top + 8, 128 * left : 128 * left + 128]
    r.sums[7 * tiles] = jnp.zeros((8, 128), single)
    send_sums = Sender(r.sm_s, r.sm_r)

    def sums_copy(step):
        peer, device = anyone(step)
        return send_sums(step - 1, r.sums.at[pl.ds(2 * peer, 2)], r.sums_recv.at[me], device)

    loop(1, everyone, lambda step: sums_copy(step).start())
    r.sums_recv[me] = r.sums[pl.ds(2 * me, 2)]
    ff_service(1, 0)
    qkv_beside()
    out_aside.wait()
    r.g_out[x] = (r.g_out[x].astype(single) + r.x_out[...].astype(single)).astype(bfloat)

    @pl.when(jnp.logical_not(owner))
    def _():
        out_along.start()


    time_pre, condition = r.time_pre[...], r.condition[...]
    sigma_time, sigma_cond = jax.nn.sigmoid(time_pre), jax.nn.sigmoid(condition)
    time_act = (time_pre * sigma_time).astype(bfloat)
    cond_act = (condition * sigma_cond).astype(bfloat)

    def gram(value, precision=None):
        return lax.dot_general(
            value,
            value,
            (((1,), (1,)), ((), ())),
            precision=precision,
            preferred_element_type=single,
        )

    send_dtime = Sender(r.dt_s, r.dt_r)

    def dtime_copy(step):
        return send_dtime(
            step - 1, r.dtime_mine, r.dtime_recv.at[d], at_dp(lax.rem(d + step, n_data))
        )

    def conditioning(mod_weight):
        load = pltpu.make_async_copy(
            r.matrices.at[:, pl.ds(D, 8 * D)], mod_weight, r.local_sem.at[0]
        )
        load.start()
        load_time = pltpu.make_async_copy(
            r.matrices.at[:, pl.ds(0, D)], r.time_low, r.local_sem.at[1]
        )
        load_time.start()
        loop(
            1,
            everyone,
            lambda step: send_dmod(
                step - 1, r.dmod_row, r.dmod_all.at[me], anyone(step)[1]
            ).wait(),
        )
        gathered = r.dmod_all[...].astype(single)
        load.wait()
        load_time.wait()
        d_cond = jnp.zeros((everyone, rows), single)
        mod_gram = jnp.zeros((everyone, everyone), single)
        bias_squares = jnp.zeros((1, 1), single)
        for kind in range(8):
            r.dtime_wide[:, 0 : D // 2] = gathered[:, 2 * kind]
            r.dtime_wide[:, D // 2 : D] = gathered[:, 2 * kind + 1]
            part = r.dtime_wide[...]
            column = jnp.sum(part, axis=0, keepdims=True)
            bias_squares = bias_squares + jnp.sum(column * column, axis=1, keepdims=True)
            r.bias_rows[3 + kind : 4 + kind] = column
            part = part.astype(bfloat)
            r.dmod[kind] = part
            d_cond = d_cond + dot(
                part, mod_weight[:, kind * D : (kind + 1) * D].astype(bfloat), ((1,), (1,))
            )
            mod_gram = mod_gram + gram(part)
        d_condition = d_cond * (sigma_cond * (1.0 + condition * (1.0 - sigma_cond)))
        r.d_condition[...] = d_condition
        r.dtime_mine[...] = d_condition.astype(bfloat)
        loop(1, n_data, lambda step: dtime_copy(step).start())
        r.dtime_recv[d] = r.dtime_mine[...]
        r.pay[2] = jnp.zeros((8, 128), single)
        r.pay[2, 0:1, 0:1] = (
            jnp.sum(jnp.sum(mod_gram * gram(cond_act), axis=1, keepdims=True), axis=0, keepdims=True)
            / n_model
            + bias_squares / everyone
        )

    pl.run_scoped(conditioning, pltpu.VMEM((rows, 8 * D), single))
    ff_service(0, 1)
    ff_service(2, 2)
    qkv_service(0)
    ff_service(1, 1)
    ff_service(0, 2)
    qkv_service(1)
    loop(1, n_data, lambda step: dtime_copy(step).wait())
    for spot in range(n_data):
        r.dtime_wide[:, spot * rows : (spot + 1) * rows] = r.dtime_recv[spot].astype(single)
    dtime = r.dtime_wide[...]
    column = jnp.sum(dtime, axis=0, keepdims=True)
    r.bias_rows[2:3] = column
    dtime = dtime.astype(bfloat)
    r.dtime[...] = dtime
    d_time_pre = dot(dtime, r.time_low[...].astype(bfloat), ((1,), (1,))) * (
        sigma_time * (1.0 + time_pre * (1.0 - sigma_time))
    )
    r.d_time_pre[...] = d_time_pre
    first_sum = jnp.sum(d_time_pre, axis=0, keepdims=True)
    facts = r.facts_all[...]
    sinus = jnp.concatenate([facts[:, 0], facts[:, 1]], axis=1).astype(bfloat)
    onehot = (
        facts[:, 2, 0:1]
        == lax.broadcasted_iota(jnp.int32, (everyone, CLASSES + 1), 1).astype(single)
    ).astype(bfloat)
    highest = lax.Precision.HIGHEST

    def total_of(value):
        return jnp.sum(jnp.sum(value, axis=1, keepdims=True), axis=0, keepdims=True)

    shared_squares = (
        total_of(gram(time_act) * gram(dtime))
        + total_of(gram(sinus) * gram(d_time_pre, highest))
        + total_of(gram(onehot) * gram(r.d_condition[...], highest))
        + total_of(first_sum * first_sum)
    ) / n_model + total_of(column * column) / everyone
    r.pay[3] = jnp.zeros((8, 128), single)
    r.pay[3, 0:1] = first_sum[:, 0:128]
    r.pay[3, 1:2, 0 : rows - 128] = first_sum[:, 128:rows]
    ff_service(1, 2)
    qkv_service(2)
    qkv_near, qkv_far, qkv_on = spread(Sender(r.qa_s, r.qa_r), r.grad_qkv)
    qkv_far.start()
    qkv_near.start()
    give = Sender(r.oa_s, r.oa_r)
    partners = [(d, near_rank), (d, far_rank), (d, lax.rem(near_rank + 2, 4))]
    gives = [
        give(spot, r.out_mine, r.out_mine, partner) for spot, partner in enumerate(partners)
    ]

    @pl.when(owner)
    def _():
        total = r.g_out[x].astype(single)
        for step in range(depth - 1):
            oz(step, r.g_out.at[x], r.z_out.at[step], at_dp(up)).wait_recv()
            total = total + r.z_out[step].astype(single)
        total = total.astype(bfloat)
        r.out_mine[...] = total
        total = total.astype(single)
        r.pay[2, 0:1, 2:3] = total_of(total * total)
        for copy in gives:
            copy.start()

    loop(1, everyone, lambda step: sums_copy(step).wait())

    def add_sums(step, held):
        return held + r.sums_recv[step]

    chunk = lax.fori_loop(0, everyone, add_sums, jnp.zeros((2, 8, 128), single))
    r.pay[0:2] = chunk
    own_squares = total_of(chunk[0] * chunk[0]) + total_of(chunk[1] * chunk[1])

    def ff_squares(at, held):
        return tuple(
            one + fold(r.grad_ff[which, at] * r.grad_ff[which, at])
            for which, one in enumerate(held)
        )

    block = jnp.zeros((8, units), single)
    for value in chunks(ff_squares, (block, block, block), 48, rows):
        own_squares = own_squares + total_of(value)
    qkv_float = r.grad_qkv[0].astype(single)
    r.pay[2, 0:1, 0:1] = (
        r.pay[2, 0:1, 0:1]
        + shared_squares
        + own_squares
        + r.pay[2, 0:1, 2:3]
        + total_of(qkv_float * qkv_float)
    )
    r.pay[2, 0:1, 1:2] = r.loss[...]
    send_late = Sender(r.lt_s, r.lt_r)

    def late_copy(step):
        return send_late(step - 1, r.pay, r.late.at[me], anyone(step)[1])

    loop(1, everyone, lambda step: late_copy(step).start())
    r.late[me] = r.pay[...]

    for spot, partner in enumerate(partners):

        @pl.when(z == partner[1])
        def _():
            gives[spot].wait_recv()

    qkv_far.wait_recv()
    qkv_on.start()
    r.grad_out[...] = r.out_mine[...]

    @pl.when(owner)
    def _():
        for copy in gives:
            copy.wait_send()

    @pl.when(jnp.logical_not(owner))
    def _():
        out_along.wait_send()

    qkv_near.wait()
    qkv_on.wait()
    qkv_far.wait_send()
    loop(1, everyone, lambda step: late_copy(step).wait())
    for top in range(7):
        for left in range(tiles):
            spot = top * tiles + left
            r.local[8 * top : 8 * top + 8, 128 * left : 128 * left + 128] = r.late[
                spot // 2, spot % 2
            ]
    r.bias_rows[0:1] = r.local[48:49]
    r.bias_rows[14:15] = r.local[49:50]
    r.bias_rows[15:16] = r.local[54:55]
    for spot in range(n_data):
        first = r.late[spot * n_model, 3]
        r.bias_rows[1:2, spot * rows : spot * rows + 128] = first[0:1]
        r.bias_rows[1:2, spot * rows + 128 : (spot + 1) * rows] = first[1:2, 0 : rows - 128]
    for rank in range(n_model):
        for part in range(3):
            r.bias_rows[11 + part : 12 + part, rank * head_cols : (rank + 1) * head_cols] = r.local[
                50 + rank : 51 + rank, part * head_cols : (part + 1) * head_cols
            ]
    for spot in range(n_data):

        @pl.when(d == spot)
        def _():
            r.own[...] = r.local[0 : 3 * CH, spot * rows : (spot + 1) * rows]

    totals = lax.fori_loop(
        0, everyone, lambda step, held: held + r.late[step, 2, 0:1], jnp.zeros((1, 128), single)
    )
    norm = jnp.sqrt(totals[:, 0:1])
    r.norm[...] = norm
    r.factor[...] = jnp.minimum(1.0, CLIP_LIMIT / norm)
    r.loss_sum[...] = totals[:, 1:2]
    for copy in (dm_near, dm_far, dm_on, db_near, db_far, db_on, *third_parts):
        copy.wait_send()
    for step in range(depth):
        qkv_aside(step).wait_send()
        for which in range(3):
            ff_aside(which, step).wait_send()
    for step in range(depth - 1):
        for part in range(2):
            qkv_along(step, part).wait_send()
            for which in range(3):
                ff_along(which, step, part).wait_send()


def backward_all(values, sizes, total_images, collective):
    n_data, n_model = sizes
    bfloat, single = jnp.bfloat16, jnp.float32
    everyone = n_data * n_model
    rows = D // n_data
    heads = HEADS // n_model
    head_cols = heads * HDIM
    length = values.clean.shape[0]
    units = values.ff.shape[2]
    half = units // 2
    depth = n_data // NX
    shapes = dict(
        grad_ff=((3, rows, units), single),
        grad_qkv=((n_model, rows, 3 * head_cols), bfloat),
        grad_out=((rows, D), bfloat),
        bias_rows=((16, D), single),
        own=((3 * CH, rows), single),
        norm=((1, 1), single),
        factor=((1, 1), single),
        loss_sum=((1, 1), single),
        dmod=((8, everyone, D), bfloat),
        dtime=((everyone, D), bfloat),
        d_condition=((everyone, rows), single),
        d_time_pre=((everyone, rows), single),
    )
    vmem, dma = pltpu.VMEM, pltpu.SemaphoreType.DMA
    scratch = dict(
        d_end=vmem((length, D), single),
        dm_rows=vmem((n_model, length, D), bfloat),
        db_rows=vmem((n_model, length, D), bfloat),
        hold_far=vmem((length, D), single),
        hold_near=vmem((length, D), single),
        parts_send=vmem((3, length, D), bfloat),
        parts_recv=vmem((3, length, D), bfloat),
        normed_end=vmem((length, D), bfloat),
        g_ff=vmem((3, D, units), bfloat),
        x_ff=vmem((3, depth, rows, units), bfloat),
        z_ff=vmem((3, depth - 1, 2, rows, half), bfloat),
        g_qkv=vmem((D, 3 * head_cols), bfloat),
        x_qkv=vmem((depth, rows, 3 * head_cols), bfloat),
        z_qkv=vmem((depth - 1, rows, 3 * head_cols), bfloat),
        g_out=vmem((NX, rows, D), bfloat),
        x_out=vmem((rows, D), bfloat),
        z_out=vmem((depth - 1, rows, D), bfloat),
        out_mine=vmem((rows, D), bfloat),
        late=vmem((everyone, 4, 8, 128), single),
        d_modulation=vmem((8, D), single),
        local=vmem((56, D), single),
        sums=vmem((2 * everyone, 8, 128), single),
        sums_recv=vmem((everyone, 2, 8, 128), single),
        pay=vmem((4, 8, 128), single),
        dmod_row=vmem((16, D // 2), bfloat),
        dmod_all=vmem((everyone, 16, D // 2), bfloat),
        dmod_wide=vmem((16, D // 2), single),
        dtime_mine=vmem((everyone, rows), bfloat),
        dtime_recv=vmem((n_data, everyone, rows), bfloat),
        dtime_wide=vmem((everyone, D), single),
        loss=vmem((1, 1), single),
        time_low=vmem((rows, D), single),
        local_sem=dma((8,)),
    )
    counts = dict(
        dm=(3,),
        db=(3,),
        pa=(3,),
        pb=(3,),
        pc=(3,),
        fx=(3, depth),
        fz=(3, depth - 1, 2),
        qx=(depth,),
        qz=(depth - 1, 2),
        ox=(1,),
        oz=(depth - 1,),
        qa=(3,),
        oa=(3,),
        sm=(everyone - 1,),
        dl=(everyone - 1,),
        dt=(n_data - 1,),
        lt=(everyone - 1,),
    )
    for name, count in counts.items():
        scratch[name + "_s"] = dma(count)
        scratch[name + "_r"] = dma(count)
    far = {
        "ff", "two_rows", "low", "trig_all", "attended", "one_rows", "qkv_weight", "out_weight",
        "matrices",
    }

    def space(name):
        return pl.BlockSpec(memory_space=pl.ANY if name in far else pltpu.VMEM)

    outs = pl.pallas_call(
        functools.partial(back_kernel, sizes, total_images),
        out_shape=[jax.ShapeDtypeStruct(*shapes[name]) for name in BackOut._fields],
        in_specs=[space(name) for name in BackIn._fields],
        out_specs=[space(name) for name in BackOut._fields],
        scratch_shapes=[scratch[name] for name in BackScratch._fields],
        compiler_params=pltpu.CompilerParams(
            collective_id=collective, has_side_effects=True, vmem_limit_bytes=62 * 2**20
        ),
    )(*values)
    return BackOut(*outs)


def forward_plain(clean_three, noise_three, patch_grid, labels, timesteps, matrices, embeddings, swiglu_weights, biases):
    bfloat = jnp.bfloat16
    single = jnp.float32
    images = labels.shape[0]
    length = clean_three.shape[1]
    n_model = lax.axis_size("mlp")
    n_data = lax.axis_size("dp")
    sizes = (n_data, n_model)
    total_images = images * n_data * n_model
    rows = D // n_data
    owned_start = lax.axis_index("dp") * rows
    data_index = lax.axis_index("dp")
    model_index = lax.axis_index("mlp")
    heads = HEADS // n_model
    head_cols = heads * HDIM
    qkv_shard = jnp.concatenate(
        [
            cut_columns(matrices, 9 * D + part * D + model_index * head_cols, head_cols)
            for part in range(3)
        ],
        axis=1,
    ).astype(bfloat)
    out_shard = matrices[:, 12 * D : 13 * D].astype(bfloat)
    swiglu_shard = swiglu_weights.astype(bfloat)
    qkv_weight = lax.all_gather(qkv_shard, "dp", axis=0, tiled=True)
    swiglu_use = lax.all_gather(swiglu_shard, "dp", axis=1, tiled=True)
    out_weight = gather_out(out_shard)

    time_second = matrices[:, :D].astype(bfloat)
    mod_weight = matrices[:, D : 9 * D].astype(bfloat)
    time_first = embeddings[CH : CH + FREQ].astype(bfloat)
    class_table = embeddings[CH + FREQ :].astype(bfloat)
    patch_bias = biases[:D]
    first_bias = biases[D : 2 * D]
    second_bias = biases[2 * D : 3 * D]
    mod_bias = biases[3 * D : 11 * D]
    qkv_bias = biases[11 * D : 14 * D]
    out_bias = biases[14 * D : 15 * D]
    final_bias = biases[15 * D :]

    facts = jnp.concatenate([timesteps[:, None], labels[:, None], patch_grid], axis=1)
    facts = jnp.pad(facts, ((0, 8 - images), (0, 124)))
    (facts_all,) = exchange([(facts, "all")], "both", sizes, 0)
    facts_all = facts_all[:, 0, :4]
    steps_all, labels_all, grid_all = facts_all[:, 0], facts_all[:, 1], facts_all[:, 2:4]
    sinus_all = sinusoid(steps_all).astype(bfloat)
    first_bias_own = lax.dynamic_slice_in_dim(first_bias, owned_start, rows)
    second_bias_own = lax.dynamic_slice_in_dim(second_bias, owned_start, rows)
    time_pre = jnp.dot(sinus_all, time_first, preferred_element_type=single) + first_bias_own
    time_act = jax.nn.silu(time_pre).astype(bfloat)
    time_part = jnp.dot(time_act, time_second, preferred_element_type=single)
    small_shard = jnp.concatenate(
        [embeddings[:CH], matrices[:, 13 * D :].T], axis=0
    ).astype(bfloat)
    time_parts, small_all = exchange(
        [
            (time_part.reshape(total_images, n_data, rows).transpose(1, 0, 2), "each"),
            (small_shard, "all"),
        ],
        "dp",
        sizes,
        1,
    )
    small_all = small_all.transpose(1, 0, 2).reshape(3 * CH, D)
    patch_weight = small_all[:CH]
    final_weight = small_all[CH:].T
    time_emb = jnp.sum(time_parts, axis=0) + second_bias_own
    onehot = (labels_all[:, None] == jnp.arange(CLASSES + 1, dtype=jnp.int32)[None, :]).astype(
        bfloat
    )
    condition = time_emb + jnp.dot(onehot, class_table, preferred_element_type=single)
    cond_act = jax.nn.silu(condition).astype(bfloat)
    cond_rank = lax.dynamic_index_in_dim(
        cond_act.reshape(n_data, n_model, rows), model_index, 1, keepdims=False
    )
    mod_part = jnp.dot(cond_rank, mod_weight, preferred_element_type=single)
    (mod_parts,) = exchange(
        [(mod_part.reshape(n_data, 8, D), "each")],
        "dp",
        sizes,
        2,
    )
    modulation = jnp.sum(mod_parts, axis=0).reshape(1, 8 * D) + mod_bias
    shift_one, scale_one, gate_one, shift_two, scale_two, gate_two, shift_end, scale_end = (
        jnp.split(modulation, 8, axis=1)
    )

    group_grid = lax.dynamic_slice_in_dim(grid_all, data_index * n_model, n_model, 0)
    group_grid = jnp.stack(
        [
            lax.dynamic_index_in_dim(group_grid, model_index ^ rank, 0, keepdims=False)
            for rank in range(n_model)
        ]
    )
    cosine, sine, mask = turn_tables(group_grid, length)
    noisy_low = noisy_input(clean_three, noise_three, timesteps).astype(bfloat)
    hidden = jnp.dot(noisy_low, patch_weight, preferred_element_type=single) + patch_bias
    normed_one = modulate(hidden, shift_one, scale_one).astype(bfloat)
    one_rows = jnp.concatenate(gather_rows(normed_one.reshape(length, D), n_model), axis=0)
    qkv_bias_own = jnp.concatenate(
        [
            lax.dynamic_slice_in_dim(qkv_bias, part * D + model_index * head_cols, head_cols)
            for part in range(3)
        ]
    )
    qkv = jnp.dot(one_rows, qkv_weight, preferred_element_type=single) + qkv_bias_own
    low, attended, log_total = attention(
        qkv.reshape(n_model, length, 3 * head_cols), cosine, sine, mask, heads
    )
    attended_rows = attended.reshape(n_model * length, head_cols)
    branch_part = jnp.dot(attended_rows, out_weight, preferred_element_type=single).astype(bfloat)
    branch_part = branch_part.reshape(n_model, length, D)
    branch = (
        scatter_rows(
            (branch_part[2], branch_part[3]), (branch_part[0], branch_part[1]), n_model
        )[None]
        + out_bias
    )
    hidden_mid = hidden + gate_one[:, None, :] * branch
    normed_two = modulate(hidden_mid, shift_two, scale_two).astype(bfloat)
    two_rows = gather_rows(normed_two.reshape(length, D), n_model)
    return SimpleNamespace(
        steps=sinus_all,
        onehot=onehot,
        time_pre=time_pre,
        condition=condition,
        modulation=modulation,
        hidden=hidden,
        one_rows=one_rows,
        qkv_weight=qkv_weight,
        out_weight=out_weight,
        swiglu=swiglu_use,
        low=low,
        attended=attended,
        totals=log_total,
        branch=branch,
        hidden_mid=hidden_mid,
        two_rows=two_rows,
        final_weight=final_weight,
        tables=(cosine, sine, mask),
    )


def forward_fused(clean_three, noise_three, patch_grid, labels, timesteps, matrices, embeddings, swiglu_weights, biases):
    bfloat = jnp.bfloat16
    single = jnp.float32
    length = clean_three.shape[1]
    n_model = lax.axis_size("mlp")
    n_data = lax.axis_size("dp")
    everyone = n_data * n_model
    rows = D // n_data
    owned_start = lax.axis_index("dp") * rows
    model_index = lax.axis_index("mlp")
    head_cols = HEADS // n_model * HDIM

    def own_bias(start, amount, offset):
        return lax.dynamic_slice_in_dim(biases, start + offset, amount)[None]

    sinus = sinusoid(timesteps).astype(bfloat).astype(single).reshape(2, 128)
    facts = jnp.concatenate(
        [labels, patch_grid[:, 0] * patch_grid[:, 1]]
    ).astype(single)
    facts = jnp.concatenate(
        [sinus, jnp.pad(facts[None], ((0, 0), (0, 126))), jnp.zeros((5, 128), single)], axis=0
    )
    cosine, sine, _ = turn_tables(patch_grid, length)
    small = jnp.concatenate(
        [
            embeddings[:CH].T,
            jnp.zeros((rows, CH), single),
            matrices[:, 13 * D :],
            jnp.zeros((rows, 64), single),
        ],
        axis=1,
    ).astype(bfloat)
    values = ForwardIn(
        facts=facts,
        trig=jnp.concatenate([cosine, sine], axis=0),
        small=small,
        time_first=embeddings[CH : CH + FREQ].astype(bfloat),
        first_bias=own_bias(D, rows, owned_start),
        second_bias=own_bias(2 * D, rows, owned_start),
        class_table=embeddings[CH + FREQ :].astype(bfloat),
        matrices=matrices,
        mod_bias=biases[3 * D : 11 * D].reshape(8, D),
        noisy=noisy_input(clean_three, noise_three, timesteps).astype(bfloat)[0],
        patch_bias=biases[None, :D],
        qkv_shard=jnp.concatenate(
            [
                cut_columns(matrices, (9 + part) * D + model_index * head_cols, head_cols)
                for part in range(3)
            ],
            axis=1,
        ).astype(bfloat),
        ff_shard=swiglu_weights.astype(bfloat),
        qkv_bias=jnp.concatenate(
            [
                own_bias((11 + part) * D, head_cols, model_index * head_cols)
                for part in range(3)
            ],
            axis=1,
        ),
        out_bias=biases[None, 14 * D : 15 * D],
    )
    out = forward_all(values, (n_data, n_model), 0)
    found = {name.removesuffix("_out"): value for name, value in out._asdict().items()}
    raw = {name: found[name] for name in BackIn._fields if name in found}
    facts_all = out.facts_all
    group = lax.dynamic_slice_in_dim(
        facts_all[:, 2, 1], lax.axis_index("dp") * n_model, n_model
    )
    spots = model_index ^ jnp.arange(n_model)
    counts = jnp.sum(
        jnp.where(spots[:, None] == jnp.arange(n_model)[None, :], group[None, :], 0.0), axis=1
    )
    mask = jnp.arange(length, dtype=jnp.int32)[None, None, :] < counts[:, None, None]
    return SimpleNamespace(
        raw=dict(
            raw,
            noisy=values.noisy,
            matrices=matrices,
        ),
        steps=facts_all[:, :2].reshape(everyone, FREQ).astype(bfloat),
        onehot=(
            facts_all[:, 2, 0:1] == jnp.arange(CLASSES + 1, dtype=jnp.int32)[None].astype(single)
        ).astype(bfloat),
        time_pre=out.time_pre,
        condition=out.condition,
        modulation=out.modulation.reshape(1, 8 * D),
        hidden=out.hidden[None],
        one_rows=out.one_rows_out.reshape(n_model * length, D),
        qkv_weight=out.qkv_weight_out,
        out_weight=out.out_weight_out,
        swiglu=out.ff,
        low=out.low_out,
        attended=out.attended_out,
        totals=out.totals,
        branch=out.branch[None],
        hidden_mid=out.hidden_mid[None],
        two_rows=tuple(out.two_rows),
        final_weight=out.small_all[:, 2 * CH : 4 * CH],
        tables=(out.trig_all_out[:, 0], out.trig_all_out[:, 1], mask.astype(single)),
    )


def backward_plain(
    kept, clean_three, noise_three, patch_grid, timesteps, biases, total_images
):
    bfloat = jnp.bfloat16
    single = jnp.float32
    images, length = clean_three.shape[:2]
    n_model = lax.axis_size("mlp")
    n_data = lax.axis_size("dp")
    rows = D // n_data
    model_index = lax.axis_index("mlp")
    heads = HEADS // n_model
    head_cols = heads * HDIM
    valid_slot = valid_slots(patch_grid, length)
    final_bias = biases[15 * D :]
    noisy_low = noisy_input(clean_three, noise_three, timesteps).astype(bfloat)
    modulation, hidden, hidden_mid, branch = kept.modulation, kept.hidden, kept.hidden_mid, kept.branch
    shift_one, scale_one, gate_one, shift_two, scale_two, gate_two, shift_end, scale_end = (
        jnp.split(modulation, 8, axis=1)
    )
    qkv_weight, out_weight, swiglu_use = kept.qkv_weight, kept.out_weight, kept.swiglu
    final_weight, one_rows, two_rows = kept.final_weight, kept.one_rows, kept.two_rows
    low, log_total = kept.low, kept.totals
    attended_rows = kept.attended.reshape(n_model * length, head_cols)
    cosine, sine, mask = kept.tables
    two_halves = (
        jnp.concatenate(two_rows[:2], axis=0),
        jnp.concatenate(two_rows[2:], axis=0),
    )
    gates, ups, acts, parts = [], [], [], []
    for part in two_halves:
        gate_val = jnp.dot(part, swiglu_use[0], preferred_element_type=single)
        up_val = jnp.dot(part, swiglu_use[1], preferred_element_type=single)
        act = (jax.nn.silu(gate_val) * up_val).astype(bfloat)
        gates.append(gate_val)
        ups.append(up_val)
        acts.append(act)
        parts.append(backward_product(act, swiglu_use[2]).astype(bfloat).reshape(2, length, D))
    mixed = scatter_rows(parts[1], parts[0], n_model)[None]
    hidden_end = hidden_mid + gate_two[:, None, :] * mixed
    normed_end = modulate(hidden_end, shift_end, scale_end).astype(bfloat)
    output = jnp.dot(normed_end, final_weight, preferred_element_type=single) + final_bias
    local_loss, loss_pull = jax.vjp(
        lambda values_out: loss_terms(values_out, clean_three, noise_three, timesteps, valid_slot),
        output,
    )
    d_output = loss_pull(jnp.asarray(1.0 / total_images, single))[0].astype(bfloat)
    d_normed_end = backward_product(d_output, final_weight)
    unused, pull_end = jax.vjp(modulate, hidden_end, shift_end, scale_end)
    d_hidden_end, d_shift_end, d_scale_end = pull_end(d_normed_end)
    d_mixed = (gate_two[:, None, :] * d_hidden_end).astype(bfloat)
    d_gate_two = jnp.sum(mixed * d_hidden_end, axis=1)
    dmixed_rows = gather_rows(d_mixed.reshape(length, D), n_model)
    dmixed_halves = (
        jnp.concatenate(dmixed_rows[:2], axis=0),
        jnp.concatenate(dmixed_rows[2:], axis=0),
    )
    d_gates, d_ups, d_parts = [], [], []
    for part, gate_val, up_val in zip(dmixed_halves, gates, ups):
        d_inner = jnp.dot(part, swiglu_use[2], preferred_element_type=single)
        unused, pull_glu = jax.vjp(
            lambda gate_in, up_in: jax.nn.silu(gate_in) * up_in, gate_val, up_val
        )
        d_gate, d_up = pull_glu(d_inner)
        d_gate, d_up = d_gate.astype(bfloat), d_up.astype(bfloat)
        d_gates.append(d_gate)
        d_ups.append(d_up)
        d_parts.append(
            (backward_product(d_gate, swiglu_use[0]) + backward_product(d_up, swiglu_use[1]))
            .astype(bfloat)
            .reshape(2, length, D)
        )
    d_normed_two = scatter_rows(d_parts[1], d_parts[0], n_model)[None]
    rows_ready = jnp.concatenate(two_halves, axis=0)
    dmixed_ready = jnp.concatenate(dmixed_halves, axis=0)

    def owned(gradient):
        return reduce_dp(gradient.reshape(n_data, rows, -1))

    grad_swiglu = jnp.stack(
        [
            owned(weight_grad(rows_ready, jnp.concatenate(d_gates, axis=0))),
            owned(weight_grad(rows_ready, jnp.concatenate(d_ups, axis=0))),
            owned(weight_grad(dmixed_ready, jnp.concatenate(acts, axis=0))),
        ]
    )
    unused, pull_two = jax.vjp(modulate, hidden_mid, shift_two, scale_two)
    d_mid_part, d_shift_two, d_scale_two = pull_two(d_normed_two)
    d_hidden_mid = d_hidden_end + d_mid_part
    d_branch = (gate_one[:, None, :] * d_hidden_mid).astype(bfloat)
    d_gate_one = jnp.sum(branch * d_hidden_mid, axis=1)

    dbranch_rows = jnp.concatenate(gather_rows(d_branch.reshape(length, D), n_model), axis=0)
    d_attended = backward_product(dbranch_rows, out_weight).astype(bfloat)
    d_qkv = attention_back(
        low,
        log_total,
        d_attended.reshape(n_model, length, head_cols),
        cosine,
        sine,
        mask,
        heads,
    ).reshape(n_model * length, 3 * head_cols)
    grad_out = reduce_out(weight_grad(attended_rows, dbranch_rows))
    grad_qkv_own = owned(weight_grad(one_rows, d_qkv))
    d_one_part = backward_product(d_qkv, qkv_weight).astype(bfloat).reshape(n_model, length, D)
    d_normed_one = scatter_rows(
        (d_one_part[2], d_one_part[3]), (d_one_part[0], d_one_part[1]), n_model
    )[None]
    unused, pull_one = jax.vjp(modulate, hidden, shift_one, scale_one)
    d_hidden_part, d_shift_one, d_scale_one = pull_one(d_normed_one)
    d_hidden = (d_hidden_mid + d_hidden_part).astype(bfloat)

    return SimpleNamespace(
        d_modulation=jnp.concatenate(
            [
                d_shift_one,
                d_scale_one,
                d_gate_one,
                d_shift_two,
                d_scale_two,
                d_gate_two,
                d_shift_end,
                d_scale_end,
            ],
            axis=1,
        ),
        hidden_sum=column_sum(d_hidden),
        branch_sum=column_sum(d_branch),
        qkv_sum=column_sum(d_qkv),
        output_sum=column_sum(d_output),
        loss=local_loss.reshape(1),
        grad_patch=weight_grad(noisy_low, d_hidden),
        grad_final=weight_grad(normed_end, d_output).T,
        grad_swiglu=grad_swiglu,
        grad_out=grad_out,
        grad_qkv=jnp.stack(gather_rows(grad_qkv_own.astype(bfloat), n_model)).astype(single),
    )


def finish_fused(
    kept, clean_three, noise_three, patch_grid, timesteps, states, biases, total_images
):
    single = jnp.float32
    length = clean_three.shape[1]
    n_data, n_model = sizes = (lax.axis_size("dp"), lax.axis_size("mlp"))
    beta_now, bar_now, bar_prev = plan(timesteps)
    consts = jnp.stack(
        [
            jnp.sqrt(bar_now),
            jnp.sqrt(1.0 - bar_now),
            jnp.log(beta_now),
            jnp.log(beta_now * (1.0 - bar_prev) / (1.0 - bar_now)),
            beta_now * jnp.sqrt(bar_prev) / (1.0 - bar_now),
        ],
        axis=1,
    )
    values = BackIn(
        **kept.raw,
        final_bias=biases[15 * D :].reshape(2, CH),
        clean=clean_three[0],
        noise=noise_three[0],
        consts=jnp.pad(consts, ((0, 7), (0, 123))),
        valid=valid_slots(patch_grid, length).astype(single).reshape(length, 1),
    )
    out = backward_all(values, sizes, total_images, 1)
    grad_time_first = jnp.dot(
        kept.steps.astype(single).T,
        out.d_time_pre,
        precision=lax.Precision.HIGHEST,
        preferred_element_type=single,
    )
    grad_table = jnp.dot(
        kept.onehot.astype(single).T,
        out.d_condition,
        precision=lax.Precision.HIGHEST,
        preferred_element_type=single,
    )
    grad_norm, factor, loss_sum = (one.reshape(()) for one in (out.norm, out.factor, out.loss_sum))
    grad_bias = jnp.concatenate([out.bias_rows[:15].reshape(-1), out.bias_rows[15, : 2 * CH]])
    mats_out = adam_matrices(
        states,
        jax.nn.silu(kept.time_pre).astype(jnp.bfloat16),
        jax.nn.silu(kept.condition).astype(jnp.bfloat16),
        out.dtime,
        out.dmod,
        out.grad_qkv,
        out.grad_out,
        jnp.pad(out.own[CH:].T, ((0, 0), (0, 128 - 2 * CH))),
        out.factor,
        n_model,
    )
    return SimpleNamespace(
        loss_sum=loss_sum,
        grad_norm=grad_norm,
        factor=factor,
        grad_bias=grad_bias,
        grad_embed=jnp.concatenate([out.own[:CH], grad_time_first, grad_table], axis=0),
        grad_swiglu=out.grad_ff,
        mats_out=mats_out,
    )


def adam_matrices_kernel(
    n_model,
    weight_ref,
    first_ref,
    second_ref,
    average_ref,
    time_act_ref,
    cond_act_ref,
    dtime_ref,
    dmod_ref,
    qkv_ref,
    out_ref,
    final_ref,
    factor_ref,
    weight_out,
    first_out,
    second_out,
    average_out,
    grad_ref,
):
    single = jnp.float32
    head_cols = HEADS // n_model * HDIM
    m = lax.axis_index("mlp")

    def outer(left, right):
        return lax.dot_general(left, right, (((0,), (0,)), ((), ())), preferred_element_type=single)

    for side in range(2):
        section = 2 * pl.program_id(0) + side
        base = side * D
        lanes = slice(base, base + D)

        @pl.when((section >= 1) & (section < 9))
        def _():
            grad_ref[:, lanes] = outer(cond_act_ref[...], dmod_ref[jnp.clip(section - 1, 0, 7)])

        if side == 0:

            @pl.when(section == 0)
            def _():
                grad_ref[:, lanes] = outer(time_act_ref[...], dtime_ref[...])

            @pl.when(section == 12)
            def _():
                grad_ref[:, lanes] = out_ref[...].astype(single)

        else:

            @pl.when(section == 13)
            def _():
                grad_ref[:, base : base + 128] = final_ref[...]

        for part in range(3):
            if (9 + part) % 2 == side:

                @pl.when(section == 9 + part)
                def _():
                    for rank in range(n_model):
                        apart = (
                            2 * lax.rem(lax.div(m, 2) + rank // 2, 2)
                            + lax.rem(lax.rem(m, 2) + rank % 2, 2)
                        )
                        start = base + rank * head_cols
                        grad_ref[:, start : start + head_cols] = qkv_ref[
                            apart, :, part * head_cols : (part + 1) * head_cols
                        ].astype(single)

    def body(step, carry):
        at = pl.ds(pl.multiple_of(step * 24, 24), 24)
        done = adam_step(
            weight_ref[at],
            first_ref[at],
            second_ref[at],
            grad_ref[at],
            average_ref[at],
            factor_ref[...],
            LEARN_RATE,
        )
        for place, value in zip((weight_out, first_out, second_out, average_out), done):
            place[at] = value
        return carry

    lax.fori_loop(0, weight_ref.shape[0] // 24, body, 0)


def adam_matrices(
    states, time_act, cond_act, dtime, dmod, grad_qkv, grad_out, grad_final, factor, n_model
):
    rows, width = states[0].shape
    whole = lambda array: pl.BlockSpec(array.shape, lambda i: (0,) * array.ndim)
    strip = pl.BlockSpec((rows, 2 * D), lambda i: (0, i))
    gradients = (time_act, cond_act, dtime, dmod, grad_qkv, grad_out, grad_final, factor)
    return pl.pallas_call(
        functools.partial(adam_matrices_kernel, n_model),
        grid=(pl.cdiv(width, 2 * D),),
        out_shape=[jax.ShapeDtypeStruct((rows, width), jnp.float32)] * 4,
        in_specs=[strip] * 4 + [whole(array) for array in gradients],
        out_specs=[strip] * 4,
        scratch_shapes=[pltpu.VMEM((rows, 2 * D), jnp.float32)],
        compiler_params=pltpu.CompilerParams(vmem_limit_bytes=62 * 2**20),
    )(*states, *gradients)


def finish_plain(
    kept, clean_three, noise_three, patch_grid, timesteps, states, biases, total_images
):
    bfloat = jnp.bfloat16
    single = jnp.float32
    matrices, matrices_first, matrices_second, matrices_average = states
    n_data, n_model = sizes = (lax.axis_size("dp"), lax.axis_size("mlp"))
    rows = D // n_data
    owned_start = lax.axis_index("dp") * rows
    model_index = lax.axis_index("mlp")
    head_cols = HEADS // n_model * HDIM
    time_pre, condition = kept.time_pre, kept.condition
    onehot, sinus_all = kept.onehot, kept.steps
    time_act = jax.nn.silu(time_pre).astype(bfloat)
    cond_act = jax.nn.silu(condition).astype(bfloat)
    time_second = matrices[:, :D].astype(bfloat)
    mod_weight = matrices[:, D : 9 * D].astype(bfloat)

    grads = backward_plain(
        kept, clean_three, noise_three, patch_grid, timesteps, biases, total_images
    )
    grad_swiglu, grad_out = grads.grad_swiglu, grads.grad_out
    grad_qkv_own = grads.grad_qkv[0]
    qkv_stack = jnp.stack(
        [
            lax.dynamic_index_in_dim(grads.grad_qkv, model_index ^ rank, 0, keepdims=False)
            for rank in range(n_model)
        ]
    )
    grad_qkv = (
        qkv_stack.reshape(n_model, rows, 3, head_cols).transpose(1, 2, 0, 3).reshape(rows, 3 * D)
    )

    d_modulation = grads.d_modulation.astype(bfloat)
    (dmod_all,) = exchange(
        [(d_modulation.reshape(16, D // 2), "all")], "both", sizes, 3
    )
    dmod_all = dmod_all.reshape(total_images, 8 * D)
    d_cond_act = backward_product(dmod_all, mod_weight)
    unused, pull_cond = jax.vjp(jax.nn.silu, condition)
    d_condition = pull_cond(d_cond_act)[0]
    d_time_emb = d_condition.astype(bfloat)
    (dtime_parts,) = exchange([(d_time_emb, "all")], "dp", sizes, 4)
    dtime_all = dtime_parts.transpose(1, 0, 2).reshape(total_images, D)
    d_time_act = backward_product(dtime_all, time_second)
    unused, pull_time = jax.vjp(jax.nn.silu, time_pre)
    d_time_pre = pull_time(d_time_act)[0]
    grad_time_second = weight_grad(time_act, dtime_all)
    grad_mod = weight_grad(cond_act, dmod_all)
    grad_time_first = jnp.dot(
        sinus_all.astype(single).T,
        d_time_pre,
        precision=lax.Precision.HIGHEST,
        preferred_element_type=single,
    )
    grad_table = jnp.dot(
        onehot.astype(single).T,
        d_condition,
        precision=lax.Precision.HIGHEST,
        preferred_element_type=single,
    )

    qkv_sums = grads.qkv_sum.reshape(3, head_cols)
    qkv_bias_part = lax.dynamic_update_slice(
        jnp.zeros((3, D), single), qkv_sums, (0, model_index * head_cols)
    )
    local_sums = jnp.concatenate(
        [
            grads.hidden_sum,
            qkv_bias_part.reshape(-1),
            grads.branch_sum,
            grads.output_sum,
            grads.loss,
            jnp.zeros((95,), single),
            grads.grad_patch.reshape(-1),
            grads.grad_final.reshape(-1),
        ]
    )
    everyone = n_data * n_model
    chunk_rows = -(-local_sums.shape[0] // (everyone * 1024)) * 8
    local_sums = jnp.pad(local_sums, (0, everyone * chunk_rows * 128 - local_sums.shape[0]))
    (sum_parts,) = exchange(
        [(local_sums.reshape(everyone, chunk_rows, 128), "each")], "both", sizes, 5
    )
    chunk = jnp.sum(sum_parts, axis=0)
    local_squares = (
        jnp.sum(grad_time_second * grad_time_second)
        + jnp.sum(grad_mod * grad_mod)
        + jnp.sum(grad_out * grad_out)
        + jnp.sum(grad_time_first * grad_time_first)
        + jnp.sum(grad_table * grad_table)
    ) / n_model + jnp.sum(grad_swiglu * grad_swiglu) + jnp.sum(grad_qkv_own * grad_qkv_own)
    extra = jnp.concatenate([jnp.sum(d_time_pre, axis=0), local_squares.reshape(1)])
    extra = jnp.pad(extra, (0, 1024 - extra.shape[0])).reshape(8, 128)
    (late,) = exchange([(jnp.concatenate([chunk, extra], axis=0), "all")], "both", sizes, 6)
    sums = late[:, :chunk_rows].reshape(-1)
    extras = late[:, chunk_rows:].reshape(everyone, 1024)
    first_bias_grad = extras.reshape(n_data, n_model, 1024)[:, 0, :rows].reshape(D)
    squares = jnp.sum(extras[:, rows])
    ends = [D, 4 * D, 5 * D, 5 * D + 2 * CH, 5 * D + 2 * CH + 1]
    base = 5 * D + 128
    loss_sum = sums[5 * D + 2 * CH]
    grad_patch = sums[base : base + CH * D].reshape(CH, D)
    grad_final = sums[base + CH * D : base + 3 * CH * D].reshape(2 * CH, D)
    grad_patch = cut_columns(grad_patch, owned_start, rows)
    grad_final_own = cut_columns(grad_final, owned_start, rows).T
    grad_bias = jnp.concatenate(
        [
            sums[:D],
            first_bias_grad,
            column_sum(dtime_all),
            column_sum(dmod_all),
            sums[D : 4 * D],
            sums[4 * D : 5 * D],
            sums[5 * D : 5 * D + 2 * CH],
        ]
    )
    shared = sums[base : base + 3 * CH * D]
    squares = squares + jnp.sum(grad_bias * grad_bias) + jnp.sum(shared * shared)
    grad_norm = jnp.sqrt(squares)
    factor = jnp.minimum(1.0, CLIP_LIMIT / grad_norm)
    grad_mats = jnp.concatenate(
        [grad_time_second, grad_mod, grad_qkv, grad_out, grad_final_own], axis=1
    )
    grad_embed = jnp.concatenate([grad_patch, grad_time_first, grad_table], axis=0)
    mats_out = adam_step(
        matrices, matrices_first, matrices_second, grad_mats, matrices_average, factor, LEARN_RATE
    )
    return SimpleNamespace(
        loss_sum=loss_sum,
        grad_norm=grad_norm,
        factor=factor,
        grad_bias=grad_bias,
        grad_embed=grad_embed,
        grad_swiglu=grad_swiglu,
        mats_out=mats_out,
    )


def on_device(
    clean_patches,
    noise_patches,
    patch_grid,
    labels,
    timesteps,
    matrices,
    embeddings,
    swiglu_weights,
    biases,
    matrices_first,
    embeddings_first,
    swiglu_first,
    biases_first,
    matrices_second,
    embeddings_second,
    swiglu_second,
    biases_second,
    matrices_average,
    embeddings_average,
    swiglu_average,
    biases_average,
):
    images = labels.shape[0]
    length = clean_patches.shape[0] // images
    n_model = lax.axis_size("mlp")
    n_data = lax.axis_size("dp")
    total_images = images * n_data * n_model

    clean_three = clean_patches.reshape(images, length, CH)
    noise_three = noise_patches.reshape(images, length, CH)
    fused = (n_data, n_model, images) == (8, 4, 1)
    forward = forward_fused if fused else forward_plain
    kept = forward(
        clean_three,
        noise_three,
        patch_grid,
        labels,
        timesteps,
        matrices,
        embeddings,
        swiglu_weights,
        biases,
    )
    finish = finish_fused if fused else finish_plain
    done = finish(
        kept,
        clean_three,
        noise_three,
        patch_grid,
        timesteps,
        (matrices, matrices_first, matrices_second, matrices_average),
        biases,
        total_images,
    )
    loss_sum, grad_norm, factor = done.loss_sum, done.grad_norm, done.factor
    grad_embed, grad_swiglu, grad_bias = done.grad_embed, done.grad_swiglu, done.grad_bias
    mats_out = done.mats_out
    embed_out = adam_step(
        embeddings,
        embeddings_first,
        embeddings_second,
        grad_embed,
        embeddings_average,
        factor,
        TABLE_RATE,
    )
    swiglu_out = adam_step(
        swiglu_weights, swiglu_first, swiglu_second, grad_swiglu, swiglu_average, factor, LEARN_RATE
    )
    bias_out = adam_step(
        biases, biases_first, biases_second, grad_bias, biases_average, factor, TABLE_RATE
    )
    return (
        loss_sum,
        grad_norm,
        mats_out[0],
        embed_out[0],
        swiglu_out[0],
        bias_out[0],
        mats_out[1],
        embed_out[1],
        swiglu_out[1],
        bias_out[1],
        mats_out[2],
        embed_out[2],
        swiglu_out[2],
        bias_out[2],
        mats_out[3],
        embed_out[3],
        swiglu_out[3],
        bias_out[3],
        grad_bias * factor,
    )


def solution(mesh):
    placed = (
        P(("dp", "mlp"), None),
        P(("dp", "mlp"), None),
        P(("dp", "mlp"), None),
        P(("dp", "mlp")),
        P(("dp", "mlp")),
        P("dp", None),
        P(None, "dp"),
        P(None, "dp", "mlp"),
        P(),
        P("dp", None),
        P(None, "dp"),
        P(None, "dp", "mlp"),
        P(),
        P("dp", None),
        P(None, "dp"),
        P(None, "dp", "mlp"),
        P(),
        P("dp", None),
        P(None, "dp"),
        P(None, "dp", "mlp"),
        P(),
    )
    return jax.shard_map(
        on_device,
        mesh=mesh,
        in_specs=placed,
        out_specs=(
            P(),
            P(),
            P("dp", None),
            P(None, "dp"),
            P(None, "dp", "mlp"),
            P(),
            P("dp", None),
            P(None, "dp"),
            P(None, "dp", "mlp"),
            P(),
            P("dp", None),
            P(None, "dp"),
            P(None, "dp", "mlp"),
            P(),
            P("dp", None),
            P(None, "dp"),
            P(None, "dp", "mlp"),
            P(),
            P(),
        ),
        check_vma=False,
    )
```
